32 devices in a mesh: groups: 2 (over y), seq: 4 (over z), head: 4 (over x, core).
Axes of the slice: x: 2, y: 2, z: 4, core: 2. Of those that a mesh axis runs over, the one named last changes fastest.
Arguments:
- source_cache: bfloat16 [4, 8, 2048, 256], P('groups', 'head', 'seq'), parts along dimension 0, may hold values from -160 to 160
- kept_blocks: int32 [4, 8, 4], P('groups'), parts along dimension 0, may hold values from 0 to 15, as said below
- new_hidden: bfloat16 [4, 4, 8192], P('groups', None, 'seq'), parts along dimension 0, may hold values from -6 to 6
- norm_gain: bfloat16 [8192], P('seq'), may hold values from 0.099609375 to 1.8984375
- w_query: bfloat16 [8192, 8192], P('seq', 'head'), may hold values from -1 to 1
- w_keyval: bfloat16 [8192, 8, 256], P('seq', 'head'), may hold values from -4 to 4
- w_out: bfloat16 [8192, 8192], P('head', 'seq'), may hold values from -0.0625 to 0.0625
Outputs:
- kept_cache: bfloat16 [4, 8, 512, 256], P('head', ('groups', 'seq')), parts along dimension 1
- decoded: bfloat16 [4, 4, 8192], P('groups', None, 'seq'), parts along dimension 0
The draws below stay inside these ranges and needn't reach their ends.
There are 2 independent parts, one for each index of `groups`. The reference program is written for one: setup_inputs(seed, part) draws one part's arguments, and reference() takes and returns one part's arrays. A program takes and returns all parts, laid end to end along the dimension named above; an argument that names none is the same for every part. Nothing has to cross between parts.
Inputs may be any that keep to these rules, and one draw needn't show every extreme that they name: `kept_blocks`: each row is increasing; block b lies on index b // 4 of seq. At most 2 kept blocks of one request and head lie on one index of seq. The number of indices that hold exactly 2 of them differs between request-head pairs, from 1 to 2; in every request some pair reaches that largest number.
All inputs are finite; a program needn't handle non-finite values.
Results may differ from the reference program's by a relative error of at most 0.0065.
Values may be sent and summed in bfloat16 or wider, within the bound.
No kernel may reach another device: no remote copies, remote signals or barrier semaphores. Data moves between devices by JAX's collectives and lax.ppermute only.
A program may use at most 128 MiB of HBM per device.

```python
import math
import jax
import jax.numpy as jnp
from jax import lax

D = 8192
HEADS = 64
GROUP_ATTN_LANES = 8
HD = 128
QPK = 8
KVL = 2
BLK = 128
BLK_SRC = 4
KEEP_SRC = 1
MOST = 2
STEPS = 4
CALLER_TOTAL = 2
NBLK = 16
INPUT_SPAN = 2048
KEEP = 4
N_SEQ = 4
N_HEAD = 4


def mixed_entries(key, shape):
    normal_key = jax.random.fold_in(key, 0)
    normal_part = jnp.clip(jax.random.normal(normal_key, shape, jnp.float32), -6.0, 6.0)
    return normal_part


def shared_query(key):
    shape = (D, GROUP_ATTN_LANES, QPK, HD)
    return mixed_entries(key, shape) * D ** (-0.5)


def draw_w_query(key, part):
    shared = shared_query(key)
    return shared.reshape(D, HEADS * HD).astype(jnp.bfloat16)


def draw_w_keyval(key, part):
    shared = shared_query(key)
    key = jax.random.fold_in(key, 17)
    noise_key, value_key = jax.random.split(key, 2)
    pull_weight = (math.log(KEEP * BLK) + 1.0) * QPK / math.sqrt(HD)
    noise_part = mixed_entries(noise_key, (D, GROUP_ATTN_LANES, HD)) * D ** (-0.5)
    key_part = pull_weight * jnp.mean(shared, axis=2) + noise_part
    value_part = mixed_entries(value_key, (D, GROUP_ATTN_LANES, HD)) * D ** (-0.5)
    return jnp.concatenate([key_part, value_part], axis=-1).astype(jnp.bfloat16)


def draw_source_cache(key, part):
    key = jax.random.fold_in(key, 5)
    primary_seed_handle = jax.random.fold_in(key, 0)
    shape = (CALLER_TOTAL, GROUP_ATTN_LANES, INPUT_SPAN, 2 * HD)
    base_values = jnp.clip(jax.random.normal(primary_seed_handle, shape, jnp.float32), -6.0, 6.0)
    multiplier_entries = jnp.ones((CALLER_TOTAL, GROUP_ATTN_LANES, INPUT_SPAN, 1), jnp.float32)
    key_columns = jnp.arange(2 * HD) < HD
    multiplier = jnp.where(key_columns[None, None, None, :], 2.0 * multiplier_entries, 1.0)
    return (base_values * multiplier).astype(jnp.bfloat16)


def draw_kept_blocks(key, part):
    key = jax.random.fold_in(key, 11)
    key_rank, key_pick, key_count, key_widest = jax.random.split(key, 4)
    rank_scores = jax.random.randint(key_rank, (CALLER_TOTAL, GROUP_ATTN_LANES, N_SEQ), 0, 1 << 20) * N_SEQ + jnp.arange(N_SEQ)
    source_rank = jnp.argsort(jnp.argsort(rank_scores, axis=-1), axis=-1)
    surplus = MOST - KEEP_SRC
    widest_count = N_SEQ // (surplus + 1)
    heavy_count = jax.random.randint(key_count, (CALLER_TOTAL, GROUP_ATTN_LANES), 1, widest_count + 1)
    widest_head = jax.random.randint(key_widest, (CALLER_TOTAL, 1), 0, GROUP_ATTN_LANES)
    heavy_count = jnp.where(jnp.arange(GROUP_ATTN_LANES)[None, :] == widest_head, widest_count, heavy_count)
    heavy_edge = heavy_count[..., None]
    light_edge = heavy_edge + heavy_edge * surplus
    source_counts = jnp.where(source_rank < heavy_edge, MOST, jnp.where(source_rank < light_edge, KEEP_SRC - 1, KEEP_SRC))
    pick_scores = jax.random.randint(key_pick, (CALLER_TOTAL, GROUP_ATTN_LANES, N_SEQ, BLK_SRC), 0, 1 << 20) * BLK_SRC + jnp.arange(BLK_SRC)
    pick_rank = jnp.argsort(jnp.argsort(pick_scores, axis=-1), axis=-1)
    chosen = (pick_rank < source_counts[..., None]).reshape(CALLER_TOTAL, GROUP_ATTN_LANES, NBLK)
    ordered = jnp.where(chosen, 0, NBLK) + jnp.arange(NBLK)
    return jnp.sort(ordered, axis=-1)[..., :KEEP].astype(jnp.int32)


def shard_levels(own_key, dims, cuts, least, top_value):
    gain = 1.0
    for position, blocks in cuts:
        steps = jax.random.uniform(jax.random.fold_in(jax.random.fold_in(own_key, 6), position), (blocks,), jnp.float32, least / len(cuts), top_value / len(cuts))
        gain = gain * jnp.repeat(jnp.exp(steps), dims[position] // blocks).reshape((-1,) + (1,) * (len(dims) - 1 - position))
    return gain


def centred(key, shape, scale, limit, shards=(), held_as=jnp.bfloat16):
    gain = shard_levels(key, shape, shards, -0.22, 0.18) if shards else 1.0
    result = jax.random.normal(key, shape, jnp.float32) * scale * gain
    return jnp.minimum(jnp.maximum(result, -limit), limit).astype(held_as)


def setup_inputs(seed: int = 0, part: int = 0) -> dict:
    splits = jax.random.split(jax.random.key(seed), 8)
    part_keys = jax.random.split(jax.random.fold_in(splits[7], part), 8)
    return {
        "source_cache": draw_source_cache(jax.random.fold_in(jax.random.fold_in(splits[7], part), 71), part),
        "kept_blocks": draw_kept_blocks(jax.random.fold_in(jax.random.fold_in(splits[7], part), 71), part),
        "new_hidden": centred(part_keys[2], (CALLER_TOTAL, STEPS, D), 1.0, 6.0, ((2, 4),)),
        "norm_gain": jnp.clip(1.0 + 0.18 * jax.random.normal(splits[3], (D,), jnp.float32), 0.099609375, 1.8984375).astype(jnp.bfloat16),
        "w_query": draw_w_query(jax.random.fold_in(splits[7], 71), part),
        "w_keyval": draw_w_keyval(jax.random.fold_in(splits[7], 71), part),
        "w_out": centred(splits[6], (HEADS * HD, D), (HEADS * HD) ** -0.5, 0.0625, ((0, 4), (1, 4))),
    }


rope_base = 500000.0

def rotate(tensor, angles):
    half_dim = tensor.shape[-1] // 2
    lower_half = tensor[..., :half_dim]
    upper_half = tensor[..., half_dim:]
    cosine = jnp.cos(angles)
    sine_part = jnp.sin(angles)
    return jnp.concatenate([lower_half * cosine - upper_half * sine_part, upper_half * cosine + lower_half * sine_part], axis=-1)

def pick_rows(source_table, row_index):
    return source_table[row_index]

def reference(source_cache, kept_blocks, new_hidden, norm_gain, w_query, w_keyval, w_out):
    hidden = new_hidden.astype(jnp.float32)
    inverse_norm = lax.rsqrt(lax.optimization_barrier(jnp.mean(hidden * hidden, axis=-1)) + 1e-05)
    scaled = (hidden * norm_gain.astype(jnp.float32)).astype(jnp.bfloat16).reshape(CALLER_TOTAL * STEPS, D)
    sum_query = jnp.dot(scaled, w_query, preferred_element_type=jnp.float32)
    sum_keyval = jnp.dot(scaled, w_keyval.reshape(D, GROUP_ATTN_LANES * 2 * HD), preferred_element_type=jnp.float32)
    positions = INPUT_SPAN + jnp.arange(STEPS, dtype=jnp.float32)
    frequency = rope_base ** (-jnp.arange(HD // 2, dtype=jnp.float32) * 2.0 / HD)
    angles = positions[:, None] * frequency[None, :]
    norm_five = inverse_norm[:, :, None, None, None]
    queries = rotate(sum_query.reshape(CALLER_TOTAL, STEPS, GROUP_ATTN_LANES, QPK, HD) * norm_five, angles[:, None, None, :]).astype(jnp.bfloat16)
    keyval = sum_keyval.reshape(CALLER_TOTAL, STEPS, GROUP_ATTN_LANES, 2, HD) * norm_five
    new_key = rotate(keyval[:, :, :, 0], angles[:, None, :]).astype(jnp.bfloat16)
    new_value = keyval[:, :, :, 1].astype(jnp.bfloat16)
    blocks = source_cache.reshape(CALLER_TOTAL, GROUP_ATTN_LANES, NBLK, BLK, 2 * HD)
    kept = jax.vmap(jax.vmap(pick_rows))(blocks, kept_blocks).reshape(CALLER_TOTAL, GROUP_ATTN_LANES, KEEP * BLK, 2 * HD)
    kept_cache = kept.reshape(CALLER_TOTAL, N_HEAD, KVL, KEEP * BLK, 2 * HD).transpose(1, 0, 2, 3, 4).reshape(N_HEAD, CALLER_TOTAL * KVL, KEEP * BLK, 2 * HD)
    pair_queries = queries.transpose(0, 2, 1, 3, 4).reshape(CALLER_TOTAL, GROUP_ATTN_LANES, STEPS * QPK, HD).astype(jnp.float32)
    cached_keys = kept[..., :HD].astype(jnp.float32)
    cached_values = kept[..., HD:].astype(jnp.float32)
    pair_keys = new_key.transpose(0, 2, 1, 3).astype(jnp.float32)
    pair_values = new_value.transpose(0, 2, 1, 3).astype(jnp.float32)
    score_scale = 1.0 / jnp.sqrt(jnp.float32(HD))
    score_kept = jnp.einsum('rgqh,rgkh->rgqk', pair_queries, cached_keys) * score_scale
    score_new = jnp.einsum('rgqh,rgth->rgqt', pair_queries, pair_keys) * score_scale
    row_step = jnp.arange(STEPS * QPK) // QPK
    allowed = jnp.arange(STEPS)[None, :] <= row_step[:, None]
    score_new = jnp.where(allowed, score_new, -jnp.inf)
    row_max = jnp.maximum(lax.optimization_barrier(jnp.max(score_kept, axis=-1)), lax.optimization_barrier(jnp.max(score_new, axis=-1)))[..., None]
    weight_kept = jnp.exp(score_kept - row_max)
    weight_new = jnp.exp(score_new - row_max)
    denominator = lax.optimization_barrier(jnp.sum(weight_kept, axis=-1)) + lax.optimization_barrier(jnp.sum(weight_new, axis=-1))
    numerator = jnp.einsum('rgqk,rgkh->rgqh', weight_kept.astype(jnp.bfloat16).astype(jnp.float32), cached_values)
    numerator = numerator + jnp.einsum('rgqt,rgth->rgqh', weight_new.astype(jnp.bfloat16).astype(jnp.float32), pair_values)
    attended = (numerator / denominator[..., None]).astype(jnp.bfloat16)
    merged = attended.reshape(CALLER_TOTAL, GROUP_ATTN_LANES, STEPS, QPK, HD).transpose(0, 2, 1, 3, 4).reshape(CALLER_TOTAL * STEPS, HEADS * HD)
    projected = jnp.dot(merged, w_out, preferred_element_type=jnp.float32).reshape(CALLER_TOTAL, STEPS, D)
    decoded = (hidden + projected).astype(jnp.bfloat16)
    return (kept_cache, decoded)
```

```python
import functools
import math

import jax
import jax.numpy as jnp
import numpy as np
from jax import lax
from jax.experimental import pallas as pl
from jax.experimental.pallas import tpu as pltpu
from jax.sharding import PartitionSpec as P

D = 8192
HD = 128
QPK = 8
BLK = 128
MOST = 2
ROPE_BASE = 500000.0
EPS = 1e-05

CONTRACT_LAST = (((1,), (1,)), ((), ()))


def rope_tables(prompt_length, step_count):
    positions = prompt_length + np.arange(2 * step_count) % step_count
    frequency = ROPE_BASE ** (-np.arange(HD // 2, dtype=np.float64) * 2.0 / HD)
    angles = positions[:, None] * frequency[None, :]
    cosine = np.concatenate([np.cos(angles)] * 2, axis=1)
    sine = np.concatenate([-np.sin(angles), np.sin(angles)], axis=1)
    return cosine.astype(np.float32), sine.astype(np.float32)


def rotate(v, cosine, sine):
    swapped = jnp.concatenate([v[..., HD // 2 :], v[..., : HD // 2]], axis=-1)
    return v * cosine + swapped * sine


def pick_kernel(kept_ref, cache_ref, out_ref, sem):
    requests, heads_local, source_tokens, _ = cache_ref.shape
    source_blocks = source_tokens // BLK
    kept_count = kept_ref.shape[2]
    me = lax.axis_index("seq")
    first_head = lax.axis_index("head") * heads_local

    def pair_body(pair, carry):
        request = lax.div(pair, heads_local)
        local = lax.rem(pair, heads_local)
        head = first_head + local

        def count(k, total):
            block = kept_ref[request, head, k]
            return total + (block < me * source_blocks).astype(jnp.int32)

        start = lax.fori_loop(0, kept_count, count, jnp.int32(0), unroll=kept_count <= 8)
        for slot in range(MOST):
            rank = jnp.minimum(start + slot, kept_count - 1)
            block = kept_ref[request, head, rank] - me * source_blocks
            block = jnp.clip(block, 0, source_blocks - 1)
            rows = pl.ds(pl.multiple_of(block * BLK, BLK), BLK)
            pltpu.make_async_copy(
                cache_ref.at[request, local, rows], out_ref.at[pair, slot], sem
            ).start()
        return carry

    pair_count = requests * heads_local
    lax.fori_loop(0, pair_count, pair_body, 0, unroll=pair_count <= 8)
    pltpu.make_async_copy(out_ref, out_ref, sem).wait()


def pick(kept_blocks, source_cache):
    requests, heads_local, _, row_width = source_cache.shape
    pair_count = requests * heads_local
    return pl.pallas_call(
        pick_kernel,
        out_shape=jax.ShapeDtypeStruct((pair_count, MOST, BLK, row_width), jnp.bfloat16),
        in_specs=[
            pl.BlockSpec(memory_space=pltpu.SMEM),
            pl.BlockSpec(memory_space=pl.ANY),
        ],
        out_specs=pl.BlockSpec(memory_space=pl.ANY),
        scratch_shapes=[pltpu.SemaphoreType.DMA],
        name="pick_blocks",
    )(kept_blocks, source_cache)


def chunk_copies(w_ref, buffer, sems, rows):
    return [
        pltpu.make_async_copy(
            w_ref.at[pl.ds(i * rows, rows)], buffer.at[pl.ds(i * rows, rows)], sems.at[i]
        )
        for i in range(w_ref.shape[0] // rows)
    ]


def project_kernel(rows, hidden_ref, gain_ref, wq_ref, wkv_ref, out_ref, wq, wkv, sem_q, sem_kv):
    requests, step_count, width = hidden_ref.shape
    copies_q = chunk_copies(wq_ref, wq, sem_q, rows)
    copies_kv = chunk_copies(wkv_ref, wkv, sem_kv, rows)
    for copy_q, copy_kv in zip(copies_q, copies_kv):
        copy_q.start()
        copy_kv.start()
    hidden = jnp.concatenate(
        [hidden_ref[r].astype(jnp.float32) for r in range(requests)], axis=0
    )
    square = jnp.sum(hidden * hidden, axis=1, keepdims=True)
    scaled = (hidden * gain_ref[...].astype(jnp.float32)).astype(jnp.bfloat16)
    query = jnp.zeros((requests * step_count, wq.shape[1]), jnp.float32)
    keyval = jnp.zeros((requests * step_count, wkv.shape[1]), jnp.float32)
    for i, (copy_q, copy_kv) in enumerate(zip(copies_q, copies_kv)):
        piece = scaled[:, i * rows : (i + 1) * rows]
        here = pl.ds(i * rows, rows)
        copy_q.wait()
        query += jnp.dot(piece, wq[here], preferred_element_type=jnp.float32)
        copy_kv.wait()
        keyval += jnp.dot(piece, wkv[here], preferred_element_type=jnp.float32)
    heads_local = out_ref.shape[0] // requests
    for r in range(requests):
        steps = slice(r * step_count, (r + 1) * step_count)
        square_rows = jnp.broadcast_to(square[steps], (step_count, HD))
        for l in range(heads_local):
            pair = r * heads_local + l
            pieces = [
                query[steps, (l * QPK + h) * HD : (l * QPK + h + 1) * HD] for h in range(QPK)
            ]
            pieces += [
                keyval[steps, (l * 2 + h) * HD : (l * 2 + h + 1) * HD] for h in range(2)
            ]
            pieces += [square_rows, square_rows]
            for j, piece in enumerate(pieces):
                out_ref[pair, j * step_count : (j + 1) * step_count, :] = piece


def project(new_hidden, norm_gain, w_query, w_keyval, pair_count):
    requests, step_count, width = new_hidden.shape
    rows = min(256, width)
    chunks = width // rows
    return pl.pallas_call(
        functools.partial(project_kernel, rows),
        out_shape=jax.ShapeDtypeStruct((pair_count, (QPK + 4) * step_count, HD), jnp.float32),
        in_specs=[
            pl.BlockSpec(memory_space=pltpu.VMEM),
            pl.BlockSpec(memory_space=pltpu.VMEM),
            pl.BlockSpec(memory_space=pl.ANY),
            pl.BlockSpec(memory_space=pl.ANY),
        ],
        out_specs=pl.BlockSpec(memory_space=pltpu.VMEM),
        scratch_shapes=[
            pltpu.VMEM(w_query.shape, jnp.bfloat16),
            pltpu.VMEM(w_keyval.shape, jnp.bfloat16),
            pltpu.SemaphoreType.DMA((chunks,)),
            pltpu.SemaphoreType.DMA((chunks,)),
        ],
        compiler_params=pltpu.CompilerParams(vmem_limit_bytes=24 * 1024 * 1024),
        cost_estimate=pl.CostEstimate(
            flops=2 * requests * step_count * width * (w_query.shape[1] + w_keyval.shape[1]),
            bytes_accessed=2 * width * (w_query.shape[1] + w_keyval.shape[1]),
            transcendentals=0,
        ),
        name="project",
    )(new_hidden, norm_gain, w_query, w_keyval)


def attend_kernel(
    source_blocks, heads_local, kept_ref, blocks_ref, parts_ref, cos_ref, sin_ref,
    cache_ref, attended_ref, kept, sem_in, sem_out,
):
    kept_count = kept_ref.shape[2]
    step_count = cos_ref.shape[0] // 2
    me = lax.axis_index("seq")
    request = lax.div(me, heads_local)
    head = lax.axis_index("head") * heads_local + lax.rem(me, heads_local)

    def start_copy(k, carry):
        previous, slot = carry
        source = lax.div(kept_ref[request, head, k], source_blocks)
        slot = jnp.where(source == previous, jnp.minimum(slot + 1, MOST - 1), 0)
        rows = pl.ds(pl.multiple_of(k * BLK, BLK), BLK)
        pltpu.make_async_copy(blocks_ref.at[source, slot], kept.at[rows], sem_in).start()
        return source, slot

    lax.fori_loop(
        0, kept_count, start_copy, (jnp.int32(-1), jnp.int32(0)), unroll=kept_count <= 8
    )
    total = jnp.sum(parts_ref[...], axis=0)
    query_rows = QPK * step_count
    inverse = lax.rsqrt(total[query_rows + 2 * step_count :] * (1.0 / D) + EPS)
    cosine, sine = cos_ref[...], sin_ref[...]
    query = total[:query_rows].reshape(QPK // 2, 2 * step_count, HD) * inverse[None]
    query = rotate(query, cosine[None], sine[None]).reshape(query_rows, HD).astype(jnp.bfloat16)
    keyval = total[query_rows : query_rows + 2 * step_count] * inverse
    new_key = rotate(keyval, cosine, sine).astype(jnp.bfloat16)
    new_value = jnp.concatenate([keyval[step_count:], keyval[:step_count]], axis=0)
    new_value = new_value.astype(jnp.bfloat16)
    scale = 1.0 / math.sqrt(HD)
    score_new = (
        lax.dot_general(query, new_key, CONTRACT_LAST, preferred_element_type=jnp.float32) * scale
    )
    row = lax.broadcasted_iota(jnp.int32, score_new.shape, 0)
    column = lax.broadcasted_iota(jnp.int32, score_new.shape, 1)
    score_new = jnp.where(column <= lax.rem(row, step_count), score_new, -jnp.inf)

    pltpu.make_async_copy(kept, kept, sem_in).wait()
    out_copy = pltpu.make_async_copy(kept, cache_ref.at[0, 0], sem_out)
    out_copy.start()
    score_kept = (
        lax.dot_general(query, kept[:, :HD], CONTRACT_LAST, preferred_element_type=jnp.float32)
        * scale
    )
    row_max = jnp.maximum(
        jnp.max(score_kept, axis=1, keepdims=True), jnp.max(score_new, axis=1, keepdims=True)
    )
    weight_kept = jnp.exp(score_kept - row_max)
    weight_new = jnp.exp(score_new - row_max)
    denominator = jnp.sum(weight_kept, axis=1, keepdims=True) + jnp.sum(
        weight_new, axis=1, keepdims=True
    )
    numerator = jnp.dot(
        weight_kept.astype(jnp.bfloat16), kept[:, HD:], preferred_element_type=jnp.float32
    )
    numerator += jnp.dot(
        weight_new.astype(jnp.bfloat16), new_value, preferred_element_type=jnp.float32
    )
    attended = (numerator / denominator).astype(jnp.bfloat16)
    for i in range(attended_ref.shape[0]):
        attended_ref[i] = attended
    out_copy.wait()


def attend(kept_blocks, blocks, parts, source_blocks, heads_local, step_count, seq_count):
    kept_count = kept_blocks.shape[2]
    row_width = blocks.shape[-1]
    cosine, sine = rope_tables(source_blocks * BLK * seq_count, step_count)
    return pl.pallas_call(
        functools.partial(attend_kernel, source_blocks, heads_local),
        out_shape=(
            jax.ShapeDtypeStruct((1, 1, kept_count * BLK, row_width), jnp.bfloat16),
            jax.ShapeDtypeStruct((seq_count, QPK * step_count, HD), jnp.bfloat16),
        ),
        in_specs=[
            pl.BlockSpec(memory_space=pltpu.SMEM),
            pl.BlockSpec(memory_space=pl.ANY),
            pl.BlockSpec(memory_space=pltpu.VMEM),
            pl.BlockSpec(memory_space=pltpu.VMEM),
            pl.BlockSpec(memory_space=pltpu.VMEM),
        ],
        out_specs=(
            pl.BlockSpec(memory_space=pl.ANY),
            pl.BlockSpec(memory_space=pltpu.VMEM),
        ),
        scratch_shapes=[
            pltpu.VMEM((kept_count * BLK, row_width), jnp.bfloat16),
            pltpu.SemaphoreType.DMA,
            pltpu.SemaphoreType.DMA,
        ],
        compiler_params=pltpu.CompilerParams(vmem_limit_bytes=24 * 1024 * 1024),
        name="attend",
    )(kept_blocks, blocks, parts, jnp.asarray(cosine), jnp.asarray(sine))


def output_kernel(rows, heads_local, gathered_ref, w_ref, out_ref, w, sems):
    copies = chunk_copies(w_ref, w, sems, rows)
    for copy in copies:
        copy.start()
    pair_count, query_rows, _ = gathered_ref.shape
    step_count = query_rows // QPK
    requests = pair_count // heads_local
    total = jnp.zeros((requests * step_count, w.shape[1]), jnp.float32)
    pairs = [gathered_ref[p].astype(jnp.float32) for p in range(pair_count)]
    for i, copy in enumerate(copies):
        pieces = []
        for column in range(i * rows // HD, (i + 1) * rows // HD):
            l, h = divmod(column, QPK)
            pieces.append(
                jnp.concatenate(
                    [
                        pairs[r * heads_local + l][h * step_count : (h + 1) * step_count]
                        for r in range(requests)
                    ],
                    axis=0,
                )
            )
        merged = jnp.concatenate(pieces, axis=1).astype(jnp.bfloat16)
        copy.wait()
        total += jnp.dot(
            merged, w[pl.ds(i * rows, rows)], preferred_element_type=jnp.float32
        )
    for i in range(out_ref.shape[0]):
        out_ref[i] = total


def output(gathered, w_out, heads_local, head_count):
    pair_count, query_rows, _ = gathered.shape
    total_rows = pair_count // heads_local * (query_rows // QPK)
    rows = 256
    return pl.pallas_call(
        functools.partial(output_kernel, rows, heads_local),
        out_shape=jax.ShapeDtypeStruct((head_count, total_rows, w_out.shape[1]), jnp.float32),
        in_specs=[
            pl.BlockSpec(memory_space=pltpu.VMEM),
            pl.BlockSpec(memory_space=pl.ANY),
        ],
        out_specs=pl.BlockSpec(memory_space=pltpu.VMEM),
        scratch_shapes=[
            pltpu.VMEM(w_out.shape, jnp.bfloat16),
            pltpu.SemaphoreType.DMA((w_out.shape[0] // rows,)),
        ],
        compiler_params=pltpu.CompilerParams(vmem_limit_bytes=24 * 1024 * 1024),
        name="output_projection",
    )(gathered, w_out)


def shards(source_cache, kept_blocks, new_hidden, norm_gain, w_query, w_keyval, w_out):
    seq_count = lax.axis_size("seq")
    head_count = lax.axis_size("head")
    requests, heads_local, source_tokens, _ = source_cache.shape
    _, step_count, width = new_hidden.shape
    pair_count = requests * heads_local

    outgoing = pick(kept_blocks, source_cache)
    blocks = lax.all_to_all(outgoing, "seq", split_axis=0, concat_axis=0, tiled=True)
    parts = project(
        new_hidden, norm_gain.reshape(1, width), w_query, w_keyval.reshape(width, -1), pair_count
    )
    parts = lax.all_to_all(parts, "seq", split_axis=0, concat_axis=0, tiled=True)
    kept_cache, attended = attend(
        kept_blocks, blocks, parts, source_tokens // BLK, heads_local, step_count, seq_count
    )
    gathered = lax.all_to_all(attended, "seq", split_axis=0, concat_axis=0, tiled=True)
    terms = output(gathered, w_out, heads_local, head_count)
    terms = lax.all_to_all(terms, "head", split_axis=0, concat_axis=0, tiled=True)
    summed = jnp.sum(terms, axis=0).reshape(requests, step_count, width)
    decoded = (new_hidden.astype(jnp.float32) + summed).astype(jnp.bfloat16)
    return (kept_cache, decoded)


def solution(mesh):
    in_specs = (
        P("groups", "head", "seq", None),
        P("groups", None, None),
        P("groups", None, "seq"),
        P("seq"),
        P("seq", "head"),
        P("seq", "head", None),
        P("head", "seq"),
    )
    out_specs = (P("head", ("groups", "seq"), None, None), P("groups", None, "seq"))
    return jax.shard_map(shards, mesh=mesh, in_specs=in_specs, out_specs=out_specs, check_vma=False)
```

```python
import functools
import math

import jax
import jax.numpy as jnp
import numpy as np
from jax import lax
from jax.experimental import pallas as pl
from jax.experimental.pallas import tpu as pltpu
from jax.sharding import PartitionSpec as P

D = 8192
HD = 128
QPK = 8
BLK = 128
MOST = 2
ROPE_BASE = 500000.0
EPS = 1e-05

CONTRACT_LAST = (((1,), (1,)), ((), ()))


def rope_tables(prompt_length, step_count):
    positions = prompt_length + np.arange(2 * step_count) % step_count
    frequency = ROPE_BASE ** (-np.arange(HD // 2, dtype=np.float64) * 2.0 / HD)
    angles = positions[:, None] * frequency[None, :]
    cosine = np.concatenate([np.cos(angles)] * 2, axis=1)
    sine = np.concatenate([-np.sin(angles), np.sin(angles)], axis=1)
    return cosine.astype(np.float32), sine.astype(np.float32)


def rotate(v, cosine, sine):
    swapped = jnp.concatenate([v[..., HD // 2 :], v[..., : HD // 2]], axis=-1)
    return v * cosine + swapped * sine


def is_direct(count):
    return count <= 8 and count & (count - 1) == 0


def exchange(outgoing, axis):
    if len(outgoing) == 1:
        return [lax.all_to_all(outgoing[0], axis, split_axis=0, concat_axis=0, tiled=True)]
    count = len(outgoing)
    return [outgoing[0]] + [
        lax.ppermute(outgoing[k], axis, [(i, i ^ k) for i in range(count)])
        for k in range(1, count)
    ]


def pick_kernel(kept_ref, cache_ref, *refs):
    outs, sem = refs[:-1], refs[-1]
    requests, heads_local, source_tokens, _ = cache_ref.shape
    source_blocks = source_tokens // BLK
    kept_count = kept_ref.shape[2]
    me = lax.axis_index("seq")
    first_head = lax.axis_index("head") * heads_local

    def copy_pair(pair, out_ref):
        request = lax.div(pair, heads_local)
        local = lax.rem(pair, heads_local)
        head = first_head + local

        def count(k, total):
            block = kept_ref[request, head, k]
            return total + (block < me * source_blocks).astype(jnp.int32)

        start = lax.fori_loop(0, kept_count, count, jnp.int32(0), unroll=kept_count <= 8)
        for slot in range(MOST):
            rank = jnp.minimum(start + slot, kept_count - 1)
            block = kept_ref[request, head, rank] - me * source_blocks
            block = jnp.clip(block, 0, source_blocks - 1)
            rows = pl.ds(pl.multiple_of(block * BLK, BLK), BLK)
            pltpu.make_async_copy(
                cache_ref.at[request, local, rows], out_ref.at[slot], sem
            ).start()

    pair_count = requests * heads_local
    if len(outs) == 1:

        def pair_body(pair, carry):
            copy_pair(pair, outs[0].at[pair])
            return carry

        lax.fori_loop(0, pair_count, pair_body, 0)
    else:
        for offset, out_ref in enumerate(outs):
            copy_pair(jnp.bitwise_xor(me, offset), out_ref)
    for out_ref in outs:
        pltpu.make_async_copy(out_ref, out_ref, sem).wait()


def pick(kept_blocks, source_cache):
    requests, heads_local, _, row_width = source_cache.shape
    pair_count = requests * heads_local
    block = (MOST, BLK, row_width)
    if is_direct(pair_count):
        shapes = [jax.ShapeDtypeStruct(block, jnp.bfloat16)] * pair_count
    else:
        shapes = [jax.ShapeDtypeStruct((pair_count,) + block, jnp.bfloat16)]
    return pl.pallas_call(
        pick_kernel,
        out_shape=shapes,
        in_specs=[
            pl.BlockSpec(memory_space=pltpu.SMEM),
            pl.BlockSpec(memory_space=pl.ANY),
        ],
        out_specs=[pl.BlockSpec(memory_space=pltpu.VMEM)] * len(shapes),
        scratch_shapes=[pltpu.SemaphoreType.DMA],
        compiler_params=pltpu.CompilerParams(vmem_limit_bytes=12 * 1024 * 1024),
        name="pick_blocks",
    )(kept_blocks, source_cache)


def project_kernel(hidden_ref, gain_ref, wq_ref, wkv_ref, *outs):
    requests, step_count, width = hidden_ref.shape
    hidden = jnp.concatenate(
        [hidden_ref[r].astype(jnp.float32) for r in range(requests)], axis=0
    )
    square = jnp.sum(hidden * hidden, axis=1, keepdims=True)
    scaled = (hidden * gain_ref[...].astype(jnp.float32)).astype(jnp.bfloat16)
    query = jnp.dot(scaled, wq_ref[...], preferred_element_type=jnp.float32)
    keyval = jnp.dot(scaled, wkv_ref[...], preferred_element_type=jnp.float32)
    heads_local = wkv_ref.shape[1] // (2 * HD)
    me = lax.axis_index("seq")

    def write_pair(out_ref, pieces):
        for j, piece in enumerate(pieces):
            out_ref[j * step_count : (j + 1) * step_count, :] = piece

    for r in range(requests):
        steps = slice(r * step_count, (r + 1) * step_count)
        square_rows = jnp.broadcast_to(square[steps], (step_count, HD))
        for l in range(heads_local):
            pair = r * heads_local + l
            pieces = [
                query[steps, (l * QPK + h) * HD : (l * QPK + h + 1) * HD] for h in range(QPK)
            ]
            pieces += [
                keyval[steps, (l * 2 + h) * HD : (l * 2 + h + 1) * HD] for h in range(2)
            ]
            pieces += [square_rows, square_rows]
            if len(outs) == 1:
                write_pair(outs[0].at[pair], pieces)
            else:
                for offset, out_ref in enumerate(outs):
                    pl.when(jnp.bitwise_xor(me, offset) == pair)(
                        functools.partial(write_pair, out_ref, pieces)
                    )


def project(new_hidden, norm_gain, w_query, w_keyval, pair_count):
    requests, step_count, width = new_hidden.shape
    block = ((QPK + 4) * step_count, HD)
    if is_direct(pair_count):
        shapes = [jax.ShapeDtypeStruct(block, jnp.float32)] * pair_count
    else:
        shapes = [jax.ShapeDtypeStruct((pair_count,) + block, jnp.float32)]
    return pl.pallas_call(
        project_kernel,
        out_shape=shapes,
        in_specs=[pl.BlockSpec(memory_space=pltpu.VMEM)] * 4,
        out_specs=[pl.BlockSpec(memory_space=pltpu.VMEM)] * len(shapes),
        compiler_params=pltpu.CompilerParams(vmem_limit_bytes=24 * 1024 * 1024),
        cost_estimate=pl.CostEstimate(
            flops=2 * requests * step_count * width * (w_query.shape[1] + w_keyval.shape[1]),
            bytes_accessed=2 * width * (w_query.shape[1] + w_keyval.shape[1]),
            transcendentals=0,
        ),
        name="project",
    )(
        new_hidden,
        norm_gain,
        pltpu.with_memory_space_constraint(w_query, pltpu.VMEM),
        pltpu.with_memory_space_constraint(w_keyval, pltpu.VMEM),
    )


def attend_kernel(source_blocks, heads_local, seq_count, kept_ref, cos_ref, sin_ref, *refs):
    arrivals = (len(refs) - 5) // 2
    blocks_refs, parts_refs = refs[:arrivals], refs[arrivals : 2 * arrivals]
    cache_ref, attended_ref, kept, sem_in, sem_out = refs[2 * arrivals :]
    kept_count = kept_ref.shape[2]
    step_count = cos_ref.shape[0] // 2
    me = lax.axis_index("seq")
    request = lax.div(me, heads_local)
    head = lax.axis_index("head") * heads_local + lax.rem(me, heads_local)

    def start_copy(k, carry):
        previous, slot = carry
        source = lax.div(kept_ref[request, head, k], source_blocks)
        slot = jnp.where(source == previous, jnp.minimum(slot + 1, MOST - 1), 0)
        rows = pl.ds(pl.multiple_of(k * BLK, BLK), BLK)
        if arrivals == 1:
            pltpu.make_async_copy(
                blocks_refs[0].at[source, slot], kept.at[rows], sem_in
            ).start()
        else:
            for offset, blocks_ref in enumerate(blocks_refs):
                pl.when(jnp.bitwise_xor(me, offset) == source)(
                    pltpu.make_async_copy(blocks_ref.at[slot], kept.at[rows], sem_in).start
                )
        return source, slot

    lax.fori_loop(
        0, kept_count, start_copy, (jnp.int32(-1), jnp.int32(0)), unroll=kept_count <= 8
    )
    if arrivals == 1:
        total = jnp.sum(parts_refs[0][...], axis=0)
    else:
        total = sum(ref[...] for ref in parts_refs)
    query_rows = QPK * step_count
    inverse = lax.rsqrt(total[query_rows + 2 * step_count :] * (1.0 / D) + EPS)
    cosine, sine = cos_ref[...], sin_ref[...]
    query = total[:query_rows].reshape(QPK // 2, 2 * step_count, HD) * inverse[None]
    query = rotate(query, cosine[None], sine[None]).reshape(query_rows, HD).astype(jnp.bfloat16)
    keyval = total[query_rows : query_rows + 2 * step_count] * inverse
    new_key = rotate(keyval, cosine, sine).astype(jnp.bfloat16)
    new_value = jnp.concatenate([keyval[step_count:], keyval[:step_count]], axis=0)
    new_value = new_value.astype(jnp.bfloat16)
    scale = 1.0 / math.sqrt(HD)
    score_new = (
        lax.dot_general(query, new_key, CONTRACT_LAST, preferred_element_type=jnp.float32) * scale
    )
    row = lax.broadcasted_iota(jnp.int32, score_new.shape, 0)
    column = lax.broadcasted_iota(jnp.int32, score_new.shape, 1)
    score_new = jnp.where(column <= lax.rem(row, step_count), score_new, -jnp.inf)

    pltpu.make_async_copy(kept, kept, sem_in).wait()
    out_copy = pltpu.make_async_copy(kept, cache_ref.at[0, 0], sem_out)
    out_copy.start()
    score_kept = (
        lax.dot_general(query, kept[:, :HD], CONTRACT_LAST, preferred_element_type=jnp.float32)
        * scale
    )
    row_max = jnp.maximum(
        jnp.max(score_kept, axis=1, keepdims=True), jnp.max(score_new, axis=1, keepdims=True)
    )
    weight_kept = jnp.exp(score_kept - row_max)
    weight_new = jnp.exp(score_new - row_max)
    denominator = jnp.sum(weight_kept, axis=1, keepdims=True) + jnp.sum(
        weight_new, axis=1, keepdims=True
    )
    numerator = jnp.dot(
        weight_kept.astype(jnp.bfloat16), kept[:, HD:], preferred_element_type=jnp.float32
    )
    numerator += jnp.dot(
        weight_new.astype(jnp.bfloat16), new_value, preferred_element_type=jnp.float32
    )
    attended = (numerator / denominator).astype(jnp.bfloat16)
    if arrivals == 1:
        for i in range(attended_ref.shape[0]):
            attended_ref[i] = attended
    else:
        attended_ref[...] = attended
    out_copy.wait()


def attend(kept_blocks, blocks, parts, source_blocks, heads_local, step_count, seq_count):
    kept_count = kept_blocks.shape[2]
    row_width = blocks[0].shape[-1]
    cosine, sine = rope_tables(source_blocks * BLK * seq_count, step_count)
    shape = (QPK * step_count, HD)
    if len(blocks) == 1:
        shape = (seq_count,) + shape
    vmem = pl.BlockSpec(memory_space=pltpu.VMEM)
    anywhere = pl.BlockSpec(memory_space=pl.ANY)
    kept_cache, attended = pl.pallas_call(
        functools.partial(attend_kernel, source_blocks, heads_local, seq_count),
        out_shape=(
            jax.ShapeDtypeStruct((1, 1, kept_count * BLK, row_width), jnp.bfloat16),
            jax.ShapeDtypeStruct(shape, jnp.bfloat16),
        ),
        in_specs=[pl.BlockSpec(memory_space=pltpu.SMEM), vmem, vmem]
        + [anywhere] * len(blocks)
        + [vmem] * len(parts),
        out_specs=(anywhere, vmem),
        scratch_shapes=[
            pltpu.VMEM((kept_count * BLK, row_width), jnp.bfloat16),
            pltpu.SemaphoreType.DMA,
            pltpu.SemaphoreType.DMA,
        ],
        compiler_params=pltpu.CompilerParams(vmem_limit_bytes=24 * 1024 * 1024),
        name="attend",
    )(kept_blocks, jnp.asarray(cosine), jnp.asarray(sine), *blocks, *parts)
    return kept_cache, [attended] * len(blocks) if len(blocks) == 1 else [attended] * seq_count


def output_kernel(heads_local, w_ref, *refs):
    gathered_refs, out_ref = refs[:-1], refs[-1]
    query_rows = gathered_refs[0].shape[-2]
    step_count = query_rows // QPK
    if len(gathered_refs) == 1:
        pair_count = gathered_refs[0].shape[0]
        pairs = [gathered_refs[0][p].astype(jnp.float32) for p in range(pair_count)]
    else:
        pair_count = len(gathered_refs)
        me = lax.axis_index("seq")
        arrived = [ref[...].astype(jnp.float32) for ref in gathered_refs]
        pairs = arrived
        bit = 1
        while bit < pair_count:
            swap = jnp.bitwise_and(me, bit) != 0
            pairs = [jnp.where(swap, pairs[p ^ bit], pairs[p]) for p in range(pair_count)]
            bit *= 2
    requests = pair_count // heads_local
    pieces = []
    for l in range(heads_local):
        for h in range(QPK):
            rows = slice(h * step_count, (h + 1) * step_count)
            pieces.append(
                jnp.concatenate(
                    [pairs[r * heads_local + l][rows] for r in range(requests)], axis=0
                )
            )
    merged = jnp.concatenate(pieces, axis=1).astype(jnp.bfloat16)
    total = jnp.dot(merged, w_ref[...], preferred_element_type=jnp.float32)
    if len(out_ref.shape) == 2:
        out_ref[...] = total
    else:
        for i in range(out_ref.shape[0]):
            out_ref[i] = total


def output(gathered, w_out, heads_local, pair_count, head_count):
    query_rows = gathered[0].shape[-2]
    total_rows = pair_count // heads_local * (query_rows // QPK)
    shape = (total_rows, w_out.shape[1])
    if not is_direct(head_count):
        shape = (head_count,) + shape
    vmem = pl.BlockSpec(memory_space=pltpu.VMEM)
    terms = pl.pallas_call(
        functools.partial(output_kernel, heads_local),
        out_shape=jax.ShapeDtypeStruct(shape, jnp.float32),
        in_specs=[vmem] * (1 + len(gathered)),
        out_specs=vmem,
        compiler_params=pltpu.CompilerParams(vmem_limit_bytes=24 * 1024 * 1024),
        name="output_projection",
    )(pltpu.with_memory_space_constraint(w_out, pltpu.VMEM), *gathered)
    return [terms] * (head_count if is_direct(head_count) else 1)


def shards(source_cache, kept_blocks, new_hidden, norm_gain, w_query, w_keyval, w_out):
    seq_count = lax.axis_size("seq")
    head_count = lax.axis_size("head")
    requests, heads_local, source_tokens, _ = source_cache.shape
    _, step_count, width = new_hidden.shape
    pair_count = requests * heads_local

    blocks = exchange(pick(kept_blocks, source_cache), "seq")
    parts = project(
        new_hidden, norm_gain.reshape(1, width), w_query, w_keyval.reshape(width, -1), pair_count
    )
    parts = exchange(parts, "seq")
    kept_cache, attended = attend(
        kept_blocks, blocks, parts, source_tokens // BLK, heads_local, step_count, seq_count
    )
    gathered = exchange(attended, "seq")
    terms = exchange(output(gathered, w_out, heads_local, pair_count, head_count), "head")
    if len(terms) == 1:
        summed = jnp.sum(terms[0], axis=0)
    else:
        while len(terms) > 1:
            terms = [terms[i] + terms[i + 1] for i in range(0, len(terms), 2)]
        summed = terms[0]
    summed = summed.reshape(requests, step_count, width)
    decoded = (new_hidden.astype(jnp.float32) + summed).astype(jnp.bfloat16)
    return (kept_cache, decoded)


def solution(mesh):
    in_specs = (
        P("groups", "head", "seq", None),
        P("groups", None, None),
        P("groups", None, "seq"),
        P("seq"),
        P("seq", "head"),
        P("seq", "head", None),
        P("head", "seq"),
    )
    out_specs = (P("head", ("groups", "seq"), None, None), P("groups", None, "seq"))
    return jax.shard_map(shards, mesh=mesh, in_specs=in_specs, out_specs=out_specs, check_vma=False)
```

```python
import functools
import math

import jax
import jax.numpy as jnp
import numpy as np
from jax import lax
from jax.experimental import pallas as pl
from jax.experimental.pallas import tpu as pltpu
from jax.sharding import PartitionSpec as P

D = 8192
HD = 128
QPK = 8
BLK = 128
MOST = 2
ROPE_BASE = 500000.0
EPS = 1e-05

CONTRACT_LAST = (((1,), (1,)), ((), ()))


def rope_tables(prompt_length, step_count):
    positions = prompt_length + np.arange(2 * step_count) % step_count
    frequency = ROPE_BASE ** (-np.arange(HD // 2, dtype=np.float64) * 2.0 / HD)
    angles = positions[:, None] * frequency[None, :]
    cosine = np.concatenate([np.cos(angles)] * 2, axis=1)
    sine = np.concatenate([-np.sin(angles), np.sin(angles)], axis=1)
    return cosine.astype(np.float32), sine.astype(np.float32)


def rotate(v, cosine, sine):
    swapped = jnp.concatenate([v[..., HD // 2 :], v[..., : HD // 2]], axis=-1)
    return v * cosine + swapped * sine


def is_direct(count):
    return count <= 8 and count & (count - 1) == 0


def exchange(outgoing, axis):
    if len(outgoing) == 1:
        return [lax.all_to_all(outgoing[0], axis, split_axis=0, concat_axis=0, tiled=True)]
    count = len(outgoing)
    return [outgoing[0]] + [
        lax.ppermute(outgoing[k], axis, [(i, i ^ k) for i in range(count)])
        for k in range(1, count)
    ]


def pick_kernel(kept_ref, cache_ref, *refs):
    outs, sem = refs[:-1], refs[-1]
    requests, heads_local, source_tokens, _ = cache_ref.shape
    source_blocks = source_tokens // BLK
    kept_count = kept_ref.shape[1]
    me = lax.axis_index("seq")
    first_head = lax.axis_index("head") * heads_local

    def copy_pair(pair, out_ref):
        request = lax.div(pair, heads_local)
        local = lax.rem(pair, heads_local)
        head = first_head + local

        def count(k, total):
            block = kept_ref[request, k, head]
            return total + (block < me * source_blocks).astype(jnp.int32)

        start = lax.fori_loop(0, kept_count, count, jnp.int32(0), unroll=kept_count <= 8)
        for slot in range(MOST):
            rank = jnp.minimum(start + slot, kept_count - 1)
            block = kept_ref[request, rank, head] - me * source_blocks
            block = jnp.clip(block, 0, source_blocks - 1)
            rows = pl.ds(pl.multiple_of(block * BLK, BLK), BLK)
            pltpu.make_async_copy(
                cache_ref.at[request, local, rows], out_ref.at[slot], sem
            ).start()

    pair_count = requests * heads_local
    if len(outs) == 1:

        def pair_body(pair, carry):
            copy_pair(pair, outs[0].at[pair])
            return carry

        lax.fori_loop(0, pair_count, pair_body, 0)
    else:
        for offset, out_ref in enumerate(outs):
            copy_pair(jnp.bitwise_xor(me, offset), out_ref)
    for out_ref in outs:
        pltpu.make_async_copy(out_ref, out_ref, sem).wait()


def pick(kept_blocks, source_cache):
    requests, heads_local, _, row_width = source_cache.shape
    pair_count = requests * heads_local
    block = (MOST, BLK, row_width)
    if is_direct(pair_count):
        shapes = [jax.ShapeDtypeStruct(block, jnp.bfloat16)] * pair_count
    else:
        shapes = [jax.ShapeDtypeStruct((pair_count,) + block, jnp.bfloat16)]
    return pl.pallas_call(
        pick_kernel,
        out_shape=shapes,
        in_specs=[
            pl.BlockSpec(memory_space=pltpu.SMEM),
            pl.BlockSpec(memory_space=pl.ANY),
        ],
        out_specs=[pl.BlockSpec(memory_space=pltpu.VMEM)] * len(shapes),
        scratch_shapes=[pltpu.SemaphoreType.DMA],
        compiler_params=pltpu.CompilerParams(vmem_limit_bytes=12 * 1024 * 1024),
        name="pick_blocks",
    )(kept_blocks, pltpu.with_memory_space_constraint(source_cache, pltpu.HBM))


def interleave(rows):
    count, width = rows.shape
    chunks = width // HD
    stacked = jnp.concatenate(
        [rows[:, c * HD : (c + 1) * HD] for c in range(chunks)], axis=0
    ).astype(jnp.bfloat16)
    source = lax.broadcasted_iota(jnp.int32, (HD, 4 * HD), 0)
    target = lax.broadcasted_iota(jnp.int32, (HD, 4 * HD), 1)
    place = jnp.where(target < 2 * HD, 2 * source, 2 * source + 1 + 2 * HD)
    spread = (place == target).astype(jnp.bfloat16)
    wide = jnp.dot(stacked, spread, preferred_element_type=jnp.float32)
    return [
        jnp.concatenate(
            [
                wide[c * count : (c + 1) * count, : 2 * HD],
                wide[c * count : (c + 1) * count, 2 * HD :],
            ],
            axis=0,
        ).astype(jnp.bfloat16)
        for c in range(chunks)
    ]


def chunk_copies(w_ref, buffer, sems, rows):
    return [
        pltpu.make_async_copy(
            w_ref.at[pl.ds(i * rows, rows)], buffer.at[pl.ds(i * rows, rows)], sems.at[i]
        )
        for i in range(w_ref.shape[0] // rows)
    ]


def project_kernel(rows, hidden_ref, gain_ref, wq_ref, wkv_ref, *refs):
    outs = refs[:-4]
    wq, wkv, sem_q, sem_kv = refs[-4:]
    copies_q = chunk_copies(wq_ref, wq, sem_q, rows)
    copies_kv = chunk_copies(wkv_ref, wkv, sem_kv, rows)
    for copy_q, copy_kv in zip(copies_q, copies_kv):
        copy_kv.start()
        copy_q.start()
    requests, step_count, width = hidden_ref.shape
    heads_local = wkv_ref.shape[1]
    row_count = requests * step_count
    hidden = jnp.concatenate(
        [hidden_ref[r].astype(jnp.float32) for r in range(requests)], axis=0
    )
    square = jnp.sum(hidden * hidden, axis=1, keepdims=True)
    scaled = (hidden * gain_ref[...].astype(jnp.float32)).astype(jnp.bfloat16)
    spread = interleave(scaled.astype(jnp.float32))
    query = jnp.zeros((row_count, wq.shape[1]), jnp.float32)
    keyval = jnp.zeros((heads_local * row_count, wkv.shape[2]), jnp.float32)
    per_chunk = rows // HD
    for i, (copy_q, copy_kv) in enumerate(zip(copies_q, copies_kv)):
        copy_kv.wait()
        for c in range(i * per_chunk, (i + 1) * per_chunk):
            keyval += jnp.dot(
                spread[c],
                wkv[c * HD : (c + 1) * HD].reshape(heads_local * HD, wkv.shape[2]),
                preferred_element_type=jnp.float32,
            )
        copy_q.wait()
        query += jnp.dot(
            scaled[:, i * rows : (i + 1) * rows],
            wq[i * rows : (i + 1) * rows, :],
            preferred_element_type=jnp.float32,
        )
    me = lax.axis_index("seq")

    def write_pair(out_ref, pieces):
        for j, piece in enumerate(pieces):
            out_ref[j * step_count : (j + 1) * step_count, :] = piece

    for r in range(requests):
        steps = slice(r * step_count, (r + 1) * step_count)
        square_rows = jnp.broadcast_to(square[steps], (step_count, HD))
        for l in range(heads_local):
            pair = r * heads_local + l
            pieces = [
                query[steps, (l * QPK + h) * HD : (l * QPK + h + 1) * HD] for h in range(QPK)
            ]
            own = keyval[l * row_count + r * step_count : l * row_count + (r + 1) * step_count]
            pieces += [own[:, :HD], own[:, HD:], square_rows, square_rows]
            if len(outs) == 1:
                write_pair(outs[0].at[pair], pieces)
            else:
                for offset, out_ref in enumerate(outs):
                    pl.when(jnp.bitwise_xor(me, offset) == pair)(
                        functools.partial(write_pair, out_ref, pieces)
                    )


def project(new_hidden, norm_gain, w_query, w_keyval, pair_count):
    requests, step_count, width = new_hidden.shape
    rows = min(256, width)
    chunks = width // rows
    block = ((QPK + 4) * step_count, HD)
    if is_direct(pair_count):
        shapes = [jax.ShapeDtypeStruct(block, jnp.float32)] * pair_count
    else:
        shapes = [jax.ShapeDtypeStruct((pair_count,) + block, jnp.float32)]
    vmem = pl.BlockSpec(memory_space=pltpu.VMEM)
    anywhere = pl.BlockSpec(memory_space=pl.ANY)
    weights = w_query.size + w_keyval.size
    return pl.pallas_call(
        functools.partial(project_kernel, rows),
        out_shape=shapes,
        in_specs=[vmem, vmem, anywhere, anywhere],
        out_specs=[vmem] * len(shapes),
        scratch_shapes=[
            pltpu.VMEM(w_query.shape, jnp.bfloat16),
            pltpu.VMEM(w_keyval.shape, jnp.bfloat16),
            pltpu.SemaphoreType.DMA((chunks,)),
            pltpu.SemaphoreType.DMA((chunks,)),
        ],
        compiler_params=pltpu.CompilerParams(vmem_limit_bytes=24 * 1024 * 1024),
        cost_estimate=pl.CostEstimate(
            flops=2 * requests * step_count * weights,
            bytes_accessed=2 * weights,
            transcendentals=0,
        ),
        name="project",
    )(
        new_hidden,
        norm_gain,
        pltpu.with_memory_space_constraint(w_query, pltpu.HBM),
        pltpu.with_memory_space_constraint(w_keyval, pltpu.HBM),
    )


def attend_kernel(source_blocks, heads_local, seq_count, kept_ref, cos_ref, sin_ref, *refs):
    direct = is_direct(seq_count)
    arrivals = seq_count if direct else 1
    blocks_refs, parts_refs = refs[:arrivals], refs[arrivals : 2 * arrivals]
    cache_ref, attended_ref, sem = refs[2 * arrivals : 2 * arrivals + 3]
    kept = cache_ref.at[0, 0] if direct else refs[-1]
    kept_count = kept_ref.shape[1]
    step_count = cos_ref.shape[0] // 2
    me = lax.axis_index("seq")
    request = lax.div(me, heads_local)
    head = lax.axis_index("head") * heads_local + lax.rem(me, heads_local)

    def start_copy(k, carry):
        previous, slot = carry
        source = lax.div(kept_ref[request, k, head], source_blocks)
        slot = jnp.where(source == previous, jnp.minimum(slot + 1, MOST - 1), 0)
        target = kept.at[pl.ds(pl.multiple_of(k * BLK, BLK), BLK)]
        if not direct:
            pltpu.make_async_copy(blocks_refs[0].at[source, slot], target, sem).start()
        else:
            for offset, blocks_ref in enumerate(blocks_refs):
                pl.when(jnp.bitwise_xor(me, offset) == source)(
                    pltpu.make_async_copy(blocks_ref.at[slot], target, sem).start
                )
        return source, slot

    lax.fori_loop(
        0, kept_count, start_copy, (jnp.int32(-1), jnp.int32(0)), unroll=kept_count <= 8
    )
    if direct:
        total = sum(ref[...] for ref in parts_refs)
    else:
        total = jnp.sum(parts_refs[0][...], axis=0)
        pltpu.make_async_copy(kept, kept, sem).wait()
        pltpu.make_async_copy(kept, cache_ref.at[0, 0], sem).start()
    query_rows = QPK * step_count
    inverse = lax.rsqrt(total[query_rows + 2 * step_count :] * (1.0 / D) + EPS)
    cosine, sine = cos_ref[...], sin_ref[...]
    query = total[:query_rows].reshape(QPK // 2, 2 * step_count, HD) * inverse[None]
    query = rotate(query, cosine[None], sine[None]).reshape(query_rows, HD).astype(jnp.bfloat16)
    keyval = total[query_rows : query_rows + 2 * step_count] * inverse
    new_key = rotate(keyval, cosine, sine).astype(jnp.bfloat16)
    new_value = jnp.concatenate([keyval[step_count:], keyval[:step_count]], axis=0)
    new_value = new_value.astype(jnp.bfloat16)
    scale = 1.0 / math.sqrt(HD)
    score = lax.dot_general(query, new_key, CONTRACT_LAST, preferred_element_type=jnp.float32)
    row = lax.broadcasted_iota(jnp.int32, score.shape, 0)
    column = lax.broadcasted_iota(jnp.int32, score.shape, 1)
    scores = [jnp.where(column <= lax.rem(row, step_count), score * scale, -jnp.inf)]
    values = [new_value]
    def add_block(block, filled):
        score = lax.dot_general(
            query, block[:, :HD], CONTRACT_LAST, preferred_element_type=jnp.float32
        )
        column = lax.broadcasted_iota(jnp.int32, score.shape, 1)
        scores.append(jnp.where(column < filled * BLK, score * scale, -jnp.inf))
        values.append(block[:, HD:])

    if direct:
        for offset, ref in enumerate(blocks_refs):
            source = jnp.bitwise_xor(me, offset)
            filled = jnp.int32(0)
            for k in range(kept_count):
                here = lax.div(kept_ref[request, k, head], source_blocks) == source
                filled += here.astype(jnp.int32)
            add_block(ref[...].reshape(MOST * BLK, 2 * HD), filled)
    else:
        add_block(kept[...], kept_count)
    row_max = functools.reduce(
        jnp.maximum, [jnp.max(score, axis=1, keepdims=True) for score in scores]
    )
    denominator = jnp.zeros((query_rows, 1), jnp.float32)
    numerator = jnp.zeros((query_rows, HD), jnp.float32)
    for score, value in zip(scores, values):
        weight = jnp.exp(score - row_max)
        denominator += jnp.sum(weight, axis=1, keepdims=True)
        numerator += jnp.dot(
            weight.astype(jnp.bfloat16), value, preferred_element_type=jnp.float32
        )
    attended = (numerator / denominator).astype(jnp.bfloat16)
    if direct:
        attended_ref[...] = attended
    else:
        for i in range(seq_count):
            attended_ref[i] = attended
    pltpu.make_async_copy(cache_ref, cache_ref, sem).wait()


def attend(kept_blocks, blocks, parts, source_blocks, heads_local, step_count, seq_count):
    kept_count = kept_blocks.shape[1]
    row_width = blocks[0].shape[-1]
    cosine, sine = rope_tables(source_blocks * BLK * seq_count, step_count)
    shape = (QPK * step_count, HD)
    if len(blocks) == 1:
        shape = (seq_count,) + shape
    vmem = pl.BlockSpec(memory_space=pltpu.VMEM)
    kept_cache, attended = pl.pallas_call(
        functools.partial(attend_kernel, source_blocks, heads_local, seq_count),
        out_shape=(
            jax.ShapeDtypeStruct((1, 1, kept_count * BLK, row_width), jnp.bfloat16),
            jax.ShapeDtypeStruct(shape, jnp.bfloat16),
        ),
        in_specs=[pl.BlockSpec(memory_space=pltpu.SMEM)]
        + [vmem] * (2 + len(blocks) + len(parts)),
        out_specs=(pl.BlockSpec(memory_space=pl.ANY), vmem),
        scratch_shapes=[pltpu.SemaphoreType.DMA]
        + ([pltpu.VMEM((kept_count * BLK, row_width), jnp.bfloat16)] if len(blocks) == 1 else []),
        compiler_params=pltpu.CompilerParams(vmem_limit_bytes=24 * 1024 * 1024),
        name="attend",
    )(kept_blocks, jnp.asarray(cosine), jnp.asarray(sine), *blocks, *parts)
    return kept_cache, [attended] * (1 if len(blocks) == 1 else seq_count)


def output_kernel(heads_local, w_ref, *refs):
    gathered_refs, out_ref = refs[:-1], refs[-1]
    query_rows = gathered_refs[0].shape[-2]
    step_count = query_rows // QPK
    if len(gathered_refs) == 1:
        pair_count = gathered_refs[0].shape[0]
        pairs = [gathered_refs[0][p].astype(jnp.float32) for p in range(pair_count)]
    else:
        pair_count = len(gathered_refs)
        me = lax.axis_index("seq")
        arrived = [ref[...].astype(jnp.float32) for ref in gathered_refs]
        pairs = arrived
        bit = 1
        while bit < pair_count:
            swap = jnp.bitwise_and(me, bit) != 0
            pairs = [jnp.where(swap, pairs[p ^ bit], pairs[p]) for p in range(pair_count)]
            bit *= 2
    requests = pair_count // heads_local
    pieces = []
    for l in range(heads_local):
        for h in range(QPK):
            rows = slice(h * step_count, (h + 1) * step_count)
            pieces.append(
                jnp.concatenate(
                    [pairs[r * heads_local + l][rows] for r in range(requests)], axis=0
                )
            )
    merged = jnp.concatenate(pieces, axis=1).astype(jnp.bfloat16)
    total = jnp.dot(merged, w_ref[...], preferred_element_type=jnp.float32)
    if len(out_ref.shape) == 2:
        out_ref[...] = total
    else:
        for i in range(out_ref.shape[0]):
            out_ref[i] = total


def output(gathered, w_out, heads_local, pair_count, head_count):
    query_rows = gathered[0].shape[-2]
    total_rows = pair_count // heads_local * (query_rows // QPK)
    shape = (total_rows, w_out.shape[1])
    if not is_direct(head_count):
        shape = (head_count,) + shape
    vmem = pl.BlockSpec(memory_space=pltpu.VMEM)
    terms = pl.pallas_call(
        functools.partial(output_kernel, heads_local),
        out_shape=jax.ShapeDtypeStruct(shape, jnp.float32),
        in_specs=[vmem] * (1 + len(gathered)),
        out_specs=vmem,
        compiler_params=pltpu.CompilerParams(vmem_limit_bytes=24 * 1024 * 1024),
        name="output_projection",
    )(pltpu.with_memory_space_constraint(w_out, pltpu.VMEM), *gathered)
    return [terms] * (head_count if is_direct(head_count) else 1)


def shards(source_cache, kept_blocks, new_hidden, norm_gain, w_query, w_keyval, w_out):
    seq_count = lax.axis_size("seq")
    head_count = lax.axis_size("head")
    requests, heads_local, source_tokens, _ = source_cache.shape
    _, step_count, width = new_hidden.shape
    pair_count = requests * heads_local

    kept_blocks = kept_blocks.transpose(0, 2, 1)
    blocks = exchange(pick(kept_blocks, source_cache), "seq")
    parts = project(new_hidden, norm_gain.reshape(1, width), w_query, w_keyval, pair_count)
    parts = exchange(parts, "seq")
    kept_cache, attended = attend(
        kept_blocks, blocks, parts, source_tokens // BLK, heads_local, step_count, seq_count
    )
    gathered = exchange(attended, "seq")
    terms = exchange(output(gathered, w_out, heads_local, pair_count, head_count), "head")
    if len(terms) == 1:
        summed = jnp.sum(terms[0], axis=0)
    else:
        while len(terms) > 1:
            terms = [terms[i] + terms[i + 1] for i in range(0, len(terms), 2)]
        summed = terms[0]
    summed = summed.reshape(requests, step_count, width)
    decoded = (new_hidden.astype(jnp.float32) + summed).astype(jnp.bfloat16)
    return (kept_cache, decoded)


def solution(mesh):
    in_specs = (
        P("groups", "head", "seq", None),
        P("groups", None, None),
        P("groups", None, "seq"),
        P("seq"),
        P("seq", "head"),
        P("seq", "head", None),
        P("head", "seq"),
    )
    out_specs = (P("head", ("groups", "seq"), None, None), P("groups", None, "seq"))
    return jax.shard_map(shards, mesh=mesh, in_specs=in_specs, out_specs=out_specs, check_vma=False)
```

```python
import functools
import math

import jax
import jax.numpy as jnp
import numpy as np
from jax import lax
from jax.experimental import pallas as pl
from jax.experimental.pallas import tpu as pltpu
from jax.sharding import PartitionSpec as P

D = 8192
HD = 128
QPK = 8
BLK = 128
MOST = 2
ROPE_BASE = 500000.0
EPS = 1e-05

CONTRACT_LAST = (((1,), (1,)), ((), ()))


def rope_tables(prompt_length, step_count):
    positions = prompt_length + np.arange(2 * step_count) % step_count
    frequency = ROPE_BASE ** (-np.arange(HD // 2, dtype=np.float64) * 2.0 / HD)
    angles = positions[:, None] * frequency[None, :]
    cosine = np.concatenate([np.cos(angles)] * 2, axis=1)
    sine = np.concatenate([-np.sin(angles), np.sin(angles)], axis=1)
    return cosine.astype(np.float32), sine.astype(np.float32)


def rotate(v, cosine, sine):
    swapped = jnp.concatenate([v[..., HD // 2 :], v[..., : HD // 2]], axis=-1)
    return v * cosine + swapped * sine


def is_direct(count):
    return count <= 4 and count & (count - 1) == 0


def swap(outgoing, axis, offset):
    count = lax.axis_size(axis)
    return lax.ppermute(outgoing, axis, [(i, i ^ offset) for i in range(count)])


def all_to_all(outgoing, axis):
    return lax.all_to_all(outgoing, axis, split_axis=0, concat_axis=0, tiled=True)


def start_picks(kept_ref, cache_ref, pair, out_ref, sem):
    _, heads_local, source_tokens, _ = cache_ref.shape
    source_blocks = source_tokens // BLK
    kept_count = kept_ref.shape[1]
    me = lax.axis_index("seq")
    request = lax.div(pair, heads_local)
    local = lax.rem(pair, heads_local)
    head = lax.axis_index("head") * heads_local + local

    def count(k, total):
        block = kept_ref[request, k, head]
        return total + (block < me * source_blocks).astype(jnp.int32)

    start = lax.fori_loop(0, kept_count, count, jnp.int32(0), unroll=kept_count <= 8)
    for slot in range(MOST):
        rank = jnp.minimum(start + slot, kept_count - 1)
        block = kept_ref[request, rank, head] - me * source_blocks
        block = jnp.clip(block, 0, source_blocks - 1)
        rows = pl.ds(pl.multiple_of(block * BLK, BLK), BLK)
        pltpu.make_async_copy(
            cache_ref.at[request, local, rows], out_ref.at[pl.ds(slot * BLK, BLK)], sem
        ).start()


def pick_kernel(offsets, kept_ref, cache_ref, *refs):
    outs, sem = refs[:-1], refs[-1]
    if offsets:
        me = lax.axis_index("seq")
        for offset, out_ref in zip(offsets, outs):
            start_picks(kept_ref, cache_ref, jnp.bitwise_xor(me, offset), out_ref, sem)
    else:

        def pair_body(pair, carry):
            start_picks(kept_ref, cache_ref, pair, outs[0].at[pair], sem)
            return carry

        lax.fori_loop(0, outs[0].shape[0], pair_body, 0)
    for out_ref in outs:
        pltpu.make_async_copy(out_ref, out_ref, sem).wait()


def pick(kept_blocks, source_cache, offsets):
    requests, heads_local, _, row_width = source_cache.shape
    block = (MOST * BLK, row_width)
    if offsets:
        shapes = [jax.ShapeDtypeStruct(block, jnp.bfloat16)] * len(offsets)
    else:
        shapes = [jax.ShapeDtypeStruct((requests * heads_local,) + block, jnp.bfloat16)]
    return pl.pallas_call(
        functools.partial(pick_kernel, offsets),
        out_shape=shapes,
        in_specs=[
            pl.BlockSpec(memory_space=pltpu.SMEM),
            pl.BlockSpec(memory_space=pl.ANY),
        ],
        out_specs=[pl.BlockSpec(memory_space=pltpu.VMEM)] * len(shapes),
        scratch_shapes=[pltpu.SemaphoreType.DMA],
        compiler_params=pltpu.CompilerParams(vmem_limit_bytes=8 * 1024 * 1024),
        cost_estimate=pl.CostEstimate(flops=10**10, bytes_accessed=0, transcendentals=0),
        name="pick_blocks",
    )(kept_blocks, pltpu.with_memory_space_constraint(source_cache, pltpu.HBM))


def interleave(rows):
    count, width = rows.shape
    chunks = width // HD
    stacked = jnp.concatenate(
        [rows[:, c * HD : (c + 1) * HD] for c in range(chunks)], axis=0
    ).astype(jnp.bfloat16)
    source = lax.broadcasted_iota(jnp.int32, (HD, 4 * HD), 0)
    target = lax.broadcasted_iota(jnp.int32, (HD, 4 * HD), 1)
    place = jnp.where(target < 2 * HD, 2 * source, 2 * source + 1 + 2 * HD)
    spread = (place == target).astype(jnp.bfloat16)
    wide = jnp.dot(stacked, spread, preferred_element_type=jnp.float32)
    return [
        jnp.concatenate(
            [
                wide[c * count : (c + 1) * count, : 2 * HD],
                wide[c * count : (c + 1) * count, 2 * HD :],
            ],
            axis=0,
        ).astype(jnp.bfloat16)
        for c in range(chunks)
    ]


def project_kernel(direct, after_ref, hidden_ref, gain_ref, wq_ref, wkv_ref, *outs):
    del after_ref
    requests, step_count, width = hidden_ref.shape
    heads_local = wkv_ref.shape[1]
    row_count = requests * step_count
    me = lax.axis_index("seq")
    hidden = jnp.concatenate(
        [hidden_ref[r].astype(jnp.float32) for r in range(requests)], axis=0
    )
    square = jnp.sum(hidden * hidden, axis=1, keepdims=True)
    gain = gain_ref[...].astype(jnp.float32)
    scaled = jnp.concatenate(
        [hidden[:, c * HD : (c + 1) * HD] * gain[c : c + 1] for c in range(width // HD)], axis=1
    ).astype(jnp.bfloat16)
    query = jnp.dot(scaled, wq_ref[...], preferred_element_type=jnp.float32)
    keyval = jnp.zeros((heads_local * row_count, wkv_ref.shape[2]), jnp.float32)
    for c, spread in enumerate(interleave(scaled.astype(jnp.float32))):
        alternate = wkv_ref[c * HD : (c + 1) * HD].reshape(heads_local * HD, wkv_ref.shape[2])
        keyval += jnp.dot(spread, alternate, preferred_element_type=jnp.float32)

    def pieces_of(r, l):
        steps = slice(r * step_count, (r + 1) * step_count)
        square_rows = jnp.broadcast_to(square[steps], (step_count, HD))
        own = keyval[l * row_count + r * step_count : l * row_count + (r + 1) * step_count]
        heads = [query[steps, (l * QPK + h) * HD : (l * QPK + h + 1) * HD] for h in range(QPK)]
        return heads + [own[:, :HD], own[:, HD:], square_rows, square_rows]

    def write_pair(out_ref, pieces):
        for j, piece in enumerate(pieces):
            out_ref[j * step_count : (j + 1) * step_count, :] = piece

    for r in range(requests):
        for l in range(heads_local):
            pair = r * heads_local + l
            pieces = pieces_of(r, l)
            if not direct:
                write_pair(outs[0].at[pair], pieces)
                continue
            for offset, out_ref in enumerate(outs):
                pl.when(jnp.bitwise_xor(me, offset) == pair)(
                    functools.partial(write_pair, out_ref, pieces)
                )


def project(after, new_hidden, norm_gain, w_query, w_keyval, pair_count, direct):
    requests, step_count, width = new_hidden.shape
    terms = ((QPK + 4) * step_count, HD)
    if direct:
        shapes = [jax.ShapeDtypeStruct(terms, jnp.float32)] * pair_count
    else:
        shapes = [jax.ShapeDtypeStruct((pair_count,) + terms, jnp.float32)]
    vmem = pl.BlockSpec(memory_space=pltpu.VMEM)
    weights = w_query.size + w_keyval.size
    return pl.pallas_call(
        functools.partial(project_kernel, direct),
        out_shape=shapes,
        in_specs=[pl.BlockSpec(memory_space=pl.ANY), vmem, vmem, vmem, vmem],
        out_specs=[vmem] * len(shapes),
        compiler_params=pltpu.CompilerParams(vmem_limit_bytes=8 * 1024 * 1024),
        cost_estimate=pl.CostEstimate(
            flops=2 * requests * step_count * weights,
            bytes_accessed=2 * weights,
            transcendentals=0,
        ),
        name="project",
    )(
        after,
        new_hidden,
        norm_gain.reshape(width // HD, HD),
        pltpu.with_memory_space_constraint(w_query, pltpu.VMEM),
        pltpu.with_memory_space_constraint(w_keyval, pltpu.VMEM),
    )


def attend_kernel(direct, source_blocks, heads_local, kept_ref, cos_ref, sin_ref, *refs):
    kept_count = kept_ref.shape[1]
    step_count = cos_ref.shape[0] // 2
    me = lax.axis_index("seq")
    request = lax.div(me, heads_local)
    head = lax.axis_index("head") * heads_local + lax.rem(me, heads_local)
    if direct:
        cache_ref, attended_ref, sem = refs[-3:]
        half = len(refs[:-3]) // 2
        by_offset, parts_refs = refs[:half][::-1], refs[half : 2 * half][::-1]
        kept = cache_ref.at[0, 0]
    else:
        parts_ref, blocks_ref, cache_ref, attended_ref, sem, kept = refs

    def start_copy(k, carry):
        previous, slot = carry
        source = lax.div(kept_ref[request, k, head], source_blocks)
        slot = jnp.where(source == previous, jnp.minimum(slot + 1, MOST - 1), 0)
        target = kept.at[pl.ds(pl.multiple_of(k * BLK, BLK), BLK)]
        rows = pl.ds(pl.multiple_of(slot * BLK, BLK), BLK)
        if direct:
            for offset, ref in enumerate(by_offset):
                pl.when(jnp.bitwise_xor(me, offset) == source)(
                    pltpu.make_async_copy(ref.at[rows], target, sem).start
                )
        else:
            pltpu.make_async_copy(blocks_ref.at[source, rows], target, sem).start()
        return source, slot

    lax.fori_loop(
        0, kept_count, start_copy, (jnp.int32(-1), jnp.int32(0)), unroll=kept_count <= 8
    )
    if direct:
        total = sum(ref[...] for ref in parts_refs)
    else:
        total = jnp.sum(parts_ref[...], axis=0)
        pltpu.make_async_copy(kept, kept, sem).wait()
        pltpu.make_async_copy(kept, cache_ref.at[0, 0], sem).start()
    query_rows = QPK * step_count
    inverse = lax.rsqrt(total[query_rows + 2 * step_count :] * (1.0 / D) + EPS)
    cosine, sine = cos_ref[...], sin_ref[...]
    query = total[:query_rows].reshape(QPK // 2, 2 * step_count, HD) * inverse[None]
    query = rotate(query, cosine[None], sine[None]).reshape(query_rows, HD).astype(jnp.bfloat16)
    keyval = total[query_rows : query_rows + 2 * step_count] * inverse
    new_key = rotate(keyval, cosine, sine).astype(jnp.bfloat16)
    new_value = jnp.concatenate([keyval[step_count:], keyval[:step_count]], axis=0)
    new_value = new_value.astype(jnp.bfloat16)
    scale = 1.0 / math.sqrt(HD)
    score = lax.dot_general(query, new_key, CONTRACT_LAST, preferred_element_type=jnp.float32)
    row = lax.broadcasted_iota(jnp.int32, score.shape, 0)
    column = lax.broadcasted_iota(jnp.int32, score.shape, 1)
    scores = [jnp.where(column <= lax.rem(row, step_count), score * scale, -jnp.inf)]
    values = [new_value]
    def add_block(block, filled):
        score = lax.dot_general(
            query, block[:, :HD], CONTRACT_LAST, preferred_element_type=jnp.float32
        )
        column = lax.broadcasted_iota(jnp.int32, score.shape, 1)
        scores.append(jnp.where(column < filled * BLK, score * scale, -jnp.inf))
        values.append(block[:, HD:])

    if direct:
        for offset, ref in enumerate(by_offset):
            source = jnp.bitwise_xor(me, offset)
            filled = jnp.int32(0)
            for k in range(kept_count):
                here = lax.div(kept_ref[request, k, head], source_blocks) == source
                filled += here.astype(jnp.int32)
            add_block(ref[: MOST * BLK, :], filled)
    else:
        add_block(kept[...], kept_count)
    row_max = functools.reduce(
        jnp.maximum, [jnp.max(score, axis=1, keepdims=True) for score in scores]
    )
    denominator = jnp.zeros((query_rows, 1), jnp.float32)
    numerator = jnp.zeros((query_rows, HD), jnp.float32)
    for score, value in zip(scores, values):
        weight = jnp.exp(score - row_max)
        denominator += jnp.sum(weight, axis=1, keepdims=True)
        numerator += jnp.dot(
            weight.astype(jnp.bfloat16), value, preferred_element_type=jnp.float32
        )
    attended = (numerator / denominator).astype(jnp.bfloat16)
    if direct:
        attended_ref[...] = attended
    else:
        for i in range(attended_ref.shape[0]):
            attended_ref[i] = attended
    pltpu.make_async_copy(cache_ref, cache_ref, sem).wait()


def attend(kept_blocks, arrivals, source_blocks, heads_local, step_count, seq_count, direct):
    kept_count = kept_blocks.shape[1]
    row_width = 2 * HD
    cosine, sine = rope_tables(source_blocks * BLK * seq_count, step_count)
    shape = (QPK * step_count, HD)
    scratch = [pltpu.SemaphoreType.DMA]
    if not direct:
        shape = (seq_count,) + shape
        scratch.append(pltpu.VMEM((kept_count * BLK, row_width), jnp.bfloat16))
    vmem = pl.BlockSpec(memory_space=pltpu.VMEM)
    return pl.pallas_call(
        functools.partial(attend_kernel, direct, source_blocks, heads_local),
        out_shape=(
            jax.ShapeDtypeStruct((1, 1, kept_count * BLK, row_width), jnp.bfloat16),
            jax.ShapeDtypeStruct(shape, jnp.bfloat16),
        ),
        in_specs=[pl.BlockSpec(memory_space=pltpu.SMEM)] + [vmem] * (2 + len(arrivals)),
        out_specs=(pl.BlockSpec(memory_space=pl.ANY), vmem),
        scratch_shapes=scratch,
        compiler_params=pltpu.CompilerParams(vmem_limit_bytes=16 * 1024 * 1024),
        name="attend",
    )(kept_blocks, jnp.asarray(cosine), jnp.asarray(sine), *arrivals)


def output_kernel(heads_local, w_ref, *refs):
    gathered_refs, out_ref = refs[:-1], refs[-1]
    query_rows = gathered_refs[0].shape[-2]
    step_count = query_rows // QPK
    if len(gathered_refs) == 1:
        pair_count = gathered_refs[0].shape[0]
        pairs = [gathered_refs[0][p].astype(jnp.float32) for p in range(pair_count)]
    else:
        pair_count = len(gathered_refs)
        me = lax.axis_index("seq")
        arrived = [ref[...].astype(jnp.float32) for ref in gathered_refs]
        pairs = arrived
        bit = 1
        while bit < pair_count:
            swap = jnp.bitwise_and(me, bit) != 0
            pairs = [jnp.where(swap, pairs[p ^ bit], pairs[p]) for p in range(pair_count)]
            bit *= 2
    requests = pair_count // heads_local
    pieces = []
    for l in range(heads_local):
        for h in range(QPK):
            rows = slice(h * step_count, (h + 1) * step_count)
            pieces.append(
                jnp.concatenate(
                    [pairs[r * heads_local + l][rows] for r in range(requests)], axis=0
                )
            )
    merged = jnp.concatenate(pieces, axis=1).astype(jnp.bfloat16)
    total = jnp.dot(merged, w_ref[...], preferred_element_type=jnp.float32)
    if len(out_ref.shape) == 2:
        out_ref[...] = total
    else:
        for i in range(out_ref.shape[0]):
            out_ref[i] = total


def output(gathered, w_out, heads_local, pair_count, head_count):
    query_rows = gathered[0].shape[-2]
    total_rows = pair_count // heads_local * (query_rows // QPK)
    shape = (total_rows, w_out.shape[1])
    if not is_direct(head_count):
        shape = (head_count,) + shape
    vmem = pl.BlockSpec(memory_space=pltpu.VMEM)
    terms = pl.pallas_call(
        functools.partial(output_kernel, heads_local),
        out_shape=jax.ShapeDtypeStruct(shape, jnp.float32),
        in_specs=[vmem] * (1 + len(gathered)),
        out_specs=vmem,
        compiler_params=pltpu.CompilerParams(vmem_limit_bytes=8 * 1024 * 1024),
        name="output_projection",
    )(pltpu.with_memory_space_constraint(w_out, pltpu.VMEM), *gathered)
    return terms


def shards(source_cache, kept_blocks, new_hidden, norm_gain, w_query, w_keyval, w_out):
    seq_count = lax.axis_size("seq")
    head_count = lax.axis_size("head")
    requests, heads_local, source_tokens, _ = source_cache.shape
    _, step_count, width = new_hidden.shape
    pair_count = requests * heads_local

    kept_blocks = kept_blocks.transpose(0, 2, 1)
    direct = is_direct(seq_count)
    weights = (new_hidden, norm_gain, w_query, w_keyval)
    if direct:
        partners = range(1, seq_count)
        own, *blocks = pick(kept_blocks, source_cache, range(seq_count))
        blocks = [own] + [swap(blocks[k - 1], "seq", k) for k in partners]
        own, *parts = project(blocks[1], *weights, pair_count, direct)
        parts = [own] + [swap(parts[k - 1], "seq", k) for k in partners]
        arrivals = blocks[::-1] + parts[::-1]
    else:
        (blocks,) = pick(kept_blocks, source_cache, ())
        (parts,) = project(blocks, *weights, pair_count, direct)
        arrivals = [all_to_all(parts, "seq"), all_to_all(blocks, "seq")]
    kept_cache, attended = attend(
        kept_blocks, arrivals, source_tokens // BLK, heads_local, step_count, seq_count, direct
    )
    if direct:
        gathered = [attended] + [swap(attended, "seq", k) for k in range(1, seq_count)]
    else:
        gathered = [all_to_all(attended, "seq")]
    terms = output(gathered, w_out, heads_local, pair_count, head_count)
    if is_direct(head_count):
        terms = [terms] + [swap(terms, "head", k) for k in range(1, head_count)]
        while len(terms) > 1:
            terms = [terms[i] + terms[i + 1] for i in range(0, len(terms), 2)]
        summed = terms[0]
    else:
        summed = jnp.sum(all_to_all(terms, "head"), axis=0)
    summed = summed.reshape(requests, step_count, width)
    decoded = (new_hidden.astype(jnp.float32) + summed).astype(jnp.bfloat16)
    return (kept_cache, decoded)


def solution(mesh):
    in_specs = (
        P("groups", "head", "seq", None),
        P("groups", None, None),
        P("groups", None, "seq"),
        P("seq"),
        P("seq", "head"),
        P("seq", "head", None),
        P("head", "seq"),
    )
    out_specs = (P("head", ("groups", "seq"), None, None), P("groups", None, "seq"))
    return jax.shard_map(shards, mesh=mesh, in_specs=in_specs, out_specs=out_specs, check_vma=False)
```

```python
import functools
import math

import jax
import jax.numpy as jnp
import numpy as np
from jax import lax
from jax.experimental import pallas as pl
from jax.experimental.pallas import tpu as pltpu
from jax.sharding import PartitionSpec as P

D = 8192
HD = 128
QPK = 8
BLK = 128
MOST = 2
ROPE_BASE = 500000.0
EPS = 1e-05

CONTRACT_LAST = (((1,), (1,)), ((), ()))


def rope_tables(prompt_length, step_count):
    positions = prompt_length + np.arange(2 * step_count) % step_count
    frequency = ROPE_BASE ** (-np.arange(HD // 2, dtype=np.float64) * 2.0 / HD)
    angles = positions[:, None] * frequency[None, :]
    cosine = np.concatenate([np.cos(angles)] * 2, axis=1)
    sine = np.concatenate([-np.sin(angles), np.sin(angles)], axis=1)
    return cosine.astype(np.float32), sine.astype(np.float32)


def rotate(v, cosine, sine):
    swapped = jnp.concatenate([v[..., HD // 2 :], v[..., : HD // 2]], axis=-1)
    return v * cosine + swapped * sine


def is_direct(count):
    return count == 4


def swap(outgoing, axis, offset):
    count = lax.axis_size(axis)
    return lax.ppermute(outgoing, axis, [(i, i ^ offset) for i in range(count)])


def all_to_all(outgoing, axis):
    return lax.all_to_all(outgoing, axis, split_axis=0, concat_axis=0, tiled=True)


def start_picks(kept_ref, cache_ref, pair, out_ref, sem):
    _, heads_local, source_tokens, _ = cache_ref.shape
    source_blocks = source_tokens // BLK
    kept_count = kept_ref.shape[1]
    me = lax.axis_index("seq")
    request = lax.div(pair, heads_local)
    local = lax.rem(pair, heads_local)
    head = lax.axis_index("head") * heads_local + local

    def count(k, total):
        block = kept_ref[request, k, head]
        return total + (block < me * source_blocks).astype(jnp.int32)

    start = lax.fori_loop(0, kept_count, count, jnp.int32(0), unroll=kept_count <= 8)
    for slot in range(MOST):
        rank = jnp.minimum(start + slot, kept_count - 1)
        block = kept_ref[request, rank, head] - me * source_blocks
        block = jnp.clip(block, 0, source_blocks - 1)
        rows = pl.ds(pl.multiple_of(block * BLK, BLK), BLK)
        pltpu.make_async_copy(
            cache_ref.at[request, local, rows], out_ref.at[pl.ds(slot * BLK, BLK)], sem
        ).start()


def pick_kernel(offsets, kept_hbm_ref, cache_ref, *refs):
    outs, kept_ref, sem = refs[:-2], refs[-2], refs[-1]
    pltpu.sync_copy(kept_hbm_ref, kept_ref)
    if offsets:
        me = lax.axis_index("seq")
        for offset, out_ref in zip(offsets, outs):
            start_picks(kept_ref, cache_ref, jnp.bitwise_xor(me, offset), out_ref, sem)
    else:

        def pair_body(pair, carry):
            start_picks(kept_ref, cache_ref, pair, outs[0].at[pair], sem)
            return carry

        lax.fori_loop(0, outs[0].shape[0], pair_body, 0)
    for out_ref in outs:
        pltpu.make_async_copy(out_ref, out_ref, sem).wait()


def pick(kept_blocks, source_cache, offsets):
    requests, heads_local, _, row_width = source_cache.shape
    block = (MOST * BLK, row_width)
    if offsets:
        shapes = [jax.ShapeDtypeStruct(block, jnp.bfloat16)] * len(offsets)
    else:
        shapes = [jax.ShapeDtypeStruct((requests * heads_local,) + block, jnp.bfloat16)]
    return pl.pallas_call(
        functools.partial(pick_kernel, offsets),
        out_shape=shapes,
        in_specs=[pl.BlockSpec(memory_space=pl.ANY)] * 2,
        out_specs=[pl.BlockSpec(memory_space=pltpu.VMEM)] * len(shapes),
        scratch_shapes=[
            pltpu.SMEM(kept_blocks.shape, jnp.int32),
            pltpu.SemaphoreType.DMA,
        ],
        compiler_params=pltpu.CompilerParams(vmem_limit_bytes=8 * 1024 * 1024),
        cost_estimate=pl.CostEstimate(flops=10**10, bytes_accessed=0, transcendentals=0),
        name="pick_blocks",
    )(
        pltpu.with_memory_space_constraint(kept_blocks, pltpu.HBM),
        pltpu.with_memory_space_constraint(source_cache, pltpu.HBM),
    )


def interleave(rows):
    count, width = rows.shape
    chunks = width // HD
    stacked = jnp.concatenate(
        [rows[:, c * HD : (c + 1) * HD] for c in range(chunks)], axis=0
    ).astype(jnp.bfloat16)
    source = lax.broadcasted_iota(jnp.int32, (HD, 4 * HD), 0)
    target = lax.broadcasted_iota(jnp.int32, (HD, 4 * HD), 1)
    place = jnp.where(target < 2 * HD, 2 * source, 2 * source + 1 + 2 * HD)
    spread = (place == target).astype(jnp.bfloat16)
    wide = jnp.dot(stacked, spread, preferred_element_type=jnp.float32)
    return [
        jnp.concatenate(
            [
                wide[c * count : (c + 1) * count, : 2 * HD],
                wide[c * count : (c + 1) * count, 2 * HD :],
            ],
            axis=0,
        ).astype(jnp.bfloat16)
        for c in range(chunks)
    ]


def project_kernel(direct, after_ref, hidden_ref, gain_ref, wq_ref, wkv_ref, *outs):
    del after_ref
    requests, step_count, width = hidden_ref.shape
    heads_local = wkv_ref.shape[1]
    row_count = requests * step_count
    me = lax.axis_index("seq")
    hidden = jnp.concatenate(
        [hidden_ref[r].astype(jnp.float32) for r in range(requests)], axis=0
    )
    square = jnp.sum(hidden * hidden, axis=1, keepdims=True)
    gain = gain_ref[...].astype(jnp.float32)
    scaled = jnp.concatenate(
        [hidden[:, c * HD : (c + 1) * HD] * gain[c : c + 1] for c in range(width // HD)], axis=1
    ).astype(jnp.bfloat16)
    query = jnp.dot(scaled, wq_ref[...], preferred_element_type=jnp.float32)
    keyval = jnp.zeros((heads_local * row_count, wkv_ref.shape[2]), jnp.float32)
    for c, spread in enumerate(interleave(scaled.astype(jnp.float32))):
        alternate = wkv_ref[c * HD : (c + 1) * HD].reshape(heads_local * HD, wkv_ref.shape[2])
        keyval += jnp.dot(spread, alternate, preferred_element_type=jnp.float32)

    def pieces_of(r, l):
        steps = slice(r * step_count, (r + 1) * step_count)
        square_rows = jnp.broadcast_to(square[steps], (step_count, HD))
        own = keyval[l * row_count + r * step_count : l * row_count + (r + 1) * step_count]
        heads = [query[steps, (l * QPK + h) * HD : (l * QPK + h + 1) * HD] for h in range(QPK)]
        return heads + [own[:, :HD], own[:, HD:], square_rows, square_rows]

    def write_pair(out_ref, pieces):
        for j, piece in enumerate(pieces):
            out_ref[j * step_count : (j + 1) * step_count, :] = piece

    for r in range(requests):
        for l in range(heads_local):
            pair = r * heads_local + l
            pieces = pieces_of(r, l)
            if not direct:
                write_pair(outs[0].at[pair], pieces)
                continue
            for offset, out_ref in enumerate(outs):
                pl.when(jnp.bitwise_xor(me, offset) == pair)(
                    functools.partial(write_pair, out_ref, pieces)
                )


def project(after, new_hidden, norm_gain, w_query, w_keyval, pair_count, direct):
    requests, step_count, width = new_hidden.shape
    terms = ((QPK + 4) * step_count, HD)
    if direct:
        shapes = [jax.ShapeDtypeStruct(terms, jnp.float32)] * pair_count
    else:
        shapes = [jax.ShapeDtypeStruct((pair_count,) + terms, jnp.float32)]
    vmem = pl.BlockSpec(memory_space=pltpu.VMEM)
    weights = w_query.size + w_keyval.size
    return pl.pallas_call(
        functools.partial(project_kernel, direct),
        out_shape=shapes,
        in_specs=[pl.BlockSpec(memory_space=pl.ANY)] + [vmem] * 4,
        out_specs=[vmem] * len(shapes),
        compiler_params=pltpu.CompilerParams(vmem_limit_bytes=8 * 1024 * 1024),
        cost_estimate=pl.CostEstimate(
            flops=2 * requests * step_count * weights,
            bytes_accessed=2 * weights,
            transcendentals=0,
        ),
        name="project",
    )(
        after,
        new_hidden,
        norm_gain.reshape(width // HD, HD),
        pltpu.with_memory_space_constraint(w_query, pltpu.VMEM),
        pltpu.with_memory_space_constraint(w_keyval, pltpu.VMEM),
    )


def attend_kernel(direct, source_blocks, heads_local, kept_ref, cos_ref, sin_ref, *refs):
    kept_count = kept_ref.shape[1]
    step_count = cos_ref.shape[0] // 2
    me = lax.axis_index("seq")
    request = lax.div(me, heads_local)
    head = lax.axis_index("head") * heads_local + lax.rem(me, heads_local)
    if direct:
        cache_ref, attended_ref, sem = refs[-3:]
        by_offset, parts_refs = refs[:4][::-1], refs[4:8][::-1]
        kept = cache_ref.at[0, 0]
    else:
        parts_ref, blocks_ref, cache_ref, attended_ref, sem, kept = refs

    def start_copy(k, carry):
        previous, slot = carry
        source = lax.div(kept_ref[request, k, head], source_blocks)
        slot = jnp.where(source == previous, jnp.minimum(slot + 1, MOST - 1), 0)
        target = kept.at[pl.ds(pl.multiple_of(k * BLK, BLK), BLK)]
        rows = pl.ds(pl.multiple_of(slot * BLK, BLK), BLK)
        if direct:
            for offset, ref in enumerate(by_offset):
                pl.when(jnp.bitwise_xor(me, offset) == source)(
                    pltpu.make_async_copy(ref.at[rows], target, sem).start
                )
        else:
            pltpu.make_async_copy(blocks_ref.at[source, rows], target, sem).start()
        return source, slot

    lax.fori_loop(
        0, kept_count, start_copy, (jnp.int32(-1), jnp.int32(0)), unroll=kept_count <= 8
    )
    if direct:
        total = sum(ref[...] for ref in parts_refs)
    else:
        total = jnp.sum(parts_ref[...], axis=0)
        pltpu.make_async_copy(kept, kept, sem).wait()
        pltpu.make_async_copy(kept, cache_ref.at[0, 0], sem).start()
    query_rows = QPK * step_count
    inverse = lax.rsqrt(total[query_rows + 2 * step_count :] * (1.0 / D) + EPS)
    cosine, sine = cos_ref[...], sin_ref[...]
    query = total[:query_rows].reshape(QPK // 2, 2 * step_count, HD) * inverse[None]
    query = rotate(query, cosine[None], sine[None]).reshape(query_rows, HD).astype(jnp.bfloat16)
    keyval = total[query_rows : query_rows + 2 * step_count] * inverse
    new_key = rotate(keyval, cosine, sine).astype(jnp.bfloat16)
    new_value = jnp.concatenate([keyval[step_count:], keyval[:step_count]], axis=0)
    new_value = new_value.astype(jnp.bfloat16)
    scale = 1.0 / math.sqrt(HD)
    score = lax.dot_general(query, new_key, CONTRACT_LAST, preferred_element_type=jnp.float32)
    row = lax.broadcasted_iota(jnp.int32, score.shape, 0)
    column = lax.broadcasted_iota(jnp.int32, score.shape, 1)
    scores = [jnp.where(column <= lax.rem(row, step_count), score * scale, -jnp.inf)]
    values = [new_value]
    def add_block(block, filled):
        score = lax.dot_general(
            query, block[:, :HD], CONTRACT_LAST, preferred_element_type=jnp.float32
        )
        column = lax.broadcasted_iota(jnp.int32, score.shape, 1)
        scores.append(jnp.where(column < filled * BLK, score * scale, -jnp.inf))
        values.append(block[:, HD:])

    if direct:
        for offset, ref in enumerate(by_offset):
            source = jnp.bitwise_xor(me, offset)
            filled = jnp.int32(0)
            for k in range(kept_count):
                here = lax.div(kept_ref[request, k, head], source_blocks) == source
                filled += here.astype(jnp.int32)
            add_block(ref[: MOST * BLK, :], filled)
    else:
        add_block(kept[...], kept_count)
    row_max = functools.reduce(
        jnp.maximum, [jnp.max(score, axis=1, keepdims=True) for score in scores]
    )
    denominator = jnp.zeros((query_rows, 1), jnp.float32)
    numerator = jnp.zeros((query_rows, HD), jnp.float32)
    for score, value in zip(scores, values):
        weight = jnp.exp(score - row_max)
        denominator += jnp.sum(weight, axis=1, keepdims=True)
        numerator += jnp.dot(
            weight.astype(jnp.bfloat16), value, preferred_element_type=jnp.float32
        )
    attended = (numerator / denominator).astype(jnp.bfloat16)
    if direct:
        attended_ref[...] = attended
    else:
        for i in range(attended_ref.shape[0]):
            attended_ref[i] = attended
    pltpu.make_async_copy(cache_ref, cache_ref, sem).wait()


def attend(kept_blocks, arrivals, source_blocks, heads_local, step_count, seq_count, direct):
    kept_count = kept_blocks.shape[1]
    row_width = 2 * HD
    cosine, sine = rope_tables(source_blocks * BLK * seq_count, step_count)
    shape = (QPK * step_count, HD)
    scratch = [pltpu.SemaphoreType.DMA]
    if not direct:
        shape = (seq_count,) + shape
        scratch.append(pltpu.VMEM((kept_count * BLK, row_width), jnp.bfloat16))
    vmem = pl.BlockSpec(memory_space=pltpu.VMEM)
    return pl.pallas_call(
        functools.partial(attend_kernel, direct, source_blocks, heads_local),
        out_shape=(
            jax.ShapeDtypeStruct((1, 1, kept_count * BLK, row_width), jnp.bfloat16),
            jax.ShapeDtypeStruct(shape, jnp.bfloat16),
        ),
        in_specs=[pl.BlockSpec(memory_space=pltpu.SMEM)] + [vmem] * (2 + len(arrivals)),
        out_specs=(pl.BlockSpec(memory_space=pl.ANY), vmem),
        scratch_shapes=scratch,
        compiler_params=pltpu.CompilerParams(vmem_limit_bytes=16 * 1024 * 1024),
        name="attend",
    )(kept_blocks, jnp.asarray(cosine), jnp.asarray(sine), *arrivals)


def output_kernel(heads_local, w_ref, *refs):
    gathered_refs, out_ref = refs[:-1], refs[-1]
    query_rows = gathered_refs[0].shape[-2]
    step_count = query_rows // QPK
    if len(gathered_refs) == 1:
        pair_count = gathered_refs[0].shape[0]
        pairs = [gathered_refs[0][p].astype(jnp.float32) for p in range(pair_count)]
    else:
        pair_count = len(gathered_refs)
        me = lax.axis_index("seq")
        arrived = [ref[...].astype(jnp.float32) for ref in gathered_refs]
        pairs = arrived
        bit = 1
        while bit < pair_count:
            swap = jnp.bitwise_and(me, bit) != 0
            pairs = [jnp.where(swap, pairs[p ^ bit], pairs[p]) for p in range(pair_count)]
            bit *= 2
    requests = pair_count // heads_local
    pieces = []
    for l in range(heads_local):
        for h in range(QPK):
            rows = slice(h * step_count, (h + 1) * step_count)
            pieces.append(
                jnp.concatenate(
                    [pairs[r * heads_local + l][rows] for r in range(requests)], axis=0
                )
            )
    merged = jnp.concatenate(pieces, axis=1).astype(jnp.bfloat16)
    total = jnp.dot(merged, w_ref[...], preferred_element_type=jnp.float32)
    if len(out_ref.shape) == 2:
        out_ref[...] = total
    else:
        for i in range(out_ref.shape[0]):
            out_ref[i] = total


def output(gathered, w_out, heads_local, pair_count, head_count):
    query_rows = gathered[0].shape[-2]
    total_rows = pair_count // heads_local * (query_rows // QPK)
    shape = (total_rows, w_out.shape[1])
    if not is_direct(head_count):
        shape = (head_count,) + shape
    vmem = pl.BlockSpec(memory_space=pltpu.VMEM)
    terms = pl.pallas_call(
        functools.partial(output_kernel, heads_local),
        out_shape=jax.ShapeDtypeStruct(shape, jnp.float32),
        in_specs=[vmem] * (1 + len(gathered)),
        out_specs=vmem,
        compiler_params=pltpu.CompilerParams(vmem_limit_bytes=8 * 1024 * 1024),
        name="output_projection",
    )(pltpu.with_memory_space_constraint(w_out, pltpu.VMEM), *gathered)
    return terms


def shards(source_cache, kept_blocks, new_hidden, norm_gain, w_query, w_keyval, w_out):
    seq_count = lax.axis_size("seq")
    head_count = lax.axis_size("head")
    requests, heads_local, source_tokens, _ = source_cache.shape
    _, step_count, width = new_hidden.shape
    pair_count = requests * heads_local

    kept_blocks = kept_blocks.transpose(0, 2, 1)
    direct = is_direct(seq_count)
    weights = (new_hidden, norm_gain, w_query, w_keyval)
    if direct:
        partners = range(1, seq_count)
        blocks = pick(kept_blocks, source_cache, range(seq_count))
        parts = project(blocks[0], *weights, pair_count, direct)
        blocks = [blocks[0]] + [swap(blocks[k], "seq", k) for k in partners]
        parts = [parts[0]] + [swap(parts[k], "seq", k) for k in partners]
        arrivals = blocks[::-1] + parts[::-1]
    else:
        (blocks,) = pick(kept_blocks, source_cache, ())
        (parts,) = project(blocks, *weights, pair_count, direct)
        arrivals = [all_to_all(parts, "seq"), all_to_all(blocks, "seq")]
    kept_cache, attended = attend(
        kept_blocks, arrivals, source_tokens // BLK, heads_local, step_count, seq_count, direct
    )
    if direct:
        gathered = [attended] + [swap(attended, "seq", k) for k in range(1, seq_count)]
    else:
        gathered = [all_to_all(attended, "seq")]
    terms = output(gathered, w_out, heads_local, pair_count, head_count)
    if is_direct(head_count):
        terms = terms + swap(terms, "head", 2)
        summed = terms + swap(terms, "head", 1)
    else:
        summed = jnp.sum(all_to_all(terms, "head"), axis=0)
    summed = summed.reshape(requests, step_count, width)
    decoded = (new_hidden.astype(jnp.float32) + summed).astype(jnp.bfloat16)
    return (kept_cache, decoded)


def solution(mesh):
    in_specs = (
        P("groups", "head", "seq", None),
        P("groups", None, None),
        P("groups", None, "seq"),
        P("seq"),
        P("seq", "head"),
        P("seq", "head", None),
        P("head", "seq"),
    )
    out_specs = (P("head", ("groups", "seq"), None, None), P("groups", None, "seq"))
    return jax.shard_map(shards, mesh=mesh, in_specs=in_specs, out_specs=out_specs, check_vma=False)
```

```python
import functools
import math

import jax
import jax.numpy as jnp
import numpy as np
from jax import lax
from jax.experimental import pallas as pl
from jax.experimental.pallas import tpu as pltpu
from jax.sharding import PartitionSpec as P

D = 8192
HD = 128
QPK = 8
BLK = 128
MOST = 2
ROPE_BASE = 500000.0
EPS = 1e-05

CONTRACT_LAST = (((1,), (1,)), ((), ()))


def rope_tables(prompt_length, step_count):
    positions = prompt_length + np.arange(2 * step_count) % step_count
    frequency = ROPE_BASE ** (-np.arange(HD // 2, dtype=np.float64) * 2.0 / HD)
    angles = positions[:, None] * frequency[None, :]
    cosine = np.concatenate([np.cos(angles)] * 2, axis=1)
    sine = np.concatenate([-np.sin(angles), np.sin(angles)], axis=1)
    return cosine.astype(np.float32), sine.astype(np.float32)


def rotate(v, cosine, sine):
    swapped = jnp.concatenate([v[..., HD // 2 :], v[..., : HD // 2]], axis=-1)
    return v * cosine + swapped * sine


def is_direct(count):
    return count == 4


def swap(outgoing, axis, offset):
    count = lax.axis_size(axis)
    return lax.ppermute(outgoing, axis, [(i, i ^ offset) for i in range(count)])


def all_to_all(outgoing, axis):
    return lax.all_to_all(outgoing, axis, split_axis=0, concat_axis=0, tiled=True)


def start_picks(kept_ref, cache_ref, pair, out_ref, sem):
    _, heads_local, source_tokens, _ = cache_ref.shape
    source_blocks = source_tokens // BLK
    kept_count = kept_ref.shape[1]
    me = lax.axis_index("seq")
    request = lax.div(pair, heads_local)
    local = lax.rem(pair, heads_local)
    head = lax.axis_index("head") * heads_local + local

    def count(k, total):
        block = kept_ref[request, k, head]
        return total + (block < me * source_blocks).astype(jnp.int32)

    start = lax.fori_loop(0, kept_count, count, jnp.int32(0), unroll=kept_count <= 8)
    for slot in range(MOST):
        rank = jnp.minimum(start + slot, kept_count - 1)
        block = kept_ref[request, rank, head] - me * source_blocks
        block = jnp.clip(block, 0, source_blocks - 1)
        rows = pl.ds(pl.multiple_of(block * BLK, BLK), BLK)
        pltpu.make_async_copy(
            cache_ref.at[request, local, rows], out_ref.at[pl.ds(slot * BLK, BLK)], sem
        ).start()


def pick_kernel(offsets, kept_hbm_ref, cache_ref, *refs):
    outs, kept_ref, sem = refs[:-2], refs[-2], refs[-1]
    pltpu.sync_copy(kept_hbm_ref, kept_ref)
    if offsets:
        me = lax.axis_index("seq")
        for offset, out_ref in zip(offsets, outs):
            start_picks(kept_ref, cache_ref, jnp.bitwise_xor(me, offset), out_ref, sem)
    else:

        def pair_body(pair, carry):
            start_picks(kept_ref, cache_ref, pair, outs[0].at[pair], sem)
            return carry

        lax.fori_loop(0, outs[0].shape[0], pair_body, 0)
    for out_ref in outs:
        pltpu.make_async_copy(out_ref, out_ref, sem).wait()


def pick(kept_blocks, source_cache, offsets):
    requests, heads_local, _, row_width = source_cache.shape
    block = (MOST * BLK, row_width)
    if offsets:
        shapes = [jax.ShapeDtypeStruct(block, jnp.bfloat16)] * len(offsets)
    else:
        shapes = [jax.ShapeDtypeStruct((requests * heads_local,) + block, jnp.bfloat16)]
    return pl.pallas_call(
        functools.partial(pick_kernel, offsets),
        out_shape=shapes,
        in_specs=[pl.BlockSpec(memory_space=pl.ANY)] * 2,
        out_specs=[pl.BlockSpec(memory_space=pltpu.VMEM)] * len(shapes),
        scratch_shapes=[
            pltpu.SMEM(kept_blocks.shape, jnp.int32),
            pltpu.SemaphoreType.DMA,
        ],
        compiler_params=pltpu.CompilerParams(vmem_limit_bytes=8 * 1024 * 1024),
        cost_estimate=pl.CostEstimate(flops=10**10, bytes_accessed=0, transcendentals=0),
        name="pick_blocks",
    )(
        pltpu.with_memory_space_constraint(kept_blocks, pltpu.HBM),
        pltpu.with_memory_space_constraint(source_cache, pltpu.HBM),
    )


def interleave(rows):
    count, width = rows.shape
    chunks = width // HD
    stacked = jnp.concatenate(
        [rows[:, c * HD : (c + 1) * HD] for c in range(chunks)], axis=0
    ).astype(jnp.bfloat16)
    source = lax.broadcasted_iota(jnp.int32, (HD, 4 * HD), 0)
    target = lax.broadcasted_iota(jnp.int32, (HD, 4 * HD), 1)
    place = jnp.where(target < 2 * HD, 2 * source, 2 * source + 1 + 2 * HD)
    spread = (place == target).astype(jnp.bfloat16)
    wide = jnp.dot(stacked, spread, preferred_element_type=jnp.float32)
    return [
        jnp.concatenate(
            [
                wide[c * count : (c + 1) * count, : 2 * HD],
                wide[c * count : (c + 1) * count, 2 * HD :],
            ],
            axis=0,
        ).astype(jnp.bfloat16)
        for c in range(chunks)
    ]


def project_kernel(direct, after_ref, hidden_ref, gain_ref, wq_ref, wkv_ref, *outs):
    del after_ref
    requests, step_count, width = hidden_ref.shape
    heads_local = wkv_ref.shape[1]
    row_count = requests * step_count
    me = lax.axis_index("seq")
    hidden = jnp.concatenate(
        [hidden_ref[r].astype(jnp.float32) for r in range(requests)], axis=0
    )
    square = jnp.sum(hidden * hidden, axis=1, keepdims=True)
    gain = gain_ref[...].astype(jnp.float32)
    scaled = jnp.concatenate(
        [hidden[:, c * HD : (c + 1) * HD] * gain[c : c + 1] for c in range(width // HD)], axis=1
    ).astype(jnp.bfloat16)
    query = jnp.dot(scaled, wq_ref[...], preferred_element_type=jnp.float32)
    keyval = jnp.zeros((heads_local * row_count, wkv_ref.shape[2]), jnp.float32)
    for c, spread in enumerate(interleave(scaled.astype(jnp.float32))):
        alternate = wkv_ref[c * HD : (c + 1) * HD].reshape(heads_local * HD, wkv_ref.shape[2])
        keyval += jnp.dot(spread, alternate, preferred_element_type=jnp.float32)

    def pieces_of(r, l):
        steps = slice(r * step_count, (r + 1) * step_count)
        square_rows = jnp.broadcast_to(square[steps], (step_count, HD))
        own = keyval[l * row_count + r * step_count : l * row_count + (r + 1) * step_count]
        heads = [query[steps, (l * QPK + h) * HD : (l * QPK + h + 1) * HD] for h in range(QPK)]
        return heads + [own[:, :HD], own[:, HD:], square_rows, square_rows]

    def write_pair(out_ref, pieces):
        for j, piece in enumerate(pieces):
            out_ref[j * step_count : (j + 1) * step_count, :] = piece

    for r in range(requests):
        for l in range(heads_local):
            pair = r * heads_local + l
            pieces = pieces_of(r, l)
            if not direct:
                write_pair(outs[0].at[pair], pieces)
                continue
            for offset, out_ref in enumerate(outs):
                pl.when(jnp.bitwise_xor(me, offset) == pair)(
                    functools.partial(write_pair, out_ref, pieces)
                )


def project(after, new_hidden, norm_gain, w_query, w_keyval, pair_count, direct):
    requests, step_count, width = new_hidden.shape
    terms = ((QPK + 4) * step_count, HD)
    if direct:
        shapes = [jax.ShapeDtypeStruct(terms, jnp.float32)] * pair_count
    else:
        shapes = [jax.ShapeDtypeStruct((pair_count,) + terms, jnp.float32)]
    vmem = pl.BlockSpec(memory_space=pltpu.VMEM)
    weights = w_query.size + w_keyval.size
    return pl.pallas_call(
        functools.partial(project_kernel, direct),
        out_shape=shapes,
        in_specs=[pl.BlockSpec(memory_space=pl.ANY)] + [vmem] * 4,
        out_specs=[vmem] * len(shapes),
        compiler_params=pltpu.CompilerParams(vmem_limit_bytes=8 * 1024 * 1024),
        cost_estimate=pl.CostEstimate(
            flops=2 * requests * step_count * weights,
            bytes_accessed=2 * weights,
            transcendentals=0,
        ),
        name="project",
    )(
        after,
        new_hidden,
        norm_gain.reshape(width // HD, HD),
        pltpu.with_memory_space_constraint(w_query, pltpu.VMEM),
        pltpu.with_memory_space_constraint(w_keyval, pltpu.VMEM),
    )


def attend_kernel(direct, source_blocks, heads_local, kept_ref, cos_ref, sin_ref, *refs):
    kept_count = kept_ref.shape[1]
    step_count = cos_ref.shape[0] // 2
    me = lax.axis_index("seq")
    request = lax.div(me, heads_local)
    head = lax.axis_index("head") * heads_local + lax.rem(me, heads_local)
    if direct:
        cache_ref, attended_ref, sem = refs[-3:]
        by_offset, parts_refs = refs[:4][::-1], refs[4:8][::-1]
        kept = cache_ref.at[0, 0]
    else:
        parts_ref, blocks_ref, cache_ref, attended_ref, sem, kept = refs

    def start_copy(k, carry):
        previous, slot = carry
        source = lax.div(kept_ref[request, k, head], source_blocks)
        slot = jnp.where(source == previous, jnp.minimum(slot + 1, MOST - 1), 0)
        target = kept.at[pl.ds(pl.multiple_of(k * BLK, BLK), BLK)]
        rows = pl.ds(pl.multiple_of(slot * BLK, BLK), BLK)
        if direct:
            for offset, ref in enumerate(by_offset):
                pl.when(jnp.bitwise_xor(me, offset) == source)(
                    pltpu.make_async_copy(ref.at[rows], target, sem).start
                )
        else:
            pltpu.make_async_copy(blocks_ref.at[source, rows], target, sem).start()
        return source, slot

    lax.fori_loop(
        0, kept_count, start_copy, (jnp.int32(-1), jnp.int32(0)), unroll=kept_count <= 8
    )
    if direct:
        total = sum(ref[...] for ref in parts_refs)
    else:
        total = jnp.sum(parts_ref[...], axis=0)
        pltpu.make_async_copy(kept, kept, sem).wait()
        pltpu.make_async_copy(kept, cache_ref.at[0, 0], sem).start()
    query_rows = QPK * step_count
    inverse = lax.rsqrt(total[query_rows + 2 * step_count :] * (1.0 / D) + EPS)
    cosine, sine = cos_ref[...], sin_ref[...]
    query = total[:query_rows].reshape(QPK // 2, 2 * step_count, HD) * inverse[None]
    query = rotate(query, cosine[None], sine[None]).reshape(query_rows, HD).astype(jnp.bfloat16)
    keyval = total[query_rows : query_rows + 2 * step_count] * inverse
    new_key = rotate(keyval, cosine, sine).astype(jnp.bfloat16)
    new_value = jnp.concatenate([keyval[step_count:], keyval[:step_count]], axis=0)
    new_value = new_value.astype(jnp.bfloat16)
    scale = 1.0 / math.sqrt(HD)
    score = lax.dot_general(query, new_key, CONTRACT_LAST, preferred_element_type=jnp.float32)
    row = lax.broadcasted_iota(jnp.int32, score.shape, 0)
    column = lax.broadcasted_iota(jnp.int32, score.shape, 1)
    scores = [jnp.where(column <= lax.rem(row, step_count), score * scale, -jnp.inf)]
    values = [new_value]
    def add_block(block, filled):
        score = lax.dot_general(
            query, block[:, :HD], CONTRACT_LAST, preferred_element_type=jnp.float32
        )
        column = lax.broadcasted_iota(jnp.int32, score.shape, 1)
        scores.append(jnp.where(column < filled * BLK, score * scale, -jnp.inf))
        values.append(block[:, HD:])

    if direct:
        for offset, ref in enumerate(by_offset):
            source = jnp.bitwise_xor(me, offset)
            filled = jnp.int32(0)
            for k in range(kept_count):
                here = lax.div(kept_ref[request, k, head], source_blocks) == source
                filled += here.astype(jnp.int32)
            add_block(ref[: MOST * BLK, :], filled)
    else:
        add_block(kept[...], kept_count)
    row_max = functools.reduce(
        jnp.maximum, [jnp.max(score, axis=1, keepdims=True) for score in scores]
    )
    denominator = jnp.zeros((query_rows, 1), jnp.float32)
    numerator = jnp.zeros((query_rows, HD), jnp.float32)
    for score, value in zip(scores, values):
        weight = jnp.exp(score - row_max)
        denominator += jnp.sum(weight, axis=1, keepdims=True)
        numerator += jnp.dot(
            weight.astype(jnp.bfloat16), value, preferred_element_type=jnp.float32
        )
    attended = (numerator / denominator).astype(jnp.bfloat16)
    if direct:
        attended_ref[...] = attended
    else:
        for i in range(attended_ref.shape[0]):
            attended_ref[i] = attended
    pltpu.make_async_copy(cache_ref, cache_ref, sem).wait()


def attend(kept_blocks, arrivals, source_blocks, heads_local, step_count, seq_count, direct):
    kept_count = kept_blocks.shape[1]
    row_width = 2 * HD
    cosine, sine = rope_tables(source_blocks * BLK * seq_count, step_count)
    shape = (QPK * step_count, HD)
    scratch = [pltpu.SemaphoreType.DMA]
    if not direct:
        shape = (seq_count,) + shape
        scratch.append(pltpu.VMEM((kept_count * BLK, row_width), jnp.bfloat16))
    vmem = pl.BlockSpec(memory_space=pltpu.VMEM)
    return pl.pallas_call(
        functools.partial(attend_kernel, direct, source_blocks, heads_local),
        out_shape=(
            jax.ShapeDtypeStruct((1, 1, kept_count * BLK, row_width), jnp.bfloat16),
            jax.ShapeDtypeStruct(shape, jnp.bfloat16),
        ),
        in_specs=[pl.BlockSpec(memory_space=pltpu.SMEM)] + [vmem] * (2 + len(arrivals)),
        out_specs=(pl.BlockSpec(memory_space=pl.ANY), vmem),
        scratch_shapes=scratch,
        compiler_params=pltpu.CompilerParams(vmem_limit_bytes=16 * 1024 * 1024),
        name="attend",
    )(kept_blocks, jnp.asarray(cosine), jnp.asarray(sine), *arrivals)


def output_kernel(heads_local, w_ref, *refs):
    gathered_refs, out_ref = refs[:-1], refs[-1]
    query_rows = gathered_refs[0].shape[-2]
    step_count = query_rows // QPK
    if len(gathered_refs) == 1:
        pair_count = gathered_refs[0].shape[0]
        pairs = [gathered_refs[0][p].astype(jnp.float32) for p in range(pair_count)]
    else:
        pair_count = len(gathered_refs)
        me = lax.axis_index("seq")
        arrived = [ref[...].astype(jnp.float32) for ref in gathered_refs]
        pairs = arrived
        bit = 1
        while bit < pair_count:
            swap = jnp.bitwise_and(me, bit) != 0
            pairs = [jnp.where(swap, pairs[p ^ bit], pairs[p]) for p in range(pair_count)]
            bit *= 2
    requests = pair_count // heads_local
    pieces = []
    for l in range(heads_local):
        for h in range(QPK):
            rows = slice(h * step_count, (h + 1) * step_count)
            pieces.append(
                jnp.concatenate(
                    [pairs[r * heads_local + l][rows] for r in range(requests)], axis=0
                )
            )
    merged = jnp.concatenate(pieces, axis=1).astype(jnp.bfloat16)
    total = jnp.dot(merged, w_ref[...], preferred_element_type=jnp.float32)
    if len(out_ref.shape) == 2:
        out_ref[...] = total
    else:
        for i in range(out_ref.shape[0]):
            out_ref[i] = total


def output(gathered, w_out, heads_local, pair_count, head_count):
    query_rows = gathered[0].shape[-2]
    total_rows = pair_count // heads_local * (query_rows // QPK)
    shape = (total_rows, w_out.shape[1])
    if not is_direct(head_count):
        shape = (head_count,) + shape
    vmem = pl.BlockSpec(memory_space=pltpu.VMEM)
    terms = pl.pallas_call(
        functools.partial(output_kernel, heads_local),
        out_shape=jax.ShapeDtypeStruct(shape, jnp.float32),
        in_specs=[vmem] * (1 + len(gathered)),
        out_specs=vmem,
        compiler_params=pltpu.CompilerParams(vmem_limit_bytes=8 * 1024 * 1024),
        name="output_projection",
    )(pltpu.with_memory_space_constraint(w_out, pltpu.VMEM), *gathered)
    return terms


def shards(source_cache, kept_blocks, new_hidden, norm_gain, w_query, w_keyval, w_out):
    seq_count = lax.axis_size("seq")
    head_count = lax.axis_size("head")
    requests, heads_local, source_tokens, _ = source_cache.shape
    _, step_count, width = new_hidden.shape
    pair_count = requests * heads_local

    kept_blocks = kept_blocks.transpose(0, 2, 1)
    direct = is_direct(seq_count)
    weights = (new_hidden, norm_gain, w_query, w_keyval)
    if direct:
        partners = range(1, seq_count)
        blocks = pick(kept_blocks, source_cache, range(seq_count))
        parts = list(project(blocks[0], *weights, pair_count, direct))
        blocks = [blocks[0]] + [swap(blocks[k], "seq", k) for k in partners]
        parts[1], blocks[1] = lax.optimization_barrier((parts[1], blocks[1]))
        parts = [parts[0]] + [swap(parts[k], "seq", k) for k in partners]
        arrivals = blocks[::-1] + parts[::-1]
    else:
        (blocks,) = pick(kept_blocks, source_cache, ())
        (parts,) = project(blocks, *weights, pair_count, direct)
        arrivals = [all_to_all(parts, "seq"), all_to_all(blocks, "seq")]
    kept_cache, attended = attend(
        kept_blocks, arrivals, source_tokens // BLK, heads_local, step_count, seq_count, direct
    )
    if direct:
        gathered = [attended] + [swap(attended, "seq", k) for k in range(1, seq_count)]
    else:
        gathered = [all_to_all(attended, "seq")]
    terms = output(gathered, w_out, heads_local, pair_count, head_count)
    if is_direct(head_count):
        terms = terms + swap(terms, "head", 2)
        summed = terms + swap(terms, "head", 1)
    else:
        summed = jnp.sum(all_to_all(terms, "head"), axis=0)
    summed = summed.reshape(requests, step_count, width)
    decoded = (new_hidden.astype(jnp.float32) + summed).astype(jnp.bfloat16)
    return (kept_cache, decoded)


def solution(mesh):
    in_specs = (
        P("groups", "head", "seq", None),
        P("groups", None, None),
        P("groups", None, "seq"),
        P("seq"),
        P("seq", "head"),
        P("seq", "head", None),
        P("head", "seq"),
    )
    out_specs = (P("head", ("groups", "seq"), None, None), P("groups", None, "seq"))
    return jax.shard_map(shards, mesh=mesh, in_specs=in_specs, out_specs=out_specs, check_vma=False)
```

```python
import functools
import math

import jax
import jax.numpy as jnp
import numpy as np
from jax import lax
from jax.experimental import pallas as pl
from jax.experimental.pallas import tpu as pltpu
from jax.sharding import PartitionSpec as P

D = 8192
HD = 128
QPK = 8
BLK = 128
MOST = 2
ROPE_BASE = 500000.0
EPS = 1e-05

CONTRACT_LAST = (((1,), (1,)), ((), ()))


def rope_tables(prompt_length, step_count):
    positions = prompt_length + np.arange(2 * step_count) % step_count
    frequency = ROPE_BASE ** (-np.arange(HD // 2, dtype=np.float64) * 2.0 / HD)
    angles = positions[:, None] * frequency[None, :]
    cosine = np.concatenate([np.cos(angles)] * 2, axis=1)
    sine = np.concatenate([-np.sin(angles), np.sin(angles)], axis=1)
    return cosine.astype(np.float32), sine.astype(np.float32)


def rotate(v, cosine, sine):
    swapped = jnp.concatenate([v[..., HD // 2 :], v[..., : HD // 2]], axis=-1)
    return v * cosine + swapped * sine


def is_direct(count):
    return count == 4


def swap(outgoing, axis, offset):
    count = lax.axis_size(axis)
    return lax.ppermute(outgoing, axis, [(i, i ^ offset) for i in range(count)])


def all_to_all(outgoing, axis):
    return lax.all_to_all(outgoing, axis, split_axis=0, concat_axis=0, tiled=True)


def start_picks(kept_ref, cache_ref, pair, out_ref, sem):
    _, heads_local, source_tokens, _ = cache_ref.shape
    source_blocks = source_tokens // BLK
    kept_count = kept_ref.shape[1]
    me = lax.axis_index("seq")
    request = lax.div(pair, heads_local)
    local = lax.rem(pair, heads_local)
    head = lax.axis_index("head") * heads_local + local

    def count(k, total):
        block = kept_ref[request, k, head]
        return total + (block < me * source_blocks).astype(jnp.int32)

    start = lax.fori_loop(0, kept_count, count, jnp.int32(0), unroll=kept_count <= 8)
    for slot in range(MOST):
        rank = jnp.minimum(start + slot, kept_count - 1)
        block = kept_ref[request, rank, head] - me * source_blocks
        block = jnp.clip(block, 0, source_blocks - 1)
        rows = pl.ds(pl.multiple_of(block * BLK, BLK), BLK)
        pltpu.make_async_copy(
            cache_ref.at[request, local, rows], out_ref.at[pl.ds(slot * BLK, BLK)], sem
        ).start()


def pick_kernel(offsets, kept_hbm_ref, cache_ref, *refs):
    outs, kept_ref, sem = refs[:-2], refs[-2], refs[-1]
    pltpu.sync_copy(kept_hbm_ref, kept_ref)
    if offsets:
        me = lax.axis_index("seq")
        for offset, out_ref in zip(offsets, outs):
            start_picks(kept_ref, cache_ref, jnp.bitwise_xor(me, offset), out_ref, sem)
    else:

        def pair_body(pair, carry):
            start_picks(kept_ref, cache_ref, pair, outs[0].at[pair], sem)
            return carry

        lax.fori_loop(0, outs[0].shape[0], pair_body, 0)
    for out_ref in outs:
        pltpu.make_async_copy(out_ref, out_ref, sem).wait()


def pick(kept_blocks, source_cache, offsets):
    requests, heads_local, _, row_width = source_cache.shape
    block = (MOST * BLK, row_width)
    if offsets:
        shapes = [jax.ShapeDtypeStruct(block, jnp.bfloat16)] * len(offsets)
    else:
        shapes = [jax.ShapeDtypeStruct((requests * heads_local,) + block, jnp.bfloat16)]
    return pl.pallas_call(
        functools.partial(pick_kernel, offsets),
        out_shape=shapes,
        in_specs=[pl.BlockSpec(memory_space=pl.ANY)] * 2,
        out_specs=[pl.BlockSpec(memory_space=pltpu.VMEM)] * len(shapes),
        scratch_shapes=[
            pltpu.SMEM(kept_blocks.shape, jnp.int32),
            pltpu.SemaphoreType.DMA,
        ],
        compiler_params=pltpu.CompilerParams(vmem_limit_bytes=8 * 1024 * 1024),
        cost_estimate=pl.CostEstimate(flops=10**10, bytes_accessed=0, transcendentals=0),
        name="pick_blocks",
    )(
        pltpu.with_memory_space_constraint(kept_blocks, pltpu.HBM),
        pltpu.with_memory_space_constraint(source_cache, pltpu.HBM),
    )


def interleave(rows):
    count, width = rows.shape
    chunks = width // HD
    stacked = jnp.concatenate(
        [rows[:, c * HD : (c + 1) * HD] for c in range(chunks)], axis=0
    ).astype(jnp.bfloat16)
    source = lax.broadcasted_iota(jnp.int32, (HD, 4 * HD), 0)
    target = lax.broadcasted_iota(jnp.int32, (HD, 4 * HD), 1)
    place = jnp.where(target < 2 * HD, 2 * source, 2 * source + 1 + 2 * HD)
    spread = (place == target).astype(jnp.bfloat16)
    wide = jnp.dot(stacked, spread, preferred_element_type=jnp.float32)
    return [
        jnp.concatenate(
            [
                wide[c * count : (c + 1) * count, : 2 * HD],
                wide[c * count : (c + 1) * count, 2 * HD :],
            ],
            axis=0,
        ).astype(jnp.bfloat16)
        for c in range(chunks)
    ]


def project_kernel(direct, after_ref, hidden_ref, gain_ref, wq_ref, wkv_ref, *outs):
    del after_ref
    requests, step_count, width = hidden_ref.shape
    heads_local = wkv_ref.shape[1]
    row_count = requests * step_count
    me = lax.axis_index("seq")
    hidden = jnp.concatenate(
        [hidden_ref[r].astype(jnp.float32) for r in range(requests)], axis=0
    )
    square = jnp.sum(hidden * hidden, axis=1, keepdims=True)
    gain = gain_ref[...].astype(jnp.float32)
    scaled = jnp.concatenate(
        [hidden[:, c * HD : (c + 1) * HD] * gain[c : c + 1] for c in range(width // HD)], axis=1
    ).astype(jnp.bfloat16)
    query = jnp.dot(scaled, wq_ref[...], preferred_element_type=jnp.float32)
    keyval = jnp.zeros((heads_local * row_count, wkv_ref.shape[2]), jnp.float32)
    for c, spread in enumerate(interleave(scaled.astype(jnp.float32))):
        alternate = wkv_ref[c * HD : (c + 1) * HD].reshape(heads_local * HD, wkv_ref.shape[2])
        keyval += jnp.dot(spread, alternate, preferred_element_type=jnp.float32)

    def pieces_of(r, l):
        steps = slice(r * step_count, (r + 1) * step_count)
        square_rows = jnp.broadcast_to(square[steps], (step_count, HD))
        own = keyval[l * row_count + r * step_count : l * row_count + (r + 1) * step_count]
        heads = [query[steps, (l * QPK + h) * HD : (l * QPK + h + 1) * HD] for h in range(QPK)]
        return heads + [own[:, :HD], own[:, HD:], square_rows, square_rows]

    def write_pair(out_ref, pieces):
        for j, piece in enumerate(pieces):
            out_ref[j * step_count : (j + 1) * step_count, :] = piece

    for r in range(requests):
        for l in range(heads_local):
            pair = r * heads_local + l
            pieces = pieces_of(r, l)
            if not direct:
                write_pair(outs[0].at[pair], pieces)
                continue
            for offset, out_ref in enumerate(outs):
                pl.when(jnp.bitwise_xor(me, offset) == pair)(
                    functools.partial(write_pair, out_ref, pieces)
                )


def project(after, new_hidden, norm_gain, w_query, w_keyval, pair_count, direct):
    requests, step_count, width = new_hidden.shape
    terms = ((QPK + 4) * step_count, HD)
    if direct:
        shapes = [jax.ShapeDtypeStruct(terms, jnp.float32)] * pair_count
    else:
        shapes = [jax.ShapeDtypeStruct((pair_count,) + terms, jnp.float32)]
    vmem = pl.BlockSpec(memory_space=pltpu.VMEM)
    weights = w_query.size + w_keyval.size
    return pl.pallas_call(
        functools.partial(project_kernel, direct),
        out_shape=shapes,
        in_specs=[pl.BlockSpec(memory_space=pl.ANY)] + [vmem] * 4,
        out_specs=[vmem] * len(shapes),
        compiler_params=pltpu.CompilerParams(vmem_limit_bytes=8 * 1024 * 1024),
        cost_estimate=pl.CostEstimate(
            flops=2 * requests * step_count * weights,
            bytes_accessed=2 * weights,
            transcendentals=0,
        ),
        name="project",
    )(
        after,
        new_hidden,
        norm_gain.reshape(width // HD, HD),
        pltpu.with_memory_space_constraint(w_query, pltpu.VMEM),
        pltpu.with_memory_space_constraint(w_keyval, pltpu.VMEM),
    )


def attend_kernel(direct, source_blocks, heads_local, kept_ref, cos_ref, sin_ref, *refs):
    kept_count = kept_ref.shape[1]
    step_count = cos_ref.shape[0] // 2
    me = lax.axis_index("seq")
    request = lax.div(me, heads_local)
    head = lax.axis_index("head") * heads_local + lax.rem(me, heads_local)
    if direct:
        cache_ref, attended_ref, sem = refs[-3:]
        by_offset, parts_refs = refs[:4][::-1], refs[4:8][::-1]
        kept = cache_ref.at[0, 0]
    else:
        parts_ref, blocks_ref, cache_ref, attended_ref, sem, kept = refs

    def start_copy(k, carry):
        previous, slot = carry
        source = lax.div(kept_ref[request, k, head], source_blocks)
        slot = jnp.where(source == previous, jnp.minimum(slot + 1, MOST - 1), 0)
        target = kept.at[pl.ds(pl.multiple_of(k * BLK, BLK), BLK)]
        rows = pl.ds(pl.multiple_of(slot * BLK, BLK), BLK)
        if direct:
            for offset, ref in enumerate(by_offset):
                pl.when(jnp.bitwise_xor(me, offset) == source)(
                    pltpu.make_async_copy(ref.at[rows], target, sem).start
                )
        else:
            pltpu.make_async_copy(blocks_ref.at[source, rows], target, sem).start()
        return source, slot

    lax.fori_loop(
        0, kept_count, start_copy, (jnp.int32(-1), jnp.int32(0)), unroll=kept_count <= 8
    )
    if direct:
        total = sum(ref[...] for ref in parts_refs)
    else:
        total = jnp.sum(parts_ref[...], axis=0)
        pltpu.make_async_copy(kept, kept, sem).wait()
        pltpu.make_async_copy(kept, cache_ref.at[0, 0], sem).start()
    query_rows = QPK * step_count
    inverse = lax.rsqrt(total[query_rows + 2 * step_count :] * (1.0 / D) + EPS)
    cosine, sine = cos_ref[...], sin_ref[...]
    query = total[:query_rows].reshape(QPK // 2, 2 * step_count, HD) * inverse[None]
    query = rotate(query, cosine[None], sine[None]).reshape(query_rows, HD).astype(jnp.bfloat16)
    keyval = total[query_rows : query_rows + 2 * step_count] * inverse
    new_key = rotate(keyval, cosine, sine).astype(jnp.bfloat16)
    new_value = jnp.concatenate([keyval[step_count:], keyval[:step_count]], axis=0)
    new_value = new_value.astype(jnp.bfloat16)
    scale = 1.0 / math.sqrt(HD)
    score = lax.dot_general(query, new_key, CONTRACT_LAST, preferred_element_type=jnp.float32)
    row = lax.broadcasted_iota(jnp.int32, score.shape, 0)
    column = lax.broadcasted_iota(jnp.int32, score.shape, 1)
    scores = [jnp.where(column <= lax.rem(row, step_count), score * scale, -jnp.inf)]
    values = [new_value]
    def add_block(block, filled):
        score = lax.dot_general(
            query, block[:, :HD], CONTRACT_LAST, preferred_element_type=jnp.float32
        )
        column = lax.broadcasted_iota(jnp.int32, score.shape, 1)
        scores.append(jnp.where(column < filled * BLK, score * scale, -jnp.inf))
        values.append(block[:, HD:])

    if direct:
        for offset, ref in enumerate(by_offset):
            source = jnp.bitwise_xor(me, offset)
            filled = jnp.int32(0)
            for k in range(kept_count):
                here = lax.div(kept_ref[request, k, head], source_blocks) == source
                filled += here.astype(jnp.int32)
            add_block(ref[: MOST * BLK, :], filled)
    else:
        add_block(kept[...], kept_count)
    row_max = functools.reduce(
        jnp.maximum, [jnp.max(score, axis=1, keepdims=True) for score in scores]
    )
    denominator = jnp.zeros((query_rows, 1), jnp.float32)
    numerator = jnp.zeros((query_rows, HD), jnp.float32)
    for score, value in zip(scores, values):
        weight = jnp.exp(score - row_max)
        denominator += jnp.sum(weight, axis=1, keepdims=True)
        numerator += jnp.dot(
            weight.astype(jnp.bfloat16), value, preferred_element_type=jnp.float32
        )
    attended = (numerator / denominator).astype(jnp.bfloat16)
    if direct:
        attended_ref[...] = attended
    else:
        for i in range(attended_ref.shape[0]):
            attended_ref[i] = attended
    pltpu.make_async_copy(cache_ref, cache_ref, sem).wait()


def attend(kept_blocks, arrivals, source_blocks, heads_local, step_count, seq_count, direct):
    kept_count = kept_blocks.shape[1]
    row_width = 2 * HD
    cosine, sine = rope_tables(source_blocks * BLK * seq_count, step_count)
    shape = (QPK * step_count, HD)
    scratch = [pltpu.SemaphoreType.DMA]
    if not direct:
        shape = (seq_count,) + shape
        scratch.append(pltpu.VMEM((kept_count * BLK, row_width), jnp.bfloat16))
    vmem = pl.BlockSpec(memory_space=pltpu.VMEM)
    return pl.pallas_call(
        functools.partial(attend_kernel, direct, source_blocks, heads_local),
        out_shape=(
            jax.ShapeDtypeStruct((1, 1, kept_count * BLK, row_width), jnp.bfloat16),
            jax.ShapeDtypeStruct(shape, jnp.bfloat16),
        ),
        in_specs=[pl.BlockSpec(memory_space=pltpu.SMEM)] + [vmem] * (2 + len(arrivals)),
        out_specs=(pl.BlockSpec(memory_space=pl.ANY), vmem),
        scratch_shapes=scratch,
        compiler_params=pltpu.CompilerParams(vmem_limit_bytes=16 * 1024 * 1024),
        name="attend",
    )(kept_blocks, jnp.asarray(cosine), jnp.asarray(sine), *arrivals)


def output_kernel(heads_local, w_ref, *refs):
    gathered_refs, out_ref = refs[:-1], refs[-1]
    query_rows = gathered_refs[0].shape[-2]
    step_count = query_rows // QPK
    if len(gathered_refs) == 1:
        pair_count = gathered_refs[0].shape[0]
        pairs = [gathered_refs[0][p].astype(jnp.float32) for p in range(pair_count)]
    else:
        pair_count = len(gathered_refs)
        me = lax.axis_index("seq")
        arrived = [ref[...].astype(jnp.float32) for ref in gathered_refs]
        pairs = arrived
        bit = 1
        while bit < pair_count:
            swap = jnp.bitwise_and(me, bit) != 0
            pairs = [jnp.where(swap, pairs[p ^ bit], pairs[p]) for p in range(pair_count)]
            bit *= 2
    requests = pair_count // heads_local
    pieces = []
    for l in range(heads_local):
        for h in range(QPK):
            rows = slice(h * step_count, (h + 1) * step_count)
            pieces.append(
                jnp.concatenate(
                    [pairs[r * heads_local + l][rows] for r in range(requests)], axis=0
                )
            )
    merged = jnp.concatenate(pieces, axis=1).astype(jnp.bfloat16)
    total = jnp.dot(merged, w_ref[...], preferred_element_type=jnp.float32)
    if len(out_ref.shape) == 2:
        out_ref[...] = total
    else:
        for i in range(out_ref.shape[0]):
            out_ref[i] = total


def output(gathered, w_out, heads_local, pair_count, head_count):
    query_rows = gathered[0].shape[-2]
    total_rows = pair_count // heads_local * (query_rows // QPK)
    shape = (total_rows, w_out.shape[1])
    if not is_direct(head_count):
        shape = (head_count,) + shape
    vmem = pl.BlockSpec(memory_space=pltpu.VMEM)
    terms = pl.pallas_call(
        functools.partial(output_kernel, heads_local),
        out_shape=jax.ShapeDtypeStruct(shape, jnp.float32),
        in_specs=[vmem] * (1 + len(gathered)),
        out_specs=vmem,
        compiler_params=pltpu.CompilerParams(vmem_limit_bytes=8 * 1024 * 1024),
        name="output_projection",
    )(pltpu.with_memory_space_constraint(w_out, pltpu.VMEM), *gathered)
    return terms


def shards(source_cache, kept_blocks, new_hidden, norm_gain, w_query, w_keyval, w_out):
    seq_count = lax.axis_size("seq")
    head_count = lax.axis_size("head")
    requests, heads_local, source_tokens, _ = source_cache.shape
    _, step_count, width = new_hidden.shape
    pair_count = requests * heads_local

    kept_blocks = kept_blocks.transpose(0, 2, 1)
    direct = is_direct(seq_count)
    weights = (new_hidden, norm_gain, w_query, w_keyval)
    if direct:
        partners = range(1, seq_count)
        blocks = pick(kept_blocks, source_cache, range(seq_count))
        parts = list(project(blocks[0], *weights, pair_count, direct))
        blocks = [blocks[0]] + [swap(blocks[k], "seq", k) for k in partners]
        parts[1], blocks[3] = lax.optimization_barrier((parts[1], blocks[3]))
        parts = [parts[0]] + [swap(parts[k], "seq", k) for k in partners]
        arrivals = blocks[::-1] + parts[::-1]
    else:
        (blocks,) = pick(kept_blocks, source_cache, ())
        (parts,) = project(blocks, *weights, pair_count, direct)
        arrivals = [all_to_all(parts, "seq"), all_to_all(blocks, "seq")]
    kept_cache, attended = attend(
        kept_blocks, arrivals, source_tokens // BLK, heads_local, step_count, seq_count, direct
    )
    if direct:
        gathered = [attended] + [swap(attended, "seq", k) for k in range(1, seq_count)]
    else:
        gathered = [all_to_all(attended, "seq")]
    terms = output(gathered, w_out, heads_local, pair_count, head_count)
    if is_direct(head_count):
        terms = terms + swap(terms, "head", 2)
        summed = terms + swap(terms, "head", 1)
    else:
        summed = jnp.sum(all_to_all(terms, "head"), axis=0)
    summed = summed.reshape(requests, step_count, width)
    decoded = (new_hidden.astype(jnp.float32) + summed).astype(jnp.bfloat16)
    return (kept_cache, decoded)


def solution(mesh):
    in_specs = (
        P("groups", "head", "seq", None),
        P("groups", None, None),
        P("groups", None, "seq"),
        P("seq"),
        P("seq", "head"),
        P("seq", "head", None),
        P("head", "seq"),
    )
    out_specs = (P("head", ("groups", "seq"), None, None), P("groups", None, "seq"))
    return jax.shard_map(shards, mesh=mesh, in_specs=in_specs, out_specs=out_specs, check_vma=False)
```

```python
import functools
import math

import jax
import jax.numpy as jnp
import numpy as np
from jax import lax
from jax.experimental import pallas as pl
from jax.experimental.pallas import tpu as pltpu
from jax.sharding import PartitionSpec as P

D = 8192
HD = 128
QPK = 8
BLK = 128
MOST = 2
ROPE_BASE = 500000.0
EPS = 1e-05

CONTRACT_LAST = (((1,), (1,)), ((), ()))


def rope_tables(prompt_length, step_count):
    positions = prompt_length + np.arange(2 * step_count) % step_count
    frequency = ROPE_BASE ** (-np.arange(HD // 2, dtype=np.float64) * 2.0 / HD)
    angles = positions[:, None] * frequency[None, :]
    cosine = np.concatenate([np.cos(angles)] * 2, axis=1)
    sine = np.concatenate([-np.sin(angles), np.sin(angles)], axis=1)
    return cosine.astype(np.float32), sine.astype(np.float32)


def rotate(v, cosine, sine):
    swapped = jnp.concatenate([v[..., HD // 2 :], v[..., : HD // 2]], axis=-1)
    return v * cosine + swapped * sine


def is_direct(count):
    return count == 4


def swap(outgoing, axis, offset):
    count = lax.axis_size(axis)
    return lax.ppermute(outgoing, axis, [(i, i ^ offset) for i in range(count)])


def all_to_all(outgoing, axis):
    return lax.all_to_all(outgoing, axis, split_axis=0, concat_axis=0, tiled=True)


def picked_rows(kept_ref, cache_shape, pair, slot):
    _, heads_local, source_tokens, _ = cache_shape
    source_blocks = source_tokens // BLK
    kept_count = kept_ref.shape[1]
    first_block = lax.axis_index("seq") * source_blocks
    request = lax.div(pair, heads_local)
    local = lax.rem(pair, heads_local)
    head = lax.axis_index("head") * heads_local + local

    def count(k, total):
        return total + (kept_ref[request, k, head] < first_block).astype(jnp.int32)

    start = lax.fori_loop(0, kept_count, count, jnp.int32(0), unroll=kept_count <= 8)
    rank = jnp.minimum(start + slot, kept_count - 1)
    block = jnp.clip(kept_ref[request, rank, head] - first_block, 0, source_blocks - 1)
    return request, local, pl.ds(pl.multiple_of(block * BLK, BLK), BLK)


def pick_near_kernel(kept_hbm_ref, cache_ref, *refs):
    *outs, kept_ref, cache, kept_sem, sem = refs
    kept_copy = pltpu.make_async_copy(kept_hbm_ref, kept_ref, kept_sem)
    cache_copy = pltpu.make_async_copy(cache_ref, cache, sem)
    kept_copy.start()
    cache_copy.start()
    kept_copy.wait()
    me = lax.axis_index("seq")
    places = [
        [picked_rows(kept_ref, cache.shape, jnp.bitwise_xor(me, k), slot) for slot in range(MOST)]
        for k in range(len(outs))
    ]
    cache_copy.wait()
    for out_ref, slots in zip(outs, places):
        for slot, (request, local, rows) in enumerate(slots):
            out_ref[slot * BLK : (slot + 1) * BLK, :] = cache[request, local, rows, :]


def pick_all_kernel(kept_hbm_ref, cache_ref, out_ref, kept_ref, sem):
    pltpu.sync_copy(kept_hbm_ref, kept_ref)

    def pair_body(pair, carry):
        for slot in range(MOST):
            request, local, rows = picked_rows(kept_ref, cache_ref.shape, pair, slot)
            pltpu.make_async_copy(
                cache_ref.at[request, local, rows],
                out_ref.at[pair, pl.ds(slot * BLK, BLK)],
                sem,
            ).start()
        return carry

    lax.fori_loop(0, out_ref.shape[0], pair_body, 0)
    pltpu.make_async_copy(out_ref, out_ref, sem).wait()


def pick(kept_blocks, source_cache, direct):
    requests, heads_local, _, row_width = source_cache.shape
    pair_count = requests * heads_local
    block = (MOST * BLK, row_width)
    kept_scratch = pltpu.SMEM(kept_blocks.shape, jnp.int32)
    if direct:
        shapes = [jax.ShapeDtypeStruct(block, jnp.bfloat16)] * pair_count
        scratch = [
            kept_scratch,
            pltpu.VMEM(source_cache.shape, jnp.bfloat16),
            pltpu.SemaphoreType.DMA,
            pltpu.SemaphoreType.DMA,
        ]
    else:
        shapes = [jax.ShapeDtypeStruct((pair_count,) + block, jnp.bfloat16)]
        scratch = [kept_scratch, pltpu.SemaphoreType.DMA]
    return pl.pallas_call(
        pick_near_kernel if direct else pick_all_kernel,
        out_shape=shapes,
        in_specs=[pl.BlockSpec(memory_space=pl.ANY)] * 2,
        out_specs=[pl.BlockSpec(memory_space=pltpu.VMEM)] * len(shapes),
        scratch_shapes=scratch,
        compiler_params=pltpu.CompilerParams(vmem_limit_bytes=8 * 1024 * 1024),
        cost_estimate=pl.CostEstimate(flops=10**10, bytes_accessed=0, transcendentals=0),
        name="pick_blocks",
    )(
        pltpu.with_memory_space_constraint(kept_blocks, pltpu.HBM),
        pltpu.with_memory_space_constraint(source_cache, pltpu.HBM),
    )


def interleave(rows):
    count, width = rows.shape
    chunks = width // HD
    stacked = jnp.concatenate(
        [rows[:, c * HD : (c + 1) * HD] for c in range(chunks)], axis=0
    ).astype(jnp.bfloat16)
    source = lax.broadcasted_iota(jnp.int32, (HD, 4 * HD), 0)
    target = lax.broadcasted_iota(jnp.int32, (HD, 4 * HD), 1)
    place = jnp.where(target < 2 * HD, 2 * source, 2 * source + 1 + 2 * HD)
    spread = (place == target).astype(jnp.bfloat16)
    wide = jnp.dot(stacked, spread, preferred_element_type=jnp.float32)
    return [
        jnp.concatenate(
            [
                wide[c * count : (c + 1) * count, : 2 * HD],
                wide[c * count : (c + 1) * count, 2 * HD :],
            ],
            axis=0,
        ).astype(jnp.bfloat16)
        for c in range(chunks)
    ]


def project_kernel(direct, after_ref, hidden_ref, gain_ref, wq_ref, wkv_ref, *outs):
    del after_ref
    requests, step_count, width = hidden_ref.shape
    heads_local = wkv_ref.shape[1]
    row_count = requests * step_count
    me = lax.axis_index("seq")
    hidden = jnp.concatenate(
        [hidden_ref[r].astype(jnp.float32) for r in range(requests)], axis=0
    )
    square = jnp.sum(hidden * hidden, axis=1, keepdims=True)
    gain = gain_ref[...].astype(jnp.float32)
    scaled = jnp.concatenate(
        [hidden[:, c * HD : (c + 1) * HD] * gain[c : c + 1] for c in range(width // HD)], axis=1
    ).astype(jnp.bfloat16)
    query = jnp.dot(scaled, wq_ref[...], preferred_element_type=jnp.float32)
    keyval = jnp.zeros((heads_local * row_count, wkv_ref.shape[2]), jnp.float32)
    for c, spread in enumerate(interleave(scaled.astype(jnp.float32))):
        alternate = wkv_ref[c * HD : (c + 1) * HD].reshape(heads_local * HD, wkv_ref.shape[2])
        keyval += jnp.dot(spread, alternate, preferred_element_type=jnp.float32)

    def pieces_of(r, l):
        steps = slice(r * step_count, (r + 1) * step_count)
        square_rows = jnp.broadcast_to(square[steps], (step_count, HD))
        own = keyval[l * row_count + r * step_count : l * row_count + (r + 1) * step_count]
        heads = [query[steps, (l * QPK + h) * HD : (l * QPK + h + 1) * HD] for h in range(QPK)]
        return heads + [own[:, :HD], own[:, HD:], square_rows, square_rows]

    def write_pair(out_ref, pieces):
        for j, piece in enumerate(pieces):
            out_ref[j * step_count : (j + 1) * step_count, :] = piece

    for r in range(requests):
        for l in range(heads_local):
            pair = r * heads_local + l
            pieces = pieces_of(r, l)
            if not direct:
                write_pair(outs[0].at[pair], pieces)
                continue
            for offset, out_ref in enumerate(outs):
                pl.when(jnp.bitwise_xor(me, offset) == pair)(
                    functools.partial(write_pair, out_ref, pieces)
                )


def project(after, new_hidden, norm_gain, w_query, w_keyval, pair_count, direct):
    requests, step_count, width = new_hidden.shape
    terms = ((QPK + 4) * step_count, HD)
    if direct:
        shapes = [jax.ShapeDtypeStruct(terms, jnp.float32)] * pair_count
    else:
        shapes = [jax.ShapeDtypeStruct((pair_count,) + terms, jnp.float32)]
    vmem = pl.BlockSpec(memory_space=pltpu.VMEM)
    weights = w_query.size + w_keyval.size
    return pl.pallas_call(
        functools.partial(project_kernel, direct),
        out_shape=shapes,
        in_specs=[pl.BlockSpec(memory_space=pl.ANY)] + [vmem] * 4,
        out_specs=[vmem] * len(shapes),
        compiler_params=pltpu.CompilerParams(vmem_limit_bytes=8 * 1024 * 1024),
        cost_estimate=pl.CostEstimate(
            flops=2 * requests * step_count * weights,
            bytes_accessed=2 * weights,
            transcendentals=0,
        ),
        name="project",
    )(
        after,
        new_hidden,
        norm_gain.reshape(width // HD, HD),
        pltpu.with_memory_space_constraint(w_query, pltpu.VMEM),
        pltpu.with_memory_space_constraint(w_keyval, pltpu.VMEM),
    )


def attend_kernel(direct, source_blocks, heads_local, kept_ref, cos_ref, sin_ref, *refs):
    kept_count = kept_ref.shape[1]
    step_count = cos_ref.shape[0] // 2
    me = lax.axis_index("seq")
    request = lax.div(me, heads_local)
    head = lax.axis_index("head") * heads_local + lax.rem(me, heads_local)
    if direct:
        cache_ref, attended_ref, sem = refs[-3:]
        by_offset, parts_refs = refs[:4][::-1], refs[4:8][::-1]
        kept = cache_ref.at[0, 0]
    else:
        parts_ref, blocks_ref, cache_ref, attended_ref, sem, kept = refs

    def start_copy(k, carry):
        previous, slot = carry
        source = lax.div(kept_ref[request, k, head], source_blocks)
        slot = jnp.where(source == previous, jnp.minimum(slot + 1, MOST - 1), 0)
        target = kept.at[pl.ds(pl.multiple_of(k * BLK, BLK), BLK)]
        rows = pl.ds(pl.multiple_of(slot * BLK, BLK), BLK)
        if direct:
            for offset, ref in enumerate(by_offset):
                pl.when(jnp.bitwise_xor(me, offset) == source)(
                    pltpu.make_async_copy(ref.at[rows], target, sem).start
                )
        else:
            pltpu.make_async_copy(blocks_ref.at[source, rows], target, sem).start()
        return source, slot

    lax.fori_loop(
        0, kept_count, start_copy, (jnp.int32(-1), jnp.int32(0)), unroll=kept_count <= 8
    )
    if direct:
        total = sum(ref[...] for ref in parts_refs)
    else:
        total = jnp.sum(parts_ref[...], axis=0)
        pltpu.make_async_copy(kept, kept, sem).wait()
        pltpu.make_async_copy(kept, cache_ref.at[0, 0], sem).start()
    query_rows = QPK * step_count
    inverse = lax.rsqrt(total[query_rows + 2 * step_count :] * (1.0 / D) + EPS)
    cosine, sine = cos_ref[...], sin_ref[...]
    query = total[:query_rows].reshape(QPK // 2, 2 * step_count, HD) * inverse[None]
    query = rotate(query, cosine[None], sine[None]).reshape(query_rows, HD).astype(jnp.bfloat16)
    keyval = total[query_rows : query_rows + 2 * step_count] * inverse
    new_key = rotate(keyval, cosine, sine).astype(jnp.bfloat16)
    new_value = jnp.concatenate([keyval[step_count:], keyval[:step_count]], axis=0)
    new_value = new_value.astype(jnp.bfloat16)
    scale = 1.0 / math.sqrt(HD)
    score = lax.dot_general(query, new_key, CONTRACT_LAST, preferred_element_type=jnp.float32)
    row = lax.broadcasted_iota(jnp.int32, score.shape, 0)
    column = lax.broadcasted_iota(jnp.int32, score.shape, 1)
    scores = [jnp.where(column <= lax.rem(row, step_count), score * scale, -jnp.inf)]
    values = [new_value]
    def add_block(block, filled):
        score = lax.dot_general(
            query, block[:, :HD], CONTRACT_LAST, preferred_element_type=jnp.float32
        )
        column = lax.broadcasted_iota(jnp.int32, score.shape, 1)
        scores.append(jnp.where(column < filled * BLK, score * scale, -jnp.inf))
        values.append(block[:, HD:])

    if direct:
        for offset, ref in enumerate(by_offset):
            source = jnp.bitwise_xor(me, offset)
            filled = jnp.int32(0)
            for k in range(kept_count):
                here = lax.div(kept_ref[request, k, head], source_blocks) == source
                filled += here.astype(jnp.int32)
            add_block(ref[: MOST * BLK, :], filled)
    else:
        add_block(kept[...], kept_count)
    row_max = functools.reduce(
        jnp.maximum, [jnp.max(score, axis=1, keepdims=True) for score in scores]
    )
    denominator = jnp.zeros((query_rows, 1), jnp.float32)
    numerator = jnp.zeros((query_rows, HD), jnp.float32)
    for score, value in zip(scores, values):
        weight = jnp.exp(score - row_max)
        denominator += jnp.sum(weight, axis=1, keepdims=True)
        numerator += jnp.dot(
            weight.astype(jnp.bfloat16), value, preferred_element_type=jnp.float32
        )
    attended = (numerator / denominator).astype(jnp.bfloat16)
    if direct:
        attended_ref[...] = attended
    else:
        for i in range(attended_ref.shape[0]):
            attended_ref[i] = attended
    pltpu.make_async_copy(cache_ref, cache_ref, sem).wait()


def attend(kept_blocks, arrivals, source_blocks, heads_local, step_count, seq_count, direct):
    kept_count = kept_blocks.shape[1]
    row_width = 2 * HD
    cosine, sine = rope_tables(source_blocks * BLK * seq_count, step_count)
    shape = (QPK * step_count, HD)
    scratch = [pltpu.SemaphoreType.DMA]
    if not direct:
        shape = (seq_count,) + shape
        scratch.append(pltpu.VMEM((kept_count * BLK, row_width), jnp.bfloat16))
    vmem = pl.BlockSpec(memory_space=pltpu.VMEM)
    return pl.pallas_call(
        functools.partial(attend_kernel, direct, source_blocks, heads_local),
        out_shape=(
            jax.ShapeDtypeStruct((1, 1, kept_count * BLK, row_width), jnp.bfloat16),
            jax.ShapeDtypeStruct(shape, jnp.bfloat16),
        ),
        in_specs=[pl.BlockSpec(memory_space=pltpu.SMEM)] + [vmem] * (2 + len(arrivals)),
        out_specs=(pl.BlockSpec(memory_space=pl.ANY), vmem),
        scratch_shapes=scratch,
        compiler_params=pltpu.CompilerParams(vmem_limit_bytes=16 * 1024 * 1024),
        cost_estimate=pl.CostEstimate(flops=10**10, bytes_accessed=0, transcendentals=0),
        name="attend",
    )(kept_blocks, jnp.asarray(cosine), jnp.asarray(sine), *arrivals)


def output_kernel(heads_local, w_ref, *refs):
    gathered_refs, out_ref = refs[:-1], refs[-1]
    query_rows = gathered_refs[0].shape[-2]
    step_count = query_rows // QPK
    if len(gathered_refs) == 1:
        pair_count = gathered_refs[0].shape[0]
        pairs = [gathered_refs[0][p].astype(jnp.float32) for p in range(pair_count)]
    else:
        pair_count = len(gathered_refs)
        me = lax.axis_index("seq")
        arrived = [ref[...].astype(jnp.float32) for ref in gathered_refs]
        pairs = arrived
        bit = 1
        while bit < pair_count:
            swap = jnp.bitwise_and(me, bit) != 0
            pairs = [jnp.where(swap, pairs[p ^ bit], pairs[p]) for p in range(pair_count)]
            bit *= 2
    requests = pair_count // heads_local
    pieces = []
    for l in range(heads_local):
        for h in range(QPK):
            rows = slice(h * step_count, (h + 1) * step_count)
            pieces.append(
                jnp.concatenate(
                    [pairs[r * heads_local + l][rows] for r in range(requests)], axis=0
                )
            )
    merged = jnp.concatenate(pieces, axis=1).astype(jnp.bfloat16)
    total = jnp.dot(merged, w_ref[...], preferred_element_type=jnp.float32)
    if len(out_ref.shape) == 2:
        out_ref[...] = total
    else:
        for i in range(out_ref.shape[0]):
            out_ref[i] = total


def output(gathered, w_out, heads_local, pair_count, head_count):
    query_rows = gathered[0].shape[-2]
    total_rows = pair_count // heads_local * (query_rows // QPK)
    shape = (total_rows, w_out.shape[1])
    if not is_direct(head_count):
        shape = (head_count,) + shape
    vmem = pl.BlockSpec(memory_space=pltpu.VMEM)
    terms = pl.pallas_call(
        functools.partial(output_kernel, heads_local),
        out_shape=jax.ShapeDtypeStruct(shape, jnp.float32),
        in_specs=[vmem] * (1 + len(gathered)),
        out_specs=vmem,
        compiler_params=pltpu.CompilerParams(vmem_limit_bytes=8 * 1024 * 1024),
        name="output_projection",
    )(pltpu.with_memory_space_constraint(w_out, pltpu.VMEM), *gathered)
    return terms


def shards(source_cache, kept_blocks, new_hidden, norm_gain, w_query, w_keyval, w_out):
    seq_count = lax.axis_size("seq")
    head_count = lax.axis_size("head")
    requests, heads_local, source_tokens, _ = source_cache.shape
    _, step_count, width = new_hidden.shape
    pair_count = requests * heads_local

    kept_blocks = kept_blocks.transpose(0, 2, 1)
    direct = is_direct(seq_count)
    weights = (new_hidden, norm_gain, w_query, w_keyval)
    if direct:
        partners = range(1, seq_count)
        blocks = pick(kept_blocks, source_cache, direct)
        parts = list(project(blocks[0], *weights, pair_count, direct))
        blocks = [blocks[0]] + [swap(blocks[k], "seq", k) for k in partners]
        parts[1], blocks[3] = lax.optimization_barrier((parts[1], blocks[3]))
        parts = [parts[0]] + [swap(parts[k], "seq", k) for k in partners]
        arrivals = blocks[::-1] + parts[::-1]
    else:
        (blocks,) = pick(kept_blocks, source_cache, direct)
        (parts,) = project(blocks, *weights, pair_count, direct)
        arrivals = [all_to_all(parts, "seq"), all_to_all(blocks, "seq")]
    kept_cache, attended = attend(
        kept_blocks, arrivals, source_tokens // BLK, heads_local, step_count, seq_count, direct
    )
    if direct:
        gathered = [attended] + [swap(attended, "seq", k) for k in range(1, seq_count)]
    else:
        gathered = [all_to_all(attended, "seq")]
    terms = output(gathered, w_out, heads_local, pair_count, head_count)
    if is_direct(head_count):
        terms = terms + swap(terms, "head", 2)
        summed = terms + swap(terms, "head", 1)
    else:
        summed = jnp.sum(all_to_all(terms, "head"), axis=0)
    summed = summed.reshape(requests, step_count, width)
    decoded = (new_hidden.astype(jnp.float32) + summed).astype(jnp.bfloat16)
    return (kept_cache, decoded)


def solution(mesh):
    in_specs = (
        P("groups", "head", "seq", None),
        P("groups", None, None),
        P("groups", None, "seq"),
        P("seq"),
        P("seq", "head"),
        P("seq", "head", None),
        P("head", "seq"),
    )
    out_specs = (P("head", ("groups", "seq"), None, None), P("groups", None, "seq"))
    return jax.shard_map(shards, mesh=mesh, in_specs=in_specs, out_specs=out_specs, check_vma=False)
```

```python
import functools
import math

import jax
import jax.numpy as jnp
import numpy as np
from jax import lax
from jax.experimental import pallas as pl
from jax.experimental.pallas import tpu as pltpu
from jax.sharding import PartitionSpec as P

D = 8192
HD = 128
QPK = 8
BLK = 128
MOST = 2
ROPE_BASE = 500000.0
EPS = 1e-05

CONTRACT_LAST = (((1,), (1,)), ((), ()))


def rope_tables(prompt_length, step_count):
    positions = prompt_length + np.arange(2 * step_count) % step_count
    frequency = ROPE_BASE ** (-np.arange(HD // 2, dtype=np.float64) * 2.0 / HD)
    angles = positions[:, None] * frequency[None, :]
    cosine = np.concatenate([np.cos(angles)] * 2, axis=1)
    sine = np.concatenate([-np.sin(angles), np.sin(angles)], axis=1)
    return cosine.astype(np.float32), sine.astype(np.float32)


def rotate(v, cosine, sine):
    swapped = jnp.concatenate([v[..., HD // 2 :], v[..., : HD // 2]], axis=-1)
    return v * cosine + swapped * sine


def is_direct(count):
    return count == 4


def swap(outgoing, axis, offset):
    count = lax.axis_size(axis)
    return lax.ppermute(outgoing, axis, [(i, i ^ offset) for i in range(count)])


def all_to_all(outgoing, axis):
    return lax.all_to_all(outgoing, axis, split_axis=0, concat_axis=0, tiled=True)


def picked_rows(kept_ref, cache_shape, pair, slot):
    _, heads_local, source_tokens, _ = cache_shape
    source_blocks = source_tokens // BLK
    kept_count = kept_ref.shape[1]
    first_block = lax.axis_index("seq") * source_blocks
    request = lax.div(pair, heads_local)
    local = lax.rem(pair, heads_local)
    head = lax.axis_index("head") * heads_local + local

    def count(k, total):
        return total + (kept_ref[request, k, head] < first_block).astype(jnp.int32)

    start = lax.fori_loop(0, kept_count, count, jnp.int32(0), unroll=kept_count <= 8)
    rank = jnp.minimum(start + slot, kept_count - 1)
    block = jnp.clip(kept_ref[request, rank, head] - first_block, 0, source_blocks - 1)
    return request, local, pl.ds(pl.multiple_of(block * BLK, BLK), BLK)


def pick_near_kernel(kept_hbm_ref, cache_ref, *refs):
    *outs, kept_ref, cache, kept_sem, sem = refs
    kept_copy = pltpu.make_async_copy(kept_hbm_ref, kept_ref, kept_sem)
    cache_copy = pltpu.make_async_copy(cache_ref, cache, sem)
    kept_copy.start()
    cache_copy.start()
    kept_copy.wait()
    me = lax.axis_index("seq")
    places = [
        [picked_rows(kept_ref, cache.shape, jnp.bitwise_xor(me, k), slot) for slot in range(MOST)]
        for k in range(len(outs))
    ]
    cache_copy.wait()
    for out_ref, slots in zip(outs, places):
        for slot, (request, local, rows) in enumerate(slots):
            out_ref[slot * BLK : (slot + 1) * BLK, :] = cache[request, local, rows, :]


def pick_all_kernel(kept_hbm_ref, cache_ref, out_ref, kept_ref, sem):
    pltpu.sync_copy(kept_hbm_ref, kept_ref)

    def pair_body(pair, carry):
        for slot in range(MOST):
            request, local, rows = picked_rows(kept_ref, cache_ref.shape, pair, slot)
            pltpu.make_async_copy(
                cache_ref.at[request, local, rows],
                out_ref.at[pair, pl.ds(slot * BLK, BLK)],
                sem,
            ).start()
        return carry

    lax.fori_loop(0, out_ref.shape[0], pair_body, 0)
    pltpu.make_async_copy(out_ref, out_ref, sem).wait()


def pick(kept_blocks, source_cache, direct):
    requests, heads_local, _, row_width = source_cache.shape
    pair_count = requests * heads_local
    block = (MOST * BLK, row_width)
    kept_scratch = pltpu.SMEM(kept_blocks.shape, jnp.int32)
    if direct:
        shapes = [jax.ShapeDtypeStruct(block, jnp.bfloat16)] * pair_count
        scratch = [
            kept_scratch,
            pltpu.VMEM(source_cache.shape, jnp.bfloat16),
            pltpu.SemaphoreType.DMA,
            pltpu.SemaphoreType.DMA,
        ]
    else:
        shapes = [jax.ShapeDtypeStruct((pair_count,) + block, jnp.bfloat16)]
        scratch = [kept_scratch, pltpu.SemaphoreType.DMA]
    return pl.pallas_call(
        pick_near_kernel if direct else pick_all_kernel,
        out_shape=shapes,
        in_specs=[pl.BlockSpec(memory_space=pl.ANY)] * 2,
        out_specs=[pl.BlockSpec(memory_space=pltpu.VMEM)] * len(shapes),
        scratch_shapes=scratch,
        compiler_params=pltpu.CompilerParams(vmem_limit_bytes=8 * 1024 * 1024),
        cost_estimate=pl.CostEstimate(flops=10**10, bytes_accessed=0, transcendentals=0),
        name="pick_blocks",
    )(
        pltpu.with_memory_space_constraint(kept_blocks, pltpu.HBM),
        pltpu.with_memory_space_constraint(source_cache, pltpu.HBM),
    )


def interleave(rows):
    count, width = rows.shape
    chunks = width // HD
    stacked = jnp.concatenate(
        [rows[:, c * HD : (c + 1) * HD] for c in range(chunks)], axis=0
    ).astype(jnp.bfloat16)
    source = lax.broadcasted_iota(jnp.int32, (HD, 4 * HD), 0)
    target = lax.broadcasted_iota(jnp.int32, (HD, 4 * HD), 1)
    place = jnp.where(target < 2 * HD, 2 * source, 2 * source + 1 + 2 * HD)
    spread = (place == target).astype(jnp.bfloat16)
    wide = jnp.dot(stacked, spread, preferred_element_type=jnp.float32)
    return [
        jnp.concatenate(
            [
                wide[c * count : (c + 1) * count, : 2 * HD],
                wide[c * count : (c + 1) * count, 2 * HD :],
            ],
            axis=0,
        ).astype(jnp.bfloat16)
        for c in range(chunks)
    ]


def project_kernel(direct, after_ref, hidden_ref, gain_ref, wq_ref, wkv_ref, *outs):
    del after_ref
    requests, step_count, width = hidden_ref.shape
    heads_local = wkv_ref.shape[1]
    row_count = requests * step_count
    me = lax.axis_index("seq")
    hidden = jnp.concatenate(
        [hidden_ref[r].astype(jnp.float32) for r in range(requests)], axis=0
    )
    square = jnp.sum(hidden * hidden, axis=1, keepdims=True)
    gain = gain_ref[...].astype(jnp.float32)
    scaled = jnp.concatenate(
        [hidden[:, c * HD : (c + 1) * HD] * gain[c : c + 1] for c in range(width // HD)], axis=1
    ).astype(jnp.bfloat16)
    query = jnp.dot(scaled, wq_ref[...], preferred_element_type=jnp.float32)
    keyval = jnp.zeros((heads_local * row_count, wkv_ref.shape[2]), jnp.float32)
    for c, spread in enumerate(interleave(scaled.astype(jnp.float32))):
        alternate = wkv_ref[c * HD : (c + 1) * HD].reshape(heads_local * HD, wkv_ref.shape[2])
        keyval += jnp.dot(spread, alternate, preferred_element_type=jnp.float32)

    def pieces_of(r, l):
        steps = slice(r * step_count, (r + 1) * step_count)
        square_rows = jnp.broadcast_to(square[steps], (step_count, HD))
        own = keyval[l * row_count + r * step_count : l * row_count + (r + 1) * step_count]
        heads = [query[steps, (l * QPK + h) * HD : (l * QPK + h + 1) * HD] for h in range(QPK)]
        return heads + [own[:, :HD], own[:, HD:], square_rows, square_rows]

    def write_pair(out_ref, pieces):
        for j, piece in enumerate(pieces):
            out_ref[j * step_count : (j + 1) * step_count, :] = piece

    for r in range(requests):
        for l in range(heads_local):
            pair = r * heads_local + l
            pieces = pieces_of(r, l)
            if not direct:
                write_pair(outs[0].at[pair], pieces)
                continue
            for offset, out_ref in enumerate(outs):
                pl.when(jnp.bitwise_xor(me, offset) == pair)(
                    functools.partial(write_pair, out_ref, pieces)
                )


def project(after, new_hidden, norm_gain, w_query, w_keyval, pair_count, direct):
    requests, step_count, width = new_hidden.shape
    terms = ((QPK + 4) * step_count, HD)
    if direct:
        shapes = [jax.ShapeDtypeStruct(terms, jnp.float32)] * pair_count
    else:
        shapes = [jax.ShapeDtypeStruct((pair_count,) + terms, jnp.float32)]
    vmem = pl.BlockSpec(memory_space=pltpu.VMEM)
    weights = w_query.size + w_keyval.size
    return pl.pallas_call(
        functools.partial(project_kernel, direct),
        out_shape=shapes,
        in_specs=[pl.BlockSpec(memory_space=pl.ANY)] + [vmem] * 4,
        out_specs=[vmem] * len(shapes),
        compiler_params=pltpu.CompilerParams(vmem_limit_bytes=8 * 1024 * 1024),
        cost_estimate=pl.CostEstimate(
            flops=2 * requests * step_count * weights,
            bytes_accessed=2 * weights,
            transcendentals=0,
        ),
        name="project",
    )(
        after,
        new_hidden,
        norm_gain.reshape(width // HD, HD),
        pltpu.with_memory_space_constraint(w_query, pltpu.VMEM),
        pltpu.with_memory_space_constraint(w_keyval, pltpu.VMEM),
    )


def place_kernel(source_blocks, heads_local, kept_ref, after_ref, *refs):
    del after_ref
    *by_offset, cache_ref, sem = refs
    me = lax.axis_index("seq")
    request = lax.div(me, heads_local)
    head = lax.axis_index("head") * heads_local + lax.rem(me, heads_local)
    previous, slot = jnp.int32(-1), jnp.int32(0)
    for k in range(kept_ref.shape[1]):
        source = lax.div(kept_ref[request, k, head], source_blocks)
        slot = jnp.where(source == previous, jnp.minimum(slot + 1, MOST - 1), 0)
        previous = source
        rows = pl.ds(pl.multiple_of(slot * BLK, BLK), BLK)
        target = cache_ref.at[0, 0, pl.ds(k * BLK, BLK)]
        for offset, ref in enumerate(by_offset):
            pl.when(jnp.bitwise_xor(me, offset) == source)(
                pltpu.make_async_copy(ref.at[rows], target, sem).start
            )
    pltpu.make_async_copy(cache_ref, cache_ref, sem).wait()


def place(kept_blocks, after, blocks, source_blocks, heads_local):
    kept_count = kept_blocks.shape[1]
    anywhere = pl.BlockSpec(memory_space=pl.ANY)
    return pl.pallas_call(
        functools.partial(place_kernel, source_blocks, heads_local),
        out_shape=jax.ShapeDtypeStruct((1, 1, kept_count * BLK, 2 * HD), jnp.bfloat16),
        in_specs=[pl.BlockSpec(memory_space=pltpu.SMEM)] + [anywhere] * (1 + len(blocks)),
        out_specs=anywhere,
        scratch_shapes=[pltpu.SemaphoreType.DMA],
        compiler_params=pltpu.CompilerParams(vmem_limit_bytes=8 * 1024 * 1024),
        cost_estimate=pl.CostEstimate(flops=10**9, bytes_accessed=0, transcendentals=0),
        name="place",
    )(kept_blocks, after, *blocks)


def attend_kernel(direct, source_blocks, heads_local, kept_ref, cos_ref, sin_ref, *refs):
    kept_count = kept_ref.shape[1]
    step_count = cos_ref.shape[0] // 2
    me = lax.axis_index("seq")
    request = lax.div(me, heads_local)
    head = lax.axis_index("head") * heads_local + lax.rem(me, heads_local)
    if direct:
        by_offset, parts_refs, attended_ref = refs[:4][::-1], refs[4:8][::-1], refs[8]
        total = sum(ref[...] for ref in parts_refs)
    else:
        parts_ref, blocks_ref, attended_ref, cache_ref, sem, kept = refs

        def start_copy(k, carry):
            previous, slot = carry
            source = lax.div(kept_ref[request, k, head], source_blocks)
            slot = jnp.where(source == previous, jnp.minimum(slot + 1, MOST - 1), 0)
            target = kept.at[pl.ds(pl.multiple_of(k * BLK, BLK), BLK)]
            rows = pl.ds(pl.multiple_of(slot * BLK, BLK), BLK)
            pltpu.make_async_copy(blocks_ref.at[source, rows], target, sem).start()
            return source, slot

        lax.fori_loop(0, kept_count, start_copy, (jnp.int32(-1), jnp.int32(0)))
        total = jnp.sum(parts_ref[...], axis=0)
        pltpu.make_async_copy(kept, kept, sem).wait()
        pltpu.make_async_copy(kept, cache_ref.at[0, 0], sem).start()
    query_rows = QPK * step_count
    inverse = lax.rsqrt(total[query_rows + 2 * step_count :] * (1.0 / D) + EPS)
    cosine, sine = cos_ref[...], sin_ref[...]
    query = total[:query_rows].reshape(QPK // 2, 2 * step_count, HD) * inverse[None]
    query = rotate(query, cosine[None], sine[None]).reshape(query_rows, HD).astype(jnp.bfloat16)
    keyval = total[query_rows : query_rows + 2 * step_count] * inverse
    new_key = rotate(keyval, cosine, sine).astype(jnp.bfloat16)
    new_value = jnp.concatenate([keyval[step_count:], keyval[:step_count]], axis=0)
    new_value = new_value.astype(jnp.bfloat16)
    scale = 1.0 / math.sqrt(HD)
    score = lax.dot_general(query, new_key, CONTRACT_LAST, preferred_element_type=jnp.float32)
    row = lax.broadcasted_iota(jnp.int32, score.shape, 0)
    column = lax.broadcasted_iota(jnp.int32, score.shape, 1)
    scores = [jnp.where(column <= lax.rem(row, step_count), score * scale, -jnp.inf)]
    values = [new_value]
    def add_block(block, filled):
        score = lax.dot_general(
            query, block[:, :HD], CONTRACT_LAST, preferred_element_type=jnp.float32
        )
        column = lax.broadcasted_iota(jnp.int32, score.shape, 1)
        scores.append(jnp.where(column < filled * BLK, score * scale, -jnp.inf))
        values.append(block[:, HD:])

    if direct:
        for offset, ref in enumerate(by_offset):
            source = jnp.bitwise_xor(me, offset)
            filled = jnp.int32(0)
            for k in range(kept_count):
                here = lax.div(kept_ref[request, k, head], source_blocks) == source
                filled += here.astype(jnp.int32)
            add_block(ref[: MOST * BLK, :], filled)
    else:
        add_block(kept[...], kept_count)
    row_max = functools.reduce(
        jnp.maximum, [jnp.max(score, axis=1, keepdims=True) for score in scores]
    )
    denominator = jnp.zeros((query_rows, 1), jnp.float32)
    numerator = jnp.zeros((query_rows, HD), jnp.float32)
    for score, value in zip(scores, values):
        weight = jnp.exp(score - row_max)
        denominator += jnp.sum(weight, axis=1, keepdims=True)
        numerator += jnp.dot(
            weight.astype(jnp.bfloat16), value, preferred_element_type=jnp.float32
        )
    attended = (numerator / denominator).astype(jnp.bfloat16)
    if direct:
        attended_ref[...] = attended
    else:
        for i in range(attended_ref.shape[0]):
            attended_ref[i] = attended
        pltpu.make_async_copy(cache_ref, cache_ref, sem).wait()


def attend(kept_blocks, arrivals, source_blocks, heads_local, step_count, seq_count, direct):
    kept_count = kept_blocks.shape[1]
    cosine, sine = rope_tables(source_blocks * BLK * seq_count, step_count)
    shape = (QPK * step_count, HD)
    vmem = pl.BlockSpec(memory_space=pltpu.VMEM)
    if direct:
        shapes = [jax.ShapeDtypeStruct(shape, jnp.bfloat16)]
        out_specs = [vmem]
        scratch = []
    else:
        cache = (1, 1, kept_count * BLK, 2 * HD)
        shapes = [
            jax.ShapeDtypeStruct((seq_count,) + shape, jnp.bfloat16),
            jax.ShapeDtypeStruct(cache, jnp.bfloat16),
        ]
        out_specs = [vmem, pl.BlockSpec(memory_space=pl.ANY)]
        scratch = [pltpu.SemaphoreType.DMA, pltpu.VMEM(cache[2:], jnp.bfloat16)]
    return pl.pallas_call(
        functools.partial(attend_kernel, direct, source_blocks, heads_local),
        out_shape=shapes,
        in_specs=[pl.BlockSpec(memory_space=pltpu.SMEM)] + [vmem] * (2 + len(arrivals)),
        out_specs=out_specs,
        scratch_shapes=scratch,
        compiler_params=pltpu.CompilerParams(vmem_limit_bytes=16 * 1024 * 1024),
        cost_estimate=pl.CostEstimate(flops=10**10, bytes_accessed=0, transcendentals=0),
        name="attend",
    )(kept_blocks, jnp.asarray(cosine), jnp.asarray(sine), *arrivals)


def merge_heads(first, second, step_count):
    pieces = []
    for h in range(QPK):
        rows = slice(h * step_count, (h + 1) * step_count)
        pieces.append(jnp.concatenate([first[rows], second[rows]], axis=0))
    return jnp.concatenate(pieces, axis=1).astype(jnp.bfloat16)


def output_half_kernel(flip, w_ref, same_ref, other_ref, *refs):
    out_ref = refs[-1]
    query_rows = same_ref.shape[0]
    me = lax.axis_index("seq")
    local = jnp.bitwise_and(me, 1)
    if flip:
        local = 1 - local
    second = me >= 2
    same = same_ref[...].astype(jnp.float32)
    other = other_ref[...].astype(jnp.float32)
    merged = merge_heads(
        jnp.where(second, other, same), jnp.where(second, same, other), query_rows // QPK
    )
    depth = w_ref.shape[0] // 2
    weights = w_ref[pl.ds(pl.multiple_of(local * depth, depth), depth), :]
    total = jnp.dot(merged, weights, preferred_element_type=jnp.float32)
    out_ref[...] = total if len(refs) == 1 else total + refs[0][...]


def output_half(flip, w_out, same, other, *addend):
    rows = 2 * same.shape[0] // QPK
    vmem = pl.BlockSpec(memory_space=pltpu.VMEM)
    return pl.pallas_call(
        functools.partial(output_half_kernel, flip),
        out_shape=jax.ShapeDtypeStruct((rows, w_out.shape[1]), jnp.float32),
        in_specs=[vmem] * (3 + len(addend)),
        out_specs=vmem,
        compiler_params=pltpu.CompilerParams(vmem_limit_bytes=8 * 1024 * 1024),
        cost_estimate=pl.CostEstimate(flops=10**9, bytes_accessed=0, transcendentals=0),
        name="output_half",
    )(w_out, same, other, *addend)


def output_kernel(heads_local, w_ref, gathered_ref, out_ref):
    pair_count, query_rows, _ = gathered_ref.shape
    step_count = query_rows // QPK
    pairs = [gathered_ref[p].astype(jnp.float32) for p in range(pair_count)]
    requests = pair_count // heads_local
    pieces = []
    for l in range(heads_local):
        for h in range(QPK):
            rows = slice(h * step_count, (h + 1) * step_count)
            pieces.append(
                jnp.concatenate(
                    [pairs[r * heads_local + l][rows] for r in range(requests)], axis=0
                )
            )
    merged = jnp.concatenate(pieces, axis=1).astype(jnp.bfloat16)
    out_ref[...] = jnp.dot(merged, w_ref[...], preferred_element_type=jnp.float32)


def output(gathered, w_out, heads_local):
    pair_count, query_rows, _ = gathered.shape
    rows = pair_count // heads_local * (query_rows // QPK)
    vmem = pl.BlockSpec(memory_space=pltpu.VMEM)
    return pl.pallas_call(
        functools.partial(output_kernel, heads_local),
        out_shape=jax.ShapeDtypeStruct((rows, w_out.shape[1]), jnp.float32),
        in_specs=[vmem] * 2,
        out_specs=vmem,
        compiler_params=pltpu.CompilerParams(vmem_limit_bytes=8 * 1024 * 1024),
        name="output_projection",
    )(w_out, gathered)


def shards(source_cache, kept_blocks, new_hidden, norm_gain, w_query, w_keyval, w_out):
    seq_count = lax.axis_size("seq")
    head_count = lax.axis_size("head")
    requests, heads_local, source_tokens, _ = source_cache.shape
    _, step_count, width = new_hidden.shape
    pair_count = requests * heads_local

    kept_blocks = kept_blocks.transpose(0, 2, 1)
    source_blocks = source_tokens // BLK
    direct = is_direct(seq_count) and heads_local == 2
    weights = (new_hidden, norm_gain, w_query, w_keyval)
    w_out = pltpu.with_memory_space_constraint(w_out, pltpu.VMEM)
    shape = (source_blocks, heads_local, step_count, seq_count, direct)
    if direct:
        partners = range(1, seq_count)
        blocks = list(pick(kept_blocks, source_cache, direct))
        parts = list(project(blocks[0], *weights, pair_count, direct))
        blocks = [blocks[0]] + [swap(blocks[k], "seq", k) for k in partners]
        parts[1], blocks[3] = lax.optimization_barrier((parts[1], blocks[3]))
        parts = [parts[0]] + [swap(parts[k], "seq", k) for k in partners]
        (attended,) = attend(kept_blocks, blocks[::-1] + parts[::-1], *shape)
        kept_cache = place(kept_blocks, attended, blocks, source_blocks, heads_local)
        first, second, third = [swap(attended, "seq", k) for k in partners]
        first, kept_cache = lax.optimization_barrier((first, kept_cache))
        terms = output_half(True, w_out, first, third)
        terms = output_half(False, w_out, attended, second, terms)
    else:
        (blocks,) = pick(kept_blocks, source_cache, direct)
        (parts,) = project(blocks, *weights, pair_count, direct)
        arrivals = [all_to_all(parts, "seq"), all_to_all(blocks, "seq")]
        attended, kept_cache = attend(kept_blocks, arrivals, *shape)
        terms = output(all_to_all(attended, "seq"), w_out, heads_local)
    if is_direct(head_count):
        terms = terms + swap(terms, "head", 2)
        summed = terms + swap(terms, "head", 1)
    else:
        summed = lax.psum(terms, "head")
    summed = summed.reshape(requests, step_count, width)
    decoded = (new_hidden.astype(jnp.float32) + summed).astype(jnp.bfloat16)
    return (kept_cache, decoded)


def solution(mesh):
    in_specs = (
        P("groups", "head", "seq", None),
        P("groups", None, None),
        P("groups", None, "seq"),
        P("seq"),
        P("seq", "head"),
        P("seq", "head", None),
        P("head", "seq"),
    )
    out_specs = (P("head", ("groups", "seq"), None, None), P("groups", None, "seq"))
    return jax.shard_map(shards, mesh=mesh, in_specs=in_specs, out_specs=out_specs, check_vma=False)
```

```python
import functools
import math

import jax
import jax.numpy as jnp
import numpy as np
from jax import lax
from jax.experimental import pallas as pl
from jax.experimental.pallas import tpu as pltpu
from jax.sharding import PartitionSpec as P

D = 8192
HD = 128
QPK = 8
BLK = 128
MOST = 2
ROPE_BASE = 500000.0
EPS = 1e-05

CONTRACT_LAST = (((1,), (1,)), ((), ()))


def rope_tables(prompt_length, step_count):
    positions = prompt_length + np.arange(2 * step_count) % step_count
    frequency = ROPE_BASE ** (-np.arange(HD // 2, dtype=np.float64) * 2.0 / HD)
    angles = positions[:, None] * frequency[None, :]
    cosine = np.concatenate([np.cos(angles)] * 2, axis=1)
    sine = np.concatenate([-np.sin(angles), np.sin(angles)], axis=1)
    return cosine.astype(np.float32), sine.astype(np.float32)


def rotate(v, cosine, sine):
    swapped = jnp.concatenate([v[..., HD // 2 :], v[..., : HD // 2]], axis=-1)
    return v * cosine + swapped * sine


def is_direct(count):
    return count == 4


def swap(outgoing, axis, offset):
    count = lax.axis_size(axis)
    return lax.ppermute(outgoing, axis, [(i, i ^ offset) for i in range(count)])


def all_to_all(outgoing, axis):
    return lax.all_to_all(outgoing, axis, split_axis=0, concat_axis=0, tiled=True)


def picked_rows(kept_ref, cache_shape, pair, slot):
    _, heads_local, source_tokens, _ = cache_shape
    source_blocks = source_tokens // BLK
    kept_count = kept_ref.shape[1]
    first_block = lax.axis_index("seq") * source_blocks
    request = lax.div(pair, heads_local)
    local = lax.rem(pair, heads_local)
    head = lax.axis_index("head") * heads_local + local

    def count(k, total):
        return total + (kept_ref[request, k, head] < first_block).astype(jnp.int32)

    start = lax.fori_loop(0, kept_count, count, jnp.int32(0), unroll=kept_count <= 8)
    rank = jnp.minimum(start + slot, kept_count - 1)
    block = jnp.clip(kept_ref[request, rank, head] - first_block, 0, source_blocks - 1)
    return request, local, pl.ds(pl.multiple_of(block * BLK, BLK), BLK)


def pick_near_kernel(kept_hbm_ref, cache_ref, *refs):
    *outs, kept_ref, cache, kept_sem, sem = refs
    kept_copy = pltpu.make_async_copy(kept_hbm_ref, kept_ref, kept_sem)
    cache_copy = pltpu.make_async_copy(cache_ref, cache, sem)
    kept_copy.start()
    cache_copy.start()
    kept_copy.wait()
    me = lax.axis_index("seq")
    places = [
        [picked_rows(kept_ref, cache.shape, jnp.bitwise_xor(me, k), slot) for slot in range(MOST)]
        for k in range(len(outs))
    ]
    cache_copy.wait()
    for out_ref, slots in zip(outs, places):
        for slot, (request, local, rows) in enumerate(slots):
            out_ref[slot * BLK : (slot + 1) * BLK, :] = cache[request, local, rows, :]


def pick_all_kernel(kept_hbm_ref, cache_ref, out_ref, kept_ref, sem):
    pltpu.sync_copy(kept_hbm_ref, kept_ref)

    def pair_body(pair, carry):
        for slot in range(MOST):
            request, local, rows = picked_rows(kept_ref, cache_ref.shape, pair, slot)
            pltpu.make_async_copy(
                cache_ref.at[request, local, rows],
                out_ref.at[pair, pl.ds(slot * BLK, BLK)],
                sem,
            ).start()
        return carry

    lax.fori_loop(0, out_ref.shape[0], pair_body, 0)
    pltpu.make_async_copy(out_ref, out_ref, sem).wait()


def pick(kept_blocks, source_cache, direct):
    requests, heads_local, _, row_width = source_cache.shape
    pair_count = requests * heads_local
    block = (MOST * BLK, row_width)
    kept_scratch = pltpu.SMEM(kept_blocks.shape, jnp.int32)
    if direct:
        shapes = [jax.ShapeDtypeStruct(block, jnp.bfloat16)] * pair_count
        scratch = [
            kept_scratch,
            pltpu.VMEM(source_cache.shape, jnp.bfloat16),
            pltpu.SemaphoreType.DMA,
            pltpu.SemaphoreType.DMA,
        ]
    else:
        shapes = [jax.ShapeDtypeStruct((pair_count,) + block, jnp.bfloat16)]
        scratch = [kept_scratch, pltpu.SemaphoreType.DMA]
    return pl.pallas_call(
        pick_near_kernel if direct else pick_all_kernel,
        out_shape=shapes,
        in_specs=[pl.BlockSpec(memory_space=pl.ANY)] * 2,
        out_specs=[pl.BlockSpec(memory_space=pltpu.VMEM)] * len(shapes),
        scratch_shapes=scratch,
        compiler_params=pltpu.CompilerParams(vmem_limit_bytes=8 * 1024 * 1024),
        cost_estimate=pl.CostEstimate(flops=10**10, bytes_accessed=0, transcendentals=0),
        name="pick_blocks",
    )(
        pltpu.with_memory_space_constraint(kept_blocks, pltpu.HBM),
        pltpu.with_memory_space_constraint(source_cache, pltpu.HBM),
    )


def interleave(rows):
    count, width = rows.shape
    chunks = width // HD
    stacked = jnp.concatenate(
        [rows[:, c * HD : (c + 1) * HD] for c in range(chunks)], axis=0
    ).astype(jnp.bfloat16)
    source = lax.broadcasted_iota(jnp.int32, (HD, 4 * HD), 0)
    target = lax.broadcasted_iota(jnp.int32, (HD, 4 * HD), 1)
    place = jnp.where(target < 2 * HD, 2 * source, 2 * source + 1 + 2 * HD)
    spread = (place == target).astype(jnp.bfloat16)
    wide = jnp.dot(stacked, spread, preferred_element_type=jnp.float32)
    return [
        jnp.concatenate(
            [
                wide[c * count : (c + 1) * count, : 2 * HD],
                wide[c * count : (c + 1) * count, 2 * HD :],
            ],
            axis=0,
        ).astype(jnp.bfloat16)
        for c in range(chunks)
    ]


def project_kernel(direct, after_ref, hidden_ref, gain_ref, wq_ref, wkv_ref, *outs):
    del after_ref
    requests, step_count, width = hidden_ref.shape
    heads_local = wkv_ref.shape[1]
    row_count = requests * step_count
    me = lax.axis_index("seq")
    hidden = jnp.concatenate(
        [hidden_ref[r].astype(jnp.float32) for r in range(requests)], axis=0
    )
    square = jnp.sum(hidden * hidden, axis=1, keepdims=True)
    gain = gain_ref[...].astype(jnp.float32)
    scaled = jnp.concatenate(
        [hidden[:, c * HD : (c + 1) * HD] * gain[c : c + 1] for c in range(width // HD)], axis=1
    ).astype(jnp.bfloat16)
    query = jnp.dot(scaled, wq_ref[...], preferred_element_type=jnp.float32)
    keyval = jnp.zeros((heads_local * row_count, wkv_ref.shape[2]), jnp.float32)
    for c, spread in enumerate(interleave(scaled.astype(jnp.float32))):
        alternate = wkv_ref[c * HD : (c + 1) * HD].reshape(heads_local * HD, wkv_ref.shape[2])
        keyval += jnp.dot(spread, alternate, preferred_element_type=jnp.float32)

    def pieces_of(r, l):
        steps = slice(r * step_count, (r + 1) * step_count)
        square_rows = jnp.broadcast_to(square[steps], (step_count, HD))
        high = square_rows.astype(jnp.bfloat16).astype(jnp.float32)
        own = keyval[l * row_count + r * step_count : l * row_count + (r + 1) * step_count]
        heads = [query[steps, (l * QPK + h) * HD : (l * QPK + h + 1) * HD] for h in range(QPK)]
        return heads + [own[:, :HD], own[:, HD:], high, square_rows - high]

    def write_pair(out_ref, pieces):
        out_ref[...] = jnp.concatenate(pieces, axis=0).astype(out_ref.dtype)

    for r in range(requests):
        for l in range(heads_local):
            pair = r * heads_local + l
            pieces = pieces_of(r, l)
            if not direct:
                write_pair(outs[0].at[pair], pieces)
                continue
            for offset, out_ref in enumerate(outs):
                pl.when(jnp.bitwise_xor(me, offset) == pair)(
                    functools.partial(write_pair, out_ref, pieces)
                )


def project(after, new_hidden, norm_gain, w_query, w_keyval, pair_count, direct):
    requests, step_count, width = new_hidden.shape
    terms = ((QPK + 4) * step_count, HD)
    if direct:
        shapes = [jax.ShapeDtypeStruct(terms, jnp.float32)]
        shapes += [jax.ShapeDtypeStruct(terms, jnp.bfloat16)] * (pair_count - 1)
    else:
        shapes = [jax.ShapeDtypeStruct((pair_count,) + terms, jnp.float32)]
    vmem = pl.BlockSpec(memory_space=pltpu.VMEM)
    weights = w_query.size + w_keyval.size
    return pl.pallas_call(
        functools.partial(project_kernel, direct),
        out_shape=shapes,
        in_specs=[pl.BlockSpec(memory_space=pl.ANY)] + [vmem] * 4,
        out_specs=[vmem] * len(shapes),
        compiler_params=pltpu.CompilerParams(vmem_limit_bytes=8 * 1024 * 1024),
        cost_estimate=pl.CostEstimate(
            flops=2 * requests * step_count * weights,
            bytes_accessed=2 * weights,
            transcendentals=0,
        ),
        name="project",
    )(
        after,
        new_hidden,
        norm_gain.reshape(width // HD, HD),
        pltpu.with_memory_space_constraint(w_query, pltpu.VMEM),
        pltpu.with_memory_space_constraint(w_keyval, pltpu.VMEM),
    )


def place_kernel(source_blocks, heads_local, kept_ref, after_ref, *refs):
    del after_ref
    *by_offset, cache_ref, sem = refs
    me = lax.axis_index("seq")
    request = lax.div(me, heads_local)
    head = lax.axis_index("head") * heads_local + lax.rem(me, heads_local)
    previous, slot = jnp.int32(-1), jnp.int32(0)
    for k in range(kept_ref.shape[1]):
        source = lax.div(kept_ref[request, k, head], source_blocks)
        slot = jnp.where(source == previous, jnp.minimum(slot + 1, MOST - 1), 0)
        previous = source
        rows = pl.ds(pl.multiple_of(slot * BLK, BLK), BLK)
        target = cache_ref.at[0, 0, pl.ds(k * BLK, BLK)]
        for offset, ref in enumerate(by_offset):
            pl.when(jnp.bitwise_xor(me, offset) == source)(
                pltpu.make_async_copy(ref.at[rows], target, sem).start
            )
    pltpu.make_async_copy(cache_ref, cache_ref, sem).wait()


def place(kept_blocks, after, blocks, source_blocks, heads_local):
    kept_count = kept_blocks.shape[1]
    anywhere = pl.BlockSpec(memory_space=pl.ANY)
    return pl.pallas_call(
        functools.partial(place_kernel, source_blocks, heads_local),
        out_shape=jax.ShapeDtypeStruct((1, 1, kept_count * BLK, 2 * HD), jnp.bfloat16),
        in_specs=[pl.BlockSpec(memory_space=pltpu.SMEM)] + [anywhere] * (1 + len(blocks)),
        out_specs=anywhere,
        scratch_shapes=[pltpu.SemaphoreType.DMA],
        compiler_params=pltpu.CompilerParams(vmem_limit_bytes=8 * 1024 * 1024),
        cost_estimate=pl.CostEstimate(flops=10**9, bytes_accessed=0, transcendentals=0),
        name="place",
    )(kept_blocks, after, *blocks)


def attend_kernel(direct, source_blocks, heads_local, kept_ref, cos_ref, sin_ref, *refs):
    kept_count = kept_ref.shape[1]
    step_count = cos_ref.shape[0] // 2
    me = lax.axis_index("seq")
    request = lax.div(me, heads_local)
    head = lax.axis_index("head") * heads_local + lax.rem(me, heads_local)
    if direct:
        by_offset, parts_refs, attended_ref = refs[:4][::-1], refs[4:8][::-1], refs[8]
        total = sum(ref[...].astype(jnp.float32) for ref in parts_refs)
    else:
        parts_ref, blocks_ref, attended_ref, cache_ref, sem, kept = refs

        def start_copy(k, carry):
            previous, slot = carry
            source = lax.div(kept_ref[request, k, head], source_blocks)
            slot = jnp.where(source == previous, jnp.minimum(slot + 1, MOST - 1), 0)
            target = kept.at[pl.ds(pl.multiple_of(k * BLK, BLK), BLK)]
            rows = pl.ds(pl.multiple_of(slot * BLK, BLK), BLK)
            pltpu.make_async_copy(blocks_ref.at[source, rows], target, sem).start()
            return source, slot

        lax.fori_loop(0, kept_count, start_copy, (jnp.int32(-1), jnp.int32(0)))
        total = jnp.sum(parts_ref[...], axis=0)
        pltpu.make_async_copy(kept, kept, sem).wait()
        pltpu.make_async_copy(kept, cache_ref.at[0, 0], sem).start()
    query_rows = QPK * step_count
    high, low = total[-2 * step_count : -step_count], total[-step_count:]
    inverse = lax.rsqrt((high + low) * (1.0 / D) + EPS)
    inverse = jnp.concatenate([inverse, inverse], axis=0)
    cosine, sine = cos_ref[...], sin_ref[...]
    query = total[:query_rows].reshape(QPK // 2, 2 * step_count, HD) * inverse[None]
    query = rotate(query, cosine[None], sine[None]).reshape(query_rows, HD).astype(jnp.bfloat16)
    keyval = total[query_rows : query_rows + 2 * step_count] * inverse
    new_key = rotate(keyval, cosine, sine).astype(jnp.bfloat16)
    new_value = jnp.concatenate([keyval[step_count:], keyval[:step_count]], axis=0)
    new_value = new_value.astype(jnp.bfloat16)
    scale = 1.0 / math.sqrt(HD)
    score = lax.dot_general(query, new_key, CONTRACT_LAST, preferred_element_type=jnp.float32)
    row = lax.broadcasted_iota(jnp.int32, score.shape, 0)
    column = lax.broadcasted_iota(jnp.int32, score.shape, 1)
    scores = [jnp.where(column <= lax.rem(row, step_count), score * scale, -jnp.inf)]
    values = [new_value]
    def add_block(block, filled):
        score = lax.dot_general(
            query, block[:, :HD], CONTRACT_LAST, preferred_element_type=jnp.float32
        )
        column = lax.broadcasted_iota(jnp.int32, score.shape, 1)
        scores.append(jnp.where(column < filled * BLK, score * scale, -jnp.inf))
        values.append(block[:, HD:])

    if direct:
        for offset, ref in enumerate(by_offset):
            source = jnp.bitwise_xor(me, offset)
            filled = jnp.int32(0)
            for k in range(kept_count):
                here = lax.div(kept_ref[request, k, head], source_blocks) == source
                filled += here.astype(jnp.int32)
            add_block(ref[: MOST * BLK, :], filled)
    else:
        add_block(kept[...], kept_count)
    row_max = functools.reduce(
        jnp.maximum, [jnp.max(score, axis=1, keepdims=True) for score in scores]
    )
    denominator = jnp.zeros((query_rows, 1), jnp.float32)
    numerator = jnp.zeros((query_rows, HD), jnp.float32)
    for score, value in zip(scores, values):
        weight = jnp.exp(score - row_max)
        denominator += jnp.sum(weight, axis=1, keepdims=True)
        numerator += jnp.dot(
            weight.astype(jnp.bfloat16), value, preferred_element_type=jnp.float32
        )
    attended = (numerator / denominator).astype(jnp.bfloat16)
    if direct:
        attended_ref[...] = attended
    else:
        for i in range(attended_ref.shape[0]):
            attended_ref[i] = attended
        pltpu.make_async_copy(cache_ref, cache_ref, sem).wait()


def attend(kept_blocks, arrivals, source_blocks, heads_local, step_count, seq_count, direct):
    kept_count = kept_blocks.shape[1]
    cosine, sine = rope_tables(source_blocks * BLK * seq_count, step_count)
    shape = (QPK * step_count, HD)
    vmem = pl.BlockSpec(memory_space=pltpu.VMEM)
    if direct:
        shapes = [jax.ShapeDtypeStruct(shape, jnp.bfloat16)]
        out_specs = [vmem]
        scratch = []
    else:
        cache = (1, 1, kept_count * BLK, 2 * HD)
        shapes = [
            jax.ShapeDtypeStruct((seq_count,) + shape, jnp.bfloat16),
            jax.ShapeDtypeStruct(cache, jnp.bfloat16),
        ]
        out_specs = [vmem, pl.BlockSpec(memory_space=pl.ANY)]
        scratch = [pltpu.SemaphoreType.DMA, pltpu.VMEM(cache[2:], jnp.bfloat16)]
    return pl.pallas_call(
        functools.partial(attend_kernel, direct, source_blocks, heads_local),
        out_shape=shapes,
        in_specs=[pl.BlockSpec(memory_space=pltpu.SMEM)] + [vmem] * (2 + len(arrivals)),
        out_specs=out_specs,
        scratch_shapes=scratch,
        compiler_params=pltpu.CompilerParams(vmem_limit_bytes=16 * 1024 * 1024),
        cost_estimate=pl.CostEstimate(flops=10**10, bytes_accessed=0, transcendentals=0),
        name="attend",
    )(kept_blocks, jnp.asarray(cosine), jnp.asarray(sine), *arrivals)


def merge_heads(first, second, step_count):
    pieces = []
    for h in range(QPK):
        rows = slice(h * step_count, (h + 1) * step_count)
        pieces.append(jnp.concatenate([first[rows], second[rows]], axis=0))
    return jnp.concatenate(pieces, axis=1).astype(jnp.bfloat16)


def output_half_kernel(flip, w_ref, same_ref, other_ref, *refs):
    out_ref = refs[-1]
    query_rows = same_ref.shape[0]
    me = lax.axis_index("seq")
    local = jnp.bitwise_and(me, 1)
    if flip:
        local = 1 - local
    second = me >= 2
    same = same_ref[...].astype(jnp.float32)
    other = other_ref[...].astype(jnp.float32)
    merged = merge_heads(
        jnp.where(second, other, same), jnp.where(second, same, other), query_rows // QPK
    )
    depth = w_ref.shape[0] // 2
    weights = w_ref[pl.ds(pl.multiple_of(local * depth, depth), depth), :]
    total = jnp.dot(merged, weights, preferred_element_type=jnp.float32)
    out_ref[...] = total if len(refs) == 1 else total + refs[0][...]


def output_half(flip, w_out, same, other, *addend):
    rows = 2 * same.shape[0] // QPK
    vmem = pl.BlockSpec(memory_space=pltpu.VMEM)
    return pl.pallas_call(
        functools.partial(output_half_kernel, flip),
        out_shape=jax.ShapeDtypeStruct((rows, w_out.shape[1]), jnp.float32),
        in_specs=[vmem] * (3 + len(addend)),
        out_specs=vmem,
        compiler_params=pltpu.CompilerParams(vmem_limit_bytes=8 * 1024 * 1024),
        cost_estimate=pl.CostEstimate(flops=10**9, bytes_accessed=0, transcendentals=0),
        name="output_half",
    )(w_out, same, other, *addend)


def output_kernel(heads_local, w_ref, gathered_ref, out_ref):
    pair_count, query_rows, _ = gathered_ref.shape
    step_count = query_rows // QPK
    pairs = [gathered_ref[p].astype(jnp.float32) for p in range(pair_count)]
    requests = pair_count // heads_local
    pieces = []
    for l in range(heads_local):
        for h in range(QPK):
            rows = slice(h * step_count, (h + 1) * step_count)
            pieces.append(
                jnp.concatenate(
                    [pairs[r * heads_local + l][rows] for r in range(requests)], axis=0
                )
            )
    merged = jnp.concatenate(pieces, axis=1).astype(jnp.bfloat16)
    out_ref[...] = jnp.dot(merged, w_ref[...], preferred_element_type=jnp.float32)


def output(gathered, w_out, heads_local):
    pair_count, query_rows, _ = gathered.shape
    rows = pair_count // heads_local * (query_rows // QPK)
    vmem = pl.BlockSpec(memory_space=pltpu.VMEM)
    return pl.pallas_call(
        functools.partial(output_kernel, heads_local),
        out_shape=jax.ShapeDtypeStruct((rows, w_out.shape[1]), jnp.float32),
        in_specs=[vmem] * 2,
        out_specs=vmem,
        compiler_params=pltpu.CompilerParams(vmem_limit_bytes=8 * 1024 * 1024),
        name="output_projection",
    )(w_out, gathered)


def shards(source_cache, kept_blocks, new_hidden, norm_gain, w_query, w_keyval, w_out):
    seq_count = lax.axis_size("seq")
    head_count = lax.axis_size("head")
    requests, heads_local, source_tokens, _ = source_cache.shape
    _, step_count, width = new_hidden.shape
    pair_count = requests * heads_local

    kept_blocks = kept_blocks.transpose(0, 2, 1)
    source_blocks = source_tokens // BLK
    direct = is_direct(seq_count) and heads_local == 2
    weights = (new_hidden, norm_gain, w_query, w_keyval)
    w_out = pltpu.with_memory_space_constraint(w_out, pltpu.VMEM)
    shape = (source_blocks, heads_local, step_count, seq_count, direct)
    if direct:
        partners = range(1, seq_count)
        blocks = list(pick(kept_blocks, source_cache, direct))
        parts = list(project(blocks[0], *weights, pair_count, direct))
        blocks = [blocks[0]] + [swap(blocks[k], "seq", k) for k in partners]
        parts[1], blocks[3] = lax.optimization_barrier((parts[1], blocks[3]))
        parts = [parts[0]] + [swap(parts[k], "seq", k) for k in partners]
        (attended,) = attend(kept_blocks, blocks[::-1] + parts[::-1], *shape)
        kept_cache = place(kept_blocks, attended, blocks, source_blocks, heads_local)
        first, second, third = [swap(attended, "seq", k) for k in partners]
        first, kept_cache = lax.optimization_barrier((first, kept_cache))
        terms = output_half(True, w_out, first, third)
        terms = output_half(False, w_out, attended, second, terms)
    else:
        (blocks,) = pick(kept_blocks, source_cache, direct)
        (parts,) = project(blocks, *weights, pair_count, direct)
        arrivals = [all_to_all(parts, "seq"), all_to_all(blocks, "seq")]
        attended, kept_cache = attend(kept_blocks, arrivals, *shape)
        terms = output(all_to_all(attended, "seq"), w_out, heads_local)
    if is_direct(head_count):
        terms = terms + swap(terms, "head", 2)
        summed = terms + swap(terms, "head", 1)
    else:
        summed = lax.psum(terms, "head")
    summed = summed.reshape(requests, step_count, width)
    decoded = (new_hidden.astype(jnp.float32) + summed).astype(jnp.bfloat16)
    return (kept_cache, decoded)


def solution(mesh):
    in_specs = (
        P("groups", "head", "seq", None),
        P("groups", None, None),
        P("groups", None, "seq"),
        P("seq"),
        P("seq", "head"),
        P("seq", "head", None),
        P("head", "seq"),
    )
    out_specs = (P("head", ("groups", "seq"), None, None), P("groups", None, "seq"))
    return jax.shard_map(shards, mesh=mesh, in_specs=in_specs, out_specs=out_specs, check_vma=False)
```

```python
import functools
import math

import jax
import jax.numpy as jnp
import numpy as np
from jax import lax
from jax.experimental import pallas as pl
from jax.experimental.pallas import tpu as pltpu
from jax.sharding import PartitionSpec as P

D = 8192
HD = 128
QPK = 8
BLK = 128
MOST = 2
ROPE_BASE = 500000.0
EPS = 1e-05

CONTRACT_LAST = (((1,), (1,)), ((), ()))


def rope_tables(prompt_length, step_count):
    positions = prompt_length + np.arange(2 * step_count) % step_count
    frequency = ROPE_BASE ** (-np.arange(HD // 2, dtype=np.float64) * 2.0 / HD)
    angles = positions[:, None] * frequency[None, :]
    cosine = np.concatenate([np.cos(angles)] * 2, axis=1)
    sine = np.concatenate([-np.sin(angles), np.sin(angles)], axis=1)
    return cosine.astype(np.float32), sine.astype(np.float32)


def rotate(v, cosine, sine):
    swapped = jnp.concatenate([v[..., HD // 2 :], v[..., : HD // 2]], axis=-1)
    return v * cosine + swapped * sine


def is_direct(count):
    return count == 4


def swap(outgoing, axis, offset):
    count = lax.axis_size(axis)
    return lax.ppermute(outgoing, axis, [(i, i ^ offset) for i in range(count)])


def all_to_all(outgoing, axis):
    return lax.all_to_all(outgoing, axis, split_axis=0, concat_axis=0, tiled=True)


def picked_rows(kept_ref, cache_shape, pair, slot):
    _, heads_local, source_tokens, _ = cache_shape
    source_blocks = source_tokens // BLK
    kept_count = kept_ref.shape[1]
    first_block = lax.axis_index("seq") * source_blocks
    request = lax.div(pair, heads_local)
    local = lax.rem(pair, heads_local)
    head = lax.axis_index("head") * heads_local + local

    def count(k, total):
        return total + (kept_ref[request, k, head] < first_block).astype(jnp.int32)

    start = lax.fori_loop(0, kept_count, count, jnp.int32(0), unroll=kept_count <= 8)
    rank = jnp.minimum(start + slot, kept_count - 1)
    block = jnp.clip(kept_ref[request, rank, head] - first_block, 0, source_blocks - 1)
    return request, local, pl.ds(pl.multiple_of(block * BLK, BLK), BLK)


def pick_near_kernel(kept_hbm_ref, cache_ref, *refs):
    *outs, kept_ref, cache, kept_sem, sem = refs
    kept_copy = pltpu.make_async_copy(kept_hbm_ref, kept_ref, kept_sem)
    cache_copy = pltpu.make_async_copy(cache_ref, cache, sem)
    kept_copy.start()
    cache_copy.start()
    kept_copy.wait()
    me = lax.axis_index("seq")
    places = [
        [picked_rows(kept_ref, cache.shape, jnp.bitwise_xor(me, k), slot) for slot in range(MOST)]
        for k in range(len(outs))
    ]
    cache_copy.wait()
    for out_ref, slots in zip(outs, places):
        for slot, (request, local, rows) in enumerate(slots):
            out_ref[slot * BLK : (slot + 1) * BLK, :] = cache[request, local, rows, :]


def pick_all_kernel(kept_hbm_ref, cache_ref, out_ref, kept_ref, sem):
    pltpu.sync_copy(kept_hbm_ref, kept_ref)

    def pair_body(pair, carry):
        for slot in range(MOST):
            request, local, rows = picked_rows(kept_ref, cache_ref.shape, pair, slot)
            pltpu.make_async_copy(
                cache_ref.at[request, local, rows],
                out_ref.at[pair, pl.ds(slot * BLK, BLK)],
                sem,
            ).start()
        return carry

    lax.fori_loop(0, out_ref.shape[0], pair_body, 0)
    pltpu.make_async_copy(out_ref, out_ref, sem).wait()


def pick(kept_blocks, source_cache, direct):
    requests, heads_local, _, row_width = source_cache.shape
    pair_count = requests * heads_local
    block = (MOST * BLK, row_width)
    kept_scratch = pltpu.SMEM(kept_blocks.shape, jnp.int32)
    if direct:
        shapes = [jax.ShapeDtypeStruct(block, jnp.bfloat16)] * pair_count
        scratch = [
            kept_scratch,
            pltpu.VMEM(source_cache.shape, jnp.bfloat16),
            pltpu.SemaphoreType.DMA,
            pltpu.SemaphoreType.DMA,
        ]
    else:
        shapes = [jax.ShapeDtypeStruct((pair_count,) + block, jnp.bfloat16)]
        scratch = [kept_scratch, pltpu.SemaphoreType.DMA]
    return pl.pallas_call(
        pick_near_kernel if direct else pick_all_kernel,
        out_shape=shapes,
        in_specs=[pl.BlockSpec(memory_space=pl.ANY)] * 2,
        out_specs=[pl.BlockSpec(memory_space=pltpu.VMEM)] * len(shapes),
        scratch_shapes=scratch,
        compiler_params=pltpu.CompilerParams(vmem_limit_bytes=8 * 1024 * 1024),
        cost_estimate=pl.CostEstimate(flops=10**10, bytes_accessed=0, transcendentals=0),
        name="pick_blocks",
    )(
        pltpu.with_memory_space_constraint(kept_blocks, pltpu.HBM),
        pltpu.with_memory_space_constraint(source_cache, pltpu.HBM),
    )


def interleave(rows):
    count, width = rows.shape
    chunks = width // HD
    stacked = jnp.concatenate(
        [rows[:, c * HD : (c + 1) * HD] for c in range(chunks)], axis=0
    ).astype(jnp.bfloat16)
    source = lax.broadcasted_iota(jnp.int32, (HD, 4 * HD), 0)
    target = lax.broadcasted_iota(jnp.int32, (HD, 4 * HD), 1)
    place = jnp.where(target < 2 * HD, 2 * source, 2 * source + 1 + 2 * HD)
    spread = (place == target).astype(jnp.bfloat16)
    wide = jnp.dot(stacked, spread, preferred_element_type=jnp.float32)
    return [
        jnp.concatenate(
            [
                wide[c * count : (c + 1) * count, : 2 * HD],
                wide[c * count : (c + 1) * count, 2 * HD :],
            ],
            axis=0,
        ).astype(jnp.bfloat16)
        for c in range(chunks)
    ]


def project_kernel(direct, after_ref, hidden_ref, gain_ref, wq_ref, wkv_ref, *outs):
    del after_ref
    requests, step_count, width = hidden_ref.shape
    heads_local = wkv_ref.shape[1]
    row_count = requests * step_count
    me = lax.axis_index("seq")
    hidden = jnp.concatenate(
        [hidden_ref[r].astype(jnp.float32) for r in range(requests)], axis=0
    )
    square = jnp.sum(hidden * hidden, axis=1, keepdims=True)
    gain = gain_ref[...].astype(jnp.float32)
    scaled = jnp.concatenate(
        [hidden[:, c * HD : (c + 1) * HD] * gain[c : c + 1] for c in range(width // HD)], axis=1
    ).astype(jnp.bfloat16)
    query = jnp.dot(scaled, wq_ref[...], preferred_element_type=jnp.float32)
    keyval = jnp.zeros((heads_local * row_count, wkv_ref.shape[2]), jnp.float32)
    for c, spread in enumerate(interleave(scaled.astype(jnp.float32))):
        alternate = wkv_ref[c * HD : (c + 1) * HD].reshape(heads_local * HD, wkv_ref.shape[2])
        keyval += jnp.dot(spread, alternate, preferred_element_type=jnp.float32)

    def pieces_of(r, l):
        steps = slice(r * step_count, (r + 1) * step_count)
        square_rows = jnp.broadcast_to(square[steps], (step_count, HD))
        own = keyval[l * row_count + r * step_count : l * row_count + (r + 1) * step_count]
        heads = [query[steps, (l * QPK + h) * HD : (l * QPK + h + 1) * HD] for h in range(QPK)]
        return heads + [own[:, :HD], own[:, HD:], square_rows, square_rows]

    def write_pair(out_ref, pieces):
        for j, piece in enumerate(pieces):
            out_ref[j * step_count : (j + 1) * step_count, :] = piece

    for r in range(requests):
        for l in range(heads_local):
            pair = r * heads_local + l
            pieces = pieces_of(r, l)
            if not direct:
                write_pair(outs[0].at[pair], pieces)
                continue
            for offset, out_ref in enumerate(outs):
                pl.when(jnp.bitwise_xor(me, offset) == pair)(
                    functools.partial(write_pair, out_ref, pieces)
                )


def project(after, new_hidden, norm_gain, w_query, w_keyval, pair_count, direct):
    requests, step_count, width = new_hidden.shape
    terms = ((QPK + 4) * step_count, HD)
    if direct:
        shapes = [jax.ShapeDtypeStruct(terms, jnp.float32)] * pair_count
    else:
        shapes = [jax.ShapeDtypeStruct((pair_count,) + terms, jnp.float32)]
    vmem = pl.BlockSpec(memory_space=pltpu.VMEM)
    weights = w_query.size + w_keyval.size
    return pl.pallas_call(
        functools.partial(project_kernel, direct),
        out_shape=shapes,
        in_specs=[pl.BlockSpec(memory_space=pl.ANY)] + [vmem] * 4,
        out_specs=[vmem] * len(shapes),
        compiler_params=pltpu.CompilerParams(vmem_limit_bytes=8 * 1024 * 1024),
        cost_estimate=pl.CostEstimate(
            flops=2 * requests * step_count * weights,
            bytes_accessed=2 * weights,
            transcendentals=0,
        ),
        name="project",
    )(
        after,
        new_hidden,
        norm_gain.reshape(width // HD, HD),
        pltpu.with_memory_space_constraint(w_query, pltpu.VMEM),
        pltpu.with_memory_space_constraint(w_keyval, pltpu.VMEM),
    )


def place_kernel(source_blocks, heads_local, kept_ref, after_ref, *refs):
    del after_ref
    *by_offset, cache_ref, sem = refs
    me = lax.axis_index("seq")
    request = lax.div(me, heads_local)
    head = lax.axis_index("head") * heads_local + lax.rem(me, heads_local)
    previous, slot = jnp.int32(-1), jnp.int32(0)
    for k in range(kept_ref.shape[1]):
        source = lax.div(kept_ref[request, k, head], source_blocks)
        slot = jnp.where(source == previous, jnp.minimum(slot + 1, MOST - 1), 0)
        previous = source
        rows = pl.ds(pl.multiple_of(slot * BLK, BLK), BLK)
        target = cache_ref.at[0, 0, pl.ds(k * BLK, BLK)]
        for offset, ref in enumerate(by_offset):
            pl.when(jnp.bitwise_xor(me, offset) == source)(
                pltpu.make_async_copy(ref.at[rows], target, sem).start
            )
    pltpu.make_async_copy(cache_ref, cache_ref, sem).wait()


def place(kept_blocks, after, blocks, source_blocks, heads_local):
    kept_count = kept_blocks.shape[1]
    anywhere = pl.BlockSpec(memory_space=pl.ANY)
    return pl.pallas_call(
        functools.partial(place_kernel, source_blocks, heads_local),
        out_shape=jax.ShapeDtypeStruct((1, 1, kept_count * BLK, 2 * HD), jnp.bfloat16),
        in_specs=[pl.BlockSpec(memory_space=pltpu.SMEM)] + [anywhere] * (1 + len(blocks)),
        out_specs=anywhere,
        scratch_shapes=[pltpu.SemaphoreType.DMA],
        compiler_params=pltpu.CompilerParams(vmem_limit_bytes=8 * 1024 * 1024),
        cost_estimate=pl.CostEstimate(flops=10**9, bytes_accessed=0, transcendentals=0),
        name="place",
    )(kept_blocks, after, *blocks)


def attend_kernel(direct, source_blocks, heads_local, kept_ref, cos_ref, sin_ref, *refs):
    kept_count = kept_ref.shape[1]
    step_count = cos_ref.shape[0] // 2
    me = lax.axis_index("seq")
    request = lax.div(me, heads_local)
    head = lax.axis_index("head") * heads_local + lax.rem(me, heads_local)
    if direct:
        by_offset, parts_refs, attended_ref = refs[:4][::-1], refs[4:8][::-1], refs[8]
        total = sum(ref[...] for ref in parts_refs)
    else:
        parts_ref, blocks_ref, attended_ref, cache_ref, sem, kept = refs

        def start_copy(k, carry):
            previous, slot = carry
            source = lax.div(kept_ref[request, k, head], source_blocks)
            slot = jnp.where(source == previous, jnp.minimum(slot + 1, MOST - 1), 0)
            target = kept.at[pl.ds(pl.multiple_of(k * BLK, BLK), BLK)]
            rows = pl.ds(pl.multiple_of(slot * BLK, BLK), BLK)
            pltpu.make_async_copy(blocks_ref.at[source, rows], target, sem).start()
            return source, slot

        lax.fori_loop(0, kept_count, start_copy, (jnp.int32(-1), jnp.int32(0)))
        total = jnp.sum(parts_ref[...], axis=0)
        pltpu.make_async_copy(kept, kept, sem).wait()
        pltpu.make_async_copy(kept, cache_ref.at[0, 0], sem).start()
    query_rows = QPK * step_count
    inverse = lax.rsqrt(total[query_rows + 2 * step_count :] * (1.0 / D) + EPS)
    cosine, sine = cos_ref[...], sin_ref[...]
    query = total[:query_rows].reshape(QPK // 2, 2 * step_count, HD) * inverse[None]
    query = rotate(query, cosine[None], sine[None]).reshape(query_rows, HD).astype(jnp.bfloat16)
    keyval = total[query_rows : query_rows + 2 * step_count] * inverse
    new_key = rotate(keyval, cosine, sine).astype(jnp.bfloat16)
    new_value = jnp.concatenate([keyval[step_count:], keyval[:step_count]], axis=0)
    new_value = new_value.astype(jnp.bfloat16)
    scale = 1.0 / math.sqrt(HD)
    score = lax.dot_general(query, new_key, CONTRACT_LAST, preferred_element_type=jnp.float32)
    row = lax.broadcasted_iota(jnp.int32, score.shape, 0)
    column = lax.broadcasted_iota(jnp.int32, score.shape, 1)
    scores = [jnp.where(column <= lax.rem(row, step_count), score * scale, -jnp.inf)]
    values = [new_value]
    def add_block(block, filled):
        score = lax.dot_general(
            query, block[:, :HD], CONTRACT_LAST, preferred_element_type=jnp.float32
        )
        column = lax.broadcasted_iota(jnp.int32, score.shape, 1)
        scores.append(jnp.where(column < filled * BLK, score * scale, -jnp.inf))
        values.append(block[:, HD:])

    if direct:
        for offset, ref in enumerate(by_offset):
            source = jnp.bitwise_xor(me, offset)
            filled = jnp.int32(0)
            for k in range(kept_count):
                here = lax.div(kept_ref[request, k, head], source_blocks) == source
                filled += here.astype(jnp.int32)
            add_block(ref[: MOST * BLK, :], filled)
    else:
        add_block(kept[...], kept_count)
    row_max = functools.reduce(
        jnp.maximum, [jnp.max(score, axis=1, keepdims=True) for score in scores]
    )
    denominator = jnp.zeros((query_rows, 1), jnp.float32)
    numerator = jnp.zeros((query_rows, HD), jnp.float32)
    for score, value in zip(scores, values):
        weight = jnp.exp(score - row_max)
        denominator += jnp.sum(weight, axis=1, keepdims=True)
        numerator += jnp.dot(
            weight.astype(jnp.bfloat16), value, preferred_element_type=jnp.float32
        )
    attended = (numerator / denominator).astype(jnp.bfloat16)
    if direct:
        attended_ref[...] = attended
    else:
        for i in range(attended_ref.shape[0]):
            attended_ref[i] = attended
        pltpu.make_async_copy(cache_ref, cache_ref, sem).wait()


def attend(kept_blocks, arrivals, source_blocks, heads_local, step_count, seq_count, direct):
    kept_count = kept_blocks.shape[1]
    cosine, sine = rope_tables(source_blocks * BLK * seq_count, step_count)
    shape = (QPK * step_count, HD)
    vmem = pl.BlockSpec(memory_space=pltpu.VMEM)
    if direct:
        shapes = [jax.ShapeDtypeStruct(shape, jnp.bfloat16)]
        out_specs = [vmem]
        scratch = []
    else:
        cache = (1, 1, kept_count * BLK, 2 * HD)
        shapes = [
            jax.ShapeDtypeStruct((seq_count,) + shape, jnp.bfloat16),
            jax.ShapeDtypeStruct(cache, jnp.bfloat16),
        ]
        out_specs = [vmem, pl.BlockSpec(memory_space=pl.ANY)]
        scratch = [pltpu.SemaphoreType.DMA, pltpu.VMEM(cache[2:], jnp.bfloat16)]
    return pl.pallas_call(
        functools.partial(attend_kernel, direct, source_blocks, heads_local),
        out_shape=shapes,
        in_specs=[pl.BlockSpec(memory_space=pltpu.SMEM)] + [vmem] * (2 + len(arrivals)),
        out_specs=out_specs,
        scratch_shapes=scratch,
        compiler_params=pltpu.CompilerParams(vmem_limit_bytes=16 * 1024 * 1024),
        cost_estimate=pl.CostEstimate(flops=10**10, bytes_accessed=0, transcendentals=0),
        name="attend",
    )(kept_blocks, jnp.asarray(cosine), jnp.asarray(sine), *arrivals)


def merge_heads(first, second, step_count):
    pieces = []
    for h in range(QPK):
        rows = slice(h * step_count, (h + 1) * step_count)
        pieces.append(jnp.concatenate([first[rows], second[rows]], axis=0))
    return jnp.concatenate(pieces, axis=1).astype(jnp.bfloat16)


def output_half_kernel(flip, w_ref, same_ref, other_ref, *refs):
    out_ref = refs[-1]
    query_rows = same_ref.shape[0]
    me = lax.axis_index("seq")
    local = jnp.bitwise_and(me, 1)
    if flip:
        local = 1 - local
    second = me >= 2
    same = same_ref[...].astype(jnp.float32)
    other = other_ref[...].astype(jnp.float32)
    merged = merge_heads(
        jnp.where(second, other, same), jnp.where(second, same, other), query_rows // QPK
    )
    depth = w_ref.shape[0] // 2
    weights = w_ref[pl.ds(pl.multiple_of(local * depth, depth), depth), :]
    total = jnp.dot(merged, weights, preferred_element_type=jnp.float32)
    if len(refs) > 1:
        total += refs[0][...]
    out_ref[...] = total.astype(out_ref.dtype)


def output_half(flip, w_out, same, other, *addend):
    rows = 2 * same.shape[0] // QPK
    dtype = jnp.bfloat16 if addend else jnp.float32
    vmem = pl.BlockSpec(memory_space=pltpu.VMEM)
    return pl.pallas_call(
        functools.partial(output_half_kernel, flip),
        out_shape=jax.ShapeDtypeStruct((rows, w_out.shape[1]), dtype),
        in_specs=[vmem] * (3 + len(addend)),
        out_specs=vmem,
        compiler_params=pltpu.CompilerParams(vmem_limit_bytes=8 * 1024 * 1024),
        cost_estimate=pl.CostEstimate(flops=10**9, bytes_accessed=0, transcendentals=0),
        name="output_half",
    )(w_out, same, other, *addend)


def output_kernel(heads_local, w_ref, gathered_ref, out_ref):
    pair_count, query_rows, _ = gathered_ref.shape
    step_count = query_rows // QPK
    pairs = [gathered_ref[p].astype(jnp.float32) for p in range(pair_count)]
    requests = pair_count // heads_local
    pieces = []
    for l in range(heads_local):
        for h in range(QPK):
            rows = slice(h * step_count, (h + 1) * step_count)
            pieces.append(
                jnp.concatenate(
                    [pairs[r * heads_local + l][rows] for r in range(requests)], axis=0
                )
            )
    merged = jnp.concatenate(pieces, axis=1).astype(jnp.bfloat16)
    out_ref[...] = jnp.dot(merged, w_ref[...], preferred_element_type=jnp.float32)


def output(gathered, w_out, heads_local):
    pair_count, query_rows, _ = gathered.shape
    rows = pair_count // heads_local * (query_rows // QPK)
    vmem = pl.BlockSpec(memory_space=pltpu.VMEM)
    return pl.pallas_call(
        functools.partial(output_kernel, heads_local),
        out_shape=jax.ShapeDtypeStruct((rows, w_out.shape[1]), jnp.float32),
        in_specs=[vmem] * 2,
        out_specs=vmem,
        compiler_params=pltpu.CompilerParams(vmem_limit_bytes=8 * 1024 * 1024),
        name="output_projection",
    )(w_out, gathered)


def shards(source_cache, kept_blocks, new_hidden, norm_gain, w_query, w_keyval, w_out):
    seq_count = lax.axis_size("seq")
    head_count = lax.axis_size("head")
    requests, heads_local, source_tokens, _ = source_cache.shape
    _, step_count, width = new_hidden.shape
    pair_count = requests * heads_local

    kept_blocks = kept_blocks.transpose(0, 2, 1)
    source_blocks = source_tokens // BLK
    direct = is_direct(seq_count) and heads_local == 2
    weights = (new_hidden, norm_gain, w_query, w_keyval)
    w_out = pltpu.with_memory_space_constraint(w_out, pltpu.VMEM)
    shape = (source_blocks, heads_local, step_count, seq_count, direct)
    if direct:
        partners = range(1, seq_count)
        blocks = list(pick(kept_blocks, source_cache, direct))
        parts = list(project(blocks[0], *weights, pair_count, direct))
        blocks = [blocks[0]] + [swap(blocks[k], "seq", k) for k in partners]
        parts[1], blocks[3] = lax.optimization_barrier((parts[1], blocks[3]))
        parts = [parts[0]] + [swap(parts[k], "seq", k) for k in partners]
        (attended,) = attend(kept_blocks, blocks[::-1] + parts[::-1], *shape)
        kept_cache = place(kept_blocks, attended, blocks, source_blocks, heads_local)
        first, second, third = [swap(attended, "seq", k) for k in partners]
        first, kept_cache = lax.optimization_barrier((first, kept_cache))
        terms = output_half(True, w_out, first, third)
        terms = output_half(False, w_out, attended, second, terms)
    else:
        (blocks,) = pick(kept_blocks, source_cache, direct)
        (parts,) = project(blocks, *weights, pair_count, direct)
        arrivals = [all_to_all(parts, "seq"), all_to_all(blocks, "seq")]
        attended, kept_cache = attend(kept_blocks, arrivals, *shape)
        terms = output(all_to_all(attended, "seq"), w_out, heads_local)
    if is_direct(head_count):
        terms = terms.astype(jnp.bfloat16)
        others = [swap(terms, "head", k) for k in range(1, head_count)]
        own, core, along, across = [t.astype(jnp.float32) for t in [terms] + others]
        summed = (own + core) + (along + across)
    else:
        summed = lax.psum(terms, "head")
    summed = summed.reshape(requests, step_count, width)
    decoded = (new_hidden.astype(jnp.float32) + summed).astype(jnp.bfloat16)
    return (kept_cache, decoded)


def solution(mesh):
    in_specs = (
        P("groups", "head", "seq", None),
        P("groups", None, None),
        P("groups", None, "seq"),
        P("seq"),
        P("seq", "head"),
        P("seq", "head", None),
        P("head", "seq"),
    )
    out_specs = (P("head", ("groups", "seq"), None, None), P("groups", None, "seq"))
    return jax.shard_map(shards, mesh=mesh, in_specs=in_specs, out_specs=out_specs, check_vma=False)
```

```python
import functools
import math

import jax
import jax.numpy as jnp
import numpy as np
from jax import lax
from jax.experimental import pallas as pl
from jax.experimental.pallas import tpu as pltpu
from jax.sharding import PartitionSpec as P

D = 8192
HD = 128
QPK = 8
BLK = 128
MOST = 2
ROPE_BASE = 500000.0
EPS = 1e-05

CONTRACT_LAST = (((1,), (1,)), ((), ()))


def rope_tables(prompt_length, step_count):
    positions = prompt_length + np.arange(2 * step_count) % step_count
    frequency = ROPE_BASE ** (-np.arange(HD // 2, dtype=np.float64) * 2.0 / HD)
    angles = positions[:, None] * frequency[None, :]
    cosine = np.concatenate([np.cos(angles)] * 2, axis=1)
    sine = np.concatenate([-np.sin(angles), np.sin(angles)], axis=1)
    return cosine.astype(np.float32), sine.astype(np.float32)


def rotate(v, cosine, sine):
    swapped = jnp.concatenate([v[..., HD // 2 :], v[..., : HD // 2]], axis=-1)
    return v * cosine + swapped * sine


def is_direct(count):
    return count == 4


def swap(outgoing, axis, offset):
    count = lax.axis_size(axis)
    return lax.ppermute(outgoing, axis, [(i, i ^ offset) for i in range(count)])


KEPT_ORDER = ((3, 2, 1), (1, 3, 2))


def kept_offset(step):
    if step == 0:
        return 0
    even, odd = (order[step - 1] for order in KEPT_ORDER)
    return jnp.where(jnp.bitwise_and(lax.axis_index("head"), 1) == 0, even, odd)


def swap_kept(outgoing, step):
    seq_count, head_count = lax.axis_size("seq"), lax.axis_size("head")
    pairs = [
        (s * head_count + h, (s ^ KEPT_ORDER[h & 1][step - 1]) * head_count + h)
        for s in range(seq_count)
        for h in range(head_count)
    ]
    return lax.ppermute(outgoing, ("seq", "head"), pairs)


def all_to_all(outgoing, axis):
    return lax.all_to_all(outgoing, axis, split_axis=0, concat_axis=0, tiled=True)


def picked_rows(kept_ref, cache_shape, pair, slot):
    _, heads_local, source_tokens, _ = cache_shape
    source_blocks = source_tokens // BLK
    kept_count = kept_ref.shape[1]
    first_block = lax.axis_index("seq") * source_blocks
    request = lax.div(pair, heads_local)
    local = lax.rem(pair, heads_local)
    head = lax.axis_index("head") * heads_local + local

    def count(k, total):
        return total + (kept_ref[request, k, head] < first_block).astype(jnp.int32)

    start = lax.fori_loop(0, kept_count, count, jnp.int32(0), unroll=kept_count <= 8)
    rank = jnp.minimum(start + slot, kept_count - 1)
    block = jnp.clip(kept_ref[request, rank, head] - first_block, 0, source_blocks - 1)
    return request, local, pl.ds(pl.multiple_of(block * BLK, BLK), BLK)


def pick_near_kernel(kept_hbm_ref, cache_ref, *refs):
    *outs, kept_ref, cache, kept_sem, sem = refs
    kept_copy = pltpu.make_async_copy(kept_hbm_ref, kept_ref, kept_sem)
    cache_copy = pltpu.make_async_copy(cache_ref, cache, sem)
    kept_copy.start()
    cache_copy.start()
    kept_copy.wait()
    me = lax.axis_index("seq")
    places = [
        [
            picked_rows(kept_ref, cache.shape, jnp.bitwise_xor(me, kept_offset(step)), slot)
            for slot in range(MOST)
        ]
        for step in range(len(outs))
    ]
    cache_copy.wait()
    for out_ref, slots in zip(outs, places):
        for slot, (request, local, rows) in enumerate(slots):
            out_ref[slot * BLK : (slot + 1) * BLK, :] = cache[request, local, rows, :]


def pick_all_kernel(kept_hbm_ref, cache_ref, out_ref, kept_ref, sem):
    pltpu.sync_copy(kept_hbm_ref, kept_ref)

    def pair_body(pair, carry):
        for slot in range(MOST):
            request, local, rows = picked_rows(kept_ref, cache_ref.shape, pair, slot)
            pltpu.make_async_copy(
                cache_ref.at[request, local, rows],
                out_ref.at[pair, pl.ds(slot * BLK, BLK)],
                sem,
            ).start()
        return carry

    lax.fori_loop(0, out_ref.shape[0], pair_body, 0)
    pltpu.make_async_copy(out_ref, out_ref, sem).wait()


def pick(kept_blocks, source_cache, direct):
    requests, heads_local, _, row_width = source_cache.shape
    pair_count = requests * heads_local
    block = (MOST * BLK, row_width)
    kept_scratch = pltpu.SMEM(kept_blocks.shape, jnp.int32)
    if direct:
        shapes = [jax.ShapeDtypeStruct(block, jnp.bfloat16)] * pair_count
        scratch = [
            kept_scratch,
            pltpu.VMEM(source_cache.shape, jnp.bfloat16),
            pltpu.SemaphoreType.DMA,
            pltpu.SemaphoreType.DMA,
        ]
    else:
        shapes = [jax.ShapeDtypeStruct((pair_count,) + block, jnp.bfloat16)]
        scratch = [kept_scratch, pltpu.SemaphoreType.DMA]
    return pl.pallas_call(
        pick_near_kernel if direct else pick_all_kernel,
        out_shape=shapes,
        in_specs=[pl.BlockSpec(memory_space=pl.ANY)] * 2,
        out_specs=[pl.BlockSpec(memory_space=pltpu.VMEM)] * len(shapes),
        scratch_shapes=scratch,
        compiler_params=pltpu.CompilerParams(vmem_limit_bytes=8 * 1024 * 1024),
        cost_estimate=pl.CostEstimate(flops=10**10, bytes_accessed=0, transcendentals=0),
        name="pick_blocks",
    )(
        pltpu.with_memory_space_constraint(kept_blocks, pltpu.HBM),
        pltpu.with_memory_space_constraint(source_cache, pltpu.HBM),
    )


def interleave(rows):
    count, width = rows.shape
    chunks = width // HD
    stacked = jnp.concatenate(
        [rows[:, c * HD : (c + 1) * HD] for c in range(chunks)], axis=0
    ).astype(jnp.bfloat16)
    source = lax.broadcasted_iota(jnp.int32, (HD, 4 * HD), 0)
    target = lax.broadcasted_iota(jnp.int32, (HD, 4 * HD), 1)
    place = jnp.where(target < 2 * HD, 2 * source, 2 * source + 1 + 2 * HD)
    spread = (place == target).astype(jnp.bfloat16)
    wide = jnp.dot(stacked, spread, preferred_element_type=jnp.float32)
    return [
        jnp.concatenate(
            [
                wide[c * count : (c + 1) * count, : 2 * HD],
                wide[c * count : (c + 1) * count, 2 * HD :],
            ],
            axis=0,
        ).astype(jnp.bfloat16)
        for c in range(chunks)
    ]


def project_kernel(direct, after_ref, hidden_ref, gain_ref, wq_ref, wkv_ref, *outs):
    del after_ref
    requests, step_count, width = hidden_ref.shape
    heads_local = wkv_ref.shape[1]
    row_count = requests * step_count
    me = lax.axis_index("seq")
    hidden = jnp.concatenate(
        [hidden_ref[r].astype(jnp.float32) for r in range(requests)], axis=0
    )
    square = jnp.sum(hidden * hidden, axis=1, keepdims=True)
    gain = gain_ref[...].astype(jnp.float32)
    scaled = jnp.concatenate(
        [hidden[:, c * HD : (c + 1) * HD] * gain[c : c + 1] for c in range(width // HD)], axis=1
    ).astype(jnp.bfloat16)
    query = jnp.dot(scaled, wq_ref[...], preferred_element_type=jnp.float32)
    keyval = jnp.zeros((heads_local * row_count, wkv_ref.shape[2]), jnp.float32)
    for c, spread in enumerate(interleave(scaled.astype(jnp.float32))):
        alternate = wkv_ref[c * HD : (c + 1) * HD].reshape(heads_local * HD, wkv_ref.shape[2])
        keyval += jnp.dot(spread, alternate, preferred_element_type=jnp.float32)

    def pieces_of(r, l):
        steps = slice(r * step_count, (r + 1) * step_count)
        square_rows = jnp.broadcast_to(square[steps], (step_count, HD))
        own = keyval[l * row_count + r * step_count : l * row_count + (r + 1) * step_count]
        heads = [query[steps, (l * QPK + h) * HD : (l * QPK + h + 1) * HD] for h in range(QPK)]
        return heads + [own[:, :HD], own[:, HD:], square_rows, square_rows]

    def write_pair(out_ref, pieces):
        for j, piece in enumerate(pieces):
            out_ref[j * step_count : (j + 1) * step_count, :] = piece

    for r in range(requests):
        for l in range(heads_local):
            pair = r * heads_local + l
            pieces = pieces_of(r, l)
            if not direct:
                write_pair(outs[0].at[pair], pieces)
                continue
            for offset, out_ref in enumerate(outs):
                pl.when(jnp.bitwise_xor(me, offset) == pair)(
                    functools.partial(write_pair, out_ref, pieces)
                )


def project(after, new_hidden, norm_gain, w_query, w_keyval, pair_count, direct):
    requests, step_count, width = new_hidden.shape
    terms = ((QPK + 4) * step_count, HD)
    if direct:
        shapes = [jax.ShapeDtypeStruct(terms, jnp.float32)] * pair_count
    else:
        shapes = [jax.ShapeDtypeStruct((pair_count,) + terms, jnp.float32)]
    vmem = pl.BlockSpec(memory_space=pltpu.VMEM)
    weights = w_query.size + w_keyval.size
    return pl.pallas_call(
        functools.partial(project_kernel, direct),
        out_shape=shapes,
        in_specs=[pl.BlockSpec(memory_space=pl.ANY)] + [vmem] * 4,
        out_specs=[vmem] * len(shapes),
        compiler_params=pltpu.CompilerParams(vmem_limit_bytes=8 * 1024 * 1024),
        cost_estimate=pl.CostEstimate(
            flops=2 * requests * step_count * weights,
            bytes_accessed=2 * weights,
            transcendentals=0,
        ),
        name="project",
    )(
        after,
        new_hidden,
        norm_gain.reshape(width // HD, HD),
        pltpu.with_memory_space_constraint(w_query, pltpu.VMEM),
        pltpu.with_memory_space_constraint(w_keyval, pltpu.VMEM),
    )


def place_kernel(source_blocks, heads_local, kept_ref, after_ref, *refs):
    del after_ref
    *by_step, cache_ref, sem = refs
    me = lax.axis_index("seq")
    request = lax.div(me, heads_local)
    head = lax.axis_index("head") * heads_local + lax.rem(me, heads_local)
    previous, slot = jnp.int32(-1), jnp.int32(0)
    for k in range(kept_ref.shape[1]):
        source = lax.div(kept_ref[request, k, head], source_blocks)
        slot = jnp.where(source == previous, jnp.minimum(slot + 1, MOST - 1), 0)
        previous = source
        rows = pl.ds(pl.multiple_of(slot * BLK, BLK), BLK)
        target = cache_ref.at[0, 0, pl.ds(k * BLK, BLK)]
        for step, ref in enumerate(by_step):
            pl.when(jnp.bitwise_xor(me, kept_offset(step)) == source)(
                pltpu.make_async_copy(ref.at[rows], target, sem).start
            )
    pltpu.make_async_copy(cache_ref, cache_ref, sem).wait()


def place(kept_blocks, after, blocks, source_blocks, heads_local):
    kept_count = kept_blocks.shape[1]
    anywhere = pl.BlockSpec(memory_space=pl.ANY)
    return pl.pallas_call(
        functools.partial(place_kernel, source_blocks, heads_local),
        out_shape=jax.ShapeDtypeStruct((1, 1, kept_count * BLK, 2 * HD), jnp.bfloat16),
        in_specs=[pl.BlockSpec(memory_space=pltpu.SMEM)] + [anywhere] * (1 + len(blocks)),
        out_specs=anywhere,
        scratch_shapes=[pltpu.SemaphoreType.DMA],
        compiler_params=pltpu.CompilerParams(vmem_limit_bytes=8 * 1024 * 1024),
        cost_estimate=pl.CostEstimate(flops=10**9, bytes_accessed=0, transcendentals=0),
        name="place",
    )(kept_blocks, after, *blocks)


def attend_kernel(direct, source_blocks, heads_local, kept_ref, cos_ref, sin_ref, *refs):
    kept_count = kept_ref.shape[1]
    step_count = cos_ref.shape[0] // 2
    me = lax.axis_index("seq")
    request = lax.div(me, heads_local)
    head = lax.axis_index("head") * heads_local + lax.rem(me, heads_local)
    if direct:
        by_step, parts_refs, attended_ref = refs[:4], refs[4:8][::-1], refs[8]
        total = sum(ref[...] for ref in parts_refs)
    else:
        parts_ref, blocks_ref, attended_ref, cache_ref, sem, kept = refs

        def start_copy(k, carry):
            previous, slot = carry
            source = lax.div(kept_ref[request, k, head], source_blocks)
            slot = jnp.where(source == previous, jnp.minimum(slot + 1, MOST - 1), 0)
            target = kept.at[pl.ds(pl.multiple_of(k * BLK, BLK), BLK)]
            rows = pl.ds(pl.multiple_of(slot * BLK, BLK), BLK)
            pltpu.make_async_copy(blocks_ref.at[source, rows], target, sem).start()
            return source, slot

        lax.fori_loop(0, kept_count, start_copy, (jnp.int32(-1), jnp.int32(0)))
        total = jnp.sum(parts_ref[...], axis=0)
        pltpu.make_async_copy(kept, kept, sem).wait()
        pltpu.make_async_copy(kept, cache_ref.at[0, 0], sem).start()
    query_rows = QPK * step_count
    inverse = lax.rsqrt(total[query_rows + 2 * step_count :] * (1.0 / D) + EPS)
    cosine, sine = cos_ref[...], sin_ref[...]
    query = total[:query_rows].reshape(QPK // 2, 2 * step_count, HD) * inverse[None]
    query = rotate(query, cosine[None], sine[None]).reshape(query_rows, HD).astype(jnp.bfloat16)
    keyval = total[query_rows : query_rows + 2 * step_count] * inverse
    new_key = rotate(keyval, cosine, sine).astype(jnp.bfloat16)
    new_value = jnp.concatenate([keyval[step_count:], keyval[:step_count]], axis=0)
    new_value = new_value.astype(jnp.bfloat16)
    scale = 1.0 / math.sqrt(HD)
    score = lax.dot_general(query, new_key, CONTRACT_LAST, preferred_element_type=jnp.float32)
    row = lax.broadcasted_iota(jnp.int32, score.shape, 0)
    column = lax.broadcasted_iota(jnp.int32, score.shape, 1)
    scores = [jnp.where(column <= lax.rem(row, step_count), score * scale, -jnp.inf)]
    values = [new_value]
    def add_block(block, filled):
        score = lax.dot_general(
            query, block[:, :HD], CONTRACT_LAST, preferred_element_type=jnp.float32
        )
        column = lax.broadcasted_iota(jnp.int32, score.shape, 1)
        scores.append(jnp.where(column < filled * BLK, score * scale, -jnp.inf))
        values.append(block[:, HD:])

    if direct:
        for step, ref in enumerate(by_step):
            source = jnp.bitwise_xor(me, kept_offset(step))
            filled = jnp.int32(0)
            for k in range(kept_count):
                here = lax.div(kept_ref[request, k, head], source_blocks) == source
                filled += here.astype(jnp.int32)
            add_block(ref[: MOST * BLK, :], filled)
    else:
        add_block(kept[...], kept_count)
    row_max = functools.reduce(
        jnp.maximum, [jnp.max(score, axis=1, keepdims=True) for score in scores]
    )
    denominator = jnp.zeros((query_rows, 1), jnp.float32)
    numerator = jnp.zeros((query_rows, HD), jnp.float32)
    for score, value in zip(scores, values):
        weight = jnp.exp(score - row_max)
        denominator += jnp.sum(weight, axis=1, keepdims=True)
        numerator += jnp.dot(
            weight.astype(jnp.bfloat16), value, preferred_element_type=jnp.float32
        )
    attended = (numerator / denominator).astype(jnp.bfloat16)
    if direct:
        attended_ref[...] = attended
    else:
        for i in range(attended_ref.shape[0]):
            attended_ref[i] = attended
        pltpu.make_async_copy(cache_ref, cache_ref, sem).wait()


def attend(kept_blocks, arrivals, source_blocks, heads_local, step_count, seq_count, direct):
    kept_count = kept_blocks.shape[1]
    cosine, sine = rope_tables(source_blocks * BLK * seq_count, step_count)
    shape = (QPK * step_count, HD)
    vmem = pl.BlockSpec(memory_space=pltpu.VMEM)
    if direct:
        shapes = [jax.ShapeDtypeStruct(shape, jnp.bfloat16)]
        out_specs = [vmem]
        scratch = []
    else:
        cache = (1, 1, kept_count * BLK, 2 * HD)
        shapes = [
            jax.ShapeDtypeStruct((seq_count,) + shape, jnp.bfloat16),
            jax.ShapeDtypeStruct(cache, jnp.bfloat16),
        ]
        out_specs = [vmem, pl.BlockSpec(memory_space=pl.ANY)]
        scratch = [pltpu.SemaphoreType.DMA, pltpu.VMEM(cache[2:], jnp.bfloat16)]
    return pl.pallas_call(
        functools.partial(attend_kernel, direct, source_blocks, heads_local),
        out_shape=shapes,
        in_specs=[pl.BlockSpec(memory_space=pltpu.SMEM)] + [vmem] * (2 + len(arrivals)),
        out_specs=out_specs,
        scratch_shapes=scratch,
        compiler_params=pltpu.CompilerParams(vmem_limit_bytes=16 * 1024 * 1024),
        cost_estimate=pl.CostEstimate(flops=10**10, bytes_accessed=0, transcendentals=0),
        name="attend",
    )(kept_blocks, jnp.asarray(cosine), jnp.asarray(sine), *arrivals)


def merge_heads(first, second, step_count):
    pieces = []
    for h in range(QPK):
        rows = slice(h * step_count, (h + 1) * step_count)
        pieces.append(jnp.concatenate([first[rows], second[rows]], axis=0))
    return jnp.concatenate(pieces, axis=1).astype(jnp.bfloat16)


def output_half_kernel(flip, w_ref, same_ref, other_ref, *refs):
    out_ref = refs[-1]
    query_rows = same_ref.shape[0]
    me = lax.axis_index("seq")
    local = jnp.bitwise_and(me, 1)
    if flip:
        local = 1 - local
    second = me >= 2
    same = same_ref[...].astype(jnp.float32)
    other = other_ref[...].astype(jnp.float32)
    merged = merge_heads(
        jnp.where(second, other, same), jnp.where(second, same, other), query_rows // QPK
    )
    depth = w_ref.shape[0] // 2
    weights = w_ref[pl.ds(pl.multiple_of(local * depth, depth), depth), :]
    total = jnp.dot(merged, weights, preferred_element_type=jnp.float32)
    if len(refs) > 1:
        total += refs[0][...]
    out_ref[...] = total.astype(out_ref.dtype)


def output_half(flip, w_out, same, other, *addend):
    rows = 2 * same.shape[0] // QPK
    dtype = jnp.bfloat16 if addend else jnp.float32
    vmem = pl.BlockSpec(memory_space=pltpu.VMEM)
    return pl.pallas_call(
        functools.partial(output_half_kernel, flip),
        out_shape=jax.ShapeDtypeStruct((rows, w_out.shape[1]), dtype),
        in_specs=[vmem] * (3 + len(addend)),
        out_specs=vmem,
        compiler_params=pltpu.CompilerParams(vmem_limit_bytes=8 * 1024 * 1024),
        cost_estimate=pl.CostEstimate(flops=10**9, bytes_accessed=0, transcendentals=0),
        name="output_half",
    )(w_out, same, other, *addend)


def output_kernel(heads_local, w_ref, gathered_ref, out_ref):
    pair_count, query_rows, _ = gathered_ref.shape
    step_count = query_rows // QPK
    pairs = [gathered_ref[p].astype(jnp.float32) for p in range(pair_count)]
    requests = pair_count // heads_local
    pieces = []
    for l in range(heads_local):
        for h in range(QPK):
            rows = slice(h * step_count, (h + 1) * step_count)
            pieces.append(
                jnp.concatenate(
                    [pairs[r * heads_local + l][rows] for r in range(requests)], axis=0
                )
            )
    merged = jnp.concatenate(pieces, axis=1).astype(jnp.bfloat16)
    out_ref[...] = jnp.dot(merged, w_ref[...], preferred_element_type=jnp.float32)


def output(gathered, w_out, heads_local):
    pair_count, query_rows, _ = gathered.shape
    rows = pair_count // heads_local * (query_rows // QPK)
    vmem = pl.BlockSpec(memory_space=pltpu.VMEM)
    return pl.pallas_call(
        functools.partial(output_kernel, heads_local),
        out_shape=jax.ShapeDtypeStruct((rows, w_out.shape[1]), jnp.float32),
        in_specs=[vmem] * 2,
        out_specs=vmem,
        compiler_params=pltpu.CompilerParams(vmem_limit_bytes=8 * 1024 * 1024),
        name="output_projection",
    )(w_out, gathered)


def shards(source_cache, kept_blocks, new_hidden, norm_gain, w_query, w_keyval, w_out):
    seq_count = lax.axis_size("seq")
    head_count = lax.axis_size("head")
    requests, heads_local, source_tokens, _ = source_cache.shape
    _, step_count, width = new_hidden.shape
    pair_count = requests * heads_local

    kept_blocks = kept_blocks.transpose(0, 2, 1)
    source_blocks = source_tokens // BLK
    direct = is_direct(seq_count) and heads_local == 2
    weights = (new_hidden, norm_gain, w_query, w_keyval)
    w_out = pltpu.with_memory_space_constraint(w_out, pltpu.VMEM)
    shape = (source_blocks, heads_local, step_count, seq_count, direct)
    if direct:
        partners = range(1, seq_count)
        blocks = list(pick(kept_blocks, source_cache, direct))
        parts = list(project(blocks[0], *weights, pair_count, direct))
        blocks = [blocks[0]] + [swap_kept(blocks[step], step) for step in partners]
        parts[1], blocks[1] = lax.optimization_barrier((parts[1], blocks[1]))
        parts = [parts[0]] + [swap(parts[k], "seq", k) for k in partners]
        (attended,) = attend(kept_blocks, blocks + parts[::-1], *shape)
        kept_cache = place(kept_blocks, attended, blocks, source_blocks, heads_local)
        first, second, third = [swap(attended, "seq", k) for k in partners]
        first, kept_cache = lax.optimization_barrier((first, kept_cache))
        terms = output_half(True, w_out, first, third)
        terms = output_half(False, w_out, attended, second, terms)
    else:
        (blocks,) = pick(kept_blocks, source_cache, direct)
        (parts,) = project(blocks, *weights, pair_count, direct)
        arrivals = [all_to_all(parts, "seq"), all_to_all(blocks, "seq")]
        attended, kept_cache = attend(kept_blocks, arrivals, *shape)
        terms = output(all_to_all(attended, "seq"), w_out, heads_local)
    if is_direct(head_count):
        terms = terms.astype(jnp.bfloat16)
        others = [swap(terms, "head", k) for k in range(1, head_count)]
        own, core, along, across = [t.astype(jnp.float32) for t in [terms] + others]
        summed = (own + core) + (along + across)
    else:
        summed = lax.psum(terms, "head")
    summed = summed.reshape(requests, step_count, width)
    decoded = (new_hidden.astype(jnp.float32) + summed).astype(jnp.bfloat16)
    return (kept_cache, decoded)


def solution(mesh):
    in_specs = (
        P("groups", "head", "seq", None),
        P("groups", None, None),
        P("groups", None, "seq"),
        P("seq"),
        P("seq", "head"),
        P("seq", "head", None),
        P("head", "seq"),
    )
    out_specs = (P("head", ("groups", "seq"), None, None), P("groups", None, "seq"))
    return jax.shard_map(shards, mesh=mesh, in_specs=in_specs, out_specs=out_specs, check_vma=False)
```

```python
import functools
import math

import jax
import jax.numpy as jnp
import numpy as np
from jax import lax
from jax.experimental import pallas as pl
from jax.experimental.pallas import tpu as pltpu
from jax.sharding import PartitionSpec as P

D = 8192
HD = 128
QPK = 8
BLK = 128
MOST = 2
ROPE_BASE = 500000.0
EPS = 1e-05
LEAST = -1e30
TINY = 1e-30
ATTEND_COST = 10**10

CONTRACT_LAST = (((1,), (1,)), ((), ()))


def rope_tables(prompt_length, step_count):
    positions = prompt_length + np.arange(2 * step_count) % step_count
    frequency = ROPE_BASE ** (-np.arange(HD // 2, dtype=np.float64) * 2.0 / HD)
    angles = positions[:, None] * frequency[None, :]
    cosine = np.concatenate([np.cos(angles)] * 2, axis=1)
    sine = np.concatenate([-np.sin(angles), np.sin(angles)], axis=1)
    return cosine.astype(np.float32), sine.astype(np.float32)


def rotate(v, cosine, sine):
    swapped = jnp.concatenate([v[..., HD // 2 :], v[..., : HD // 2]], axis=-1)
    return v * cosine + swapped * sine


def is_direct(count):
    return count == 4


def swap(outgoing, axis, offset):
    count = lax.axis_size(axis)
    return lax.ppermute(outgoing, axis, [(i, i ^ offset) for i in range(count)])


def all_to_all(outgoing, axis):
    return lax.all_to_all(outgoing, axis, split_axis=0, concat_axis=0, tiled=True)


def picked_rows(kept_ref, cache_shape, pair, slot):
    _, heads_local, source_tokens, _ = cache_shape
    source_blocks = source_tokens // BLK
    kept_count = kept_ref.shape[1]
    first_block = lax.axis_index("seq") * source_blocks
    request = lax.div(pair, heads_local)
    local = lax.rem(pair, heads_local)
    head = lax.axis_index("head") * heads_local + local

    def count(k, total):
        return total + (kept_ref[request, k, head] < first_block).astype(jnp.int32)

    start = lax.fori_loop(0, kept_count, count, jnp.int32(0), unroll=kept_count <= 8)
    rank = jnp.minimum(start + slot, kept_count - 1)
    block = jnp.clip(kept_ref[request, rank, head] - first_block, 0, source_blocks - 1)
    return request, local, pl.ds(pl.multiple_of(block * BLK, BLK), BLK)


def pick_near_kernel(kept_hbm_ref, cache_ref, *refs):
    *outs, kept_ref, cache, kept_sem, sem = refs
    kept_copy = pltpu.make_async_copy(kept_hbm_ref, kept_ref, kept_sem)
    cache_copy = pltpu.make_async_copy(cache_ref, cache, sem)
    kept_copy.start()
    cache_copy.start()
    kept_copy.wait()
    me = lax.axis_index("seq")
    places = [
        [picked_rows(kept_ref, cache.shape, jnp.bitwise_xor(me, k), slot) for slot in range(MOST)]
        for k in range(len(outs))
    ]
    cache_copy.wait()
    for out_ref, slots in zip(outs, places):
        for slot, (request, local, rows) in enumerate(slots):
            out_ref[slot * BLK : (slot + 1) * BLK, :] = cache[request, local, rows, :]


def pick_all_kernel(kept_hbm_ref, cache_ref, out_ref, kept_ref, sem):
    pltpu.sync_copy(kept_hbm_ref, kept_ref)

    def pair_body(pair, carry):
        for slot in range(MOST):
            request, local, rows = picked_rows(kept_ref, cache_ref.shape, pair, slot)
            pltpu.make_async_copy(
                cache_ref.at[request, local, rows],
                out_ref.at[pair, pl.ds(slot * BLK, BLK)],
                sem,
            ).start()
        return carry

    lax.fori_loop(0, out_ref.shape[0], pair_body, 0)
    pltpu.make_async_copy(out_ref, out_ref, sem).wait()


def pick(kept_blocks, source_cache, direct):
    requests, heads_local, _, row_width = source_cache.shape
    pair_count = requests * heads_local
    block = (MOST * BLK, row_width)
    kept_scratch = pltpu.SMEM(kept_blocks.shape, jnp.int32)
    if direct:
        shapes = [jax.ShapeDtypeStruct(block, jnp.bfloat16)] * pair_count
        scratch = [
            kept_scratch,
            pltpu.VMEM(source_cache.shape, jnp.bfloat16),
            pltpu.SemaphoreType.DMA,
            pltpu.SemaphoreType.DMA,
        ]
    else:
        shapes = [jax.ShapeDtypeStruct((pair_count,) + block, jnp.bfloat16)]
        scratch = [kept_scratch, pltpu.SemaphoreType.DMA]
    return pl.pallas_call(
        pick_near_kernel if direct else pick_all_kernel,
        out_shape=shapes,
        in_specs=[pl.BlockSpec(memory_space=pl.ANY)] * 2,
        out_specs=[pl.BlockSpec(memory_space=pltpu.VMEM)] * len(shapes),
        scratch_shapes=scratch,
        compiler_params=pltpu.CompilerParams(vmem_limit_bytes=8 * 1024 * 1024),
        cost_estimate=pl.CostEstimate(flops=10**10, bytes_accessed=0, transcendentals=0),
        name="pick_blocks",
    )(
        pltpu.with_memory_space_constraint(kept_blocks, pltpu.HBM),
        pltpu.with_memory_space_constraint(source_cache, pltpu.HBM),
    )


def interleave(rows):
    count, width = rows.shape
    chunks = width // HD
    stacked = jnp.concatenate(
        [rows[:, c * HD : (c + 1) * HD] for c in range(chunks)], axis=0
    ).astype(jnp.bfloat16)
    source = lax.broadcasted_iota(jnp.int32, (HD, 4 * HD), 0)
    target = lax.broadcasted_iota(jnp.int32, (HD, 4 * HD), 1)
    place = jnp.where(target < 2 * HD, 2 * source, 2 * source + 1 + 2 * HD)
    spread = (place == target).astype(jnp.bfloat16)
    wide = jnp.dot(stacked, spread, preferred_element_type=jnp.float32)
    return [
        jnp.concatenate(
            [
                wide[c * count : (c + 1) * count, : 2 * HD],
                wide[c * count : (c + 1) * count, 2 * HD :],
            ],
            axis=0,
        ).astype(jnp.bfloat16)
        for c in range(chunks)
    ]


def project_kernel(direct, after_ref, hidden_ref, gain_ref, wq_ref, wkv_ref, *outs):
    del after_ref
    requests, step_count, width = hidden_ref.shape
    heads_local = wkv_ref.shape[1]
    row_count = requests * step_count
    me = lax.axis_index("seq")
    hidden = jnp.concatenate(
        [hidden_ref[r].astype(jnp.float32) for r in range(requests)], axis=0
    )
    square = jnp.sum(hidden * hidden, axis=1, keepdims=True)
    gain = gain_ref[...].astype(jnp.float32)
    scaled = jnp.concatenate(
        [hidden[:, c * HD : (c + 1) * HD] * gain[c : c + 1] for c in range(width // HD)], axis=1
    ).astype(jnp.bfloat16)
    query = jnp.dot(scaled, wq_ref[...], preferred_element_type=jnp.float32)
    keyval = jnp.zeros((heads_local * row_count, wkv_ref.shape[2]), jnp.float32)
    for c, spread in enumerate(interleave(scaled.astype(jnp.float32))):
        alternate = wkv_ref[c * HD : (c + 1) * HD].reshape(heads_local * HD, wkv_ref.shape[2])
        keyval += jnp.dot(spread, alternate, preferred_element_type=jnp.float32)

    def pieces_of(r, l):
        steps = slice(r * step_count, (r + 1) * step_count)
        square_rows = jnp.broadcast_to(square[steps], (step_count, HD))
        own = keyval[l * row_count + r * step_count : l * row_count + (r + 1) * step_count]
        heads = [query[steps, (l * QPK + h) * HD : (l * QPK + h + 1) * HD] for h in range(QPK)]
        return heads + [own[:, :HD], own[:, HD:], square_rows, square_rows]

    def write_pair(out_ref, first_piece, pieces):
        for j, piece in enumerate(pieces, first_piece):
            out_ref[j * step_count : (j + 1) * step_count, :] = piece

    for r in range(requests):
        for l in range(heads_local):
            pair = r * heads_local + l
            pieces = pieces_of(r, l)
            if not direct:
                write_pair(outs[0].at[pair], 0, pieces)
                continue
            for offset, out_ref in enumerate(outs):
                pl.when(jnp.bitwise_xor(me, offset) == pair)(
                    functools.partial(write_pair, out_ref, 0, pieces)
                )
                pl.when(jnp.bitwise_xor(me, offset ^ 2) == pair)(
                    functools.partial(
                        write_pair, out_ref, len(pieces), pieces[:QPK] + pieces[-2:]
                    )
                )


def project(after, new_hidden, norm_gain, w_query, w_keyval, pair_count, direct):
    requests, step_count, width = new_hidden.shape
    terms = ((QPK + 4) * step_count, HD)
    if direct:
        two_pairs = (terms[0] + (QPK + 2) * step_count, HD)
        shapes = [jax.ShapeDtypeStruct(two_pairs, jnp.float32)] * pair_count
    else:
        shapes = [jax.ShapeDtypeStruct((pair_count,) + terms, jnp.float32)]
    vmem = pl.BlockSpec(memory_space=pltpu.VMEM)
    weights = w_query.size + w_keyval.size
    return pl.pallas_call(
        functools.partial(project_kernel, direct),
        out_shape=shapes,
        in_specs=[pl.BlockSpec(memory_space=pl.ANY)] + [vmem] * 4,
        out_specs=[vmem] * len(shapes),
        compiler_params=pltpu.CompilerParams(vmem_limit_bytes=8 * 1024 * 1024),
        cost_estimate=pl.CostEstimate(
            flops=2 * requests * step_count * weights,
            bytes_accessed=2 * weights,
            transcendentals=0,
        ),
        name="project",
    )(
        after,
        new_hidden,
        norm_gain.reshape(width // HD, HD),
        pltpu.with_memory_space_constraint(w_query, pltpu.VMEM),
        pltpu.with_memory_space_constraint(w_keyval, pltpu.VMEM),
    )


def place_kernel(source_blocks, heads_local, kept_ref, after_ref, *refs):
    del after_ref
    *by_offset, cache_ref, sem = refs
    me = lax.axis_index("seq")
    request = lax.div(me, heads_local)
    head = lax.axis_index("head") * heads_local + lax.rem(me, heads_local)
    previous, slot = jnp.int32(-1), jnp.int32(0)
    for k in range(kept_ref.shape[1]):
        source = lax.div(kept_ref[request, k, head], source_blocks)
        slot = jnp.where(source == previous, jnp.minimum(slot + 1, MOST - 1), 0)
        previous = source
        rows = pl.ds(pl.multiple_of(slot * BLK, BLK), BLK)
        target = cache_ref.at[0, 0, pl.ds(k * BLK, BLK)]
        for offset, ref in enumerate(by_offset):
            pl.when(jnp.bitwise_xor(me, offset) == source)(
                pltpu.make_async_copy(ref.at[rows], target, sem).start
            )
    pltpu.make_async_copy(cache_ref, cache_ref, sem).wait()


def place(kept_blocks, after, blocks, source_blocks, heads_local):
    kept_count = kept_blocks.shape[1]
    anywhere = pl.BlockSpec(memory_space=pl.ANY)
    return pl.pallas_call(
        functools.partial(place_kernel, source_blocks, heads_local),
        out_shape=jax.ShapeDtypeStruct((1, 1, kept_count * BLK, 2 * HD), jnp.bfloat16),
        in_specs=[pl.BlockSpec(memory_space=pltpu.SMEM)] + [anywhere] * (1 + len(blocks)),
        out_specs=anywhere,
        scratch_shapes=[pltpu.SemaphoreType.DMA],
        compiler_params=pltpu.CompilerParams(vmem_limit_bytes=8 * 1024 * 1024),
        cost_estimate=pl.CostEstimate(flops=10**9, bytes_accessed=0, transcendentals=0),
        name="place",
    )(kept_blocks, after, *blocks)


def split_three(value):
    parts = []
    for _ in range(3):
        parts.append(value.astype(jnp.bfloat16))
        value = value - parts[-1].astype(jnp.float32)
    return parts


def norm_of(square_rows):
    return lax.rsqrt(square_rows * (1.0 / D) + EPS)


def rotated_queries(terms, inverse, cosine, sine):
    rows = terms.shape[0]
    query = terms.reshape(rows // inverse.shape[0], inverse.shape[0], HD) * inverse[None]
    return rotate(query, cosine[None], sine[None]).reshape(rows, HD).astype(jnp.bfloat16)


def new_steps(terms, inverse, cosine, sine, step_count):
    keyval = terms * inverse
    new_key = rotate(keyval, cosine, sine).astype(jnp.bfloat16)
    new_value = jnp.concatenate([keyval[step_count:], keyval[:step_count]], axis=0)
    return new_key, new_value.astype(jnp.bfloat16)


def scores_of(query, keys, filled=None, step_count=None):
    score = lax.dot_general(query, keys, CONTRACT_LAST, preferred_element_type=jnp.float32)
    score = score * (1.0 / math.sqrt(HD))
    column = lax.broadcasted_iota(jnp.int32, score.shape, 1)
    if step_count is None:
        return jnp.where(column < filled * BLK, score, -jnp.inf)
    row = lax.broadcasted_iota(jnp.int32, score.shape, 0)
    return jnp.where(column <= lax.rem(row, step_count), score, -jnp.inf)


def softmax_values(scores, values):
    row_max = functools.reduce(
        jnp.maximum, [jnp.max(score, axis=1, keepdims=True) for score in scores]
    )
    row_max = jnp.maximum(row_max, LEAST)
    denominator = jnp.zeros(row_max.shape, jnp.float32)
    numerator = jnp.zeros((row_max.shape[0], HD), jnp.float32)
    for score, value in zip(scores, values):
        weight = jnp.exp(score - row_max)
        denominator += jnp.sum(weight, axis=1, keepdims=True)
        numerator += jnp.dot(
            weight.astype(jnp.bfloat16), value, preferred_element_type=jnp.float32
        )
    attended = numerator / jnp.maximum(denominator, TINY)
    return attended, row_max, denominator


def attend_near_kernel(source_blocks, heads_local, kept_ref, cos_ref, sin_ref, *refs):
    own_ref, near_ref, far_ref, other_ref = refs[:4]
    parts_refs, out_ref = refs[4:8], refs[8]
    kept_count = kept_ref.shape[1]
    step_count = cos_ref.shape[0] // 2
    me = lax.axis_index("seq")
    request = lax.div(me, heads_local)
    head = lax.axis_index("head") * heads_local + lax.rem(me, heads_local)
    cosine, sine = cos_ref[...], sin_ref[...]
    total = (parts_refs[0][...] + parts_refs[1][...]) + (parts_refs[2][...] + parts_refs[3][...])
    query_rows = QPK * step_count
    pair_rows = (QPK + 4) * step_count

    def filled_blocks(request, source):
        filled = jnp.int32(0)
        for k in range(kept_count):
            here = lax.div(kept_ref[request, k, head], source_blocks) == source
            filled += here.astype(jnp.int32)
        return filled

    inverse = norm_of(total[pair_rows - 2 * step_count : pair_rows])
    query = rotated_queries(total[:query_rows], inverse, cosine, sine)
    new_key, new_value = new_steps(
        total[query_rows : query_rows + 2 * step_count], inverse, cosine, sine, step_count
    )
    scores = [scores_of(query, new_key, step_count=step_count)]
    values = [new_value]
    for offset, ref in ((0, own_ref), (1, near_ref), (3, far_ref)):
        filled = filled_blocks(request, jnp.bitwise_xor(me, offset))
        scores.append(scores_of(query, ref[:, :HD], filled))
        values.append(ref[:, HD:])

    other_inverse = norm_of(total[-2 * step_count :])
    other_query = rotated_queries(
        total[pair_rows : pair_rows + query_rows], other_inverse, cosine, sine
    )
    filled = filled_blocks(1 - request, me)
    other_scores = [scores_of(other_query, other_ref[:, :HD], filled)]

    attended, row_max, denominator = softmax_values(scores, values)
    other, other_max, other_denominator = softmax_values(other_scores, [other_ref[:, HD:]])
    out_ref[:query_rows, :] = attended.astype(jnp.bfloat16)
    out_ref[query_rows : 2 * query_rows, :] = other.astype(jnp.bfloat16)
    row_max = jnp.concatenate([row_max, other_max], axis=0)
    denominator = jnp.concatenate([denominator, other_denominator], axis=0)
    log_sum = row_max + jnp.log(jnp.maximum(denominator, TINY))
    columns = jnp.concatenate(
        [jnp.broadcast_to(log_sum, (2 * query_rows, HD)), jnp.zeros((HD - 2 * query_rows, HD))],
        axis=0,
    )
    across = jnp.transpose(columns)[:16]
    row = lax.broadcasted_iota(jnp.int32, across.shape, 0)
    high, middle, low = [part.astype(jnp.float32) for part in split_three(across)]
    stats = jnp.where(row == 0, high, jnp.where(row == 1, middle, low))
    out_ref[2 * query_rows :, :] = stats.astype(jnp.bfloat16)


def attend_all_kernel(
    source_blocks, heads_local, kept_ref, cos_ref, sin_ref, parts_ref, blocks_ref,
    attended_ref, cache_ref, sem, kept,
):
    kept_count = kept_ref.shape[1]
    step_count = cos_ref.shape[0] // 2
    me = lax.axis_index("seq")
    request = lax.div(me, heads_local)
    head = lax.axis_index("head") * heads_local + lax.rem(me, heads_local)

    def start_copy(k, carry):
        previous, slot = carry
        source = lax.div(kept_ref[request, k, head], source_blocks)
        slot = jnp.where(source == previous, jnp.minimum(slot + 1, MOST - 1), 0)
        target = kept.at[pl.ds(pl.multiple_of(k * BLK, BLK), BLK)]
        rows = pl.ds(pl.multiple_of(slot * BLK, BLK), BLK)
        pltpu.make_async_copy(blocks_ref.at[source, rows], target, sem).start()
        return source, slot

    lax.fori_loop(0, kept_count, start_copy, (jnp.int32(-1), jnp.int32(0)))
    total = jnp.sum(parts_ref[...], axis=0)
    pltpu.make_async_copy(kept, kept, sem).wait()
    pltpu.make_async_copy(kept, cache_ref.at[0, 0], sem).start()
    query_rows = QPK * step_count
    cosine, sine = cos_ref[...], sin_ref[...]
    inverse = norm_of(total[-2 * step_count :])
    query = rotated_queries(total[:query_rows], inverse, cosine, sine)
    new_key, new_value = new_steps(
        total[query_rows : query_rows + 2 * step_count], inverse, cosine, sine, step_count
    )
    scores = [
        scores_of(query, new_key, step_count=step_count),
        scores_of(query, kept[:, :HD], kept_count),
    ]
    attended, _, _ = softmax_values(scores, [new_value, kept[:, HD:]])
    for i in range(attended_ref.shape[0]):
        attended_ref[i] = attended.astype(jnp.bfloat16)
    pltpu.make_async_copy(cache_ref, cache_ref, sem).wait()


def attend(kept_blocks, arrivals, source_blocks, heads_local, step_count, seq_count, direct):
    kept_count = kept_blocks.shape[1]
    cosine, sine = rope_tables(source_blocks * BLK * seq_count, step_count)
    query_rows = QPK * step_count
    vmem = pl.BlockSpec(memory_space=pltpu.VMEM)
    if direct:
        shapes = [jax.ShapeDtypeStruct((2 * query_rows + 16, HD), jnp.bfloat16)]
        out_specs = [vmem]
        scratch = []
    else:
        cache = (1, 1, kept_count * BLK, 2 * HD)
        shapes = [
            jax.ShapeDtypeStruct((seq_count, query_rows, HD), jnp.bfloat16),
            jax.ShapeDtypeStruct(cache, jnp.bfloat16),
        ]
        out_specs = [vmem, pl.BlockSpec(memory_space=pl.ANY)]
        scratch = [pltpu.SemaphoreType.DMA, pltpu.VMEM(cache[2:], jnp.bfloat16)]
    return pl.pallas_call(
        functools.partial(
            attend_near_kernel if direct else attend_all_kernel, source_blocks, heads_local
        ),
        out_shape=shapes,
        in_specs=[pl.BlockSpec(memory_space=pltpu.SMEM)] + [vmem] * (2 + len(arrivals)),
        out_specs=out_specs,
        scratch_shapes=scratch,
        compiler_params=pltpu.CompilerParams(vmem_limit_bytes=16 * 1024 * 1024),
        cost_estimate=pl.CostEstimate(flops=ATTEND_COST, bytes_accessed=0, transcendentals=0),
        name="attend",
    )(kept_blocks, jnp.asarray(cosine), jnp.asarray(sine), *arrivals)


def join(values, log_sum, other_values, other_log_sum):
    largest = jnp.maximum(log_sum, other_log_sum)
    weight = jnp.exp(log_sum - largest)
    other_weight = jnp.exp(other_log_sum - largest)
    return (weight * values + other_weight * other_values) / (weight + other_weight)


def read_values(ref, query_rows):
    values = ref[: 2 * query_rows, :].astype(jnp.float32)
    stats = ref[2 * query_rows :, :].astype(jnp.float32)
    log_sum = (stats[0:1] + stats[1:2]) + stats[2:3]
    columns = jnp.transpose(jnp.broadcast_to(log_sum, (HD, HD)))
    return (
        (values[:query_rows], columns[:query_rows]),
        (values[query_rows:], columns[query_rows : 2 * query_rows]),
    )


def merge_heads(first, second, step_count):
    pieces = []
    for h in range(QPK):
        rows = slice(h * step_count, (h + 1) * step_count)
        pieces.append(jnp.concatenate([first[rows], second[rows]], axis=0))
    return jnp.concatenate(pieces, axis=1).astype(jnp.bfloat16)


def output_half_kernel(flip, w_ref, same_ref, other_ref, *refs):
    out_ref = refs[-1]
    query_rows = (same_ref.shape[0] - 16) // 2
    me = lax.axis_index("seq")
    local = jnp.bitwise_and(me, 1)
    if flip:
        local = 1 - local
    second = me >= 2
    same_first, other_second = read_values(same_ref, query_rows)
    other_first, same_second = read_values(other_ref, query_rows)
    same = join(*same_first, *same_second)
    other = join(*other_first, *other_second)
    merged = merge_heads(
        jnp.where(second, other, same), jnp.where(second, same, other), query_rows // QPK
    )
    depth = w_ref.shape[0] // 2
    weights = w_ref[pl.ds(pl.multiple_of(local * depth, depth), depth), :]
    total = jnp.dot(merged, weights, preferred_element_type=jnp.float32)
    if len(refs) > 1:
        total += refs[0][...]
    out_ref[...] = total.astype(out_ref.dtype)


def output_half(flip, w_out, same, other, *addend):
    rows = (same.shape[0] - 16) // QPK
    dtype = jnp.bfloat16 if addend else jnp.float32
    vmem = pl.BlockSpec(memory_space=pltpu.VMEM)
    return pl.pallas_call(
        functools.partial(output_half_kernel, flip),
        out_shape=jax.ShapeDtypeStruct((rows, w_out.shape[1]), dtype),
        in_specs=[vmem] * (3 + len(addend)),
        out_specs=vmem,
        compiler_params=pltpu.CompilerParams(vmem_limit_bytes=8 * 1024 * 1024),
        cost_estimate=pl.CostEstimate(flops=10**9, bytes_accessed=0, transcendentals=0),
        name="output_half",
    )(w_out, same, other, *addend)


def output_kernel(heads_local, w_ref, gathered_ref, out_ref):
    pair_count, query_rows, _ = gathered_ref.shape
    step_count = query_rows // QPK
    pairs = [gathered_ref[p].astype(jnp.float32) for p in range(pair_count)]
    requests = pair_count // heads_local
    pieces = []
    for l in range(heads_local):
        for h in range(QPK):
            rows = slice(h * step_count, (h + 1) * step_count)
            pieces.append(
                jnp.concatenate(
                    [pairs[r * heads_local + l][rows] for r in range(requests)], axis=0
                )
            )
    merged = jnp.concatenate(pieces, axis=1).astype(jnp.bfloat16)
    out_ref[...] = jnp.dot(merged, w_ref[...], preferred_element_type=jnp.float32)


def output(gathered, w_out, heads_local):
    pair_count, query_rows, _ = gathered.shape
    rows = pair_count // heads_local * (query_rows // QPK)
    vmem = pl.BlockSpec(memory_space=pltpu.VMEM)
    return pl.pallas_call(
        functools.partial(output_kernel, heads_local),
        out_shape=jax.ShapeDtypeStruct((rows, w_out.shape[1]), jnp.float32),
        in_specs=[vmem] * 2,
        out_specs=vmem,
        compiler_params=pltpu.CompilerParams(vmem_limit_bytes=8 * 1024 * 1024),
        name="output_projection",
    )(w_out, gathered)


def shards(source_cache, kept_blocks, new_hidden, norm_gain, w_query, w_keyval, w_out):
    seq_count = lax.axis_size("seq")
    head_count = lax.axis_size("head")
    requests, heads_local, source_tokens, _ = source_cache.shape
    _, step_count, width = new_hidden.shape
    pair_count = requests * heads_local

    kept_blocks = kept_blocks.transpose(0, 2, 1)
    source_blocks = source_tokens // BLK
    direct = is_direct(seq_count) and heads_local == 2
    weights = (new_hidden, norm_gain, w_query, w_keyval)
    w_out = pltpu.with_memory_space_constraint(w_out, pltpu.VMEM)
    shape = (source_blocks, heads_local, step_count, seq_count, direct)
    if direct:
        partners = range(1, seq_count)
        sent = list(pick(kept_blocks, source_cache, direct))
        parts = list(project(sent[0], *weights, pair_count, direct))
        far, near = swap(sent[3], "seq", 3), swap(sent[1], "seq", 1)
        parts = [parts[0]] + [swap(parts[k], "seq", k) for k in partners]
        late, near = lax.optimization_barrier((sent[2], near))
        late = swap(late, "seq", 2)
        (values,) = attend(kept_blocks, [sent[0], near, far, sent[2]] + parts[::-1], *shape)
        first, second, third = [swap(values, "seq", k) for k in partners]
        third, late = lax.optimization_barrier((third, late))
        terms = output_half(False, w_out, values, second)
        terms = output_half(True, w_out, first, third, terms)
        blocks = [sent[0], near, late, far]
        kept_cache = place(kept_blocks, values, blocks, source_blocks, heads_local)
    else:
        (blocks,) = pick(kept_blocks, source_cache, direct)
        (parts,) = project(blocks, *weights, pair_count, direct)
        arrivals = [all_to_all(parts, "seq"), all_to_all(blocks, "seq")]
        attended, kept_cache = attend(kept_blocks, arrivals, *shape)
        terms = output(all_to_all(attended, "seq"), w_out, heads_local)
    if is_direct(head_count):
        terms = terms.astype(jnp.bfloat16)
        others = [swap(terms, "head", k) for k in range(1, head_count)]
        others[1], kept_cache = lax.optimization_barrier((others[1], kept_cache))
        own, core, along, across = [t.astype(jnp.float32) for t in [terms] + others]
        summed = (own + core) + (along + across)
    else:
        summed = lax.psum(terms, "head")
    summed = summed.reshape(requests, step_count, width)
    decoded = (new_hidden.astype(jnp.float32) + summed).astype(jnp.bfloat16)
    return (kept_cache, decoded)


def solution(mesh):
    in_specs = (
        P("groups", "head", "seq", None),
        P("groups", None, None),
        P("groups", None, "seq"),
        P("seq"),
        P("seq", "head"),
        P("seq", "head", None),
        P("head", "seq"),
    )
    out_specs = (P("head", ("groups", "seq"), None, None), P("groups", None, "seq"))
    return jax.shard_map(shards, mesh=mesh, in_specs=in_specs, out_specs=out_specs, check_vma=False)
```

```python
import functools
import math

import jax
import jax.numpy as jnp
import numpy as np
from jax import lax
from jax.experimental import pallas as pl
from jax.experimental.pallas import tpu as pltpu
from jax.sharding import PartitionSpec as P

D = 8192
HD = 128
QPK = 8
BLK = 128
MOST = 2
ROPE_BASE = 500000.0
EPS = 1e-05

CONTRACT_LAST = (((1,), (1,)), ((), ()))


def rope_tables(prompt_length, step_count):
    positions = prompt_length + np.arange(2 * step_count) % step_count
    frequency = ROPE_BASE ** (-np.arange(HD // 2, dtype=np.float64) * 2.0 / HD)
    angles = positions[:, None] * frequency[None, :]
    cosine = np.concatenate([np.cos(angles)] * 2, axis=1)
    sine = np.concatenate([-np.sin(angles), np.sin(angles)], axis=1)
    return cosine.astype(np.float32), sine.astype(np.float32)


def rotate(v, cosine, sine):
    swapped = jnp.concatenate([v[..., HD // 2 :], v[..., : HD // 2]], axis=-1)
    return v * cosine + swapped * sine


def is_direct(count):
    return count == 4


def swap(outgoing, axis, offset):
    count = lax.axis_size(axis)
    return lax.ppermute(outgoing, axis, [(i, i ^ offset) for i in range(count)])


VALUE_PAIRS = (
    ((2, 1), (3, 0)),
    ((1, 0), (3, 2)),
    ((0, 2), (1, 3), (2, 0), (3, 1)),
    ((0, 1), (1, 2), (2, 3)),
    ((0, 3),),
)


def all_to_all(outgoing, axis):
    return lax.all_to_all(outgoing, axis, split_axis=0, concat_axis=0, tiled=True)


def picked_rows(kept_ref, cache_shape, pair, slot):
    _, heads_local, source_tokens, _ = cache_shape
    source_blocks = source_tokens // BLK
    kept_count = kept_ref.shape[1]
    first_block = lax.axis_index("seq") * source_blocks
    request = lax.div(pair, heads_local)
    local = lax.rem(pair, heads_local)
    head = lax.axis_index("head") * heads_local + local

    def count(k, total):
        return total + (kept_ref[request, k, head] < first_block).astype(jnp.int32)

    start = lax.fori_loop(0, kept_count, count, jnp.int32(0), unroll=kept_count <= 8)
    rank = jnp.minimum(start + slot, kept_count - 1)
    block = jnp.clip(kept_ref[request, rank, head] - first_block, 0, source_blocks - 1)
    return request, local, pl.ds(pl.multiple_of(block * BLK, BLK), BLK)


def pick_near_kernel(kept_hbm_ref, cache_ref, *refs):
    *outs, kept_ref, cache, kept_sem, sem = refs
    kept_copy = pltpu.make_async_copy(kept_hbm_ref, kept_ref, kept_sem)
    cache_copy = pltpu.make_async_copy(cache_ref, cache, sem)
    kept_copy.start()
    cache_copy.start()
    kept_copy.wait()
    me = lax.axis_index("seq")
    places = [
        [picked_rows(kept_ref, cache.shape, jnp.bitwise_xor(me, k), slot) for slot in range(MOST)]
        for k in range(len(outs))
    ]
    cache_copy.wait()
    for out_ref, slots in zip(outs, places):
        for slot, (request, local, rows) in enumerate(slots):
            out_ref[slot * BLK : (slot + 1) * BLK, :] = cache[request, local, rows, :]


def pick_all_kernel(kept_hbm_ref, cache_ref, out_ref, kept_ref, sem):
    pltpu.sync_copy(kept_hbm_ref, kept_ref)

    def pair_body(pair, carry):
        for slot in range(MOST):
            request, local, rows = picked_rows(kept_ref, cache_ref.shape, pair, slot)
            pltpu.make_async_copy(
                cache_ref.at[request, local, rows],
                out_ref.at[pair, pl.ds(slot * BLK, BLK)],
                sem,
            ).start()
        return carry

    lax.fori_loop(0, out_ref.shape[0], pair_body, 0)
    pltpu.make_async_copy(out_ref, out_ref, sem).wait()


def pick(kept_blocks, source_cache, direct):
    requests, heads_local, _, row_width = source_cache.shape
    pair_count = requests * heads_local
    block = (MOST * BLK, row_width)
    kept_scratch = pltpu.SMEM(kept_blocks.shape, jnp.int32)
    if direct:
        shapes = [jax.ShapeDtypeStruct(block, jnp.bfloat16)] * pair_count
        scratch = [
            kept_scratch,
            pltpu.VMEM(source_cache.shape, jnp.bfloat16),
            pltpu.SemaphoreType.DMA,
            pltpu.SemaphoreType.DMA,
        ]
    else:
        shapes = [jax.ShapeDtypeStruct((pair_count,) + block, jnp.bfloat16)]
        scratch = [kept_scratch, pltpu.SemaphoreType.DMA]
    return pl.pallas_call(
        pick_near_kernel if direct else pick_all_kernel,
        out_shape=shapes,
        in_specs=[pl.BlockSpec(memory_space=pl.ANY)] * 2,
        out_specs=[pl.BlockSpec(memory_space=pltpu.VMEM)] * len(shapes),
        scratch_shapes=scratch,
        compiler_params=pltpu.CompilerParams(vmem_limit_bytes=8 * 1024 * 1024),
        cost_estimate=pl.CostEstimate(flops=10**10, bytes_accessed=0, transcendentals=0),
        name="pick_blocks",
    )(
        pltpu.with_memory_space_constraint(kept_blocks, pltpu.HBM),
        pltpu.with_memory_space_constraint(source_cache, pltpu.HBM),
    )


def interleave(rows):
    count, width = rows.shape
    chunks = width // HD
    stacked = jnp.concatenate(
        [rows[:, c * HD : (c + 1) * HD] for c in range(chunks)], axis=0
    ).astype(jnp.bfloat16)
    source = lax.broadcasted_iota(jnp.int32, (HD, 4 * HD), 0)
    target = lax.broadcasted_iota(jnp.int32, (HD, 4 * HD), 1)
    place = jnp.where(target < 2 * HD, 2 * source, 2 * source + 1 + 2 * HD)
    spread = (place == target).astype(jnp.bfloat16)
    wide = jnp.dot(stacked, spread, preferred_element_type=jnp.float32)
    return [
        jnp.concatenate(
            [
                wide[c * count : (c + 1) * count, : 2 * HD],
                wide[c * count : (c + 1) * count, 2 * HD :],
            ],
            axis=0,
        ).astype(jnp.bfloat16)
        for c in range(chunks)
    ]


def project_kernel(direct, after_ref, hidden_ref, gain_ref, wq_ref, wkv_ref, *outs):
    del after_ref
    requests, step_count, width = hidden_ref.shape
    heads_local = wkv_ref.shape[1]
    row_count = requests * step_count
    me = lax.axis_index("seq")
    hidden = jnp.concatenate(
        [hidden_ref[r].astype(jnp.float32) for r in range(requests)], axis=0
    )
    square = jnp.sum(hidden * hidden, axis=1, keepdims=True)
    gain = gain_ref[...].astype(jnp.float32)
    scaled = jnp.concatenate(
        [hidden[:, c * HD : (c + 1) * HD] * gain[c : c + 1] for c in range(width // HD)], axis=1
    ).astype(jnp.bfloat16)
    query = jnp.dot(scaled, wq_ref[...], preferred_element_type=jnp.float32)
    keyval = jnp.zeros((heads_local * row_count, wkv_ref.shape[2]), jnp.float32)
    for c, spread in enumerate(interleave(scaled.astype(jnp.float32))):
        alternate = wkv_ref[c * HD : (c + 1) * HD].reshape(heads_local * HD, wkv_ref.shape[2])
        keyval += jnp.dot(spread, alternate, preferred_element_type=jnp.float32)

    def pieces_of(r, l):
        steps = slice(r * step_count, (r + 1) * step_count)
        square_rows = jnp.broadcast_to(square[steps], (step_count, HD))
        own = keyval[l * row_count + r * step_count : l * row_count + (r + 1) * step_count]
        heads = [query[steps, (l * QPK + h) * HD : (l * QPK + h + 1) * HD] for h in range(QPK)]
        return heads + [own[:, :HD], own[:, HD:], square_rows, square_rows]

    def write_pair(out_ref, pieces):
        for j, piece in enumerate(pieces):
            out_ref[j * step_count : (j + 1) * step_count, :] = piece

    for r in range(requests):
        for l in range(heads_local):
            pair = r * heads_local + l
            pieces = pieces_of(r, l)
            if not direct:
                write_pair(outs[0].at[pair], pieces)
                continue
            for offset, out_ref in enumerate(outs):
                pl.when(jnp.bitwise_xor(me, offset) == pair)(
                    functools.partial(write_pair, out_ref, pieces)
                )


def project(after, new_hidden, norm_gain, w_query, w_keyval, pair_count, direct):
    requests, step_count, width = new_hidden.shape
    terms = ((QPK + 4) * step_count, HD)
    if direct:
        shapes = [jax.ShapeDtypeStruct(terms, jnp.float32)] * pair_count
    else:
        shapes = [jax.ShapeDtypeStruct((pair_count,) + terms, jnp.float32)]
    vmem = pl.BlockSpec(memory_space=pltpu.VMEM)
    weights = w_query.size + w_keyval.size
    return pl.pallas_call(
        functools.partial(project_kernel, direct),
        out_shape=shapes,
        in_specs=[pl.BlockSpec(memory_space=pl.ANY)] + [vmem] * 4,
        out_specs=[vmem] * len(shapes),
        compiler_params=pltpu.CompilerParams(vmem_limit_bytes=8 * 1024 * 1024),
        cost_estimate=pl.CostEstimate(
            flops=2 * requests * step_count * weights,
            bytes_accessed=2 * weights,
            transcendentals=0,
        ),
        name="project",
    )(
        after,
        new_hidden,
        norm_gain.reshape(width // HD, HD),
        pltpu.with_memory_space_constraint(w_query, pltpu.VMEM),
        pltpu.with_memory_space_constraint(w_keyval, pltpu.VMEM),
    )


def place_kernel(source_blocks, heads_local, kept_ref, after_ref, *refs):
    del after_ref
    *by_offset, cache_ref, sem = refs
    me = lax.axis_index("seq")
    request = lax.div(me, heads_local)
    head = lax.axis_index("head") * heads_local + lax.rem(me, heads_local)
    previous, slot = jnp.int32(-1), jnp.int32(0)
    for k in range(kept_ref.shape[1]):
        source = lax.div(kept_ref[request, k, head], source_blocks)
        slot = jnp.where(source == previous, jnp.minimum(slot + 1, MOST - 1), 0)
        previous = source
        rows = pl.ds(pl.multiple_of(slot * BLK, BLK), BLK)
        target = cache_ref.at[0, 0, pl.ds(k * BLK, BLK)]
        for offset, ref in enumerate(by_offset):
            pl.when(jnp.bitwise_xor(me, offset) == source)(
                pltpu.make_async_copy(ref.at[rows], target, sem).start
            )
    pltpu.make_async_copy(cache_ref, cache_ref, sem).wait()


def place(kept_blocks, after, blocks, source_blocks, heads_local):
    kept_count = kept_blocks.shape[1]
    anywhere = pl.BlockSpec(memory_space=pl.ANY)
    return pl.pallas_call(
        functools.partial(place_kernel, source_blocks, heads_local),
        out_shape=jax.ShapeDtypeStruct((1, 1, kept_count * BLK, 2 * HD), jnp.bfloat16),
        in_specs=[pl.BlockSpec(memory_space=pltpu.SMEM)] + [anywhere] * (1 + len(blocks)),
        out_specs=anywhere,
        scratch_shapes=[pltpu.SemaphoreType.DMA],
        compiler_params=pltpu.CompilerParams(vmem_limit_bytes=8 * 1024 * 1024),
        cost_estimate=pl.CostEstimate(flops=10**9, bytes_accessed=0, transcendentals=0),
        name="place",
    )(kept_blocks, after, *blocks)


def attend_kernel(direct, source_blocks, heads_local, kept_ref, cos_ref, sin_ref, *refs):
    kept_count = kept_ref.shape[1]
    step_count = cos_ref.shape[0] // 2
    me = lax.axis_index("seq")
    request = lax.div(me, heads_local)
    head = lax.axis_index("head") * heads_local + lax.rem(me, heads_local)
    if direct:
        by_offset, parts_refs, attended_ref = refs[:4][::-1], refs[4:8][::-1], refs[8]
        total = sum(ref[...] for ref in parts_refs)
    else:
        parts_ref, blocks_ref, attended_ref, cache_ref, sem, kept = refs

        def start_copy(k, carry):
            previous, slot = carry
            source = lax.div(kept_ref[request, k, head], source_blocks)
            slot = jnp.where(source == previous, jnp.minimum(slot + 1, MOST - 1), 0)
            target = kept.at[pl.ds(pl.multiple_of(k * BLK, BLK), BLK)]
            rows = pl.ds(pl.multiple_of(slot * BLK, BLK), BLK)
            pltpu.make_async_copy(blocks_ref.at[source, rows], target, sem).start()
            return source, slot

        lax.fori_loop(0, kept_count, start_copy, (jnp.int32(-1), jnp.int32(0)))
        total = jnp.sum(parts_ref[...], axis=0)
        pltpu.make_async_copy(kept, kept, sem).wait()
        pltpu.make_async_copy(kept, cache_ref.at[0, 0], sem).start()
    query_rows = QPK * step_count
    inverse = lax.rsqrt(total[query_rows + 2 * step_count :] * (1.0 / D) + EPS)
    cosine, sine = cos_ref[...], sin_ref[...]
    query = total[:query_rows].reshape(QPK // 2, 2 * step_count, HD) * inverse[None]
    query = rotate(query, cosine[None], sine[None]).reshape(query_rows, HD).astype(jnp.bfloat16)
    keyval = total[query_rows : query_rows + 2 * step_count] * inverse
    new_key = rotate(keyval, cosine, sine).astype(jnp.bfloat16)
    new_value = jnp.concatenate([keyval[step_count:], keyval[:step_count]], axis=0)
    new_value = new_value.astype(jnp.bfloat16)
    scale = 1.0 / math.sqrt(HD)
    score = lax.dot_general(query, new_key, CONTRACT_LAST, preferred_element_type=jnp.float32)
    row = lax.broadcasted_iota(jnp.int32, score.shape, 0)
    column = lax.broadcasted_iota(jnp.int32, score.shape, 1)
    scores = [jnp.where(column <= lax.rem(row, step_count), score * scale, -jnp.inf)]
    values = [new_value]
    def add_block(block, filled):
        score = lax.dot_general(
            query, block[:, :HD], CONTRACT_LAST, preferred_element_type=jnp.float32
        )
        column = lax.broadcasted_iota(jnp.int32, score.shape, 1)
        scores.append(jnp.where(column < filled * BLK, score * scale, -jnp.inf))
        values.append(block[:, HD:])

    if direct:
        for offset, ref in enumerate(by_offset):
            source = jnp.bitwise_xor(me, offset)
            filled = jnp.int32(0)
            for k in range(kept_count):
                here = lax.div(kept_ref[request, k, head], source_blocks) == source
                filled += here.astype(jnp.int32)
            add_block(ref[: MOST * BLK, :], filled)
    else:
        add_block(kept[...], kept_count)
    row_max = functools.reduce(
        jnp.maximum, [jnp.max(score, axis=1, keepdims=True) for score in scores]
    )
    denominator = jnp.zeros((query_rows, 1), jnp.float32)
    numerator = jnp.zeros((query_rows, HD), jnp.float32)
    for score, value in zip(scores, values):
        weight = jnp.exp(score - row_max)
        denominator += jnp.sum(weight, axis=1, keepdims=True)
        numerator += jnp.dot(
            weight.astype(jnp.bfloat16), value, preferred_element_type=jnp.float32
        )
    attended = (numerator / denominator).astype(jnp.bfloat16)
    if direct:
        attended_ref[...] = attended
    else:
        for i in range(attended_ref.shape[0]):
            attended_ref[i] = attended
        pltpu.make_async_copy(cache_ref, cache_ref, sem).wait()


def attend(kept_blocks, arrivals, source_blocks, heads_local, step_count, seq_count, direct):
    kept_count = kept_blocks.shape[1]
    cosine, sine = rope_tables(source_blocks * BLK * seq_count, step_count)
    shape = (QPK * step_count, HD)
    vmem = pl.BlockSpec(memory_space=pltpu.VMEM)
    if direct:
        shapes = [jax.ShapeDtypeStruct(shape, jnp.bfloat16)]
        out_specs = [vmem]
        scratch = []
    else:
        cache = (1, 1, kept_count * BLK, 2 * HD)
        shapes = [
            jax.ShapeDtypeStruct((seq_count,) + shape, jnp.bfloat16),
            jax.ShapeDtypeStruct(cache, jnp.bfloat16),
        ]
        out_specs = [vmem, pl.BlockSpec(memory_space=pl.ANY)]
        scratch = [pltpu.SemaphoreType.DMA, pltpu.VMEM(cache[2:], jnp.bfloat16)]
    return pl.pallas_call(
        functools.partial(attend_kernel, direct, source_blocks, heads_local),
        out_shape=shapes,
        in_specs=[pl.BlockSpec(memory_space=pltpu.SMEM)] + [vmem] * (2 + len(arrivals)),
        out_specs=out_specs,
        scratch_shapes=scratch,
        compiler_params=pltpu.CompilerParams(vmem_limit_bytes=16 * 1024 * 1024),
        cost_estimate=pl.CostEstimate(flops=10**10, bytes_accessed=0, transcendentals=0),
        name="attend",
    )(kept_blocks, jnp.asarray(cosine), jnp.asarray(sine), *arrivals)


def merge_heads(first, second, step_count):
    pieces = []
    for h in range(QPK):
        rows = slice(h * step_count, (h + 1) * step_count)
        pieces.append(jnp.concatenate([first[rows], second[rows]], axis=0))
    return jnp.concatenate(pieces, axis=1).astype(jnp.bfloat16)


def output_same_kernel(w_ref, own_ref, second_ref, out_ref):
    me = lax.axis_index("seq")
    out_ref[...] = output_terms(w_ref, jnp.bitwise_and(me, 1), me >= 2, own_ref, second_ref)


def output_other_kernel(w_ref, *refs):
    transfers, addend_ref, out_ref = refs[:4], refs[4], refs[5]
    me = lax.axis_index("seq")
    five, four, two, one = [ref[...].astype(jnp.float32) for ref in transfers]
    even = jnp.bitwise_and(me, 1) == 0
    first = jnp.where(even, two, four)
    third = jnp.where(me < 2, one, jnp.where(even, four, five))
    terms = output_terms(w_ref, 1 - jnp.bitwise_and(me, 1), me >= 2, first, third)
    out_ref[...] = (terms + addend_ref[...]).astype(out_ref.dtype)


def output_terms(w_ref, local, second, same, other):
    same = same[...].astype(jnp.float32)
    other = other[...].astype(jnp.float32)
    merged = merge_heads(
        jnp.where(second, other, same),
        jnp.where(second, same, other),
        same.shape[0] // QPK,
    )
    depth = w_ref.shape[0] // 2
    weights = w_ref[pl.ds(pl.multiple_of(local * depth, depth), depth), :]
    return jnp.dot(merged, weights, preferred_element_type=jnp.float32)


def output_half(kernel, dtype, w_out, values, *arrivals):
    rows = 2 * values.shape[0] // QPK
    vmem = pl.BlockSpec(memory_space=pltpu.VMEM)
    return pl.pallas_call(
        kernel,
        out_shape=jax.ShapeDtypeStruct((rows, w_out.shape[1]), dtype),
        in_specs=[vmem] * (2 + len(arrivals)),
        out_specs=vmem,
        compiler_params=pltpu.CompilerParams(vmem_limit_bytes=8 * 1024 * 1024),
        cost_estimate=pl.CostEstimate(flops=10**9, bytes_accessed=0, transcendentals=0),
        name="output_half",
    )(w_out, values, *arrivals)


def output_kernel(heads_local, w_ref, gathered_ref, out_ref):
    pair_count, query_rows, _ = gathered_ref.shape
    step_count = query_rows // QPK
    pairs = [gathered_ref[p].astype(jnp.float32) for p in range(pair_count)]
    requests = pair_count // heads_local
    pieces = []
    for l in range(heads_local):
        for h in range(QPK):
            rows = slice(h * step_count, (h + 1) * step_count)
            pieces.append(
                jnp.concatenate(
                    [pairs[r * heads_local + l][rows] for r in range(requests)], axis=0
                )
            )
    merged = jnp.concatenate(pieces, axis=1).astype(jnp.bfloat16)
    out_ref[...] = jnp.dot(merged, w_ref[...], preferred_element_type=jnp.float32)


def output(gathered, w_out, heads_local):
    pair_count, query_rows, _ = gathered.shape
    rows = pair_count // heads_local * (query_rows // QPK)
    vmem = pl.BlockSpec(memory_space=pltpu.VMEM)
    return pl.pallas_call(
        functools.partial(output_kernel, heads_local),
        out_shape=jax.ShapeDtypeStruct((rows, w_out.shape[1]), jnp.float32),
        in_specs=[vmem] * 2,
        out_specs=vmem,
        compiler_params=pltpu.CompilerParams(vmem_limit_bytes=8 * 1024 * 1024),
        name="output_projection",
    )(w_out, gathered)


def shards(source_cache, kept_blocks, new_hidden, norm_gain, w_query, w_keyval, w_out):
    seq_count = lax.axis_size("seq")
    head_count = lax.axis_size("head")
    requests, heads_local, source_tokens, _ = source_cache.shape
    _, step_count, width = new_hidden.shape
    pair_count = requests * heads_local

    kept_blocks = kept_blocks.transpose(0, 2, 1)
    source_blocks = source_tokens // BLK
    direct = is_direct(seq_count) and heads_local == 2
    weights = (new_hidden, norm_gain, w_query, w_keyval)
    w_out = pltpu.with_memory_space_constraint(w_out, pltpu.VMEM)
    shape = (source_blocks, heads_local, step_count, seq_count, direct)
    if direct:
        partners = range(1, seq_count)
        blocks = list(pick(kept_blocks, source_cache, direct))
        parts = list(project(blocks[0], *weights, pair_count, direct))
        blocks = [blocks[0]] + [swap(blocks[k], "seq", k) for k in partners]
        parts[1], blocks[3] = lax.optimization_barrier((parts[1], blocks[3]))
        parts = [parts[0]] + [swap(parts[k], "seq", k) for k in partners]
        (attended,) = attend(kept_blocks, blocks[::-1] + parts[::-1], *shape)
        one, two, three, four, five = [lax.ppermute(attended, "seq", p) for p in VALUE_PAIRS]
        three, two, one = lax.optimization_barrier((three, two, one))
        terms = output_half(output_same_kernel, jnp.float32, w_out, attended, three)
        terms = output_half(
            output_other_kernel, jnp.bfloat16, w_out, five, four, two, one, terms
        )
        kept_cache = place(kept_blocks, attended, blocks, source_blocks, heads_local)
    else:
        (blocks,) = pick(kept_blocks, source_cache, direct)
        (parts,) = project(blocks, *weights, pair_count, direct)
        arrivals = [all_to_all(parts, "seq"), all_to_all(blocks, "seq")]
        attended, kept_cache = attend(kept_blocks, arrivals, *shape)
        terms = output(all_to_all(attended, "seq"), w_out, heads_local)
    if is_direct(head_count):
        terms = terms.astype(jnp.bfloat16)
        others = [swap(terms, "head", k) for k in range(1, head_count)]
        others[2], kept_cache = lax.optimization_barrier((others[2], kept_cache))
        own, core, along, across = [t.astype(jnp.float32) for t in [terms] + others]
        summed = (own + core) + (along + across)
    else:
        summed = lax.psum(terms, "head")
    summed = summed.reshape(requests, step_count, width)
    decoded = (new_hidden.astype(jnp.float32) + summed).astype(jnp.bfloat16)
    return (kept_cache, decoded)


def solution(mesh):
    in_specs = (
        P("groups", "head", "seq", None),
        P("groups", None, None),
        P("groups", None, "seq"),
        P("seq"),
        P("seq", "head"),
        P("seq", "head", None),
        P("head", "seq"),
    )
    out_specs = (P("head", ("groups", "seq"), None, None), P("groups", None, "seq"))
    return jax.shard_map(shards, mesh=mesh, in_specs=in_specs, out_specs=out_specs, check_vma=False)
```

```python
import functools
import math

import jax
import jax.numpy as jnp
import numpy as np
from jax import lax
from jax.experimental import pallas as pl
from jax.experimental.pallas import tpu as pltpu
from jax.sharding import PartitionSpec as P

D = 8192
HD = 128
QPK = 8
BLK = 128
MOST = 2
ROPE_BASE = 500000.0
EPS = 1e-05

CONTRACT_LAST = (((1,), (1,)), ((), ()))


def rope_tables(prompt_length, step_count):
    positions = prompt_length + np.arange(2 * step_count) % step_count
    frequency = ROPE_BASE ** (-np.arange(HD // 2, dtype=np.float64) * 2.0 / HD)
    angles = positions[:, None] * frequency[None, :]
    cosine = np.concatenate([np.cos(angles)] * 2, axis=1)
    sine = np.concatenate([-np.sin(angles), np.sin(angles)], axis=1)
    return cosine.astype(np.float32), sine.astype(np.float32)


def rotate(v, cosine, sine):
    swapped = jnp.concatenate([v[..., HD // 2 :], v[..., : HD // 2]], axis=-1)
    return v * cosine + swapped * sine


def is_direct(count):
    return count == 4


def swap(outgoing, axis, offset):
    count = lax.axis_size(axis)
    return lax.ppermute(outgoing, axis, [(i, i ^ offset) for i in range(count)])


def shift(outgoing, axis, step):
    count = lax.axis_size(axis)
    return lax.ppermute(outgoing, axis, [(i, (i + step) % count) for i in range(count)])


def all_to_all(outgoing, axis):
    return lax.all_to_all(outgoing, axis, split_axis=0, concat_axis=0, tiled=True)


def picked_rows(kept_ref, cache_shape, pair, slot):
    _, heads_local, source_tokens, _ = cache_shape
    source_blocks = source_tokens // BLK
    kept_count = kept_ref.shape[1]
    first_block = lax.axis_index("seq") * source_blocks
    request = lax.div(pair, heads_local)
    local = lax.rem(pair, heads_local)
    head = lax.axis_index("head") * heads_local + local

    def count(k, total):
        return total + (kept_ref[request, k, head] < first_block).astype(jnp.int32)

    start = lax.fori_loop(0, kept_count, count, jnp.int32(0), unroll=kept_count <= 8)
    rank = jnp.minimum(start + slot, kept_count - 1)
    block = jnp.clip(kept_ref[request, rank, head] - first_block, 0, source_blocks - 1)
    return request, local, pl.ds(pl.multiple_of(block * BLK, BLK), BLK)


def pick_near_kernel(kept_hbm_ref, cache_ref, *refs):
    *outs, kept_ref, cache, kept_sem, sem = refs
    kept_copy = pltpu.make_async_copy(kept_hbm_ref, kept_ref, kept_sem)
    cache_copy = pltpu.make_async_copy(cache_ref, cache, sem)
    kept_copy.start()
    cache_copy.start()
    kept_copy.wait()
    me = lax.axis_index("seq")
    places = [
        [picked_rows(kept_ref, cache.shape, jnp.bitwise_xor(me, k), slot) for slot in range(MOST)]
        for k in range(len(outs))
    ]
    cache_copy.wait()
    for out_ref, slots in zip(outs, places):
        for slot, (request, local, rows) in enumerate(slots):
            out_ref[slot * BLK : (slot + 1) * BLK, :] = cache[request, local, rows, :]


def pick_all_kernel(kept_hbm_ref, cache_ref, out_ref, kept_ref, sem):
    pltpu.sync_copy(kept_hbm_ref, kept_ref)

    def pair_body(pair, carry):
        for slot in range(MOST):
            request, local, rows = picked_rows(kept_ref, cache_ref.shape, pair, slot)
            pltpu.make_async_copy(
                cache_ref.at[request, local, rows],
                out_ref.at[pair, pl.ds(slot * BLK, BLK)],
                sem,
            ).start()
        return carry

    lax.fori_loop(0, out_ref.shape[0], pair_body, 0)
    pltpu.make_async_copy(out_ref, out_ref, sem).wait()


def pick(kept_blocks, source_cache, direct):
    requests, heads_local, _, row_width = source_cache.shape
    pair_count = requests * heads_local
    block = (MOST * BLK, row_width)
    kept_scratch = pltpu.SMEM(kept_blocks.shape, jnp.int32)
    if direct:
        shapes = [jax.ShapeDtypeStruct(block, jnp.bfloat16)] * pair_count
        scratch = [
            kept_scratch,
            pltpu.VMEM(source_cache.shape, jnp.bfloat16),
            pltpu.SemaphoreType.DMA,
            pltpu.SemaphoreType.DMA,
        ]
    else:
        shapes = [jax.ShapeDtypeStruct((pair_count,) + block, jnp.bfloat16)]
        scratch = [kept_scratch, pltpu.SemaphoreType.DMA]
    return pl.pallas_call(
        pick_near_kernel if direct else pick_all_kernel,
        out_shape=shapes,
        in_specs=[pl.BlockSpec(memory_space=pl.ANY)] * 2,
        out_specs=[pl.BlockSpec(memory_space=pltpu.VMEM)] * len(shapes),
        scratch_shapes=scratch,
        compiler_params=pltpu.CompilerParams(vmem_limit_bytes=8 * 1024 * 1024),
        cost_estimate=pl.CostEstimate(flops=10**10, bytes_accessed=0, transcendentals=0),
        name="pick_blocks",
    )(
        pltpu.with_memory_space_constraint(kept_blocks, pltpu.HBM),
        pltpu.with_memory_space_constraint(source_cache, pltpu.HBM),
    )


def interleave(rows):
    count, width = rows.shape
    chunks = width // HD
    stacked = jnp.concatenate(
        [rows[:, c * HD : (c + 1) * HD] for c in range(chunks)], axis=0
    ).astype(jnp.bfloat16)
    source = lax.broadcasted_iota(jnp.int32, (HD, 4 * HD), 0)
    target = lax.broadcasted_iota(jnp.int32, (HD, 4 * HD), 1)
    place = jnp.where(target < 2 * HD, 2 * source, 2 * source + 1 + 2 * HD)
    spread = (place == target).astype(jnp.bfloat16)
    wide = jnp.dot(stacked, spread, preferred_element_type=jnp.float32)
    return [
        jnp.concatenate(
            [
                wide[c * count : (c + 1) * count, : 2 * HD],
                wide[c * count : (c + 1) * count, 2 * HD :],
            ],
            axis=0,
        ).astype(jnp.bfloat16)
        for c in range(chunks)
    ]


def project_kernel(direct, after_ref, hidden_ref, gain_ref, wq_ref, wkv_ref, *outs):
    del after_ref
    requests, step_count, width = hidden_ref.shape
    heads_local = wkv_ref.shape[1]
    row_count = requests * step_count
    me = lax.axis_index("seq")
    hidden = jnp.concatenate(
        [hidden_ref[r].astype(jnp.float32) for r in range(requests)], axis=0
    )
    square = jnp.sum(hidden * hidden, axis=1, keepdims=True)
    gain = gain_ref[...].astype(jnp.float32)
    scaled = jnp.concatenate(
        [hidden[:, c * HD : (c + 1) * HD] * gain[c : c + 1] for c in range(width // HD)], axis=1
    ).astype(jnp.bfloat16)
    query = jnp.dot(scaled, wq_ref[...], preferred_element_type=jnp.float32)
    keyval = jnp.zeros((heads_local * row_count, wkv_ref.shape[2]), jnp.float32)
    for c, spread in enumerate(interleave(scaled.astype(jnp.float32))):
        alternate = wkv_ref[c * HD : (c + 1) * HD].reshape(heads_local * HD, wkv_ref.shape[2])
        keyval += jnp.dot(spread, alternate, preferred_element_type=jnp.float32)

    def pieces_of(r, l):
        steps = slice(r * step_count, (r + 1) * step_count)
        square_rows = jnp.broadcast_to(square[steps], (step_count, HD))
        own = keyval[l * row_count + r * step_count : l * row_count + (r + 1) * step_count]
        heads = [query[steps, (l * QPK + h) * HD : (l * QPK + h + 1) * HD] for h in range(QPK)]
        return heads + [own[:, :HD], own[:, HD:], square_rows, square_rows]

    def write_pair(out_ref, pieces):
        for j, piece in enumerate(pieces):
            out_ref[j * step_count : (j + 1) * step_count, :] = piece

    for r in range(requests):
        for l in range(heads_local):
            pair = r * heads_local + l
            pieces = pieces_of(r, l)
            if not direct:
                write_pair(outs[0].at[pair], pieces)
                continue
            for offset, out_ref in enumerate(outs):
                pl.when(jnp.bitwise_xor(me, offset) == pair)(
                    functools.partial(write_pair, out_ref, pieces)
                )


def project(after, new_hidden, norm_gain, w_query, w_keyval, pair_count, direct):
    requests, step_count, width = new_hidden.shape
    terms = ((QPK + 4) * step_count, HD)
    if direct:
        shapes = [jax.ShapeDtypeStruct(terms, jnp.float32)] * pair_count
    else:
        shapes = [jax.ShapeDtypeStruct((pair_count,) + terms, jnp.float32)]
    vmem = pl.BlockSpec(memory_space=pltpu.VMEM)
    weights = w_query.size + w_keyval.size
    return pl.pallas_call(
        functools.partial(project_kernel, direct),
        out_shape=shapes,
        in_specs=[pl.BlockSpec(memory_space=pl.ANY)] + [vmem] * 4,
        out_specs=[vmem] * len(shapes),
        compiler_params=pltpu.CompilerParams(vmem_limit_bytes=8 * 1024 * 1024),
        cost_estimate=pl.CostEstimate(
            flops=2 * requests * step_count * weights,
            bytes_accessed=2 * weights,
            transcendentals=0,
        ),
        name="project",
    )(
        after,
        new_hidden,
        norm_gain.reshape(width // HD, HD),
        pltpu.with_memory_space_constraint(w_query, pltpu.VMEM),
        pltpu.with_memory_space_constraint(w_keyval, pltpu.VMEM),
    )


def place_kernel(source_blocks, heads_local, kept_ref, after_ref, *refs):
    del after_ref
    *by_offset, cache_ref, sem = refs
    me = lax.axis_index("seq")
    request = lax.div(me, heads_local)
    head = lax.axis_index("head") * heads_local + lax.rem(me, heads_local)
    previous, slot = jnp.int32(-1), jnp.int32(0)
    for k in range(kept_ref.shape[1]):
        source = lax.div(kept_ref[request, k, head], source_blocks)
        slot = jnp.where(source == previous, jnp.minimum(slot + 1, MOST - 1), 0)
        previous = source
        rows = pl.ds(pl.multiple_of(slot * BLK, BLK), BLK)
        target = cache_ref.at[0, 0, pl.ds(k * BLK, BLK)]
        for offset, ref in enumerate(by_offset):
            pl.when(jnp.bitwise_xor(me, offset) == source)(
                pltpu.make_async_copy(ref.at[rows], target, sem).start
            )
    pltpu.make_async_copy(cache_ref, cache_ref, sem).wait()


def place(kept_blocks, after, blocks, source_blocks, heads_local):
    kept_count = kept_blocks.shape[1]
    anywhere = pl.BlockSpec(memory_space=pl.ANY)
    return pl.pallas_call(
        functools.partial(place_kernel, source_blocks, heads_local),
        out_shape=jax.ShapeDtypeStruct((1, 1, kept_count * BLK, 2 * HD), jnp.bfloat16),
        in_specs=[pl.BlockSpec(memory_space=pltpu.SMEM)] + [anywhere] * (1 + len(blocks)),
        out_specs=anywhere,
        scratch_shapes=[pltpu.SemaphoreType.DMA],
        compiler_params=pltpu.CompilerParams(vmem_limit_bytes=8 * 1024 * 1024),
        cost_estimate=pl.CostEstimate(flops=10**9, bytes_accessed=0, transcendentals=0),
        name="place",
    )(kept_blocks, after, *blocks)


def attend_kernel(direct, source_blocks, heads_local, kept_ref, cos_ref, sin_ref, *refs):
    kept_count = kept_ref.shape[1]
    step_count = cos_ref.shape[0] // 2
    me = lax.axis_index("seq")
    request = lax.div(me, heads_local)
    head = lax.axis_index("head") * heads_local + lax.rem(me, heads_local)
    if direct:
        by_offset, parts_refs, attended_ref = refs[:4][::-1], refs[4:8][::-1], refs[8]
        total = sum(ref[...] for ref in parts_refs)
    else:
        parts_ref, blocks_ref, attended_ref, cache_ref, sem, kept = refs

        def start_copy(k, carry):
            previous, slot = carry
            source = lax.div(kept_ref[request, k, head], source_blocks)
            slot = jnp.where(source == previous, jnp.minimum(slot + 1, MOST - 1), 0)
            target = kept.at[pl.ds(pl.multiple_of(k * BLK, BLK), BLK)]
            rows = pl.ds(pl.multiple_of(slot * BLK, BLK), BLK)
            pltpu.make_async_copy(blocks_ref.at[source, rows], target, sem).start()
            return source, slot

        lax.fori_loop(0, kept_count, start_copy, (jnp.int32(-1), jnp.int32(0)))
        total = jnp.sum(parts_ref[...], axis=0)
        pltpu.make_async_copy(kept, kept, sem).wait()
        pltpu.make_async_copy(kept, cache_ref.at[0, 0], sem).start()
    query_rows = QPK * step_count
    inverse = lax.rsqrt(total[query_rows + 2 * step_count :] * (1.0 / D) + EPS)
    cosine, sine = cos_ref[...], sin_ref[...]
    query = total[:query_rows].reshape(QPK // 2, 2 * step_count, HD) * inverse[None]
    query = rotate(query, cosine[None], sine[None]).reshape(query_rows, HD).astype(jnp.bfloat16)
    keyval = total[query_rows : query_rows + 2 * step_count] * inverse
    new_key = rotate(keyval, cosine, sine).astype(jnp.bfloat16)
    new_value = jnp.concatenate([keyval[step_count:], keyval[:step_count]], axis=0)
    new_value = new_value.astype(jnp.bfloat16)
    scale = 1.0 / math.sqrt(HD)
    score = lax.dot_general(query, new_key, CONTRACT_LAST, preferred_element_type=jnp.float32)
    row = lax.broadcasted_iota(jnp.int32, score.shape, 0)
    column = lax.broadcasted_iota(jnp.int32, score.shape, 1)
    scores = [jnp.where(column <= lax.rem(row, step_count), score * scale, -jnp.inf)]
    values = [new_value]
    def add_block(block, filled):
        score = lax.dot_general(
            query, block[:, :HD], CONTRACT_LAST, preferred_element_type=jnp.float32
        )
        column = lax.broadcasted_iota(jnp.int32, score.shape, 1)
        scores.append(jnp.where(column < filled * BLK, score * scale, -jnp.inf))
        values.append(block[:, HD:])

    if direct:
        for offset, ref in enumerate(by_offset):
            source = jnp.bitwise_xor(me, offset)
            filled = jnp.int32(0)
            for k in range(kept_count):
                here = lax.div(kept_ref[request, k, head], source_blocks) == source
                filled += here.astype(jnp.int32)
            add_block(ref[: MOST * BLK, :], filled)
    else:
        add_block(kept[...], kept_count)
    row_max = functools.reduce(
        jnp.maximum, [jnp.max(score, axis=1, keepdims=True) for score in scores]
    )
    denominator = jnp.zeros((query_rows, 1), jnp.float32)
    numerator = jnp.zeros((query_rows, HD), jnp.float32)
    for score, value in zip(scores, values):
        weight = jnp.exp(score - row_max)
        denominator += jnp.sum(weight, axis=1, keepdims=True)
        numerator += jnp.dot(
            weight.astype(jnp.bfloat16), value, preferred_element_type=jnp.float32
        )
    attended = (numerator / denominator).astype(jnp.bfloat16)
    if direct:
        attended_ref[...] = attended
    else:
        for i in range(attended_ref.shape[0]):
            attended_ref[i] = attended
        pltpu.make_async_copy(cache_ref, cache_ref, sem).wait()


def attend(kept_blocks, arrivals, source_blocks, heads_local, step_count, seq_count, direct):
    kept_count = kept_blocks.shape[1]
    cosine, sine = rope_tables(source_blocks * BLK * seq_count, step_count)
    shape = (QPK * step_count, HD)
    vmem = pl.BlockSpec(memory_space=pltpu.VMEM)
    if direct:
        shapes = [jax.ShapeDtypeStruct(shape, jnp.bfloat16)]
        out_specs = [vmem]
        scratch = []
    else:
        cache = (1, 1, kept_count * BLK, 2 * HD)
        shapes = [
            jax.ShapeDtypeStruct((seq_count,) + shape, jnp.bfloat16),
            jax.ShapeDtypeStruct(cache, jnp.bfloat16),
        ]
        out_specs = [vmem, pl.BlockSpec(memory_space=pl.ANY)]
        scratch = [pltpu.SemaphoreType.DMA, pltpu.VMEM(cache[2:], jnp.bfloat16)]
    return pl.pallas_call(
        functools.partial(attend_kernel, direct, source_blocks, heads_local),
        out_shape=shapes,
        in_specs=[pl.BlockSpec(memory_space=pltpu.SMEM)] + [vmem] * (2 + len(arrivals)),
        out_specs=out_specs,
        scratch_shapes=scratch,
        compiler_params=pltpu.CompilerParams(vmem_limit_bytes=16 * 1024 * 1024),
        cost_estimate=pl.CostEstimate(flops=10**10, bytes_accessed=0, transcendentals=0),
        name="attend",
    )(kept_blocks, jnp.asarray(cosine), jnp.asarray(sine), *arrivals)


def merge_heads(first, second, step_count):
    pieces = []
    for h in range(QPK):
        rows = slice(h * step_count, (h + 1) * step_count)
        pieces.append(jnp.concatenate([first[rows], second[rows]], axis=0))
    return jnp.concatenate(pieces, axis=1).astype(jnp.bfloat16)


def output_same_kernel(w_ref, own_ref, second_ref, out_ref):
    me = lax.axis_index("seq")
    out_ref[...] = output_terms(w_ref, jnp.bitwise_and(me, 1), me >= 2, own_ref, second_ref)


def output_other_kernel(w_ref, above_ref, below_ref, addend_ref, out_ref):
    me = lax.axis_index("seq")
    even = jnp.bitwise_and(me, 1) == 0
    below = below_ref[...].astype(jnp.float32)
    above = above_ref[...].astype(jnp.float32)
    first = jnp.where(even, above, below)
    third = jnp.where(even, below, above)
    terms = output_terms(w_ref, 1 - jnp.bitwise_and(me, 1), me >= 2, first, third)
    out_ref[...] = (terms + addend_ref[...]).astype(out_ref.dtype)


def output_terms(w_ref, local, second, same, other):
    same = same[...].astype(jnp.float32)
    other = other[...].astype(jnp.float32)
    merged = merge_heads(
        jnp.where(second, other, same),
        jnp.where(second, same, other),
        same.shape[0] // QPK,
    )
    depth = w_ref.shape[0] // 2
    weights = w_ref[pl.ds(pl.multiple_of(local * depth, depth), depth), :]
    return jnp.dot(merged, weights, preferred_element_type=jnp.float32)


def output_half(kernel, dtype, w_out, values, *arrivals):
    rows = 2 * values.shape[0] // QPK
    vmem = pl.BlockSpec(memory_space=pltpu.VMEM)
    return pl.pallas_call(
        kernel,
        out_shape=jax.ShapeDtypeStruct((rows, w_out.shape[1]), dtype),
        in_specs=[vmem] * (2 + len(arrivals)),
        out_specs=vmem,
        compiler_params=pltpu.CompilerParams(vmem_limit_bytes=8 * 1024 * 1024),
        cost_estimate=pl.CostEstimate(flops=10**9, bytes_accessed=0, transcendentals=0),
        name="output_half",
    )(w_out, values, *arrivals)


def output_kernel(heads_local, w_ref, gathered_ref, out_ref):
    pair_count, query_rows, _ = gathered_ref.shape
    step_count = query_rows // QPK
    pairs = [gathered_ref[p].astype(jnp.float32) for p in range(pair_count)]
    requests = pair_count // heads_local
    pieces = []
    for l in range(heads_local):
        for h in range(QPK):
            rows = slice(h * step_count, (h + 1) * step_count)
            pieces.append(
                jnp.concatenate(
                    [pairs[r * heads_local + l][rows] for r in range(requests)], axis=0
                )
            )
    merged = jnp.concatenate(pieces, axis=1).astype(jnp.bfloat16)
    out_ref[...] = jnp.dot(merged, w_ref[...], preferred_element_type=jnp.float32)


def output(gathered, w_out, heads_local):
    pair_count, query_rows, _ = gathered.shape
    rows = pair_count // heads_local * (query_rows // QPK)
    vmem = pl.BlockSpec(memory_space=pltpu.VMEM)
    return pl.pallas_call(
        functools.partial(output_kernel, heads_local),
        out_shape=jax.ShapeDtypeStruct((rows, w_out.shape[1]), jnp.float32),
        in_specs=[vmem] * 2,
        out_specs=vmem,
        compiler_params=pltpu.CompilerParams(vmem_limit_bytes=8 * 1024 * 1024),
        name="output_projection",
    )(w_out, gathered)


def shards(source_cache, kept_blocks, new_hidden, norm_gain, w_query, w_keyval, w_out):
    seq_count = lax.axis_size("seq")
    head_count = lax.axis_size("head")
    requests, heads_local, source_tokens, _ = source_cache.shape
    _, step_count, width = new_hidden.shape
    pair_count = requests * heads_local

    kept_blocks = kept_blocks.transpose(0, 2, 1)
    source_blocks = source_tokens // BLK
    direct = is_direct(seq_count) and heads_local == 2
    weights = (new_hidden, norm_gain, w_query, w_keyval)
    w_out = pltpu.with_memory_space_constraint(w_out, pltpu.VMEM)
    shape = (source_blocks, heads_local, step_count, seq_count, direct)
    if direct:
        partners = range(1, seq_count)
        blocks = list(pick(kept_blocks, source_cache, direct))
        parts = list(project(blocks[0], *weights, pair_count, direct))
        blocks = [blocks[0]] + [swap(blocks[k], "seq", k) for k in partners]
        parts[1], blocks[3] = lax.optimization_barrier((parts[1], blocks[3]))
        parts = [parts[0]] + [swap(parts[k], "seq", k) for k in partners]
        (attended,) = attend(kept_blocks, blocks[::-1] + parts[::-1], *shape)
        kept_cache = place(kept_blocks, attended, blocks, source_blocks, heads_local)
        below, second, above = [shift(attended, "seq", step) for step in (1, 2, -1)]
        second, below = lax.optimization_barrier((second, below))
        terms = output_half(output_same_kernel, jnp.float32, w_out, attended, second)
        terms = output_half(output_other_kernel, jnp.bfloat16, w_out, above, below, terms)
    else:
        (blocks,) = pick(kept_blocks, source_cache, direct)
        (parts,) = project(blocks, *weights, pair_count, direct)
        arrivals = [all_to_all(parts, "seq"), all_to_all(blocks, "seq")]
        attended, kept_cache = attend(kept_blocks, arrivals, *shape)
        terms = output(all_to_all(attended, "seq"), w_out, heads_local)
    if is_direct(head_count):
        terms = terms.astype(jnp.bfloat16)
        terms, kept_cache = lax.optimization_barrier((terms, kept_cache))
        others = [swap(terms, "head", k) for k in range(1, head_count)]
        own, core, along, across = [t.astype(jnp.float32) for t in [terms] + others]
        summed = (own + core) + (along + across)
    else:
        summed = lax.psum(terms, "head")
    summed = summed.reshape(requests, step_count, width)
    decoded = (new_hidden.astype(jnp.float32) + summed).astype(jnp.bfloat16)
    return (kept_cache, decoded)


def solution(mesh):
    in_specs = (
        P("groups", "head", "seq", None),
        P("groups", None, None),
        P("groups", None, "seq"),
        P("seq"),
        P("seq", "head"),
        P("seq", "head", None),
        P("head", "seq"),
    )
    out_specs = (P("head", ("groups", "seq"), None, None), P("groups", None, "seq"))
    return jax.shard_map(shards, mesh=mesh, in_specs=in_specs, out_specs=out_specs, check_vma=False)
```

```python
import functools
import math

import jax
import jax.numpy as jnp
import numpy as np
from jax import lax
from jax.experimental import pallas as pl
from jax.experimental.pallas import tpu as pltpu
from jax.sharding import PartitionSpec as P

D = 8192
HD = 128
QPK = 8
BLK = 128
MOST = 2
ROPE_BASE = 500000.0
EPS = 1e-05

CONTRACT_LAST = (((1,), (1,)), ((), ()))


def rope_tables(prompt_length, step_count):
    positions = prompt_length + np.arange(2 * step_count) % step_count
    frequency = ROPE_BASE ** (-np.arange(HD // 2, dtype=np.float64) * 2.0 / HD)
    angles = positions[:, None] * frequency[None, :]
    cosine = np.concatenate([np.cos(angles)] * 2, axis=1)
    sine = np.concatenate([-np.sin(angles), np.sin(angles)], axis=1)
    return cosine.astype(np.float32), sine.astype(np.float32)


def rotate(v, cosine, sine):
    swapped = jnp.concatenate([v[..., HD // 2 :], v[..., : HD // 2]], axis=-1)
    return v * cosine + swapped * sine


def is_direct(count):
    return count == 4


def swap(outgoing, axis, offset):
    count = lax.axis_size(axis)
    return lax.ppermute(outgoing, axis, [(i, i ^ offset) for i in range(count)])


def shift(outgoing, axis, step):
    count = lax.axis_size(axis)
    return lax.ppermute(outgoing, axis, [(i, (i + step) % count) for i in range(count)])


def all_to_all(outgoing, axis):
    return lax.all_to_all(outgoing, axis, split_axis=0, concat_axis=0, tiled=True)


def picked_rows(kept_ref, cache_shape, pair, slot):
    _, heads_local, source_tokens, _ = cache_shape
    source_blocks = source_tokens // BLK
    kept_count = kept_ref.shape[1]
    first_block = lax.axis_index("seq") * source_blocks
    request = lax.div(pair, heads_local)
    local = lax.rem(pair, heads_local)
    head = lax.axis_index("head") * heads_local + local

    def count(k, total):
        return total + (kept_ref[request, k, head] < first_block).astype(jnp.int32)

    start = lax.fori_loop(0, kept_count, count, jnp.int32(0), unroll=kept_count <= 8)
    rank = jnp.minimum(start + slot, kept_count - 1)
    block = jnp.clip(kept_ref[request, rank, head] - first_block, 0, source_blocks - 1)
    return request, local, pl.ds(pl.multiple_of(block * BLK, BLK), BLK)


def pick_near_kernel(kept_hbm_ref, cache_ref, *refs):
    *outs, kept_ref, cache, kept_sem, sem = refs
    kept_copy = pltpu.make_async_copy(kept_hbm_ref, kept_ref, kept_sem)
    cache_copy = pltpu.make_async_copy(cache_ref, cache, sem)
    kept_copy.start()
    cache_copy.start()
    kept_copy.wait()
    me = lax.axis_index("seq")
    places = [
        [picked_rows(kept_ref, cache.shape, jnp.bitwise_xor(me, k), slot) for slot in range(MOST)]
        for k in range(len(outs))
    ]
    cache_copy.wait()
    for out_ref, slots in zip(outs, places):
        for slot, (request, local, rows) in enumerate(slots):
            out_ref[slot * BLK : (slot + 1) * BLK, :] = cache[request, local, rows, :]


def pick_all_kernel(kept_hbm_ref, cache_ref, out_ref, kept_ref, sem):
    pltpu.sync_copy(kept_hbm_ref, kept_ref)

    def pair_body(pair, carry):
        for slot in range(MOST):
            request, local, rows = picked_rows(kept_ref, cache_ref.shape, pair, slot)
            pltpu.make_async_copy(
                cache_ref.at[request, local, rows],
                out_ref.at[pair, pl.ds(slot * BLK, BLK)],
                sem,
            ).start()
        return carry

    lax.fori_loop(0, out_ref.shape[0], pair_body, 0)
    pltpu.make_async_copy(out_ref, out_ref, sem).wait()


def pick(kept_blocks, source_cache, direct):
    requests, heads_local, _, row_width = source_cache.shape
    pair_count = requests * heads_local
    block = (MOST * BLK, row_width)
    kept_scratch = pltpu.SMEM(kept_blocks.shape, jnp.int32)
    if direct:
        shapes = [jax.ShapeDtypeStruct(block, jnp.bfloat16)] * pair_count
        scratch = [
            kept_scratch,
            pltpu.VMEM(source_cache.shape, jnp.bfloat16),
            pltpu.SemaphoreType.DMA,
            pltpu.SemaphoreType.DMA,
        ]
    else:
        shapes = [jax.ShapeDtypeStruct((pair_count,) + block, jnp.bfloat16)]
        scratch = [kept_scratch, pltpu.SemaphoreType.DMA]
    return pl.pallas_call(
        pick_near_kernel if direct else pick_all_kernel,
        out_shape=shapes,
        in_specs=[pl.BlockSpec(memory_space=pl.ANY)] * 2,
        out_specs=[pl.BlockSpec(memory_space=pltpu.VMEM)] * len(shapes),
        scratch_shapes=scratch,
        compiler_params=pltpu.CompilerParams(vmem_limit_bytes=8 * 1024 * 1024),
        cost_estimate=pl.CostEstimate(flops=10**10, bytes_accessed=0, transcendentals=0),
        name="pick_blocks",
    )(
        pltpu.with_memory_space_constraint(kept_blocks, pltpu.HBM),
        pltpu.with_memory_space_constraint(source_cache, pltpu.HBM),
    )


def interleave(rows):
    count, width = rows.shape
    chunks = width // HD
    stacked = jnp.concatenate(
        [rows[:, c * HD : (c + 1) * HD] for c in range(chunks)], axis=0
    ).astype(jnp.bfloat16)
    source = lax.broadcasted_iota(jnp.int32, (HD, 4 * HD), 0)
    target = lax.broadcasted_iota(jnp.int32, (HD, 4 * HD), 1)
    place = jnp.where(target < 2 * HD, 2 * source, 2 * source + 1 + 2 * HD)
    spread = (place == target).astype(jnp.bfloat16)
    wide = jnp.dot(stacked, spread, preferred_element_type=jnp.float32)
    return [
        jnp.concatenate(
            [
                wide[c * count : (c + 1) * count, : 2 * HD],
                wide[c * count : (c + 1) * count, 2 * HD :],
            ],
            axis=0,
        ).astype(jnp.bfloat16)
        for c in range(chunks)
    ]


def project_kernel(direct, after_ref, hidden_ref, gain_ref, wq_ref, wkv_ref, *outs):
    del after_ref
    requests, step_count, width = hidden_ref.shape
    heads_local = wkv_ref.shape[1]
    row_count = requests * step_count
    me = lax.axis_index("seq")
    hidden = jnp.concatenate(
        [hidden_ref[r].astype(jnp.float32) for r in range(requests)], axis=0
    )
    square = jnp.sum(hidden * hidden, axis=1, keepdims=True)
    gain = gain_ref[...].astype(jnp.float32)
    scaled = jnp.concatenate(
        [hidden[:, c * HD : (c + 1) * HD] * gain[c : c + 1] for c in range(width // HD)], axis=1
    ).astype(jnp.bfloat16)
    query = jnp.dot(scaled, wq_ref[...], preferred_element_type=jnp.float32)
    keyval = jnp.zeros((heads_local * row_count, wkv_ref.shape[2]), jnp.float32)
    for c, spread in enumerate(interleave(scaled.astype(jnp.float32))):
        alternate = wkv_ref[c * HD : (c + 1) * HD].reshape(heads_local * HD, wkv_ref.shape[2])
        keyval += jnp.dot(spread, alternate, preferred_element_type=jnp.float32)

    def pieces_of(r, l):
        steps = slice(r * step_count, (r + 1) * step_count)
        square_rows = jnp.broadcast_to(square[steps], (step_count, HD))
        own = keyval[l * row_count + r * step_count : l * row_count + (r + 1) * step_count]
        heads = [query[steps, (l * QPK + h) * HD : (l * QPK + h + 1) * HD] for h in range(QPK)]
        return heads + [own[:, :HD], own[:, HD:], square_rows, square_rows]

    def write_pair(out_ref, pieces):
        for j, piece in enumerate(pieces):
            out_ref[j * step_count : (j + 1) * step_count, :] = piece

    for r in range(requests):
        for l in range(heads_local):
            pair = r * heads_local + l
            pieces = pieces_of(r, l)
            if not direct:
                write_pair(outs[0].at[pair], pieces)
                continue
            for offset, out_ref in enumerate(outs):
                pl.when(jnp.bitwise_xor(me, offset) == pair)(
                    functools.partial(write_pair, out_ref, pieces)
                )


def project(after, new_hidden, norm_gain, w_query, w_keyval, pair_count, direct):
    requests, step_count, width = new_hidden.shape
    terms = ((QPK + 4) * step_count, HD)
    if direct:
        shapes = [jax.ShapeDtypeStruct(terms, jnp.float32)] * pair_count
    else:
        shapes = [jax.ShapeDtypeStruct((pair_count,) + terms, jnp.float32)]
    vmem = pl.BlockSpec(memory_space=pltpu.VMEM)
    weights = w_query.size + w_keyval.size
    return pl.pallas_call(
        functools.partial(project_kernel, direct),
        out_shape=shapes,
        in_specs=[pl.BlockSpec(memory_space=pl.ANY)] + [vmem] * 4,
        out_specs=[vmem] * len(shapes),
        compiler_params=pltpu.CompilerParams(vmem_limit_bytes=8 * 1024 * 1024),
        cost_estimate=pl.CostEstimate(
            flops=2 * requests * step_count * weights,
            bytes_accessed=2 * weights,
            transcendentals=0,
        ),
        name="project",
    )(
        after,
        new_hidden,
        norm_gain.reshape(width // HD, HD),
        pltpu.with_memory_space_constraint(w_query, pltpu.VMEM),
        pltpu.with_memory_space_constraint(w_keyval, pltpu.VMEM),
    )


def place_kernel(source_blocks, heads_local, kept_ref, after_ref, *refs):
    del after_ref
    *by_offset, cache_ref, sem = refs
    me = lax.axis_index("seq")
    request = lax.div(me, heads_local)
    head = lax.axis_index("head") * heads_local + lax.rem(me, heads_local)
    previous, slot = jnp.int32(-1), jnp.int32(0)
    for k in range(kept_ref.shape[1]):
        source = lax.div(kept_ref[request, k, head], source_blocks)
        slot = jnp.where(source == previous, jnp.minimum(slot + 1, MOST - 1), 0)
        previous = source
        rows = pl.ds(pl.multiple_of(slot * BLK, BLK), BLK)
        target = cache_ref.at[0, 0, pl.ds(k * BLK, BLK)]
        for offset, ref in enumerate(by_offset):
            pl.when(jnp.bitwise_xor(me, offset) == source)(
                pltpu.make_async_copy(ref.at[rows], target, sem).start
            )
    pltpu.make_async_copy(cache_ref, cache_ref, sem).wait()


def place(kept_blocks, after, blocks, source_blocks, heads_local):
    kept_count = kept_blocks.shape[1]
    anywhere = pl.BlockSpec(memory_space=pl.ANY)
    return pl.pallas_call(
        functools.partial(place_kernel, source_blocks, heads_local),
        out_shape=jax.ShapeDtypeStruct((1, 1, kept_count * BLK, 2 * HD), jnp.bfloat16),
        in_specs=[pl.BlockSpec(memory_space=pltpu.SMEM)] + [anywhere] * (1 + len(blocks)),
        out_specs=anywhere,
        scratch_shapes=[pltpu.SemaphoreType.DMA],
        compiler_params=pltpu.CompilerParams(vmem_limit_bytes=8 * 1024 * 1024),
        cost_estimate=pl.CostEstimate(flops=10**9, bytes_accessed=0, transcendentals=0),
        name="place",
    )(kept_blocks, after, *blocks)


def attend_kernel(direct, source_blocks, heads_local, kept_ref, cos_ref, sin_ref, *refs):
    kept_count = kept_ref.shape[1]
    step_count = cos_ref.shape[0] // 2
    me = lax.axis_index("seq")
    request = lax.div(me, heads_local)
    head = lax.axis_index("head") * heads_local + lax.rem(me, heads_local)
    if direct:
        by_offset, parts_refs, attended_ref = refs[:4][::-1], refs[4:8][::-1], refs[8]
        total = sum(ref[...] for ref in parts_refs)
    else:
        parts_ref, blocks_ref, attended_ref, cache_ref, sem, kept = refs

        def start_copy(k, carry):
            previous, slot = carry
            source = lax.div(kept_ref[request, k, head], source_blocks)
            slot = jnp.where(source == previous, jnp.minimum(slot + 1, MOST - 1), 0)
            target = kept.at[pl.ds(pl.multiple_of(k * BLK, BLK), BLK)]
            rows = pl.ds(pl.multiple_of(slot * BLK, BLK), BLK)
            pltpu.make_async_copy(blocks_ref.at[source, rows], target, sem).start()
            return source, slot

        lax.fori_loop(0, kept_count, start_copy, (jnp.int32(-1), jnp.int32(0)))
        total = jnp.sum(parts_ref[...], axis=0)
        pltpu.make_async_copy(kept, kept, sem).wait()
        pltpu.make_async_copy(kept, cache_ref.at[0, 0], sem).start()
    query_rows = QPK * step_count
    inverse = lax.rsqrt(total[query_rows + 2 * step_count :] * (1.0 / D) + EPS)
    cosine, sine = cos_ref[...], sin_ref[...]
    query = total[:query_rows].reshape(QPK // 2, 2 * step_count, HD) * inverse[None]
    query = rotate(query, cosine[None], sine[None]).reshape(query_rows, HD).astype(jnp.bfloat16)
    keyval = total[query_rows : query_rows + 2 * step_count] * inverse
    new_key = rotate(keyval, cosine, sine).astype(jnp.bfloat16)
    new_value = jnp.concatenate([keyval[step_count:], keyval[:step_count]], axis=0)
    new_value = new_value.astype(jnp.bfloat16)
    scale = 1.0 / math.sqrt(HD)
    score = lax.dot_general(query, new_key, CONTRACT_LAST, preferred_element_type=jnp.float32)
    row = lax.broadcasted_iota(jnp.int32, score.shape, 0)
    column = lax.broadcasted_iota(jnp.int32, score.shape, 1)
    scores = [jnp.where(column <= lax.rem(row, step_count), score * scale, -jnp.inf)]
    values = [new_value]
    def add_block(block, filled):
        score = lax.dot_general(
            query, block[:, :HD], CONTRACT_LAST, preferred_element_type=jnp.float32
        )
        column = lax.broadcasted_iota(jnp.int32, score.shape, 1)
        scores.append(jnp.where(column < filled * BLK, score * scale, -jnp.inf))
        values.append(block[:, HD:])

    if direct:
        for offset, ref in enumerate(by_offset):
            source = jnp.bitwise_xor(me, offset)
            filled = jnp.int32(0)
            for k in range(kept_count):
                here = lax.div(kept_ref[request, k, head], source_blocks) == source
                filled += here.astype(jnp.int32)
            add_block(ref[: MOST * BLK, :], filled)
    else:
        add_block(kept[...], kept_count)
    row_max = functools.reduce(
        jnp.maximum, [jnp.max(score, axis=1, keepdims=True) for score in scores]
    )
    denominator = jnp.zeros((query_rows, 1), jnp.float32)
    numerator = jnp.zeros((query_rows, HD), jnp.float32)
    for score, value in zip(scores, values):
        weight = jnp.exp(score - row_max)
        denominator += jnp.sum(weight, axis=1, keepdims=True)
        numerator += jnp.dot(
            weight.astype(jnp.bfloat16), value, preferred_element_type=jnp.float32
        )
    attended = (numerator / denominator).astype(jnp.bfloat16)
    if direct:
        attended_ref[...] = attended
    else:
        for i in range(attended_ref.shape[0]):
            attended_ref[i] = attended
        pltpu.make_async_copy(cache_ref, cache_ref, sem).wait()


def attend(kept_blocks, arrivals, source_blocks, heads_local, step_count, seq_count, direct):
    kept_count = kept_blocks.shape[1]
    cosine, sine = rope_tables(source_blocks * BLK * seq_count, step_count)
    shape = (QPK * step_count, HD)
    vmem = pl.BlockSpec(memory_space=pltpu.VMEM)
    if direct:
        shapes = [jax.ShapeDtypeStruct(shape, jnp.bfloat16)]
        out_specs = [vmem]
        scratch = []
    else:
        cache = (1, 1, kept_count * BLK, 2 * HD)
        shapes = [
            jax.ShapeDtypeStruct((seq_count,) + shape, jnp.bfloat16),
            jax.ShapeDtypeStruct(cache, jnp.bfloat16),
        ]
        out_specs = [vmem, pl.BlockSpec(memory_space=pl.ANY)]
        scratch = [pltpu.SemaphoreType.DMA, pltpu.VMEM(cache[2:], jnp.bfloat16)]
    return pl.pallas_call(
        functools.partial(attend_kernel, direct, source_blocks, heads_local),
        out_shape=shapes,
        in_specs=[pl.BlockSpec(memory_space=pltpu.SMEM)] + [vmem] * (2 + len(arrivals)),
        out_specs=out_specs,
        scratch_shapes=scratch,
        compiler_params=pltpu.CompilerParams(vmem_limit_bytes=16 * 1024 * 1024),
        cost_estimate=pl.CostEstimate(flops=10**10, bytes_accessed=0, transcendentals=0),
        name="attend",
    )(kept_blocks, jnp.asarray(cosine), jnp.asarray(sine), *arrivals)


def merge_heads(first, second, step_count):
    pieces = []
    for h in range(QPK):
        rows = slice(h * step_count, (h + 1) * step_count)
        pieces.append(jnp.concatenate([first[rows], second[rows]], axis=0))
    return jnp.concatenate(pieces, axis=1).astype(jnp.bfloat16)


def output_same_kernel(w_ref, own_ref, second_ref, out_ref):
    me = lax.axis_index("seq")
    out_ref[...] = output_terms(w_ref, jnp.bitwise_and(me, 1), me >= 2, own_ref, second_ref)


def output_other_kernel(w_ref, above_ref, below_ref, addend_ref, out_ref):
    me = lax.axis_index("seq")
    even = jnp.bitwise_and(me, 1) == 0
    below = below_ref[...].astype(jnp.float32)
    above = above_ref[...].astype(jnp.float32)
    first = jnp.where(even, above, below)
    third = jnp.where(even, below, above)
    terms = output_terms(w_ref, 1 - jnp.bitwise_and(me, 1), me >= 2, first, third)
    out_ref[...] = (terms + addend_ref[...]).astype(out_ref.dtype)


def output_terms(w_ref, local, second, same, other):
    same = same[...].astype(jnp.float32)
    other = other[...].astype(jnp.float32)
    merged = merge_heads(
        jnp.where(second, other, same),
        jnp.where(second, same, other),
        same.shape[0] // QPK,
    )
    depth = w_ref.shape[0] // 2
    weights = w_ref[pl.ds(pl.multiple_of(local * depth, depth), depth), :]
    return jnp.dot(merged, weights, preferred_element_type=jnp.float32)


def output_half(kernel, dtype, w_out, values, *arrivals):
    rows = 2 * values.shape[0] // QPK
    vmem = pl.BlockSpec(memory_space=pltpu.VMEM)
    return pl.pallas_call(
        kernel,
        out_shape=jax.ShapeDtypeStruct((rows, w_out.shape[1]), dtype),
        in_specs=[vmem] * (2 + len(arrivals)),
        out_specs=vmem,
        compiler_params=pltpu.CompilerParams(vmem_limit_bytes=8 * 1024 * 1024),
        cost_estimate=pl.CostEstimate(flops=10**9, bytes_accessed=0, transcendentals=0),
        name="output_half",
    )(w_out, values, *arrivals)


def output_kernel(heads_local, w_ref, gathered_ref, out_ref):
    pair_count, query_rows, _ = gathered_ref.shape
    step_count = query_rows // QPK
    pairs = [gathered_ref[p].astype(jnp.float32) for p in range(pair_count)]
    requests = pair_count // heads_local
    pieces = []
    for l in range(heads_local):
        for h in range(QPK):
            rows = slice(h * step_count, (h + 1) * step_count)
            pieces.append(
                jnp.concatenate(
                    [pairs[r * heads_local + l][rows] for r in range(requests)], axis=0
                )
            )
    merged = jnp.concatenate(pieces, axis=1).astype(jnp.bfloat16)
    out_ref[...] = jnp.dot(merged, w_ref[...], preferred_element_type=jnp.float32)


def output(gathered, w_out, heads_local):
    pair_count, query_rows, _ = gathered.shape
    rows = pair_count // heads_local * (query_rows // QPK)
    vmem = pl.BlockSpec(memory_space=pltpu.VMEM)
    return pl.pallas_call(
        functools.partial(output_kernel, heads_local),
        out_shape=jax.ShapeDtypeStruct((rows, w_out.shape[1]), jnp.float32),
        in_specs=[vmem] * 2,
        out_specs=vmem,
        compiler_params=pltpu.CompilerParams(vmem_limit_bytes=8 * 1024 * 1024),
        name="output_projection",
    )(w_out, gathered)


def shards(source_cache, kept_blocks, new_hidden, norm_gain, w_query, w_keyval, w_out):
    seq_count = lax.axis_size("seq")
    head_count = lax.axis_size("head")
    requests, heads_local, source_tokens, _ = source_cache.shape
    _, step_count, width = new_hidden.shape
    pair_count = requests * heads_local

    kept_blocks = kept_blocks.transpose(0, 2, 1)
    source_blocks = source_tokens // BLK
    direct = is_direct(seq_count) and heads_local == 2
    weights = (new_hidden, norm_gain, w_query, w_keyval)
    w_out = pltpu.with_memory_space_constraint(w_out, pltpu.VMEM)
    shape = (source_blocks, heads_local, step_count, seq_count, direct)
    if direct:
        partners = range(1, seq_count)
        blocks = list(pick(kept_blocks, source_cache, direct))
        parts = list(project(blocks[0], *weights, pair_count, direct))
        blocks = [blocks[0]] + [swap(blocks[k], "seq", k) for k in partners]
        parts[1], blocks[3] = lax.optimization_barrier((parts[1], blocks[3]))
        parts = [parts[0]] + [swap(parts[k], "seq", k) for k in partners]
        (attended,) = attend(kept_blocks, blocks[::-1] + parts[::-1], *shape)
        kept_cache = place(kept_blocks, attended, blocks, source_blocks, heads_local)
        below, second, above = [shift(attended, "seq", step) for step in (1, 2, -1)]
        second, below = lax.optimization_barrier((second, below))
        terms = output_half(output_same_kernel, jnp.float32, w_out, attended, second)
        terms = output_half(output_other_kernel, jnp.bfloat16, w_out, above, below, terms)
    else:
        (blocks,) = pick(kept_blocks, source_cache, direct)
        (parts,) = project(blocks, *weights, pair_count, direct)
        arrivals = [all_to_all(parts, "seq"), all_to_all(blocks, "seq")]
        attended, kept_cache = attend(kept_blocks, arrivals, *shape)
        terms = output(all_to_all(attended, "seq"), w_out, heads_local)
    if is_direct(head_count):
        terms = terms.astype(jnp.bfloat16)
        others = [swap(terms, "head", k) for k in range(1, head_count)]
        others[0], others[1], others[2], kept_cache = lax.optimization_barrier((others[0], others[1], others[2], kept_cache))
        own, core, along, across = [t.astype(jnp.float32) for t in [terms] + others]
        summed = (own + core) + (along + across)
    else:
        summed = lax.psum(terms, "head")
    summed = summed.reshape(requests, step_count, width)
    decoded = (new_hidden.astype(jnp.float32) + summed).astype(jnp.bfloat16)
    return (kept_cache, decoded)


def solution(mesh):
    in_specs = (
        P("groups", "head", "seq", None),
        P("groups", None, None),
        P("groups", None, "seq"),
        P("seq"),
        P("seq", "head"),
        P("seq", "head", None),
        P("head", "seq"),
    )
    out_specs = (P("head", ("groups", "seq"), None, None), P("groups", None, "seq"))
    return jax.shard_map(shards, mesh=mesh, in_specs=in_specs, out_specs=out_specs, check_vma=False)
```

```python
import functools
import math

import jax
import jax.numpy as jnp
import numpy as np
from jax import lax
from jax.experimental import pallas as pl
from jax.experimental.pallas import tpu as pltpu
from jax.sharding import PartitionSpec as P

D = 8192
HD = 128
QPK = 8
BLK = 128
MOST = 2
ROPE_BASE = 500000.0
EPS = 1e-05

CONTRACT_LAST = (((1,), (1,)), ((), ()))


def rope_tables(prompt_length, step_count):
    positions = prompt_length + np.arange(2 * step_count) % step_count
    frequency = ROPE_BASE ** (-np.arange(HD // 2, dtype=np.float64) * 2.0 / HD)
    angles = positions[:, None] * frequency[None, :]
    cosine = np.concatenate([np.cos(angles)] * 2, axis=1)
    sine = np.concatenate([-np.sin(angles), np.sin(angles)], axis=1)
    return cosine.astype(np.float32), sine.astype(np.float32)


def rotate(v, cosine, sine):
    swapped = jnp.concatenate([v[..., HD // 2 :], v[..., : HD // 2]], axis=-1)
    return v * cosine + swapped * sine


def is_direct(count):
    return count == 4


def swap(outgoing, axis, offset):
    count = lax.axis_size(axis)
    return lax.ppermute(outgoing, axis, [(i, i ^ offset) for i in range(count)])


def shift(outgoing, axis, step):
    count = lax.axis_size(axis)
    return lax.ppermute(outgoing, axis, [(i, (i + step) % count) for i in range(count)])


def all_to_all(outgoing, axis):
    return lax.all_to_all(outgoing, axis, split_axis=0, concat_axis=0, tiled=True)


def picked_rows(kept_ref, cache_shape, pair, slot):
    _, heads_local, source_tokens, _ = cache_shape
    source_blocks = source_tokens // BLK
    kept_count = kept_ref.shape[1]
    first_block = lax.axis_index("seq") * source_blocks
    request = lax.div(pair, heads_local)
    local = lax.rem(pair, heads_local)
    head = lax.axis_index("head") * heads_local + local

    def count(k, total):
        return total + (kept_ref[request, k, head] < first_block).astype(jnp.int32)

    start = lax.fori_loop(0, kept_count, count, jnp.int32(0), unroll=kept_count <= 8)
    rank = jnp.minimum(start + slot, kept_count - 1)
    block = jnp.clip(kept_ref[request, rank, head] - first_block, 0, source_blocks - 1)
    return request, local, pl.ds(pl.multiple_of(block * BLK, BLK), BLK)


def pick_near_kernel(kept_hbm_ref, cache_ref, *refs):
    *outs, kept_ref, cache, kept_sem, sem = refs
    heads_local = cache.shape[1]
    me = lax.axis_index("seq")

    def pair_copy(pair):
        place = (lax.div(pair, heads_local), lax.rem(pair, heads_local))
        return pltpu.make_async_copy(cache_ref.at[place], cache.at[place], sem.at[pair])

    kept_copy = pltpu.make_async_copy(kept_hbm_ref, kept_ref, kept_sem)
    kept_copy.start()
    offsets = list(reversed(range(len(outs))))
    for offset in offsets:
        pair_copy(jnp.bitwise_xor(me, offset)).start()
    kept_copy.wait()
    places = {
        offset: [
            picked_rows(kept_ref, cache.shape, jnp.bitwise_xor(me, offset), slot)
            for slot in range(MOST)
        ]
        for offset in offsets
    }
    for offset in offsets:
        pair_copy(jnp.bitwise_xor(me, offset)).wait()
        for slot, (request, local, rows) in enumerate(places[offset]):
            out = outs[offset]
            out[slot * BLK : (slot + 1) * BLK, :] = cache[request, local, rows, :]


def pick_all_kernel(kept_hbm_ref, cache_ref, out_ref, kept_ref, sem):
    pltpu.sync_copy(kept_hbm_ref, kept_ref)

    def pair_body(pair, carry):
        for slot in range(MOST):
            request, local, rows = picked_rows(kept_ref, cache_ref.shape, pair, slot)
            pltpu.make_async_copy(
                cache_ref.at[request, local, rows],
                out_ref.at[pair, pl.ds(slot * BLK, BLK)],
                sem,
            ).start()
        return carry

    lax.fori_loop(0, out_ref.shape[0], pair_body, 0)
    pltpu.make_async_copy(out_ref, out_ref, sem).wait()


def pick(kept_blocks, source_cache, direct):
    requests, heads_local, _, row_width = source_cache.shape
    pair_count = requests * heads_local
    block = (MOST * BLK, row_width)
    kept_scratch = pltpu.SMEM(kept_blocks.shape, jnp.int32)
    if direct:
        shapes = [jax.ShapeDtypeStruct(block, jnp.bfloat16)] * pair_count
        scratch = [
            kept_scratch,
            pltpu.VMEM(source_cache.shape, jnp.bfloat16),
            pltpu.SemaphoreType.DMA,
            pltpu.SemaphoreType.DMA((pair_count,)),
        ]
    else:
        shapes = [jax.ShapeDtypeStruct((pair_count,) + block, jnp.bfloat16)]
        scratch = [kept_scratch, pltpu.SemaphoreType.DMA]
    return pl.pallas_call(
        pick_near_kernel if direct else pick_all_kernel,
        out_shape=shapes,
        in_specs=[pl.BlockSpec(memory_space=pl.ANY)] * 2,
        out_specs=[pl.BlockSpec(memory_space=pltpu.VMEM)] * len(shapes),
        scratch_shapes=scratch,
        compiler_params=pltpu.CompilerParams(vmem_limit_bytes=8 * 1024 * 1024),
        cost_estimate=pl.CostEstimate(flops=10**10, bytes_accessed=0, transcendentals=0),
        name="pick_blocks",
    )(
        pltpu.with_memory_space_constraint(kept_blocks, pltpu.HBM),
        pltpu.with_memory_space_constraint(source_cache, pltpu.HBM),
    )


def interleave(rows):
    count, width = rows.shape
    chunks = width // HD
    stacked = jnp.concatenate(
        [rows[:, c * HD : (c + 1) * HD] for c in range(chunks)], axis=0
    ).astype(jnp.bfloat16)
    source = lax.broadcasted_iota(jnp.int32, (HD, 4 * HD), 0)
    target = lax.broadcasted_iota(jnp.int32, (HD, 4 * HD), 1)
    place = jnp.where(target < 2 * HD, 2 * source, 2 * source + 1 + 2 * HD)
    spread = (place == target).astype(jnp.bfloat16)
    wide = jnp.dot(stacked, spread, preferred_element_type=jnp.float32)
    return [
        jnp.concatenate(
            [
                wide[c * count : (c + 1) * count, : 2 * HD],
                wide[c * count : (c + 1) * count, 2 * HD :],
            ],
            axis=0,
        ).astype(jnp.bfloat16)
        for c in range(chunks)
    ]


def project_kernel(direct, source_blocks, after_ref, hidden_ref, gain_ref, wq_ref, wkv_ref, *refs):
    del after_ref
    outs = refs
    requests, step_count, width = hidden_ref.shape
    heads_local = wkv_ref.shape[1]
    row_count = requests * step_count
    me = lax.axis_index("seq")
    if direct:
        kept_ref, *outs, mask_ref = refs
        request = lax.div(me, heads_local)
        head = lax.axis_index("head") * heads_local + lax.rem(me, heads_local)
        column = lax.broadcasted_iota(jnp.int32, mask_ref.shape[1:], 1)
        for offset in range(mask_ref.shape[0]):
            filled = jnp.int32(0)
            for k in range(kept_ref.shape[1]):
                source = lax.div(kept_ref[request, k, head], source_blocks)
                filled += (source == jnp.bitwise_xor(me, offset)).astype(jnp.int32)
            mask_ref[offset] = jnp.where(column < filled * BLK, 0.0, -jnp.inf)
    hidden = jnp.concatenate(
        [hidden_ref[r].astype(jnp.float32) for r in range(requests)], axis=0
    )
    square = jnp.sum(hidden * hidden, axis=1, keepdims=True)
    gain = gain_ref[...].astype(jnp.float32)
    scaled = jnp.concatenate(
        [hidden[:, c * HD : (c + 1) * HD] * gain[c : c + 1] for c in range(width // HD)], axis=1
    ).astype(jnp.bfloat16)
    query = jnp.dot(scaled, wq_ref[...], preferred_element_type=jnp.float32)
    keyval = jnp.zeros((heads_local * row_count, wkv_ref.shape[2]), jnp.float32)
    for c, spread in enumerate(interleave(scaled.astype(jnp.float32))):
        alternate = wkv_ref[c * HD : (c + 1) * HD].reshape(heads_local * HD, wkv_ref.shape[2])
        keyval += jnp.dot(spread, alternate, preferred_element_type=jnp.float32)

    def pieces_of(r, l):
        steps = slice(r * step_count, (r + 1) * step_count)
        square_rows = jnp.broadcast_to(square[steps], (step_count, HD))
        own = keyval[l * row_count + r * step_count : l * row_count + (r + 1) * step_count]
        heads = [query[steps, (l * QPK + h) * HD : (l * QPK + h + 1) * HD] for h in range(QPK)]
        return heads + [own[:, :HD], own[:, HD:], square_rows, square_rows]

    def write_pair(out_ref, pieces):
        for j, piece in enumerate(pieces):
            out_ref[j * step_count : (j + 1) * step_count, :] = piece

    for r in range(requests):
        for l in range(heads_local):
            pair = r * heads_local + l
            pieces = pieces_of(r, l)
            if not direct:
                write_pair(outs[0].at[pair], pieces)
                continue
            for offset, out_ref in enumerate(outs):
                pl.when(jnp.bitwise_xor(me, offset) == pair)(
                    functools.partial(write_pair, out_ref, pieces)
                )


def project(after, new_hidden, norm_gain, w_query, w_keyval, kept_blocks, source_blocks, direct):
    requests, step_count, width = new_hidden.shape
    pair_count = requests * w_keyval.shape[1]
    terms = ((QPK + 4) * step_count, HD)
    if direct:
        shapes = [jax.ShapeDtypeStruct(terms, jnp.float32)] * pair_count
        shapes.append(jax.ShapeDtypeStruct((pair_count, 8, MOST * BLK), jnp.float32))
    else:
        shapes = [jax.ShapeDtypeStruct((pair_count,) + terms, jnp.float32)]
    vmem = pl.BlockSpec(memory_space=pltpu.VMEM)
    weights = w_query.size + w_keyval.size
    return pl.pallas_call(
        functools.partial(project_kernel, direct, source_blocks),
        out_shape=shapes,
        in_specs=[pl.BlockSpec(memory_space=pl.ANY)]
        + [vmem] * 4
        + [pl.BlockSpec(memory_space=pltpu.SMEM)] * direct,
        out_specs=[vmem] * len(shapes),
        compiler_params=pltpu.CompilerParams(vmem_limit_bytes=8 * 1024 * 1024),
        cost_estimate=pl.CostEstimate(
            flops=2 * requests * step_count * weights,
            bytes_accessed=2 * weights,
            transcendentals=0,
        ),
        name="project",
    )(
        after,
        new_hidden,
        norm_gain.reshape(width // HD, HD),
        pltpu.with_memory_space_constraint(w_query, pltpu.VMEM),
        pltpu.with_memory_space_constraint(w_keyval, pltpu.VMEM),
        *([kept_blocks] if direct else []),
    )


def place_kernel(source_blocks, heads_local, kept_ref, after_ref, *refs):
    del after_ref
    *by_offset, cache_ref, sem = refs
    me = lax.axis_index("seq")
    request = lax.div(me, heads_local)
    head = lax.axis_index("head") * heads_local + lax.rem(me, heads_local)
    previous, slot = jnp.int32(-1), jnp.int32(0)
    for k in range(kept_ref.shape[1]):
        source = lax.div(kept_ref[request, k, head], source_blocks)
        slot = jnp.where(source == previous, jnp.minimum(slot + 1, MOST - 1), 0)
        previous = source
        rows = pl.ds(pl.multiple_of(slot * BLK, BLK), BLK)
        target = cache_ref.at[0, 0, pl.ds(k * BLK, BLK)]
        for offset, ref in enumerate(by_offset):
            pl.when(jnp.bitwise_xor(me, offset) == source)(
                pltpu.make_async_copy(ref.at[rows], target, sem).start
            )
    pltpu.make_async_copy(cache_ref, cache_ref, sem).wait()


def place(kept_blocks, after, blocks, source_blocks, heads_local):
    kept_count = kept_blocks.shape[1]
    anywhere = pl.BlockSpec(memory_space=pl.ANY)
    return pl.pallas_call(
        functools.partial(place_kernel, source_blocks, heads_local),
        out_shape=jax.ShapeDtypeStruct((1, 1, kept_count * BLK, 2 * HD), jnp.bfloat16),
        in_specs=[pl.BlockSpec(memory_space=pltpu.SMEM)] + [anywhere] * (1 + len(blocks)),
        out_specs=anywhere,
        scratch_shapes=[pltpu.SemaphoreType.DMA],
        compiler_params=pltpu.CompilerParams(vmem_limit_bytes=8 * 1024 * 1024),
        cost_estimate=pl.CostEstimate(flops=10**9, bytes_accessed=0, transcendentals=0),
        name="place",
    )(kept_blocks, after, *blocks)


def attend_kernel(direct, source_blocks, heads_local, which_ref, cos_ref, sin_ref, *refs):
    step_count = cos_ref.shape[0] // 2
    if direct:
        by_offset, parts_refs, attended_ref = refs[:4][::-1], refs[4:8][::-1], refs[8]
        total = sum(ref[...] for ref in parts_refs)
    else:
        parts_ref, blocks_ref, attended_ref, cache_ref, sem, kept = refs
        kept_count = which_ref.shape[1]
        me = lax.axis_index("seq")
        request = lax.div(me, heads_local)
        head = lax.axis_index("head") * heads_local + lax.rem(me, heads_local)

        def start_copy(k, carry):
            previous, slot = carry
            source = lax.div(which_ref[request, k, head], source_blocks)
            slot = jnp.where(source == previous, jnp.minimum(slot + 1, MOST - 1), 0)
            target = kept.at[pl.ds(pl.multiple_of(k * BLK, BLK), BLK)]
            rows = pl.ds(pl.multiple_of(slot * BLK, BLK), BLK)
            pltpu.make_async_copy(blocks_ref.at[source, rows], target, sem).start()
            return source, slot

        lax.fori_loop(0, kept_count, start_copy, (jnp.int32(-1), jnp.int32(0)))
        total = jnp.sum(parts_ref[...], axis=0)
        pltpu.make_async_copy(kept, kept, sem).wait()
        pltpu.make_async_copy(kept, cache_ref.at[0, 0], sem).start()
    query_rows = QPK * step_count
    inverse = lax.rsqrt(total[query_rows + 2 * step_count :] * (1.0 / D) + EPS)
    cosine, sine = cos_ref[...], sin_ref[...]
    query = total[:query_rows].reshape(QPK // 2, 2 * step_count, HD) * inverse[None]
    query = rotate(query, cosine[None], sine[None]).reshape(query_rows, HD).astype(jnp.bfloat16)
    keyval = total[query_rows : query_rows + 2 * step_count] * inverse
    new_key = rotate(keyval, cosine, sine).astype(jnp.bfloat16)
    new_value = jnp.concatenate([keyval[step_count:], keyval[:step_count]], axis=0)
    new_value = new_value.astype(jnp.bfloat16)
    scale = 1.0 / math.sqrt(HD)
    score = lax.dot_general(query, new_key, CONTRACT_LAST, preferred_element_type=jnp.float32)
    row = lax.broadcasted_iota(jnp.int32, score.shape, 0)
    column = lax.broadcasted_iota(jnp.int32, score.shape, 1)
    scores = [jnp.where(column <= lax.rem(row, step_count), score * scale, -jnp.inf)]
    values = [new_value]

    def add_block(block):
        score = lax.dot_general(
            query, block[:, :HD], CONTRACT_LAST, preferred_element_type=jnp.float32
        )
        scores.append(score * scale)
        values.append(block[:, HD:])

    if direct:
        for offset, ref in enumerate(by_offset):
            add_block(ref[...])
            scores[-1] += which_ref[offset, :1, :]
    else:
        add_block(kept[...])
    row_max = functools.reduce(
        jnp.maximum, [jnp.max(score, axis=1, keepdims=True) for score in scores]
    )
    denominator = jnp.zeros((query_rows, 1), jnp.float32)
    numerator = jnp.zeros((query_rows, HD), jnp.float32)
    for score, value in zip(scores, values):
        weight = jnp.exp(score - row_max)
        denominator += jnp.sum(weight, axis=1, keepdims=True)
        numerator += jnp.dot(
            weight.astype(jnp.bfloat16), value, preferred_element_type=jnp.float32
        )
    attended = (numerator / denominator).astype(jnp.bfloat16)
    if direct:
        attended_ref[...] = attended
    else:
        for i in range(attended_ref.shape[0]):
            attended_ref[i] = attended
        pltpu.make_async_copy(cache_ref, cache_ref, sem).wait()


def attend(which, arrivals, source_blocks, heads_local, step_count, seq_count, direct):
    cosine, sine = rope_tables(source_blocks * BLK * seq_count, step_count)
    shape = (QPK * step_count, HD)
    vmem = pl.BlockSpec(memory_space=pltpu.VMEM)
    if direct:
        shapes = [jax.ShapeDtypeStruct(shape, jnp.bfloat16)]
        out_specs = [vmem]
        scratch = []
    else:
        cache = (1, 1, which.shape[1] * BLK, 2 * HD)
        shapes = [
            jax.ShapeDtypeStruct((seq_count,) + shape, jnp.bfloat16),
            jax.ShapeDtypeStruct(cache, jnp.bfloat16),
        ]
        out_specs = [vmem, pl.BlockSpec(memory_space=pl.ANY)]
        scratch = [pltpu.SemaphoreType.DMA, pltpu.VMEM(cache[2:], jnp.bfloat16)]
    return pl.pallas_call(
        functools.partial(attend_kernel, direct, source_blocks, heads_local),
        out_shape=shapes,
        in_specs=[vmem if direct else pl.BlockSpec(memory_space=pltpu.SMEM)] + [vmem] * (2 + len(arrivals)),
        out_specs=out_specs,
        scratch_shapes=scratch,
        compiler_params=pltpu.CompilerParams(vmem_limit_bytes=16 * 1024 * 1024),
        cost_estimate=pl.CostEstimate(flops=10**10, bytes_accessed=0, transcendentals=0),
        name="attend",
    )(which, jnp.asarray(cosine), jnp.asarray(sine), *arrivals)


def merge_heads(first, second, step_count):
    pieces = []
    for h in range(QPK):
        rows = slice(h * step_count, (h + 1) * step_count)
        pieces.append(jnp.concatenate([first[rows], second[rows]], axis=0))
    return jnp.concatenate(pieces, axis=1).astype(jnp.bfloat16)


def output_same_kernel(w_ref, own_ref, second_ref, out_ref):
    me = lax.axis_index("seq")
    out_ref[...] = output_terms(w_ref, jnp.bitwise_and(me, 1), me >= 2, own_ref, second_ref)


def output_other_kernel(w_ref, above_ref, below_ref, addend_ref, out_ref):
    me = lax.axis_index("seq")
    even = jnp.bitwise_and(me, 1) == 0
    below = below_ref[...].astype(jnp.float32)
    above = above_ref[...].astype(jnp.float32)
    first = jnp.where(even, above, below)
    third = jnp.where(even, below, above)
    terms = output_terms(w_ref, 1 - jnp.bitwise_and(me, 1), me >= 2, first, third)
    out_ref[...] = (terms + addend_ref[...]).astype(out_ref.dtype)


def output_terms(w_ref, local, second, same, other):
    same = same[...].astype(jnp.float32)
    other = other[...].astype(jnp.float32)
    merged = merge_heads(
        jnp.where(second, other, same),
        jnp.where(second, same, other),
        same.shape[0] // QPK,
    )
    depth = w_ref.shape[0] // 2
    weights = w_ref[pl.ds(pl.multiple_of(local * depth, depth), depth), :]
    return jnp.dot(merged, weights, preferred_element_type=jnp.float32)


def output_half(kernel, dtype, w_out, values, *arrivals):
    rows = 2 * values.shape[0] // QPK
    vmem = pl.BlockSpec(memory_space=pltpu.VMEM)
    return pl.pallas_call(
        kernel,
        out_shape=jax.ShapeDtypeStruct((rows, w_out.shape[1]), dtype),
        in_specs=[vmem] * (2 + len(arrivals)),
        out_specs=vmem,
        compiler_params=pltpu.CompilerParams(vmem_limit_bytes=8 * 1024 * 1024),
        cost_estimate=pl.CostEstimate(flops=10**9, bytes_accessed=0, transcendentals=0),
        name="output_half",
    )(w_out, values, *arrivals)


def output_kernel(heads_local, w_ref, gathered_ref, out_ref):
    pair_count, query_rows, _ = gathered_ref.shape
    step_count = query_rows // QPK
    pairs = [gathered_ref[p].astype(jnp.float32) for p in range(pair_count)]
    requests = pair_count // heads_local
    pieces = []
    for l in range(heads_local):
        for h in range(QPK):
            rows = slice(h * step_count, (h + 1) * step_count)
            pieces.append(
                jnp.concatenate(
                    [pairs[r * heads_local + l][rows] for r in range(requests)], axis=0
                )
            )
    merged = jnp.concatenate(pieces, axis=1).astype(jnp.bfloat16)
    out_ref[...] = jnp.dot(merged, w_ref[...], preferred_element_type=jnp.float32)


def output(gathered, w_out, heads_local):
    pair_count, query_rows, _ = gathered.shape
    rows = pair_count // heads_local * (query_rows // QPK)
    vmem = pl.BlockSpec(memory_space=pltpu.VMEM)
    return pl.pallas_call(
        functools.partial(output_kernel, heads_local),
        out_shape=jax.ShapeDtypeStruct((rows, w_out.shape[1]), jnp.float32),
        in_specs=[vmem] * 2,
        out_specs=vmem,
        compiler_params=pltpu.CompilerParams(vmem_limit_bytes=8 * 1024 * 1024),
        name="output_projection",
    )(w_out, gathered)


def shards(source_cache, kept_blocks, new_hidden, norm_gain, w_query, w_keyval, w_out):
    seq_count = lax.axis_size("seq")
    head_count = lax.axis_size("head")
    requests, heads_local, source_tokens, _ = source_cache.shape
    _, step_count, width = new_hidden.shape
    pair_count = requests * heads_local

    kept_blocks = kept_blocks.transpose(0, 2, 1)
    source_blocks = source_tokens // BLK
    direct = is_direct(seq_count) and heads_local == 2
    weights = (new_hidden, norm_gain, w_query, w_keyval)
    w_out = pltpu.with_memory_space_constraint(w_out, pltpu.VMEM)
    shape = (source_blocks, heads_local, step_count, seq_count, direct)
    if direct:
        partners = range(1, seq_count)
        blocks = list(pick(kept_blocks, source_cache, direct))
        *parts, mask = project(blocks[0], *weights, kept_blocks, source_blocks, direct)
        blocks = [blocks[0]] + [swap(blocks[k], "seq", k) for k in partners]
        parts[1], blocks[3] = lax.optimization_barrier((parts[1], blocks[3]))
        parts = [parts[0]] + [swap(parts[k], "seq", k) for k in partners]
        (attended,) = attend(mask, blocks[::-1] + parts[::-1], *shape)
        kept_cache = place(kept_blocks, attended, blocks, source_blocks, heads_local)
        below, second, above = [shift(attended, "seq", step) for step in (1, 2, -1)]
        second, below = lax.optimization_barrier((second, below))
        terms = output_half(output_same_kernel, jnp.float32, w_out, attended, second)
        terms = output_half(output_other_kernel, jnp.bfloat16, w_out, above, below, terms)
    else:
        (blocks,) = pick(kept_blocks, source_cache, direct)
        (parts,) = project(blocks, *weights, kept_blocks, source_blocks, direct)
        arrivals = [all_to_all(parts, "seq"), all_to_all(blocks, "seq")]
        attended, kept_cache = attend(kept_blocks, arrivals, *shape)
        terms = output(all_to_all(attended, "seq"), w_out, heads_local)
    if is_direct(head_count):
        terms = terms.astype(jnp.bfloat16)
        others = [swap(terms, "head", k) for k in range(1, head_count)]
        others[0], others[1], others[2], kept_cache = lax.optimization_barrier((others[0], others[1], others[2], kept_cache))
        own, core, along, across = [t.astype(jnp.float32) for t in [terms] + others]
        summed = (own + core) + (along + across)
    else:
        summed = lax.psum(terms, "head")
    summed = summed.reshape(requests, step_count, width)
    decoded = (new_hidden.astype(jnp.float32) + summed).astype(jnp.bfloat16)
    return (kept_cache, decoded)


def solution(mesh):
    in_specs = (
        P("groups", "head", "seq", None),
        P("groups", None, None),
        P("groups", None, "seq"),
        P("seq"),
        P("seq", "head"),
        P("seq", "head", None),
        P("head", "seq"),
    )
    out_specs = (P("head", ("groups", "seq"), None, None), P("groups", None, "seq"))
    return jax.shard_map(shards, mesh=mesh, in_specs=in_specs, out_specs=out_specs, check_vma=False)
```

```python
import functools
import math

import jax
import jax.numpy as jnp
import numpy as np
from jax import lax
from jax.experimental import pallas as pl
from jax.experimental.pallas import tpu as pltpu
from jax.sharding import PartitionSpec as P

D = 8192
HD = 128
QPK = 8
BLK = 128
MOST = 2
ROPE_BASE = 500000.0
EPS = 1e-05

CONTRACT_LAST = (((1,), (1,)), ((), ()))


def rope_tables(prompt_length, step_count):
    positions = prompt_length + np.arange(2 * step_count) % step_count
    frequency = ROPE_BASE ** (-np.arange(HD // 2, dtype=np.float64) * 2.0 / HD)
    angles = positions[:, None] * frequency[None, :]
    cosine = np.concatenate([np.cos(angles)] * 2, axis=1)
    sine = np.concatenate([-np.sin(angles), np.sin(angles)], axis=1)
    return cosine.astype(np.float32), sine.astype(np.float32)


def rotate(v, cosine, sine):
    swapped = jnp.concatenate([v[..., HD // 2 :], v[..., : HD // 2]], axis=-1)
    return v * cosine + swapped * sine


def is_direct(count):
    return count == 4


def swap(outgoing, axis, offset):
    count = lax.axis_size(axis)
    return lax.ppermute(outgoing, axis, [(i, i ^ offset) for i in range(count)])


def shift(outgoing, axis, step):
    count = lax.axis_size(axis)
    return lax.ppermute(outgoing, axis, [(i, (i + step) % count) for i in range(count)])


def all_to_all(outgoing, axis):
    return lax.all_to_all(outgoing, axis, split_axis=0, concat_axis=0, tiled=True)


def picked_rows(kept_ref, cache_shape, pair, slot):
    _, heads_local, source_tokens, _ = cache_shape
    source_blocks = source_tokens // BLK
    kept_count = kept_ref.shape[1]
    first_block = lax.axis_index("seq") * source_blocks
    request = lax.div(pair, heads_local)
    local = lax.rem(pair, heads_local)
    head = lax.axis_index("head") * heads_local + local

    def count(k, total):
        return total + (kept_ref[request, k, head] < first_block).astype(jnp.int32)

    start = lax.fori_loop(0, kept_count, count, jnp.int32(0), unroll=kept_count <= 8)
    rank = jnp.minimum(start + slot, kept_count - 1)
    block = jnp.clip(kept_ref[request, rank, head] - first_block, 0, source_blocks - 1)
    return request, local, pl.ds(pl.multiple_of(block * BLK, BLK), BLK)


def pick_near_kernel(kept_hbm_ref, cache_ref, *refs):
    *outs, kept_ref, cache, kept_sem, sem = refs
    heads_local = cache.shape[1]
    me = lax.axis_index("seq")

    def pair_copy(pair):
        place = (lax.div(pair, heads_local), lax.rem(pair, heads_local))
        return pltpu.make_async_copy(cache_ref.at[place], cache.at[place], sem.at[pair])

    kept_copy = pltpu.make_async_copy(kept_hbm_ref, kept_ref, kept_sem)
    kept_copy.start()
    offsets = list(reversed(range(len(outs))))
    for offset in offsets:
        pair_copy(jnp.bitwise_xor(me, offset)).start()
    kept_copy.wait()
    places = {
        offset: [
            picked_rows(kept_ref, cache.shape, jnp.bitwise_xor(me, offset), slot)
            for slot in range(MOST)
        ]
        for offset in offsets
    }
    for offset in offsets:
        pair_copy(jnp.bitwise_xor(me, offset)).wait()
        for slot, (request, local, rows) in enumerate(places[offset]):
            out = outs[offset]
            out[slot * BLK : (slot + 1) * BLK, :] = cache[request, local, rows, :]


def pick_all_kernel(kept_hbm_ref, cache_ref, out_ref, kept_ref, sem):
    pltpu.sync_copy(kept_hbm_ref, kept_ref)

    def pair_body(pair, carry):
        for slot in range(MOST):
            request, local, rows = picked_rows(kept_ref, cache_ref.shape, pair, slot)
            pltpu.make_async_copy(
                cache_ref.at[request, local, rows],
                out_ref.at[pair, pl.ds(slot * BLK, BLK)],
                sem,
            ).start()
        return carry

    lax.fori_loop(0, out_ref.shape[0], pair_body, 0)
    pltpu.make_async_copy(out_ref, out_ref, sem).wait()


def pick(kept_blocks, source_cache, direct):
    requests, heads_local, _, row_width = source_cache.shape
    pair_count = requests * heads_local
    block = (MOST * BLK, row_width)
    kept_scratch = pltpu.SMEM(kept_blocks.shape, jnp.int32)
    if direct:
        shapes = [jax.ShapeDtypeStruct(block, jnp.bfloat16)] * pair_count
        scratch = [
            kept_scratch,
            pltpu.VMEM(source_cache.shape, jnp.bfloat16),
            pltpu.SemaphoreType.DMA,
            pltpu.SemaphoreType.DMA((pair_count,)),
        ]
    else:
        shapes = [jax.ShapeDtypeStruct((pair_count,) + block, jnp.bfloat16)]
        scratch = [kept_scratch, pltpu.SemaphoreType.DMA]
    return pl.pallas_call(
        pick_near_kernel if direct else pick_all_kernel,
        out_shape=shapes,
        in_specs=[pl.BlockSpec(memory_space=pl.ANY)] * 2,
        out_specs=[pl.BlockSpec(memory_space=pltpu.VMEM)] * len(shapes),
        scratch_shapes=scratch,
        compiler_params=pltpu.CompilerParams(vmem_limit_bytes=8 * 1024 * 1024),
        cost_estimate=pl.CostEstimate(flops=10**10, bytes_accessed=0, transcendentals=0),
        name="pick_blocks",
    )(
        pltpu.with_memory_space_constraint(kept_blocks, pltpu.HBM),
        pltpu.with_memory_space_constraint(source_cache, pltpu.HBM),
    )


def interleave(rows):
    count, width = rows.shape
    chunks = width // HD
    stacked = jnp.concatenate(
        [rows[:, c * HD : (c + 1) * HD] for c in range(chunks)], axis=0
    ).astype(jnp.bfloat16)
    source = lax.broadcasted_iota(jnp.int32, (HD, 4 * HD), 0)
    target = lax.broadcasted_iota(jnp.int32, (HD, 4 * HD), 1)
    place = jnp.where(target < 2 * HD, 2 * source, 2 * source + 1 + 2 * HD)
    spread = (place == target).astype(jnp.bfloat16)
    wide = jnp.dot(stacked, spread, preferred_element_type=jnp.float32)
    return [
        jnp.concatenate(
            [
                wide[c * count : (c + 1) * count, : 2 * HD],
                wide[c * count : (c + 1) * count, 2 * HD :],
            ],
            axis=0,
        ).astype(jnp.bfloat16)
        for c in range(chunks)
    ]


def project_kernel(direct, source_blocks, after_ref, hidden_ref, gain_ref, wq_ref, wkv_ref, *refs):
    del after_ref
    outs = refs
    if direct:
        kept_hbm_ref, *outs, mask_ref, kept_ref, sem = refs
        kept_copy = pltpu.make_async_copy(kept_hbm_ref, kept_ref, sem)
        kept_copy.start()
    requests, step_count, width = hidden_ref.shape
    heads_local = wkv_ref.shape[1]
    row_count = requests * step_count
    me = lax.axis_index("seq")
    hidden = jnp.concatenate(
        [hidden_ref[r].astype(jnp.float32) for r in range(requests)], axis=0
    )
    square = jnp.sum(hidden * hidden, axis=1, keepdims=True)
    gain = gain_ref[...].astype(jnp.float32)
    scaled = jnp.concatenate(
        [hidden[:, c * HD : (c + 1) * HD] * gain[c : c + 1] for c in range(width // HD)], axis=1
    ).astype(jnp.bfloat16)
    query = jnp.dot(scaled, wq_ref[...], preferred_element_type=jnp.float32)
    keyval = jnp.zeros((heads_local * row_count, wkv_ref.shape[2]), jnp.float32)
    for c, spread in enumerate(interleave(scaled.astype(jnp.float32))):
        alternate = wkv_ref[c * HD : (c + 1) * HD].reshape(heads_local * HD, wkv_ref.shape[2])
        keyval += jnp.dot(spread, alternate, preferred_element_type=jnp.float32)

    def pieces_of(r, l):
        steps = slice(r * step_count, (r + 1) * step_count)
        square_rows = jnp.broadcast_to(square[steps], (step_count, HD))
        own = keyval[l * row_count + r * step_count : l * row_count + (r + 1) * step_count]
        heads = [query[steps, (l * QPK + h) * HD : (l * QPK + h + 1) * HD] for h in range(QPK)]
        return heads + [own[:, :HD], own[:, HD:], square_rows, square_rows]

    def write_pair(out_ref, pieces):
        for j, piece in enumerate(pieces):
            out_ref[j * step_count : (j + 1) * step_count, :] = piece

    for r in range(requests):
        for l in range(heads_local):
            pair = r * heads_local + l
            pieces = pieces_of(r, l)
            if not direct:
                write_pair(outs[0].at[pair], pieces)
                continue
            for offset, out_ref in enumerate(outs):
                pl.when(jnp.bitwise_xor(me, offset) == pair)(
                    functools.partial(write_pair, out_ref, pieces)
                )
    if direct:
        kept_copy.wait()
        request = lax.div(me, heads_local)
        head = lax.axis_index("head") * heads_local + lax.rem(me, heads_local)
        column = lax.broadcasted_iota(jnp.int32, mask_ref.shape[1:], 1)
        for offset in range(mask_ref.shape[0]):
            filled = jnp.int32(0)
            for k in range(kept_ref.shape[1]):
                source = lax.div(kept_ref[request, k, head], source_blocks)
                filled += (source == jnp.bitwise_xor(me, offset)).astype(jnp.int32)
            mask_ref[offset] = jnp.where(column < filled * BLK, 0.0, -jnp.inf)


def project(after, new_hidden, norm_gain, w_query, w_keyval, kept_blocks, source_blocks, direct):
    requests, step_count, width = new_hidden.shape
    pair_count = requests * w_keyval.shape[1]
    terms = ((QPK + 4) * step_count, HD)
    if direct:
        shapes = [jax.ShapeDtypeStruct(terms, jnp.float32)] * pair_count
        shapes.append(jax.ShapeDtypeStruct((pair_count, 8, MOST * BLK), jnp.float32))
    else:
        shapes = [jax.ShapeDtypeStruct((pair_count,) + terms, jnp.float32)]
    vmem = pl.BlockSpec(memory_space=pltpu.VMEM)
    weights = w_query.size + w_keyval.size
    return pl.pallas_call(
        functools.partial(project_kernel, direct, source_blocks),
        out_shape=shapes,
        in_specs=[pl.BlockSpec(memory_space=pl.ANY)]
        + [vmem] * 4
        + [pl.BlockSpec(memory_space=pl.ANY)] * direct,
        out_specs=[vmem] * len(shapes),
        scratch_shapes=[pltpu.SMEM(kept_blocks.shape, jnp.int32), pltpu.SemaphoreType.DMA]
        if direct
        else [],
        compiler_params=pltpu.CompilerParams(vmem_limit_bytes=8 * 1024 * 1024),
        cost_estimate=pl.CostEstimate(
            flops=2 * requests * step_count * weights,
            bytes_accessed=2 * weights,
            transcendentals=0,
        ),
        name="project",
    )(
        after,
        new_hidden,
        norm_gain.reshape(width // HD, HD),
        pltpu.with_memory_space_constraint(w_query, pltpu.VMEM),
        pltpu.with_memory_space_constraint(w_keyval, pltpu.VMEM),
        *([pltpu.with_memory_space_constraint(kept_blocks, pltpu.HBM)] if direct else []),
    )


def place_kernel(source_blocks, heads_local, kept_ref, after_ref, *refs):
    del after_ref
    *by_offset, cache_ref, sem = refs
    me = lax.axis_index("seq")
    request = lax.div(me, heads_local)
    head = lax.axis_index("head") * heads_local + lax.rem(me, heads_local)
    previous, slot = jnp.int32(-1), jnp.int32(0)
    for k in range(kept_ref.shape[1]):
        source = lax.div(kept_ref[request, k, head], source_blocks)
        slot = jnp.where(source == previous, jnp.minimum(slot + 1, MOST - 1), 0)
        previous = source
        rows = pl.ds(pl.multiple_of(slot * BLK, BLK), BLK)
        target = cache_ref.at[0, 0, pl.ds(k * BLK, BLK)]
        for offset, ref in enumerate(by_offset):
            pl.when(jnp.bitwise_xor(me, offset) == source)(
                pltpu.make_async_copy(ref.at[rows], target, sem).start
            )
    pltpu.make_async_copy(cache_ref, cache_ref, sem).wait()


def place(kept_blocks, after, blocks, source_blocks, heads_local):
    kept_count = kept_blocks.shape[1]
    anywhere = pl.BlockSpec(memory_space=pl.ANY)
    return pl.pallas_call(
        functools.partial(place_kernel, source_blocks, heads_local),
        out_shape=jax.ShapeDtypeStruct((1, 1, kept_count * BLK, 2 * HD), jnp.bfloat16),
        in_specs=[pl.BlockSpec(memory_space=pltpu.SMEM)] + [anywhere] * (1 + len(blocks)),
        out_specs=anywhere,
        scratch_shapes=[pltpu.SemaphoreType.DMA],
        compiler_params=pltpu.CompilerParams(vmem_limit_bytes=8 * 1024 * 1024),
        cost_estimate=pl.CostEstimate(flops=10**9, bytes_accessed=0, transcendentals=0),
        name="place",
    )(kept_blocks, after, *blocks)


def attend_kernel(direct, source_blocks, heads_local, which_ref, cos_ref, sin_ref, *refs):
    step_count = cos_ref.shape[0] // 2
    if direct:
        by_offset, parts_refs, attended_ref = refs[:4][::-1], refs[4:8][::-1], refs[8]
        total = sum(ref[...] for ref in parts_refs)
    else:
        parts_ref, blocks_ref, attended_ref, cache_ref, sem, kept = refs
        kept_count = which_ref.shape[1]
        me = lax.axis_index("seq")
        request = lax.div(me, heads_local)
        head = lax.axis_index("head") * heads_local + lax.rem(me, heads_local)

        def start_copy(k, carry):
            previous, slot = carry
            source = lax.div(which_ref[request, k, head], source_blocks)
            slot = jnp.where(source == previous, jnp.minimum(slot + 1, MOST - 1), 0)
            target = kept.at[pl.ds(pl.multiple_of(k * BLK, BLK), BLK)]
            rows = pl.ds(pl.multiple_of(slot * BLK, BLK), BLK)
            pltpu.make_async_copy(blocks_ref.at[source, rows], target, sem).start()
            return source, slot

        lax.fori_loop(0, kept_count, start_copy, (jnp.int32(-1), jnp.int32(0)))
        total = jnp.sum(parts_ref[...], axis=0)
        pltpu.make_async_copy(kept, kept, sem).wait()
        pltpu.make_async_copy(kept, cache_ref.at[0, 0], sem).start()
    query_rows = QPK * step_count
    inverse = lax.rsqrt(total[query_rows + 2 * step_count :] * (1.0 / D) + EPS)
    cosine, sine = cos_ref[...], sin_ref[...]
    query = total[:query_rows].reshape(QPK // 2, 2 * step_count, HD) * inverse[None]
    query = rotate(query, cosine[None], sine[None]).reshape(query_rows, HD).astype(jnp.bfloat16)
    keyval = total[query_rows : query_rows + 2 * step_count] * inverse
    new_key = rotate(keyval, cosine, sine).astype(jnp.bfloat16)
    new_value = jnp.concatenate([keyval[step_count:], keyval[:step_count]], axis=0)
    new_value = new_value.astype(jnp.bfloat16)
    scale = 1.0 / math.sqrt(HD)
    score = lax.dot_general(query, new_key, CONTRACT_LAST, preferred_element_type=jnp.float32)
    row = lax.broadcasted_iota(jnp.int32, score.shape, 0)
    column = lax.broadcasted_iota(jnp.int32, score.shape, 1)
    scores = [jnp.where(column <= lax.rem(row, step_count), score * scale, -jnp.inf)]
    values = [new_value]

    def add_block(block):
        score = lax.dot_general(
            query, block[:, :HD], CONTRACT_LAST, preferred_element_type=jnp.float32
        )
        scores.append(score * scale)
        values.append(block[:, HD:])

    if direct:
        for offset, ref in enumerate(by_offset):
            add_block(ref[...])
            scores[-1] += which_ref[offset, :1, :]
    else:
        add_block(kept[...])
    row_max = functools.reduce(
        jnp.maximum, [jnp.max(score, axis=1, keepdims=True) for score in scores]
    )
    denominator = jnp.zeros((query_rows, 1), jnp.float32)
    numerator = jnp.zeros((query_rows, HD), jnp.float32)
    for score, value in zip(scores, values):
        weight = jnp.exp(score - row_max)
        denominator += jnp.sum(weight, axis=1, keepdims=True)
        numerator += jnp.dot(
            weight.astype(jnp.bfloat16), value, preferred_element_type=jnp.float32
        )
    attended = (numerator / denominator).astype(jnp.bfloat16)
    if direct:
        attended_ref[...] = attended
    else:
        for i in range(attended_ref.shape[0]):
            attended_ref[i] = attended
        pltpu.make_async_copy(cache_ref, cache_ref, sem).wait()


def attend(which, arrivals, source_blocks, heads_local, step_count, seq_count, direct):
    cosine, sine = rope_tables(source_blocks * BLK * seq_count, step_count)
    shape = (QPK * step_count, HD)
    vmem = pl.BlockSpec(memory_space=pltpu.VMEM)
    if direct:
        shapes = [jax.ShapeDtypeStruct(shape, jnp.bfloat16)]
        out_specs = [vmem]
        scratch = []
    else:
        cache = (1, 1, which.shape[1] * BLK, 2 * HD)
        shapes = [
            jax.ShapeDtypeStruct((seq_count,) + shape, jnp.bfloat16),
            jax.ShapeDtypeStruct(cache, jnp.bfloat16),
        ]
        out_specs = [vmem, pl.BlockSpec(memory_space=pl.ANY)]
        scratch = [pltpu.SemaphoreType.DMA, pltpu.VMEM(cache[2:], jnp.bfloat16)]
    return pl.pallas_call(
        functools.partial(attend_kernel, direct, source_blocks, heads_local),
        out_shape=shapes,
        in_specs=[vmem if direct else pl.BlockSpec(memory_space=pltpu.SMEM)] + [vmem] * (2 + len(arrivals)),
        out_specs=out_specs,
        scratch_shapes=scratch,
        compiler_params=pltpu.CompilerParams(vmem_limit_bytes=16 * 1024 * 1024),
        cost_estimate=pl.CostEstimate(flops=10**10, bytes_accessed=0, transcendentals=0),
        name="attend",
    )(which, jnp.asarray(cosine), jnp.asarray(sine), *arrivals)


def merge_heads(first, second, step_count):
    pieces = []
    for h in range(QPK):
        rows = slice(h * step_count, (h + 1) * step_count)
        pieces.append(jnp.concatenate([first[rows], second[rows]], axis=0))
    return jnp.concatenate(pieces, axis=1).astype(jnp.bfloat16)


def output_same_kernel(w_ref, own_ref, second_ref, out_ref):
    me = lax.axis_index("seq")
    out_ref[...] = output_terms(w_ref, jnp.bitwise_and(me, 1), me >= 2, own_ref, second_ref)


def output_other_kernel(w_ref, above_ref, below_ref, addend_ref, out_ref):
    me = lax.axis_index("seq")
    even = jnp.bitwise_and(me, 1) == 0
    below = below_ref[...].astype(jnp.float32)
    above = above_ref[...].astype(jnp.float32)
    first = jnp.where(even, above, below)
    third = jnp.where(even, below, above)
    terms = output_terms(w_ref, 1 - jnp.bitwise_and(me, 1), me >= 2, first, third)
    out_ref[...] = (terms + addend_ref[...]).astype(out_ref.dtype)


def output_terms(w_ref, local, second, same, other):
    same = same[...].astype(jnp.float32)
    other = other[...].astype(jnp.float32)
    merged = merge_heads(
        jnp.where(second, other, same),
        jnp.where(second, same, other),
        same.shape[0] // QPK,
    )
    depth = w_ref.shape[0] // 2
    weights = w_ref[pl.ds(pl.multiple_of(local * depth, depth), depth), :]
    return jnp.dot(merged, weights, preferred_element_type=jnp.float32)


def output_half(kernel, dtype, w_out, values, *arrivals):
    rows = 2 * values.shape[0] // QPK
    vmem = pl.BlockSpec(memory_space=pltpu.VMEM)
    return pl.pallas_call(
        kernel,
        out_shape=jax.ShapeDtypeStruct((rows, w_out.shape[1]), dtype),
        in_specs=[vmem] * (2 + len(arrivals)),
        out_specs=vmem,
        compiler_params=pltpu.CompilerParams(vmem_limit_bytes=8 * 1024 * 1024),
        cost_estimate=pl.CostEstimate(flops=10**9, bytes_accessed=0, transcendentals=0),
        name="output_half",
    )(w_out, values, *arrivals)


def output_kernel(heads_local, w_ref, gathered_ref, out_ref):
    pair_count, query_rows, _ = gathered_ref.shape
    step_count = query_rows // QPK
    pairs = [gathered_ref[p].astype(jnp.float32) for p in range(pair_count)]
    requests = pair_count // heads_local
    pieces = []
    for l in range(heads_local):
        for h in range(QPK):
            rows = slice(h * step_count, (h + 1) * step_count)
            pieces.append(
                jnp.concatenate(
                    [pairs[r * heads_local + l][rows] for r in range(requests)], axis=0
                )
            )
    merged = jnp.concatenate(pieces, axis=1).astype(jnp.bfloat16)
    out_ref[...] = jnp.dot(merged, w_ref[...], preferred_element_type=jnp.float32)


def output(gathered, w_out, heads_local):
    pair_count, query_rows, _ = gathered.shape
    rows = pair_count // heads_local * (query_rows // QPK)
    vmem = pl.BlockSpec(memory_space=pltpu.VMEM)
    return pl.pallas_call(
        functools.partial(output_kernel, heads_local),
        out_shape=jax.ShapeDtypeStruct((rows, w_out.shape[1]), jnp.float32),
        in_specs=[vmem] * 2,
        out_specs=vmem,
        compiler_params=pltpu.CompilerParams(vmem_limit_bytes=8 * 1024 * 1024),
        name="output_projection",
    )(w_out, gathered)


def shards(source_cache, kept_blocks, new_hidden, norm_gain, w_query, w_keyval, w_out):
    seq_count = lax.axis_size("seq")
    head_count = lax.axis_size("head")
    requests, heads_local, source_tokens, _ = source_cache.shape
    _, step_count, width = new_hidden.shape
    pair_count = requests * heads_local

    kept_blocks = kept_blocks.transpose(0, 2, 1)
    source_blocks = source_tokens // BLK
    direct = is_direct(seq_count) and heads_local == 2
    weights = (new_hidden, norm_gain, w_query, w_keyval)
    w_out = pltpu.with_memory_space_constraint(w_out, pltpu.VMEM)
    shape = (source_blocks, heads_local, step_count, seq_count, direct)
    if direct:
        partners = range(1, seq_count)
        blocks = list(pick(kept_blocks, source_cache, direct))
        *parts, mask = project(blocks[0], *weights, kept_blocks, source_blocks, direct)
        blocks = [blocks[0]] + [swap(blocks[k], "seq", k) for k in partners]
        parts[1], blocks[3] = lax.optimization_barrier((parts[1], blocks[3]))
        parts = [parts[0]] + [swap(parts[k], "seq", k) for k in partners]
        (attended,) = attend(mask, blocks[::-1] + parts[::-1], *shape)
        kept_cache = place(kept_blocks, attended, blocks, source_blocks, heads_local)
        below, second, above = [shift(attended, "seq", step) for step in (1, 2, -1)]
        second, below = lax.optimization_barrier((second, below))
        terms = output_half(output_same_kernel, jnp.float32, w_out, attended, second)
        terms = output_half(output_other_kernel, jnp.bfloat16, w_out, above, below, terms)
    else:
        (blocks,) = pick(kept_blocks, source_cache, direct)
        (parts,) = project(blocks, *weights, kept_blocks, source_blocks, direct)
        arrivals = [all_to_all(parts, "seq"), all_to_all(blocks, "seq")]
        attended, kept_cache = attend(kept_blocks, arrivals, *shape)
        terms = output(all_to_all(attended, "seq"), w_out, heads_local)
    if is_direct(head_count):
        terms = terms.astype(jnp.bfloat16)
        others = [swap(terms, "head", k) for k in range(1, head_count)]
        others[0], others[1], others[2], kept_cache = lax.optimization_barrier((others[0], others[1], others[2], kept_cache))
        own, core, along, across = [t.astype(jnp.float32) for t in [terms] + others]
        summed = (own + core) + (along + across)
    else:
        summed = lax.psum(terms, "head")
    summed = summed.reshape(requests, step_count, width)
    decoded = (new_hidden.astype(jnp.float32) + summed).astype(jnp.bfloat16)
    return (kept_cache, decoded)


def solution(mesh):
    in_specs = (
        P("groups", "head", "seq", None),
        P("groups", None, None),
        P("groups", None, "seq"),
        P("seq"),
        P("seq", "head"),
        P("seq", "head", None),
        P("head", "seq"),
    )
    out_specs = (P("head", ("groups", "seq"), None, None), P("groups", None, "seq"))
    return jax.shard_map(shards, mesh=mesh, in_specs=in_specs, out_specs=out_specs, check_vma=False)
```

```python
import functools
import math

import jax
import jax.numpy as jnp
import numpy as np
from jax import lax
from jax.experimental import pallas as pl
from jax.experimental.pallas import tpu as pltpu
from jax.sharding import PartitionSpec as P

D = 8192
HD = 128
QPK = 8
BLK = 128
MOST = 2
ROPE_BASE = 500000.0
EPS = 1e-05

CONTRACT_LAST = (((1,), (1,)), ((), ()))


def rope_tables(prompt_length, step_count):
    positions = prompt_length + np.arange(2 * step_count) % step_count
    frequency = ROPE_BASE ** (-np.arange(HD // 2, dtype=np.float64) * 2.0 / HD)
    angles = positions[:, None] * frequency[None, :]
    cosine = np.concatenate([np.cos(angles)] * 2, axis=1)
    sine = np.concatenate([-np.sin(angles), np.sin(angles)], axis=1)
    return cosine.astype(np.float32), sine.astype(np.float32)


def rotate(v, cosine, sine):
    swapped = jnp.concatenate([v[..., HD // 2 :], v[..., : HD // 2]], axis=-1)
    return v * cosine + swapped * sine


def is_direct(count):
    return count == 4


def swap(outgoing, axis, offset):
    count = lax.axis_size(axis)
    return lax.ppermute(outgoing, axis, [(i, i ^ offset) for i in range(count)])


def shift(outgoing, axis, step):
    count = lax.axis_size(axis)
    return lax.ppermute(outgoing, axis, [(i, (i + step) % count) for i in range(count)])


def all_to_all(outgoing, axis):
    return lax.all_to_all(outgoing, axis, split_axis=0, concat_axis=0, tiled=True)


def split_index(index, size):
    if size & (size - 1):
        return lax.div(index, size), lax.rem(index, size)
    shift = jnp.full_like(index, size.bit_length() - 1)
    return lax.shift_right_logical(index, shift), jnp.bitwise_and(index, size - 1)


def picked_rows(kept_ref, cache_shape, pair):
    _, heads_local, source_tokens, _ = cache_shape
    source_blocks = source_tokens // BLK
    kept_count = kept_ref.shape[1]
    first_block = lax.axis_index("seq") * source_blocks
    request, local = split_index(pair, heads_local)
    head = lax.axis_index("head") * heads_local + local

    def count(k, total):
        return total + (kept_ref[request, k, head] < first_block).astype(jnp.int32)

    start = lax.fori_loop(0, kept_count, count, jnp.int32(0), unroll=kept_count <= 8)
    places = []
    for slot in range(MOST):
        rank = jnp.minimum(start + slot, kept_count - 1)
        block = jnp.clip(kept_ref[request, rank, head] - first_block, 0, source_blocks - 1)
        places.append((request, local, pl.ds(pl.multiple_of(block * BLK, BLK), BLK)))
    return places


def pick_near_kernel(kept_hbm_ref, cache_ref, *refs):
    *outs, kept_ref, cache, kept_sem, sem = refs
    heads_local = cache.shape[1]
    me = lax.axis_index("seq")
    kept_copy = pltpu.make_async_copy(kept_hbm_ref, kept_ref, kept_sem)
    kept_copy.start()

    def pair_copy(pair):
        place = split_index(pair, heads_local)
        return pltpu.make_async_copy(cache_ref.at[place], cache.at[place], sem.at[pair])

    offsets = list(reversed(range(len(outs))))
    copies = {offset: pair_copy(jnp.bitwise_xor(me, offset)) for offset in offsets}
    for offset in offsets:
        copies[offset].start()
    kept_copy.wait()
    for offset in offsets:
        places = picked_rows(kept_ref, cache.shape, jnp.bitwise_xor(me, offset))
        copies[offset].wait()
        for slot, (request, local, rows) in enumerate(places):
            outs[offset][slot * BLK : (slot + 1) * BLK, :] = cache[request, local, rows, :]


def pick_all_kernel(kept_hbm_ref, cache_ref, out_ref, kept_ref, sem):
    pltpu.sync_copy(kept_hbm_ref, kept_ref)

    def pair_body(pair, carry):
        for slot, place in enumerate(picked_rows(kept_ref, cache_ref.shape, pair)):
            pltpu.make_async_copy(
                cache_ref.at[place], out_ref.at[pair, pl.ds(slot * BLK, BLK)], sem
            ).start()
        return carry

    lax.fori_loop(0, out_ref.shape[0], pair_body, 0)
    pltpu.make_async_copy(out_ref, out_ref, sem).wait()


def pick(kept_blocks, source_cache, direct):
    requests, heads_local, _, row_width = source_cache.shape
    pair_count = requests * heads_local
    block = (MOST * BLK, row_width)
    kept_scratch = pltpu.SMEM(kept_blocks.shape, jnp.int32)
    if direct:
        shapes = [jax.ShapeDtypeStruct(block, jnp.bfloat16)] * pair_count
        scratch = [
            kept_scratch,
            pltpu.VMEM(source_cache.shape, jnp.bfloat16),
            pltpu.SemaphoreType.DMA,
            pltpu.SemaphoreType.DMA((pair_count,)),
        ]
    else:
        shapes = [jax.ShapeDtypeStruct((pair_count,) + block, jnp.bfloat16)]
        scratch = [kept_scratch, pltpu.SemaphoreType.DMA]
    return pl.pallas_call(
        pick_near_kernel if direct else pick_all_kernel,
        out_shape=shapes,
        in_specs=[pl.BlockSpec(memory_space=pl.ANY)] * 2,
        out_specs=[pl.BlockSpec(memory_space=pltpu.VMEM)] * len(shapes),
        scratch_shapes=scratch,
        compiler_params=pltpu.CompilerParams(vmem_limit_bytes=8 * 1024 * 1024),
        cost_estimate=pl.CostEstimate(flops=10**10, bytes_accessed=0, transcendentals=0),
        name="pick_blocks",
    )(
        pltpu.with_memory_space_constraint(kept_blocks, pltpu.HBM),
        pltpu.with_memory_space_constraint(source_cache, pltpu.HBM),
    )


def interleave(rows):
    count, width = rows.shape
    chunks = width // HD
    stacked = jnp.concatenate(
        [rows[:, c * HD : (c + 1) * HD] for c in range(chunks)], axis=0
    ).astype(jnp.bfloat16)
    source = lax.broadcasted_iota(jnp.int32, (HD, 4 * HD), 0)
    target = lax.broadcasted_iota(jnp.int32, (HD, 4 * HD), 1)
    place = jnp.where(target < 2 * HD, 2 * source, 2 * source + 1 + 2 * HD)
    spread = (place == target).astype(jnp.bfloat16)
    wide = jnp.dot(stacked, spread, preferred_element_type=jnp.float32)
    return [
        jnp.concatenate(
            [
                wide[c * count : (c + 1) * count, : 2 * HD],
                wide[c * count : (c + 1) * count, 2 * HD :],
            ],
            axis=0,
        ).astype(jnp.bfloat16)
        for c in range(chunks)
    ]


def project_kernel(direct, source_blocks, after_ref, hidden_ref, gain_ref, wq_ref, wkv_ref, *refs):
    del after_ref
    outs = refs
    if direct:
        kept_hbm_ref, *outs, mask_ref, kept_ref, sem = refs
        kept_copy = pltpu.make_async_copy(kept_hbm_ref, kept_ref, sem)
        kept_copy.start()
    requests, step_count, width = hidden_ref.shape
    heads_local = wkv_ref.shape[1]
    row_count = requests * step_count
    me = lax.axis_index("seq")
    hidden = jnp.concatenate(
        [hidden_ref[r].astype(jnp.float32) for r in range(requests)], axis=0
    )
    square = jnp.sum(hidden * hidden, axis=1, keepdims=True)
    gain = gain_ref[...].astype(jnp.float32)
    scaled = jnp.concatenate(
        [hidden[:, c * HD : (c + 1) * HD] * gain[c : c + 1] for c in range(width // HD)], axis=1
    ).astype(jnp.bfloat16)
    query = jnp.dot(scaled, wq_ref[...], preferred_element_type=jnp.float32)
    keyval = jnp.zeros((heads_local * row_count, wkv_ref.shape[2]), jnp.float32)
    for c, spread in enumerate(interleave(scaled.astype(jnp.float32))):
        alternate = wkv_ref[c * HD : (c + 1) * HD].reshape(heads_local * HD, wkv_ref.shape[2])
        keyval += jnp.dot(spread, alternate, preferred_element_type=jnp.float32)

    def pieces_of(r, l):
        steps = slice(r * step_count, (r + 1) * step_count)
        square_rows = jnp.broadcast_to(square[steps], (step_count, HD))
        own = keyval[l * row_count + r * step_count : l * row_count + (r + 1) * step_count]
        heads = [query[steps, (l * QPK + h) * HD : (l * QPK + h + 1) * HD] for h in range(QPK)]
        return heads + [own[:, :HD], own[:, HD:], square_rows, square_rows]

    def write_pair(out_ref, pieces):
        for j, piece in enumerate(pieces):
            out_ref[j * step_count : (j + 1) * step_count, :] = piece

    for r in range(requests):
        for l in range(heads_local):
            pair = r * heads_local + l
            pieces = pieces_of(r, l)
            if not direct:
                write_pair(outs[0].at[pair], pieces)
                continue
            for offset, out_ref in enumerate(outs):
                pl.when(jnp.bitwise_xor(me, offset) == pair)(
                    functools.partial(write_pair, out_ref, pieces)
                )
    if direct:
        kept_copy.wait()
        request, local = split_index(me, heads_local)
        head = lax.axis_index("head") * heads_local + local
        kept = [kept_ref[request, k, head] for k in range(kept_ref.shape[1])]
        column = lax.broadcasted_iota(jnp.int32, mask_ref.shape[1:], 1)
        for offset in range(mask_ref.shape[0]):
            first_block = jnp.bitwise_xor(me, offset) * source_blocks
            filled = jnp.int32(0)
            for block in kept:
                here = (block >= first_block) & (block < first_block + source_blocks)
                filled += here.astype(jnp.int32)
            mask_ref[offset] = jnp.where(column < filled * BLK, 0.0, -jnp.inf)


def project(after, new_hidden, norm_gain, w_query, w_keyval, kept_blocks, source_blocks, direct):
    requests, step_count, width = new_hidden.shape
    pair_count = requests * w_keyval.shape[1]
    terms = ((QPK + 4) * step_count, HD)
    if direct:
        shapes = [jax.ShapeDtypeStruct(terms, jnp.float32)] * pair_count
        shapes.append(jax.ShapeDtypeStruct((pair_count, 8, MOST * BLK), jnp.float32))
    else:
        shapes = [jax.ShapeDtypeStruct((pair_count,) + terms, jnp.float32)]
    vmem = pl.BlockSpec(memory_space=pltpu.VMEM)
    weights = w_query.size + w_keyval.size
    return pl.pallas_call(
        functools.partial(project_kernel, direct, source_blocks),
        out_shape=shapes,
        in_specs=[pl.BlockSpec(memory_space=pl.ANY)]
        + [vmem] * 4
        + [pl.BlockSpec(memory_space=pl.ANY)] * direct,
        out_specs=[vmem] * len(shapes),
        scratch_shapes=[pltpu.SMEM(kept_blocks.shape, jnp.int32), pltpu.SemaphoreType.DMA]
        if direct
        else [],
        compiler_params=pltpu.CompilerParams(vmem_limit_bytes=8 * 1024 * 1024),
        cost_estimate=pl.CostEstimate(
            flops=2 * requests * step_count * weights,
            bytes_accessed=2 * weights,
            transcendentals=0,
        ),
        name="project",
    )(
        after,
        new_hidden,
        norm_gain.reshape(width // HD, HD),
        pltpu.with_memory_space_constraint(w_query, pltpu.VMEM),
        pltpu.with_memory_space_constraint(w_keyval, pltpu.VMEM),
        *([pltpu.with_memory_space_constraint(kept_blocks, pltpu.HBM)] if direct else []),
    )


def place_kernel(source_blocks, heads_local, kept_ref, after_ref, *refs):
    del after_ref
    *by_offset, cache_ref, sem = refs
    me = lax.axis_index("seq")
    request, local = split_index(me, heads_local)
    head = lax.axis_index("head") * heads_local + local
    previous, slot = jnp.int32(-1), jnp.int32(0)
    for k in range(kept_ref.shape[1]):
        source, _ = split_index(kept_ref[request, k, head], source_blocks)
        slot = jnp.where(source == previous, jnp.minimum(slot + 1, MOST - 1), 0)
        previous = source
        rows = pl.ds(pl.multiple_of(slot * BLK, BLK), BLK)
        target = cache_ref.at[0, 0, pl.ds(k * BLK, BLK)]
        for offset, ref in enumerate(by_offset):
            pl.when(jnp.bitwise_xor(me, offset) == source)(
                pltpu.make_async_copy(ref.at[rows], target, sem).start
            )
    pltpu.make_async_copy(cache_ref, cache_ref, sem).wait()


def place(kept_blocks, after, blocks, source_blocks, heads_local):
    kept_count = kept_blocks.shape[1]
    anywhere = pl.BlockSpec(memory_space=pl.ANY)
    return pl.pallas_call(
        functools.partial(place_kernel, source_blocks, heads_local),
        out_shape=jax.ShapeDtypeStruct((1, 1, kept_count * BLK, 2 * HD), jnp.bfloat16),
        in_specs=[pl.BlockSpec(memory_space=pltpu.SMEM)] + [anywhere] * (1 + len(blocks)),
        out_specs=anywhere,
        scratch_shapes=[pltpu.SemaphoreType.DMA],
        compiler_params=pltpu.CompilerParams(vmem_limit_bytes=8 * 1024 * 1024),
        cost_estimate=pl.CostEstimate(flops=10**9, bytes_accessed=0, transcendentals=0),
        name="place",
    )(kept_blocks, after, *blocks)


def attend_kernel(direct, source_blocks, heads_local, which_ref, cos_ref, sin_ref, *refs):
    step_count = cos_ref.shape[0] // 2
    if direct:
        by_offset, parts_refs, attended_ref = refs[:4][::-1], refs[4:8][::-1], refs[8]
        total = sum(ref[...] for ref in parts_refs)
    else:
        parts_ref, blocks_ref, attended_ref, cache_ref, sem, kept = refs
        kept_count = which_ref.shape[1]
        me = lax.axis_index("seq")
        request, local = split_index(me, heads_local)
        head = lax.axis_index("head") * heads_local + local

        def start_copy(k, carry):
            previous, slot = carry
            source, _ = split_index(which_ref[request, k, head], source_blocks)
            slot = jnp.where(source == previous, jnp.minimum(slot + 1, MOST - 1), 0)
            target = kept.at[pl.ds(pl.multiple_of(k * BLK, BLK), BLK)]
            rows = pl.ds(pl.multiple_of(slot * BLK, BLK), BLK)
            pltpu.make_async_copy(blocks_ref.at[source, rows], target, sem).start()
            return source, slot

        lax.fori_loop(0, kept_count, start_copy, (jnp.int32(-1), jnp.int32(0)))
        total = jnp.sum(parts_ref[...], axis=0)
        pltpu.make_async_copy(kept, kept, sem).wait()
        pltpu.make_async_copy(kept, cache_ref.at[0, 0], sem).start()
    query_rows = QPK * step_count
    inverse = lax.rsqrt(total[query_rows + 2 * step_count :] * (1.0 / D) + EPS)
    cosine, sine = cos_ref[...], sin_ref[...]
    query = total[:query_rows].reshape(QPK // 2, 2 * step_count, HD) * inverse[None]
    query = rotate(query, cosine[None], sine[None]).reshape(query_rows, HD).astype(jnp.bfloat16)
    keyval = total[query_rows : query_rows + 2 * step_count] * inverse
    new_key = rotate(keyval, cosine, sine).astype(jnp.bfloat16)
    new_value = jnp.concatenate([keyval[step_count:], keyval[:step_count]], axis=0)
    new_value = new_value.astype(jnp.bfloat16)
    scale = 1.0 / math.sqrt(HD)
    score = lax.dot_general(query, new_key, CONTRACT_LAST, preferred_element_type=jnp.float32)
    row = lax.broadcasted_iota(jnp.int32, score.shape, 0)
    column = lax.broadcasted_iota(jnp.int32, score.shape, 1)
    scores = [jnp.where(column <= split_index(row, step_count)[1], score * scale, -jnp.inf)]
    values = [new_value]

    def add_block(block):
        score = lax.dot_general(
            query, block[:, :HD], CONTRACT_LAST, preferred_element_type=jnp.float32
        )
        scores.append(score * scale)
        values.append(block[:, HD:])

    if direct:
        for offset, ref in enumerate(by_offset):
            add_block(ref[...])
            scores[-1] += which_ref[offset, :1, :]
    else:
        add_block(kept[...])
    row_max = functools.reduce(
        jnp.maximum, [jnp.max(score, axis=1, keepdims=True) for score in scores]
    )
    denominator = jnp.zeros((query_rows, 1), jnp.float32)
    numerator = jnp.zeros((query_rows, HD), jnp.float32)
    for score, value in zip(scores, values):
        weight = jnp.exp(score - row_max)
        denominator += jnp.sum(weight, axis=1, keepdims=True)
        numerator += jnp.dot(
            weight.astype(jnp.bfloat16), value, preferred_element_type=jnp.float32
        )
    attended = (numerator / denominator).astype(jnp.bfloat16)
    if direct:
        attended_ref[...] = attended
    else:
        for i in range(attended_ref.shape[0]):
            attended_ref[i] = attended
        pltpu.make_async_copy(cache_ref, cache_ref, sem).wait()


def attend(which, arrivals, source_blocks, heads_local, step_count, seq_count, direct):
    cosine, sine = rope_tables(source_blocks * BLK * seq_count, step_count)
    shape = (QPK * step_count, HD)
    vmem = pl.BlockSpec(memory_space=pltpu.VMEM)
    if direct:
        shapes = [jax.ShapeDtypeStruct(shape, jnp.bfloat16)]
        out_specs = [vmem]
        scratch = []
    else:
        cache = (1, 1, which.shape[1] * BLK, 2 * HD)
        shapes = [
            jax.ShapeDtypeStruct((seq_count,) + shape, jnp.bfloat16),
            jax.ShapeDtypeStruct(cache, jnp.bfloat16),
        ]
        out_specs = [vmem, pl.BlockSpec(memory_space=pl.ANY)]
        scratch = [pltpu.SemaphoreType.DMA, pltpu.VMEM(cache[2:], jnp.bfloat16)]
    return pl.pallas_call(
        functools.partial(attend_kernel, direct, source_blocks, heads_local),
        out_shape=shapes,
        in_specs=[vmem if direct else pl.BlockSpec(memory_space=pltpu.SMEM)] + [vmem] * (2 + len(arrivals)),
        out_specs=out_specs,
        scratch_shapes=scratch,
        compiler_params=pltpu.CompilerParams(vmem_limit_bytes=16 * 1024 * 1024),
        cost_estimate=pl.CostEstimate(flops=10**10, bytes_accessed=0, transcendentals=0),
        name="attend",
    )(which, jnp.asarray(cosine), jnp.asarray(sine), *arrivals)


def merge_heads(first, second, step_count):
    pieces = []
    for h in range(QPK):
        rows = slice(h * step_count, (h + 1) * step_count)
        pieces.append(jnp.concatenate([first[rows], second[rows]], axis=0))
    return jnp.concatenate(pieces, axis=1).astype(jnp.bfloat16)


def output_same_kernel(w_ref, own_ref, second_ref, out_ref):
    me = lax.axis_index("seq")
    out_ref[...] = output_terms(w_ref, jnp.bitwise_and(me, 1), me >= 2, own_ref, second_ref)


def output_other_kernel(w_ref, above_ref, below_ref, addend_ref, out_ref):
    me = lax.axis_index("seq")
    even = jnp.bitwise_and(me, 1) == 0
    below = below_ref[...].astype(jnp.float32)
    above = above_ref[...].astype(jnp.float32)
    first = jnp.where(even, above, below)
    third = jnp.where(even, below, above)
    terms = output_terms(w_ref, 1 - jnp.bitwise_and(me, 1), me >= 2, first, third)
    out_ref[...] = (terms + addend_ref[...]).astype(out_ref.dtype)


def output_terms(w_ref, local, second, same, other):
    same = same[...].astype(jnp.float32)
    other = other[...].astype(jnp.float32)
    merged = merge_heads(
        jnp.where(second, other, same),
        jnp.where(second, same, other),
        same.shape[0] // QPK,
    )
    depth = w_ref.shape[0] // 2
    weights = w_ref[pl.ds(pl.multiple_of(local * depth, depth), depth), :]
    return jnp.dot(merged, weights, preferred_element_type=jnp.float32)


def output_half(kernel, dtype, w_out, values, *arrivals):
    rows = 2 * values.shape[0] // QPK
    vmem = pl.BlockSpec(memory_space=pltpu.VMEM)
    return pl.pallas_call(
        kernel,
        out_shape=jax.ShapeDtypeStruct((rows, w_out.shape[1]), dtype),
        in_specs=[vmem] * (2 + len(arrivals)),
        out_specs=vmem,
        compiler_params=pltpu.CompilerParams(vmem_limit_bytes=8 * 1024 * 1024),
        cost_estimate=pl.CostEstimate(flops=10**9, bytes_accessed=0, transcendentals=0),
        name="output_half",
    )(w_out, values, *arrivals)


def output_kernel(heads_local, w_ref, gathered_ref, out_ref):
    pair_count, query_rows, _ = gathered_ref.shape
    step_count = query_rows // QPK
    pairs = [gathered_ref[p].astype(jnp.float32) for p in range(pair_count)]
    requests = pair_count // heads_local
    pieces = []
    for l in range(heads_local):
        for h in range(QPK):
            rows = slice(h * step_count, (h + 1) * step_count)
            pieces.append(
                jnp.concatenate(
                    [pairs[r * heads_local + l][rows] for r in range(requests)], axis=0
                )
            )
    merged = jnp.concatenate(pieces, axis=1).astype(jnp.bfloat16)
    out_ref[...] = jnp.dot(merged, w_ref[...], preferred_element_type=jnp.float32)


def output(gathered, w_out, heads_local):
    pair_count, query_rows, _ = gathered.shape
    rows = pair_count // heads_local * (query_rows // QPK)
    vmem = pl.BlockSpec(memory_space=pltpu.VMEM)
    return pl.pallas_call(
        functools.partial(output_kernel, heads_local),
        out_shape=jax.ShapeDtypeStruct((rows, w_out.shape[1]), jnp.float32),
        in_specs=[vmem] * 2,
        out_specs=vmem,
        compiler_params=pltpu.CompilerParams(vmem_limit_bytes=8 * 1024 * 1024),
        name="output_projection",
    )(w_out, gathered)


def shards(source_cache, kept_blocks, new_hidden, norm_gain, w_query, w_keyval, w_out):
    seq_count = lax.axis_size("seq")
    head_count = lax.axis_size("head")
    requests, heads_local, source_tokens, _ = source_cache.shape
    _, step_count, width = new_hidden.shape
    pair_count = requests * heads_local

    kept_blocks = kept_blocks.transpose(0, 2, 1)
    source_blocks = source_tokens // BLK
    direct = is_direct(seq_count) and heads_local == 2
    weights = (new_hidden, norm_gain, w_query, w_keyval)
    w_out = pltpu.with_memory_space_constraint(w_out, pltpu.VMEM)
    shape = (source_blocks, heads_local, step_count, seq_count, direct)
    if direct:
        partners = range(1, seq_count)
        blocks = list(pick(kept_blocks, source_cache, direct))
        *parts, mask = project(blocks[0], *weights, kept_blocks, source_blocks, direct)
        blocks = [blocks[0]] + [swap(blocks[k], "seq", k) for k in partners]
        parts[1], blocks[3] = lax.optimization_barrier((parts[1], blocks[3]))
        parts = [parts[0]] + [swap(parts[k], "seq", k) for k in partners]
        (attended,) = attend(mask, blocks[::-1] + parts[::-1], *shape)
        kept_cache = place(kept_blocks, attended, blocks, source_blocks, heads_local)
        below, second, above = [shift(attended, "seq", step) for step in (1, 2, -1)]
        second, below = lax.optimization_barrier((second, below))
        terms = output_half(output_same_kernel, jnp.float32, w_out, attended, second)
        terms = output_half(output_other_kernel, jnp.bfloat16, w_out, above, below, terms)
    else:
        (blocks,) = pick(kept_blocks, source_cache, direct)
        (parts,) = project(blocks, *weights, kept_blocks, source_blocks, direct)
        arrivals = [all_to_all(parts, "seq"), all_to_all(blocks, "seq")]
        attended, kept_cache = attend(kept_blocks, arrivals, *shape)
        terms = output(all_to_all(attended, "seq"), w_out, heads_local)
    if is_direct(head_count):
        terms = terms.astype(jnp.bfloat16)
        others = [swap(terms, "head", k) for k in range(1, head_count)]
        others[0], others[1], others[2], kept_cache = lax.optimization_barrier((others[0], others[1], others[2], kept_cache))
        own, core, along, across = [t.astype(jnp.float32) for t in [terms] + others]
        summed = (own + core) + (along + across)
    else:
        summed = lax.psum(terms, "head")
    summed = summed.reshape(requests, step_count, width)
    decoded = (new_hidden.astype(jnp.float32) + summed).astype(jnp.bfloat16)
    return (kept_cache, decoded)


def solution(mesh):
    in_specs = (
        P("groups", "head", "seq", None),
        P("groups", None, None),
        P("groups", None, "seq"),
        P("seq"),
        P("seq", "head"),
        P("seq", "head", None),
        P("head", "seq"),
    )
    out_specs = (P("head", ("groups", "seq"), None, None), P("groups", None, "seq"))
    return jax.shard_map(shards, mesh=mesh, in_specs=in_specs, out_specs=out_specs, check_vma=False)
```

```python
import functools
import math

import jax
import jax.numpy as jnp
import numpy as np
from jax import lax
from jax.experimental import pallas as pl
from jax.experimental.pallas import tpu as pltpu
from jax.sharding import PartitionSpec as P

D = 8192
HD = 128
QPK = 8
BLK = 128
MOST = 2
ROPE_BASE = 500000.0
EPS = 1e-05

CONTRACT_LAST = (((1,), (1,)), ((), ()))


def rope_tables(prompt_length, step_count):
    positions = prompt_length + np.arange(2 * step_count) % step_count
    frequency = ROPE_BASE ** (-np.arange(HD // 2, dtype=np.float64) * 2.0 / HD)
    angles = positions[:, None] * frequency[None, :]
    cosine = np.concatenate([np.cos(angles)] * 2, axis=1)
    sine = np.concatenate([-np.sin(angles), np.sin(angles)], axis=1)
    return cosine.astype(np.float32), sine.astype(np.float32)


def rotate(v, cosine, sine):
    swapped = jnp.concatenate([v[..., HD // 2 :], v[..., : HD // 2]], axis=-1)
    return v * cosine + swapped * sine


def is_direct(count):
    return count == 4


def swap(outgoing, axis, offset):
    count = lax.axis_size(axis)
    return lax.ppermute(outgoing, axis, [(i, i ^ offset) for i in range(count)])


def shift(outgoing, axis, step):
    count = lax.axis_size(axis)
    return lax.ppermute(outgoing, axis, [(i, (i + step) % count) for i in range(count)])


def all_to_all(outgoing, axis):
    return lax.all_to_all(outgoing, axis, split_axis=0, concat_axis=0, tiled=True)


def split_index(index, size):
    if size & (size - 1):
        return lax.div(index, size), lax.rem(index, size)
    shift = jnp.full_like(index, size.bit_length() - 1)
    return lax.shift_right_logical(index, shift), jnp.bitwise_and(index, size - 1)


def picked_rows(kept_ref, cache_shape, pair):
    _, heads_local, source_tokens, _ = cache_shape
    source_blocks = source_tokens // BLK
    kept_count = kept_ref.shape[1]
    first_block = lax.axis_index("seq") * source_blocks
    request, local = split_index(pair, heads_local)
    head = lax.axis_index("head") * heads_local + local

    def count(k, total):
        return total + (kept_ref[request, k, head] < first_block).astype(jnp.int32)

    start = lax.fori_loop(0, kept_count, count, jnp.int32(0), unroll=kept_count <= 8)
    places = []
    for slot in range(MOST):
        rank = jnp.minimum(start + slot, kept_count - 1)
        block = jnp.clip(kept_ref[request, rank, head] - first_block, 0, source_blocks - 1)
        places.append((request, local, pl.ds(pl.multiple_of(block * BLK, BLK), BLK)))
    return places


def pick_near_kernel(kept_hbm_ref, cache_ref, *refs):
    *outs, kept_ref, cache, kept_sem, sem = refs
    heads_local = cache.shape[1]
    me = lax.axis_index("seq")
    kept_copy = pltpu.make_async_copy(kept_hbm_ref, kept_ref, kept_sem)
    kept_copy.start()

    def pair_copy(pair):
        place = split_index(pair, heads_local)
        return pltpu.make_async_copy(cache_ref.at[place], cache.at[place], sem.at[pair])

    offsets = list(reversed(range(len(outs))))
    copies = {offset: pair_copy(jnp.bitwise_xor(me, offset)) for offset in offsets}
    for offset in offsets:
        copies[offset].start()
    kept_copy.wait()
    for offset in offsets:
        places = picked_rows(kept_ref, cache.shape, jnp.bitwise_xor(me, offset))
        copies[offset].wait()
        for slot, (request, local, rows) in enumerate(places):
            outs[offset][slot * BLK : (slot + 1) * BLK, :] = cache[request, local, rows, :]


def pick_all_kernel(kept_hbm_ref, cache_ref, out_ref, kept_ref, sem):
    pltpu.sync_copy(kept_hbm_ref, kept_ref)

    def pair_body(pair, carry):
        for slot, place in enumerate(picked_rows(kept_ref, cache_ref.shape, pair)):
            pltpu.make_async_copy(
                cache_ref.at[place], out_ref.at[pair, pl.ds(slot * BLK, BLK)], sem
            ).start()
        return carry

    lax.fori_loop(0, out_ref.shape[0], pair_body, 0)
    pltpu.make_async_copy(out_ref, out_ref, sem).wait()


def pick(kept_blocks, source_cache, direct):
    requests, heads_local, _, row_width = source_cache.shape
    pair_count = requests * heads_local
    block = (MOST * BLK, row_width)
    kept_scratch = pltpu.SMEM(kept_blocks.shape, jnp.int32)
    if direct:
        shapes = [jax.ShapeDtypeStruct(block, jnp.bfloat16)] * pair_count
        scratch = [
            kept_scratch,
            pltpu.VMEM(source_cache.shape, jnp.bfloat16),
            pltpu.SemaphoreType.DMA,
            pltpu.SemaphoreType.DMA((pair_count,)),
        ]
    else:
        shapes = [jax.ShapeDtypeStruct((pair_count,) + block, jnp.bfloat16)]
        scratch = [kept_scratch, pltpu.SemaphoreType.DMA]
    return pl.pallas_call(
        pick_near_kernel if direct else pick_all_kernel,
        out_shape=shapes,
        in_specs=[pl.BlockSpec(memory_space=pl.ANY)] * 2,
        out_specs=[pl.BlockSpec(memory_space=pltpu.VMEM)] * len(shapes),
        scratch_shapes=scratch,
        compiler_params=pltpu.CompilerParams(vmem_limit_bytes=8 * 1024 * 1024),
        cost_estimate=pl.CostEstimate(flops=10**10, bytes_accessed=0, transcendentals=0),
        name="pick_blocks",
    )(
        pltpu.with_memory_space_constraint(kept_blocks, pltpu.HBM),
        pltpu.with_memory_space_constraint(source_cache, pltpu.HBM),
    )


def interleave(rows):
    count, width = rows.shape
    chunks = width // HD
    stacked = jnp.concatenate(
        [rows[:, c * HD : (c + 1) * HD] for c in range(chunks)], axis=0
    ).astype(jnp.bfloat16)
    source = lax.broadcasted_iota(jnp.int32, (HD, 4 * HD), 0)
    target = lax.broadcasted_iota(jnp.int32, (HD, 4 * HD), 1)
    place = jnp.where(target < 2 * HD, 2 * source, 2 * source + 1 + 2 * HD)
    spread = (place == target).astype(jnp.bfloat16)
    wide = jnp.dot(stacked, spread, preferred_element_type=jnp.float32)
    return [
        jnp.concatenate(
            [
                wide[c * count : (c + 1) * count, : 2 * HD],
                wide[c * count : (c + 1) * count, 2 * HD :],
            ],
            axis=0,
        ).astype(jnp.bfloat16)
        for c in range(chunks)
    ]


def project_kernel(direct, source_blocks, after_ref, hidden_ref, gain_ref, wq_ref, wkv_ref, *refs):
    del after_ref
    outs = refs
    if direct:
        kept_ref, *outs, mask_ref = refs
    requests, step_count, width = hidden_ref.shape
    heads_local = wkv_ref.shape[1]
    row_count = requests * step_count
    me = lax.axis_index("seq")
    hidden = jnp.concatenate(
        [hidden_ref[r].astype(jnp.float32) for r in range(requests)], axis=0
    )
    square = jnp.sum(hidden * hidden, axis=1, keepdims=True)
    gain = gain_ref[...].astype(jnp.float32)
    scaled = jnp.concatenate(
        [hidden[:, c * HD : (c + 1) * HD] * gain[c : c + 1] for c in range(width // HD)], axis=1
    ).astype(jnp.bfloat16)
    query = jnp.dot(scaled, wq_ref[...], preferred_element_type=jnp.float32)
    keyval = jnp.zeros((heads_local * row_count, wkv_ref.shape[2]), jnp.float32)
    for c, spread in enumerate(interleave(scaled.astype(jnp.float32))):
        alternate = wkv_ref[c * HD : (c + 1) * HD].reshape(heads_local * HD, wkv_ref.shape[2])
        keyval += jnp.dot(spread, alternate, preferred_element_type=jnp.float32)

    def pieces_of(r, l):
        steps = slice(r * step_count, (r + 1) * step_count)
        square_rows = jnp.broadcast_to(square[steps], (step_count, HD))
        own = keyval[l * row_count + r * step_count : l * row_count + (r + 1) * step_count]
        heads = [query[steps, (l * QPK + h) * HD : (l * QPK + h + 1) * HD] for h in range(QPK)]
        return heads + [own[:, :HD], own[:, HD:], square_rows, square_rows]

    def write_pair(out_ref, pieces):
        for j, piece in enumerate(pieces):
            out_ref[j * step_count : (j + 1) * step_count, :] = piece

    for r in range(requests):
        for l in range(heads_local):
            pair = r * heads_local + l
            pieces = pieces_of(r, l)
            if not direct:
                write_pair(outs[0].at[pair], pieces)
                continue
            for offset, out_ref in enumerate(outs):
                pl.when(jnp.bitwise_xor(me, offset) == pair)(
                    functools.partial(write_pair, out_ref, pieces)
                )
    if direct:
        request, local = split_index(me, heads_local)
        head = lax.axis_index("head") * heads_local + local
        kept = jnp.where(request == 0, kept_ref[0], kept_ref[1]).astype(jnp.float32)
        lane = lax.broadcasted_iota(jnp.int32, kept.shape, 1)
        kept = jnp.sum(jnp.where(lane == head, kept, 0.0), axis=1, keepdims=True)
        column = lax.broadcasted_iota(jnp.int32, mask_ref.shape[1:], 1).astype(jnp.float32)
        for offset in range(mask_ref.shape[0]):
            first_block = (jnp.bitwise_xor(me, offset) * source_blocks).astype(jnp.float32)
            here = (kept >= first_block) & (kept < first_block + source_blocks)
            filled = jnp.sum(jnp.where(here, float(BLK), 0.0), axis=0, keepdims=True)
            mask_ref[offset] = jnp.where(column < filled, 0.0, -jnp.inf)


def project(after, new_hidden, norm_gain, w_query, w_keyval, kept_blocks, source_blocks, direct):
    requests, step_count, width = new_hidden.shape
    pair_count = requests * w_keyval.shape[1]
    terms = ((QPK + 4) * step_count, HD)
    if direct:
        shapes = [jax.ShapeDtypeStruct(terms, jnp.float32)] * pair_count
        shapes.append(jax.ShapeDtypeStruct((pair_count, 8, MOST * BLK), jnp.float32))
    else:
        shapes = [jax.ShapeDtypeStruct((pair_count,) + terms, jnp.float32)]
    vmem = pl.BlockSpec(memory_space=pltpu.VMEM)
    weights = w_query.size + w_keyval.size
    return pl.pallas_call(
        functools.partial(project_kernel, direct, source_blocks),
        out_shape=shapes,
        in_specs=[pl.BlockSpec(memory_space=pl.ANY)] + [vmem] * (4 + direct),
        out_specs=[vmem] * len(shapes),
        compiler_params=pltpu.CompilerParams(vmem_limit_bytes=8 * 1024 * 1024),
        cost_estimate=pl.CostEstimate(
            flops=2 * requests * step_count * weights,
            bytes_accessed=2 * weights,
            transcendentals=0,
        ),
        name="project",
    )(
        after,
        new_hidden,
        norm_gain.reshape(width // HD, HD),
        pltpu.with_memory_space_constraint(w_query, pltpu.VMEM),
        pltpu.with_memory_space_constraint(w_keyval, pltpu.VMEM),
        *([kept_blocks] if direct else []),
    )


def place_kernel(source_blocks, heads_local, kept_ref, after_ref, *refs):
    del after_ref
    *by_offset, cache_ref, sem = refs
    me = lax.axis_index("seq")
    request, local = split_index(me, heads_local)
    head = lax.axis_index("head") * heads_local + local
    previous, slot = jnp.int32(-1), jnp.int32(0)
    for k in range(kept_ref.shape[1]):
        source, _ = split_index(kept_ref[request, k, head], source_blocks)
        slot = jnp.where(source == previous, jnp.minimum(slot + 1, MOST - 1), 0)
        previous = source
        rows = pl.ds(pl.multiple_of(slot * BLK, BLK), BLK)
        target = cache_ref.at[0, 0, pl.ds(k * BLK, BLK)]
        for offset, ref in enumerate(by_offset):
            pl.when(jnp.bitwise_xor(me, offset) == source)(
                pltpu.make_async_copy(ref.at[rows], target, sem).start
            )
    pltpu.make_async_copy(cache_ref, cache_ref, sem).wait()


def place(kept_blocks, after, blocks, source_blocks, heads_local):
    kept_count = kept_blocks.shape[1]
    anywhere = pl.BlockSpec(memory_space=pl.ANY)
    return pl.pallas_call(
        functools.partial(place_kernel, source_blocks, heads_local),
        out_shape=jax.ShapeDtypeStruct((1, 1, kept_count * BLK, 2 * HD), jnp.bfloat16),
        in_specs=[pl.BlockSpec(memory_space=pltpu.SMEM)] + [anywhere] * (1 + len(blocks)),
        out_specs=anywhere,
        scratch_shapes=[pltpu.SemaphoreType.DMA],
        compiler_params=pltpu.CompilerParams(vmem_limit_bytes=8 * 1024 * 1024),
        cost_estimate=pl.CostEstimate(flops=10**9, bytes_accessed=0, transcendentals=0),
        name="place",
    )(kept_blocks, after, *blocks)


def attend_kernel(direct, source_blocks, heads_local, which_ref, cos_ref, sin_ref, *refs):
    step_count = cos_ref.shape[0] // 2
    if direct:
        by_offset, parts_refs, attended_ref = refs[:4][::-1], refs[4:8][::-1], refs[8]
        total = sum(ref[...] for ref in parts_refs)
    else:
        parts_ref, blocks_ref, attended_ref, cache_ref, sem, kept = refs
        kept_count = which_ref.shape[1]
        me = lax.axis_index("seq")
        request, local = split_index(me, heads_local)
        head = lax.axis_index("head") * heads_local + local

        def start_copy(k, carry):
            previous, slot = carry
            source, _ = split_index(which_ref[request, k, head], source_blocks)
            slot = jnp.where(source == previous, jnp.minimum(slot + 1, MOST - 1), 0)
            target = kept.at[pl.ds(pl.multiple_of(k * BLK, BLK), BLK)]
            rows = pl.ds(pl.multiple_of(slot * BLK, BLK), BLK)
            pltpu.make_async_copy(blocks_ref.at[source, rows], target, sem).start()
            return source, slot

        lax.fori_loop(0, kept_count, start_copy, (jnp.int32(-1), jnp.int32(0)))
        total = jnp.sum(parts_ref[...], axis=0)
        pltpu.make_async_copy(kept, kept, sem).wait()
        pltpu.make_async_copy(kept, cache_ref.at[0, 0], sem).start()
    query_rows = QPK * step_count
    inverse = lax.rsqrt(total[query_rows + 2 * step_count :] * (1.0 / D) + EPS)
    cosine, sine = cos_ref[...], sin_ref[...]
    query = total[:query_rows].reshape(QPK // 2, 2 * step_count, HD) * inverse[None]
    query = rotate(query, cosine[None], sine[None]).reshape(query_rows, HD).astype(jnp.bfloat16)
    keyval = total[query_rows : query_rows + 2 * step_count] * inverse
    new_key = rotate(keyval, cosine, sine).astype(jnp.bfloat16)
    new_value = jnp.concatenate([keyval[step_count:], keyval[:step_count]], axis=0)
    new_value = new_value.astype(jnp.bfloat16)
    scale = 1.0 / math.sqrt(HD)
    score = lax.dot_general(query, new_key, CONTRACT_LAST, preferred_element_type=jnp.float32)
    row = lax.broadcasted_iota(jnp.int32, score.shape, 0)
    column = lax.broadcasted_iota(jnp.int32, score.shape, 1)
    scores = [jnp.where(column <= split_index(row, step_count)[1], score * scale, -jnp.inf)]
    values = [new_value]

    def add_block(block):
        score = lax.dot_general(
            query, block[:, :HD], CONTRACT_LAST, preferred_element_type=jnp.float32
        )
        scores.append(score * scale)
        values.append(block[:, HD:])

    if direct:
        for offset, ref in enumerate(by_offset):
            add_block(ref[...])
            scores[-1] += which_ref[offset, :1, :]
    else:
        add_block(kept[...])
    row_max = functools.reduce(
        jnp.maximum, [jnp.max(score, axis=1, keepdims=True) for score in scores]
    )
    denominator = jnp.zeros((query_rows, 1), jnp.float32)
    numerator = jnp.zeros((query_rows, HD), jnp.float32)
    for score, value in zip(scores, values):
        weight = jnp.exp(score - row_max)
        denominator += jnp.sum(weight, axis=1, keepdims=True)
        numerator += jnp.dot(
            weight.astype(jnp.bfloat16), value, preferred_element_type=jnp.float32
        )
    attended = (numerator / denominator).astype(jnp.bfloat16)
    if direct:
        attended_ref[...] = attended
    else:
        for i in range(attended_ref.shape[0]):
            attended_ref[i] = attended
        pltpu.make_async_copy(cache_ref, cache_ref, sem).wait()


def attend(which, arrivals, source_blocks, heads_local, step_count, seq_count, direct):
    cosine, sine = rope_tables(source_blocks * BLK * seq_count, step_count)
    shape = (QPK * step_count, HD)
    vmem = pl.BlockSpec(memory_space=pltpu.VMEM)
    if direct:
        shapes = [jax.ShapeDtypeStruct(shape, jnp.bfloat16)]
        out_specs = [vmem]
        scratch = []
    else:
        cache = (1, 1, which.shape[1] * BLK, 2 * HD)
        shapes = [
            jax.ShapeDtypeStruct((seq_count,) + shape, jnp.bfloat16),
            jax.ShapeDtypeStruct(cache, jnp.bfloat16),
        ]
        out_specs = [vmem, pl.BlockSpec(memory_space=pl.ANY)]
        scratch = [pltpu.SemaphoreType.DMA, pltpu.VMEM(cache[2:], jnp.bfloat16)]
    return pl.pallas_call(
        functools.partial(attend_kernel, direct, source_blocks, heads_local),
        out_shape=shapes,
        in_specs=[vmem if direct else pl.BlockSpec(memory_space=pltpu.SMEM)] + [vmem] * (2 + len(arrivals)),
        out_specs=out_specs,
        scratch_shapes=scratch,
        compiler_params=pltpu.CompilerParams(vmem_limit_bytes=16 * 1024 * 1024),
        cost_estimate=pl.CostEstimate(flops=10**10, bytes_accessed=0, transcendentals=0),
        name="attend",
    )(which, jnp.asarray(cosine), jnp.asarray(sine), *arrivals)


def merge_heads(first, second, step_count):
    pieces = []
    for h in range(QPK):
        rows = slice(h * step_count, (h + 1) * step_count)
        pieces.append(jnp.concatenate([first[rows], second[rows]], axis=0))
    return jnp.concatenate(pieces, axis=1).astype(jnp.bfloat16)


def output_same_kernel(w_ref, own_ref, second_ref, out_ref):
    me = lax.axis_index("seq")
    out_ref[...] = output_terms(w_ref, jnp.bitwise_and(me, 1), me >= 2, own_ref, second_ref)


def output_other_kernel(w_ref, above_ref, below_ref, addend_ref, out_ref):
    me = lax.axis_index("seq")
    even = jnp.bitwise_and(me, 1) == 0
    below = below_ref[...].astype(jnp.float32)
    above = above_ref[...].astype(jnp.float32)
    first = jnp.where(even, above, below)
    third = jnp.where(even, below, above)
    terms = output_terms(w_ref, 1 - jnp.bitwise_and(me, 1), me >= 2, first, third)
    out_ref[...] = (terms + addend_ref[...]).astype(out_ref.dtype)


def output_terms(w_ref, local, second, same, other):
    same = same[...].astype(jnp.float32)
    other = other[...].astype(jnp.float32)
    merged = merge_heads(
        jnp.where(second, other, same),
        jnp.where(second, same, other),
        same.shape[0] // QPK,
    )
    depth = w_ref.shape[0] // 2
    weights = w_ref[pl.ds(pl.multiple_of(local * depth, depth), depth), :]
    return jnp.dot(merged, weights, preferred_element_type=jnp.float32)


def output_half(kernel, dtype, w_out, values, *arrivals):
    rows = 2 * values.shape[0] // QPK
    vmem = pl.BlockSpec(memory_space=pltpu.VMEM)
    return pl.pallas_call(
        kernel,
        out_shape=jax.ShapeDtypeStruct((rows, w_out.shape[1]), dtype),
        in_specs=[vmem] * (2 + len(arrivals)),
        out_specs=vmem,
        compiler_params=pltpu.CompilerParams(vmem_limit_bytes=8 * 1024 * 1024),
        cost_estimate=pl.CostEstimate(flops=10**9, bytes_accessed=0, transcendentals=0),
        name="output_half",
    )(w_out, values, *arrivals)


def output_kernel(heads_local, w_ref, gathered_ref, out_ref):
    pair_count, query_rows, _ = gathered_ref.shape
    step_count = query_rows // QPK
    pairs = [gathered_ref[p].astype(jnp.float32) for p in range(pair_count)]
    requests = pair_count // heads_local
    pieces = []
    for l in range(heads_local):
        for h in range(QPK):
            rows = slice(h * step_count, (h + 1) * step_count)
            pieces.append(
                jnp.concatenate(
                    [pairs[r * heads_local + l][rows] for r in range(requests)], axis=0
                )
            )
    merged = jnp.concatenate(pieces, axis=1).astype(jnp.bfloat16)
    out_ref[...] = jnp.dot(merged, w_ref[...], preferred_element_type=jnp.float32)


def output(gathered, w_out, heads_local):
    pair_count, query_rows, _ = gathered.shape
    rows = pair_count // heads_local * (query_rows // QPK)
    vmem = pl.BlockSpec(memory_space=pltpu.VMEM)
    return pl.pallas_call(
        functools.partial(output_kernel, heads_local),
        out_shape=jax.ShapeDtypeStruct((rows, w_out.shape[1]), jnp.float32),
        in_specs=[vmem] * 2,
        out_specs=vmem,
        compiler_params=pltpu.CompilerParams(vmem_limit_bytes=8 * 1024 * 1024),
        name="output_projection",
    )(w_out, gathered)


def shards(source_cache, kept_blocks, new_hidden, norm_gain, w_query, w_keyval, w_out):
    seq_count = lax.axis_size("seq")
    head_count = lax.axis_size("head")
    requests, heads_local, source_tokens, _ = source_cache.shape
    _, step_count, width = new_hidden.shape
    pair_count = requests * heads_local

    kept_blocks = kept_blocks.transpose(0, 2, 1)
    source_blocks = source_tokens // BLK
    direct = is_direct(seq_count) and heads_local == 2 and requests == 2
    weights = (new_hidden, norm_gain, w_query, w_keyval)
    w_out = pltpu.with_memory_space_constraint(w_out, pltpu.VMEM)
    shape = (source_blocks, heads_local, step_count, seq_count, direct)
    if direct:
        partners = range(1, seq_count)
        blocks = list(pick(kept_blocks, source_cache, direct))
        *parts, mask = project(blocks[0], *weights, kept_blocks, source_blocks, direct)
        blocks = [blocks[0]] + [swap(blocks[k], "seq", k) for k in partners]
        parts[1], blocks[3] = lax.optimization_barrier((parts[1], blocks[3]))
        parts = [parts[0]] + [swap(parts[k], "seq", k) for k in partners]
        (attended,) = attend(mask, blocks[::-1] + parts[::-1], *shape)
        kept_cache = place(kept_blocks, attended, blocks, source_blocks, heads_local)
        below, second, above = [shift(attended, "seq", step) for step in (1, 2, -1)]
        second, below = lax.optimization_barrier((second, below))
        terms = output_half(output_same_kernel, jnp.float32, w_out, attended, second)
        terms = output_half(output_other_kernel, jnp.bfloat16, w_out, above, below, terms)
    else:
        (blocks,) = pick(kept_blocks, source_cache, direct)
        (parts,) = project(blocks, *weights, kept_blocks, source_blocks, direct)
        arrivals = [all_to_all(parts, "seq"), all_to_all(blocks, "seq")]
        attended, kept_cache = attend(kept_blocks, arrivals, *shape)
        terms = output(all_to_all(attended, "seq"), w_out, heads_local)
    if is_direct(head_count):
        terms = terms.astype(jnp.bfloat16)
        others = [swap(terms, "head", k) for k in range(1, head_count)]
        others[0], others[1], others[2], kept_cache = lax.optimization_barrier((others[0], others[1], others[2], kept_cache))
        own, core, along, across = [t.astype(jnp.float32) for t in [terms] + others]
        summed = (own + core) + (along + across)
    else:
        summed = lax.psum(terms, "head")
    summed = summed.reshape(requests, step_count, width)
    decoded = (new_hidden.astype(jnp.float32) + summed).astype(jnp.bfloat16)
    return (kept_cache, decoded)


def solution(mesh):
    in_specs = (
        P("groups", "head", "seq", None),
        P("groups", None, None),
        P("groups", None, "seq"),
        P("seq"),
        P("seq", "head"),
        P("seq", "head", None),
        P("head", "seq"),
    )
    out_specs = (P("head", ("groups", "seq"), None, None), P("groups", None, "seq"))
    return jax.shard_map(shards, mesh=mesh, in_specs=in_specs, out_specs=out_specs, check_vma=False)
```

```python
import functools
import math

import jax
import jax.numpy as jnp
import numpy as np
from jax import lax
from jax.experimental import pallas as pl
from jax.experimental.pallas import tpu as pltpu
from jax.sharding import PartitionSpec as P

D = 8192
HD = 128
QPK = 8
BLK = 128
MOST = 2
ROPE_BASE = 500000.0
EPS = 1e-05

CONTRACT_LAST = (((1,), (1,)), ((), ()))


def rope_tables(prompt_length, step_count):
    positions = prompt_length + np.arange(2 * step_count) % step_count
    frequency = ROPE_BASE ** (-np.arange(HD // 2, dtype=np.float64) * 2.0 / HD)
    angles = positions[:, None] * frequency[None, :]
    cosine = np.concatenate([np.cos(angles)] * 2, axis=1)
    sine = np.concatenate([-np.sin(angles), np.sin(angles)], axis=1)
    return cosine.astype(np.float32), sine.astype(np.float32)


def rotate(v, cosine, sine):
    swapped = jnp.concatenate([v[..., HD // 2 :], v[..., : HD // 2]], axis=-1)
    return v * cosine + swapped * sine


def is_direct(count):
    return count == 4


def swap(outgoing, axis, offset):
    count = lax.axis_size(axis)
    return lax.ppermute(outgoing, axis, [(i, i ^ offset) for i in range(count)])


def shift(outgoing, axis, step):
    count = lax.axis_size(axis)
    return lax.ppermute(outgoing, axis, [(i, (i + step) % count) for i in range(count)])


def all_to_all(outgoing, axis):
    return lax.all_to_all(outgoing, axis, split_axis=0, concat_axis=0, tiled=True)


def split_index(index, size):
    if size & (size - 1):
        return lax.div(index, size), lax.rem(index, size)
    shift = jnp.full_like(index, size.bit_length() - 1)
    return lax.shift_right_logical(index, shift), jnp.bitwise_and(index, size - 1)


def picked_rows(kept_ref, cache_shape, pair):
    _, heads_local, source_tokens, _ = cache_shape
    source_blocks = source_tokens // BLK
    kept_count = kept_ref.shape[1]
    first_block = lax.axis_index("seq") * source_blocks
    request, local = split_index(pair, heads_local)
    head = lax.axis_index("head") * heads_local + local

    def count(k, total):
        return total + (kept_ref[request, k, head] < first_block).astype(jnp.int32)

    start = lax.fori_loop(0, kept_count, count, jnp.int32(0), unroll=kept_count <= 8)
    places = []
    for slot in range(MOST):
        rank = jnp.minimum(start + slot, kept_count - 1)
        block = jnp.clip(kept_ref[request, rank, head] - first_block, 0, source_blocks - 1)
        places.append((request, local, pl.ds(pl.multiple_of(block * BLK, BLK), BLK)))
    return places


def pick_near_kernel(kept_hbm_ref, cache_ref, *refs):
    *outs, kept_ref, cache, kept_sem, sem = refs
    heads_local, source_tokens = cache.shape[1:3]
    source_blocks = source_tokens // BLK
    me = lax.axis_index("seq")
    first_head = lax.axis_index("head") * heads_local
    kept_copy = pltpu.make_async_copy(kept_hbm_ref, kept_ref, kept_sem)
    kept_copy.start()

    def pair_copy(pair):
        place = split_index(pair, heads_local)
        return pltpu.make_async_copy(cache_ref.at[place], cache.at[place], sem.at[pair])

    offsets = list(reversed(range(len(outs))))
    copies = {offset: pair_copy(jnp.bitwise_xor(me, offset)) for offset in offsets}
    for offset in offsets:
        copies[offset].start()
    kept_copy.wait()
    past = float(2**30)
    first_block = me * source_blocks
    by_request = [kept_ref[r].astype(jnp.float32) for r in range(kept_ref.shape[0])]
    lane = lax.broadcasted_iota(jnp.int32, by_request[0].shape, 1)
    places = {}
    for offset in offsets:
        request, local = split_index(jnp.bitwise_xor(me, offset), heads_local)
        row = jnp.where(request == 0, by_request[0], by_request[1])
        row = jnp.where(lane == first_head + local, row, past)
        least = first_block.astype(jnp.float32)
        places[offset] = []
        for _ in range(MOST):
            found = jnp.min(jnp.where(row >= least, row, past))
            least = found + 1.0
            block = jnp.clip(found.astype(jnp.int32) - first_block, 0, source_blocks - 1)
            rows = pl.ds(pl.multiple_of(block * BLK, BLK), BLK)
            places[offset].append((request, local, rows))
    for offset in offsets:
        copies[offset].wait()
        for slot, (request, local, rows) in enumerate(places[offset]):
            outs[offset][slot * BLK : (slot + 1) * BLK, :] = cache[request, local, rows, :]


def pick_all_kernel(kept_hbm_ref, cache_ref, out_ref, kept_ref, sem):
    pltpu.sync_copy(kept_hbm_ref, kept_ref)

    def pair_body(pair, carry):
        for slot, place in enumerate(picked_rows(kept_ref, cache_ref.shape, pair)):
            pltpu.make_async_copy(
                cache_ref.at[place], out_ref.at[pair, pl.ds(slot * BLK, BLK)], sem
            ).start()
        return carry

    lax.fori_loop(0, out_ref.shape[0], pair_body, 0)
    pltpu.make_async_copy(out_ref, out_ref, sem).wait()


def pick(kept_blocks, source_cache, direct):
    requests, heads_local, _, row_width = source_cache.shape
    pair_count = requests * heads_local
    block = (MOST * BLK, row_width)
    if direct:
        shapes = [jax.ShapeDtypeStruct(block, jnp.bfloat16)] * pair_count
        scratch = [
            pltpu.VMEM(kept_blocks.shape, jnp.int32),
            pltpu.VMEM(source_cache.shape, jnp.bfloat16),
            pltpu.SemaphoreType.DMA,
            pltpu.SemaphoreType.DMA((pair_count,)),
        ]
    else:
        shapes = [jax.ShapeDtypeStruct((pair_count,) + block, jnp.bfloat16)]
        scratch = [pltpu.SMEM(kept_blocks.shape, jnp.int32), pltpu.SemaphoreType.DMA]
    return pl.pallas_call(
        pick_near_kernel if direct else pick_all_kernel,
        out_shape=shapes,
        in_specs=[pl.BlockSpec(memory_space=pl.ANY)] * 2,
        out_specs=[pl.BlockSpec(memory_space=pltpu.VMEM)] * len(shapes),
        scratch_shapes=scratch,
        compiler_params=pltpu.CompilerParams(vmem_limit_bytes=8 * 1024 * 1024),
        cost_estimate=pl.CostEstimate(flops=10**10, bytes_accessed=0, transcendentals=0),
        name="pick_blocks",
    )(
        pltpu.with_memory_space_constraint(kept_blocks, pltpu.HBM),
        pltpu.with_memory_space_constraint(source_cache, pltpu.HBM),
    )


def interleave(rows):
    count, width = rows.shape
    chunks = width // HD
    stacked = jnp.concatenate(
        [rows[:, c * HD : (c + 1) * HD] for c in range(chunks)], axis=0
    ).astype(jnp.bfloat16)
    source = lax.broadcasted_iota(jnp.int32, (HD, 4 * HD), 0)
    target = lax.broadcasted_iota(jnp.int32, (HD, 4 * HD), 1)
    place = jnp.where(target < 2 * HD, 2 * source, 2 * source + 1 + 2 * HD)
    spread = (place == target).astype(jnp.bfloat16)
    wide = jnp.dot(stacked, spread, preferred_element_type=jnp.float32)
    return [
        jnp.concatenate(
            [
                wide[c * count : (c + 1) * count, : 2 * HD],
                wide[c * count : (c + 1) * count, 2 * HD :],
            ],
            axis=0,
        ).astype(jnp.bfloat16)
        for c in range(chunks)
    ]


def project_kernel(direct, source_blocks, after_ref, hidden_ref, gain_ref, wq_ref, wkv_ref, *refs):
    del after_ref
    outs = refs
    if direct:
        kept_ref, *outs, mask_ref = refs
    requests, step_count, width = hidden_ref.shape
    heads_local = wkv_ref.shape[1]
    row_count = requests * step_count
    me = lax.axis_index("seq")
    hidden = jnp.concatenate(
        [hidden_ref[r].astype(jnp.float32) for r in range(requests)], axis=0
    )
    square = jnp.sum(hidden * hidden, axis=1, keepdims=True)
    gain = gain_ref[...].astype(jnp.float32)
    scaled = jnp.concatenate(
        [hidden[:, c * HD : (c + 1) * HD] * gain[c : c + 1] for c in range(width // HD)], axis=1
    ).astype(jnp.bfloat16)
    query = jnp.dot(scaled, wq_ref[...], preferred_element_type=jnp.float32)
    keyval = jnp.zeros((heads_local * row_count, wkv_ref.shape[2]), jnp.float32)
    for c, spread in enumerate(interleave(scaled.astype(jnp.float32))):
        alternate = wkv_ref[c * HD : (c + 1) * HD].reshape(heads_local * HD, wkv_ref.shape[2])
        keyval += jnp.dot(spread, alternate, preferred_element_type=jnp.float32)

    def pieces_of(r, l):
        steps = slice(r * step_count, (r + 1) * step_count)
        square_rows = jnp.broadcast_to(square[steps], (step_count, HD))
        own = keyval[l * row_count + r * step_count : l * row_count + (r + 1) * step_count]
        heads = [query[steps, (l * QPK + h) * HD : (l * QPK + h + 1) * HD] for h in range(QPK)]
        return heads + [own[:, :HD], own[:, HD:], square_rows, square_rows]

    def write_pair(out_ref, pieces):
        for j, piece in enumerate(pieces):
            out_ref[j * step_count : (j + 1) * step_count, :] = piece

    for r in range(requests):
        for l in range(heads_local):
            pair = r * heads_local + l
            pieces = pieces_of(r, l)
            if not direct:
                write_pair(outs[0].at[pair], pieces)
                continue
            for offset, out_ref in enumerate(outs):
                pl.when(jnp.bitwise_xor(me, offset) == pair)(
                    functools.partial(write_pair, out_ref, pieces)
                )
    if direct:
        request, local = split_index(me, heads_local)
        head = lax.axis_index("head") * heads_local + local
        kept = jnp.where(request == 0, kept_ref[0], kept_ref[1]).astype(jnp.float32)
        lane = lax.broadcasted_iota(jnp.int32, kept.shape, 1)
        kept = jnp.sum(jnp.where(lane == head, kept, 0.0), axis=1, keepdims=True)
        column = lax.broadcasted_iota(jnp.int32, mask_ref.shape[1:], 1).astype(jnp.float32)
        for offset in range(mask_ref.shape[0]):
            first_block = (jnp.bitwise_xor(me, offset) * source_blocks).astype(jnp.float32)
            here = (kept >= first_block) & (kept < first_block + source_blocks)
            filled = jnp.sum(jnp.where(here, float(BLK), 0.0), axis=0, keepdims=True)
            mask_ref[offset] = jnp.where(column < filled, 0.0, -jnp.inf)


def project(after, new_hidden, norm_gain, w_query, w_keyval, kept_blocks, source_blocks, direct):
    requests, step_count, width = new_hidden.shape
    pair_count = requests * w_keyval.shape[1]
    terms = ((QPK + 4) * step_count, HD)
    if direct:
        shapes = [jax.ShapeDtypeStruct(terms, jnp.float32)] * pair_count
        shapes.append(jax.ShapeDtypeStruct((pair_count, 8, MOST * BLK), jnp.float32))
    else:
        shapes = [jax.ShapeDtypeStruct((pair_count,) + terms, jnp.float32)]
    vmem = pl.BlockSpec(memory_space=pltpu.VMEM)
    weights = w_query.size + w_keyval.size
    return pl.pallas_call(
        functools.partial(project_kernel, direct, source_blocks),
        out_shape=shapes,
        in_specs=[pl.BlockSpec(memory_space=pl.ANY)] + [vmem] * (4 + direct),
        out_specs=[vmem] * len(shapes),
        compiler_params=pltpu.CompilerParams(vmem_limit_bytes=8 * 1024 * 1024),
        cost_estimate=pl.CostEstimate(
            flops=2 * requests * step_count * weights,
            bytes_accessed=2 * weights,
            transcendentals=0,
        ),
        name="project",
    )(
        after,
        new_hidden,
        norm_gain.reshape(width // HD, HD),
        pltpu.with_memory_space_constraint(w_query, pltpu.VMEM),
        pltpu.with_memory_space_constraint(w_keyval, pltpu.VMEM),
        *([kept_blocks] if direct else []),
    )


def place_kernel(source_blocks, heads_local, kept_ref, after_ref, *refs):
    del after_ref
    *by_offset, cache_ref, sem = refs
    me = lax.axis_index("seq")
    request, local = split_index(me, heads_local)
    head = lax.axis_index("head") * heads_local + local
    previous, slot = jnp.int32(-1), jnp.int32(0)
    for k in range(kept_ref.shape[1]):
        source, _ = split_index(kept_ref[request, k, head], source_blocks)
        slot = jnp.where(source == previous, jnp.minimum(slot + 1, MOST - 1), 0)
        previous = source
        rows = pl.ds(pl.multiple_of(slot * BLK, BLK), BLK)
        target = cache_ref.at[0, 0, pl.ds(k * BLK, BLK)]
        for offset, ref in enumerate(by_offset):
            pl.when(jnp.bitwise_xor(me, offset) == source)(
                pltpu.make_async_copy(ref.at[rows], target, sem).start
            )
    pltpu.make_async_copy(cache_ref, cache_ref, sem).wait()


def place(kept_blocks, after, blocks, source_blocks, heads_local):
    kept_count = kept_blocks.shape[1]
    anywhere = pl.BlockSpec(memory_space=pl.ANY)
    return pl.pallas_call(
        functools.partial(place_kernel, source_blocks, heads_local),
        out_shape=jax.ShapeDtypeStruct((1, 1, kept_count * BLK, 2 * HD), jnp.bfloat16),
        in_specs=[pl.BlockSpec(memory_space=pltpu.SMEM)] + [anywhere] * (1 + len(blocks)),
        out_specs=anywhere,
        scratch_shapes=[pltpu.SemaphoreType.DMA],
        compiler_params=pltpu.CompilerParams(vmem_limit_bytes=8 * 1024 * 1024),
        cost_estimate=pl.CostEstimate(flops=10**9, bytes_accessed=0, transcendentals=0),
        name="place",
    )(kept_blocks, after, *blocks)


def attend_kernel(direct, source_blocks, heads_local, which_ref, cos_ref, sin_ref, *refs):
    step_count = cos_ref.shape[0] // 2
    if direct:
        by_offset, parts_refs, attended_ref = refs[:4][::-1], refs[4:8][::-1], refs[8]
        total = sum(ref[...] for ref in parts_refs)
    else:
        parts_ref, blocks_ref, attended_ref, cache_ref, sem, kept = refs
        kept_count = which_ref.shape[1]
        me = lax.axis_index("seq")
        request, local = split_index(me, heads_local)
        head = lax.axis_index("head") * heads_local + local

        def start_copy(k, carry):
            previous, slot = carry
            source, _ = split_index(which_ref[request, k, head], source_blocks)
            slot = jnp.where(source == previous, jnp.minimum(slot + 1, MOST - 1), 0)
            target = kept.at[pl.ds(pl.multiple_of(k * BLK, BLK), BLK)]
            rows = pl.ds(pl.multiple_of(slot * BLK, BLK), BLK)
            pltpu.make_async_copy(blocks_ref.at[source, rows], target, sem).start()
            return source, slot

        lax.fori_loop(0, kept_count, start_copy, (jnp.int32(-1), jnp.int32(0)))
        total = jnp.sum(parts_ref[...], axis=0)
        pltpu.make_async_copy(kept, kept, sem).wait()
        pltpu.make_async_copy(kept, cache_ref.at[0, 0], sem).start()
    query_rows = QPK * step_count
    inverse = lax.rsqrt(total[query_rows + 2 * step_count :] * (1.0 / D) + EPS)
    cosine, sine = cos_ref[...], sin_ref[...]
    query = total[:query_rows].reshape(QPK // 2, 2 * step_count, HD) * inverse[None]
    query = rotate(query, cosine[None], sine[None]).reshape(query_rows, HD).astype(jnp.bfloat16)
    keyval = total[query_rows : query_rows + 2 * step_count] * inverse
    new_key = rotate(keyval, cosine, sine).astype(jnp.bfloat16)
    new_value = jnp.concatenate([keyval[step_count:], keyval[:step_count]], axis=0)
    new_value = new_value.astype(jnp.bfloat16)
    scale = 1.0 / math.sqrt(HD)
    score = lax.dot_general(query, new_key, CONTRACT_LAST, preferred_element_type=jnp.float32)
    row = lax.broadcasted_iota(jnp.int32, score.shape, 0)
    column = lax.broadcasted_iota(jnp.int32, score.shape, 1)
    scores = [jnp.where(column <= split_index(row, step_count)[1], score * scale, -jnp.inf)]
    values = [new_value]

    def add_block(block):
        score = lax.dot_general(
            query, block[:, :HD], CONTRACT_LAST, preferred_element_type=jnp.float32
        )
        scores.append(score * scale)
        values.append(block[:, HD:])

    if direct:
        for offset, ref in enumerate(by_offset):
            add_block(ref[...])
            scores[-1] += which_ref[offset, :1, :]
    else:
        add_block(kept[...])
    row_max = functools.reduce(
        jnp.maximum, [jnp.max(score, axis=1, keepdims=True) for score in scores]
    )
    denominator = jnp.zeros((query_rows, 1), jnp.float32)
    numerator = jnp.zeros((query_rows, HD), jnp.float32)
    for score, value in zip(scores, values):
        weight = jnp.exp(score - row_max)
        denominator += jnp.sum(weight, axis=1, keepdims=True)
        numerator += jnp.dot(
            weight.astype(jnp.bfloat16), value, preferred_element_type=jnp.float32
        )
    attended = (numerator / denominator).astype(jnp.bfloat16)
    if direct:
        attended_ref[...] = attended
    else:
        for i in range(attended_ref.shape[0]):
            attended_ref[i] = attended
        pltpu.make_async_copy(cache_ref, cache_ref, sem).wait()


def attend(which, arrivals, source_blocks, heads_local, step_count, seq_count, direct):
    cosine, sine = rope_tables(source_blocks * BLK * seq_count, step_count)
    shape = (QPK * step_count, HD)
    vmem = pl.BlockSpec(memory_space=pltpu.VMEM)
    if direct:
        shapes = [jax.ShapeDtypeStruct(shape, jnp.bfloat16)]
        out_specs = [vmem]
        scratch = []
    else:
        cache = (1, 1, which.shape[1] * BLK, 2 * HD)
        shapes = [
            jax.ShapeDtypeStruct((seq_count,) + shape, jnp.bfloat16),
            jax.ShapeDtypeStruct(cache, jnp.bfloat16),
        ]
        out_specs = [vmem, pl.BlockSpec(memory_space=pl.ANY)]
        scratch = [pltpu.SemaphoreType.DMA, pltpu.VMEM(cache[2:], jnp.bfloat16)]
    return pl.pallas_call(
        functools.partial(attend_kernel, direct, source_blocks, heads_local),
        out_shape=shapes,
        in_specs=[vmem if direct else pl.BlockSpec(memory_space=pltpu.SMEM)] + [vmem] * (2 + len(arrivals)),
        out_specs=out_specs,
        scratch_shapes=scratch,
        compiler_params=pltpu.CompilerParams(vmem_limit_bytes=16 * 1024 * 1024),
        cost_estimate=pl.CostEstimate(flops=10**10, bytes_accessed=0, transcendentals=0),
        name="attend",
    )(which, jnp.asarray(cosine), jnp.asarray(sine), *arrivals)


def merge_heads(first, second, step_count):
    pieces = []
    for h in range(QPK):
        rows = slice(h * step_count, (h + 1) * step_count)
        pieces.append(jnp.concatenate([first[rows], second[rows]], axis=0))
    return jnp.concatenate(pieces, axis=1).astype(jnp.bfloat16)


def output_same_kernel(w_ref, own_ref, second_ref, out_ref):
    me = lax.axis_index("seq")
    out_ref[...] = output_terms(w_ref, jnp.bitwise_and(me, 1), me >= 2, own_ref, second_ref)


def output_other_kernel(w_ref, above_ref, below_ref, addend_ref, out_ref):
    me = lax.axis_index("seq")
    even = jnp.bitwise_and(me, 1) == 0
    below = below_ref[...].astype(jnp.float32)
    above = above_ref[...].astype(jnp.float32)
    first = jnp.where(even, above, below)
    third = jnp.where(even, below, above)
    terms = output_terms(w_ref, 1 - jnp.bitwise_and(me, 1), me >= 2, first, third)
    out_ref[...] = (terms + addend_ref[...]).astype(out_ref.dtype)


def output_terms(w_ref, local, second, same, other):
    same = same[...].astype(jnp.float32)
    other = other[...].astype(jnp.float32)
    merged = merge_heads(
        jnp.where(second, other, same),
        jnp.where(second, same, other),
        same.shape[0] // QPK,
    )
    depth = w_ref.shape[0] // 2
    weights = w_ref[pl.ds(pl.multiple_of(local * depth, depth), depth), :]
    return jnp.dot(merged, weights, preferred_element_type=jnp.float32)


def output_half(kernel, dtype, w_out, values, *arrivals):
    rows = 2 * values.shape[0] // QPK
    vmem = pl.BlockSpec(memory_space=pltpu.VMEM)
    return pl.pallas_call(
        kernel,
        out_shape=jax.ShapeDtypeStruct((rows, w_out.shape[1]), dtype),
        in_specs=[vmem] * (2 + len(arrivals)),
        out_specs=vmem,
        compiler_params=pltpu.CompilerParams(vmem_limit_bytes=8 * 1024 * 1024),
        cost_estimate=pl.CostEstimate(flops=10**9, bytes_accessed=0, transcendentals=0),
        name="output_half",
    )(w_out, values, *arrivals)


def output_kernel(heads_local, w_ref, gathered_ref, out_ref):
    pair_count, query_rows, _ = gathered_ref.shape
    step_count = query_rows // QPK
    pairs = [gathered_ref[p].astype(jnp.float32) for p in range(pair_count)]
    requests = pair_count // heads_local
    pieces = []
    for l in range(heads_local):
        for h in range(QPK):
            rows = slice(h * step_count, (h + 1) * step_count)
            pieces.append(
                jnp.concatenate(
                    [pairs[r * heads_local + l][rows] for r in range(requests)], axis=0
                )
            )
    merged = jnp.concatenate(pieces, axis=1).astype(jnp.bfloat16)
    out_ref[...] = jnp.dot(merged, w_ref[...], preferred_element_type=jnp.float32)


def output(gathered, w_out, heads_local):
    pair_count, query_rows, _ = gathered.shape
    rows = pair_count // heads_local * (query_rows // QPK)
    vmem = pl.BlockSpec(memory_space=pltpu.VMEM)
    return pl.pallas_call(
        functools.partial(output_kernel, heads_local),
        out_shape=jax.ShapeDtypeStruct((rows, w_out.shape[1]), jnp.float32),
        in_specs=[vmem] * 2,
        out_specs=vmem,
        compiler_params=pltpu.CompilerParams(vmem_limit_bytes=8 * 1024 * 1024),
        name="output_projection",
    )(w_out, gathered)


def shards(source_cache, kept_blocks, new_hidden, norm_gain, w_query, w_keyval, w_out):
    seq_count = lax.axis_size("seq")
    head_count = lax.axis_size("head")
    requests, heads_local, source_tokens, _ = source_cache.shape
    _, step_count, width = new_hidden.shape
    pair_count = requests * heads_local

    kept_blocks = kept_blocks.transpose(0, 2, 1)
    source_blocks = source_tokens // BLK
    direct = is_direct(seq_count) and heads_local == 2 and requests == 2
    weights = (new_hidden, norm_gain, w_query, w_keyval)
    w_out = pltpu.with_memory_space_constraint(w_out, pltpu.VMEM)
    shape = (source_blocks, heads_local, step_count, seq_count, direct)
    if direct:
        partners = range(1, seq_count)
        blocks = list(pick(kept_blocks, source_cache, direct))
        *parts, mask = project(blocks[0], *weights, kept_blocks, source_blocks, direct)
        blocks = [blocks[0]] + [swap(blocks[k], "seq", k) for k in partners]
        parts[1], blocks[3] = lax.optimization_barrier((parts[1], blocks[3]))
        parts = [parts[0]] + [swap(parts[k], "seq", k) for k in partners]
        (attended,) = attend(mask, blocks[::-1] + parts[::-1], *shape)
        kept_cache = place(kept_blocks, attended, blocks, source_blocks, heads_local)
        below, second, above = [shift(attended, "seq", step) for step in (1, 2, -1)]
        second, below = lax.optimization_barrier((second, below))
        terms = output_half(output_same_kernel, jnp.float32, w_out, attended, second)
        terms = output_half(output_other_kernel, jnp.bfloat16, w_out, above, below, terms)
    else:
        (blocks,) = pick(kept_blocks, source_cache, direct)
        (parts,) = project(blocks, *weights, kept_blocks, source_blocks, direct)
        arrivals = [all_to_all(parts, "seq"), all_to_all(blocks, "seq")]
        attended, kept_cache = attend(kept_blocks, arrivals, *shape)
        terms = output(all_to_all(attended, "seq"), w_out, heads_local)
    if is_direct(head_count):
        terms = terms.astype(jnp.bfloat16)
        others = [swap(terms, "head", k) for k in range(1, head_count)]
        others[0], others[1], others[2], kept_cache = lax.optimization_barrier((others[0], others[1], others[2], kept_cache))
        own, core, along, across = [t.astype(jnp.float32) for t in [terms] + others]
        summed = (own + core) + (along + across)
    else:
        summed = lax.psum(terms, "head")
    summed = summed.reshape(requests, step_count, width)
    decoded = (new_hidden.astype(jnp.float32) + summed).astype(jnp.bfloat16)
    return (kept_cache, decoded)


def solution(mesh):
    in_specs = (
        P("groups", "head", "seq", None),
        P("groups", None, None),
        P("groups", None, "seq"),
        P("seq"),
        P("seq", "head"),
        P("seq", "head", None),
        P("head", "seq"),
    )
    out_specs = (P("head", ("groups", "seq"), None, None), P("groups", None, "seq"))
    return jax.shard_map(shards, mesh=mesh, in_specs=in_specs, out_specs=out_specs, check_vma=False)
```

```python
import functools
import math

import jax
import jax.numpy as jnp
import numpy as np
from jax import lax
from jax.experimental import pallas as pl
from jax.experimental.pallas import tpu as pltpu
from jax.sharding import PartitionSpec as P

D = 8192
HD = 128
QPK = 8
BLK = 128
MOST = 2
ROPE_BASE = 500000.0
TERM_ORDER = (2, 3, 1, 0)
EPS = 1e-05

CONTRACT_LAST = (((1,), (1,)), ((), ()))


def rope_tables(prompt_length, step_count):
    positions = prompt_length + np.arange(2 * step_count) % step_count
    frequency = ROPE_BASE ** (-np.arange(HD // 2, dtype=np.float64) * 2.0 / HD)
    angles = positions[:, None] * frequency[None, :]
    cosine = np.concatenate([np.cos(angles)] * 2, axis=1)
    sine = np.concatenate([-np.sin(angles), np.sin(angles)], axis=1)
    return cosine.astype(np.float32), sine.astype(np.float32)


def rotate(v, cosine, sine):
    swapped = jnp.concatenate([v[..., HD // 2 :], v[..., : HD // 2]], axis=-1)
    return v * cosine + swapped * sine


def is_direct(count):
    return count == 4


def swap(outgoing, axis, offset):
    count = lax.axis_size(axis)
    return lax.ppermute(outgoing, axis, [(i, i ^ offset) for i in range(count)])


def shift(outgoing, axis, step):
    count = lax.axis_size(axis)
    return lax.ppermute(outgoing, axis, [(i, (i + step) % count) for i in range(count)])


def all_to_all(outgoing, axis):
    return lax.all_to_all(outgoing, axis, split_axis=0, concat_axis=0, tiled=True)


def split_index(index, size):
    if size & (size - 1):
        return lax.div(index, size), lax.rem(index, size)
    shift = jnp.full_like(index, size.bit_length() - 1)
    return lax.shift_right_logical(index, shift), jnp.bitwise_and(index, size - 1)


def picked_rows(kept_ref, cache_shape, pair):
    _, heads_local, source_tokens, _ = cache_shape
    source_blocks = source_tokens // BLK
    kept_count = kept_ref.shape[1]
    first_block = lax.axis_index("seq") * source_blocks
    request, local = split_index(pair, heads_local)
    head = lax.axis_index("head") * heads_local + local

    def count(k, total):
        return total + (kept_ref[request, k, head] < first_block).astype(jnp.int32)

    start = lax.fori_loop(0, kept_count, count, jnp.int32(0), unroll=kept_count <= 8)
    places = []
    for slot in range(MOST):
        rank = jnp.minimum(start + slot, kept_count - 1)
        block = jnp.clip(kept_ref[request, rank, head] - first_block, 0, source_blocks - 1)
        places.append((request, local, pl.ds(pl.multiple_of(block * BLK, BLK), BLK)))
    return places


def pick_near_kernel(kept_hbm_ref, cache_ref, *refs):
    *outs, kept_ref, cache, kept_sem, sem = refs
    heads_local = cache.shape[1]
    me = lax.axis_index("seq")
    kept_copy = pltpu.make_async_copy(kept_hbm_ref, kept_ref, kept_sem)
    kept_copy.start()

    def pair_copy(pair):
        place = split_index(pair, heads_local)
        return pltpu.make_async_copy(cache_ref.at[place], cache.at[place], sem.at[pair])

    offsets = list(reversed(range(len(outs))))
    copies = {offset: pair_copy(jnp.bitwise_xor(me, offset)) for offset in offsets}
    for offset in offsets:
        copies[offset].start()
    kept_copy.wait()
    for offset in offsets:
        places = picked_rows(kept_ref, cache.shape, jnp.bitwise_xor(me, offset))
        copies[offset].wait()
        for slot, (request, local, rows) in enumerate(places):
            outs[offset][slot * BLK : (slot + 1) * BLK, :] = cache[request, local, rows, :]


def pick_all_kernel(kept_hbm_ref, cache_ref, out_ref, kept_ref, sem):
    pltpu.sync_copy(kept_hbm_ref, kept_ref)

    def pair_body(pair, carry):
        for slot, place in enumerate(picked_rows(kept_ref, cache_ref.shape, pair)):
            pltpu.make_async_copy(
                cache_ref.at[place], out_ref.at[pair, pl.ds(slot * BLK, BLK)], sem
            ).start()
        return carry

    lax.fori_loop(0, out_ref.shape[0], pair_body, 0)
    pltpu.make_async_copy(out_ref, out_ref, sem).wait()


def pick(kept_blocks, source_cache, direct):
    requests, heads_local, _, row_width = source_cache.shape
    pair_count = requests * heads_local
    block = (MOST * BLK, row_width)
    kept_scratch = pltpu.SMEM(kept_blocks.shape, jnp.int32)
    if direct:
        shapes = [jax.ShapeDtypeStruct(block, jnp.bfloat16)] * pair_count
        scratch = [
            kept_scratch,
            pltpu.VMEM(source_cache.shape, jnp.bfloat16),
            pltpu.SemaphoreType.DMA,
            pltpu.SemaphoreType.DMA((pair_count,)),
        ]
    else:
        shapes = [jax.ShapeDtypeStruct((pair_count,) + block, jnp.bfloat16)]
        scratch = [kept_scratch, pltpu.SemaphoreType.DMA]
    return pl.pallas_call(
        pick_near_kernel if direct else pick_all_kernel,
        out_shape=shapes,
        in_specs=[pl.BlockSpec(memory_space=pl.ANY)] * 2,
        out_specs=[pl.BlockSpec(memory_space=pltpu.VMEM)] * len(shapes),
        scratch_shapes=scratch,
        compiler_params=pltpu.CompilerParams(vmem_limit_bytes=8 * 1024 * 1024),
        cost_estimate=pl.CostEstimate(flops=10**10, bytes_accessed=0, transcendentals=0),
        name="pick_blocks",
    )(
        pltpu.with_memory_space_constraint(kept_blocks, pltpu.HBM),
        pltpu.with_memory_space_constraint(source_cache, pltpu.HBM),
    )


def interleave(rows):
    count, width = rows.shape
    chunks = width // HD
    stacked = jnp.concatenate(
        [rows[:, c * HD : (c + 1) * HD] for c in range(chunks)], axis=0
    ).astype(jnp.bfloat16)
    source = lax.broadcasted_iota(jnp.int32, (HD, 4 * HD), 0)
    target = lax.broadcasted_iota(jnp.int32, (HD, 4 * HD), 1)
    place = jnp.where(target < 2 * HD, 2 * source, 2 * source + 1 + 2 * HD)
    spread = (place == target).astype(jnp.bfloat16)
    wide = jnp.dot(stacked, spread, preferred_element_type=jnp.float32)
    return [
        jnp.concatenate(
            [
                wide[c * count : (c + 1) * count, : 2 * HD],
                wide[c * count : (c + 1) * count, 2 * HD :],
            ],
            axis=0,
        ).astype(jnp.bfloat16)
        for c in range(chunks)
    ]


def project_kernel(direct, source_blocks, after_ref, hidden_ref, gain_ref, wq_ref, wkv_ref, *refs):
    del after_ref
    outs = refs
    if direct:
        kept_ref, *outs, mask_ref = refs
    requests, step_count, width = hidden_ref.shape
    heads_local = wkv_ref.shape[1]
    row_count = requests * step_count
    me = lax.axis_index("seq")
    hidden = jnp.concatenate(
        [hidden_ref[r].astype(jnp.float32) for r in range(requests)], axis=0
    )
    square = jnp.sum(hidden * hidden, axis=1, keepdims=True)
    gain = gain_ref[...].astype(jnp.float32)
    scaled = jnp.concatenate(
        [hidden[:, c * HD : (c + 1) * HD] * gain[c : c + 1] for c in range(width // HD)], axis=1
    ).astype(jnp.bfloat16)
    query = jnp.dot(scaled, wq_ref[...], preferred_element_type=jnp.float32)
    keyval = jnp.zeros((heads_local * row_count, wkv_ref.shape[2]), jnp.float32)
    for c, spread in enumerate(interleave(scaled.astype(jnp.float32))):
        alternate = wkv_ref[c * HD : (c + 1) * HD].reshape(heads_local * HD, wkv_ref.shape[2])
        keyval += jnp.dot(spread, alternate, preferred_element_type=jnp.float32)

    def pieces_of(r, l):
        steps = slice(r * step_count, (r + 1) * step_count)
        square_rows = jnp.broadcast_to(square[steps], (step_count, HD))
        own = keyval[l * row_count + r * step_count : l * row_count + (r + 1) * step_count]
        heads = [query[steps, (l * QPK + h) * HD : (l * QPK + h + 1) * HD] for h in range(QPK)]
        return heads + [own[:, :HD], own[:, HD:], square_rows, square_rows]

    def write_pair(out_ref, pieces):
        for j, piece in enumerate(pieces):
            out_ref[j * step_count : (j + 1) * step_count, :] = piece

    for r in range(requests):
        for l in range(heads_local):
            pair = r * heads_local + l
            pieces = pieces_of(r, l)
            if not direct:
                write_pair(outs[0].at[pair], pieces)
                continue
            for offset, out_ref in enumerate(outs):
                pl.when(jnp.bitwise_xor(me, offset) == pair)(
                    functools.partial(write_pair, out_ref, pieces)
                )
    if direct:
        request, local = split_index(me, heads_local)
        head = lax.axis_index("head") * heads_local + local
        kept = jnp.where(request == 0, kept_ref[0], kept_ref[1]).astype(jnp.float32)
        lane = lax.broadcasted_iota(jnp.int32, kept.shape, 1)
        kept = jnp.sum(jnp.where(lane == head, kept, 0.0), axis=1, keepdims=True)
        column = lax.broadcasted_iota(jnp.int32, mask_ref.shape[1:], 1).astype(jnp.float32)
        for offset in range(mask_ref.shape[0]):
            first_block = (jnp.bitwise_xor(me, offset) * source_blocks).astype(jnp.float32)
            here = (kept >= first_block) & (kept < first_block + source_blocks)
            filled = jnp.sum(jnp.where(here, float(BLK), 0.0), axis=0, keepdims=True)
            mask_ref[offset] = jnp.where(column < filled, 0.0, -jnp.inf)


def project(after, new_hidden, norm_gain, w_query, w_keyval, kept_blocks, source_blocks, direct):
    requests, step_count, width = new_hidden.shape
    pair_count = requests * w_keyval.shape[1]
    terms = ((QPK + 4) * step_count, HD)
    if direct:
        shapes = [jax.ShapeDtypeStruct(terms, jnp.float32)] * pair_count
        shapes.append(jax.ShapeDtypeStruct((pair_count, 8, MOST * BLK), jnp.float32))
    else:
        shapes = [jax.ShapeDtypeStruct((pair_count,) + terms, jnp.float32)]
    vmem = pl.BlockSpec(memory_space=pltpu.VMEM)
    weights = w_query.size + w_keyval.size
    return pl.pallas_call(
        functools.partial(project_kernel, direct, source_blocks),
        out_shape=shapes,
        in_specs=[pl.BlockSpec(memory_space=pl.ANY)] + [vmem] * (4 + direct),
        out_specs=[vmem] * len(shapes),
        compiler_params=pltpu.CompilerParams(vmem_limit_bytes=8 * 1024 * 1024),
        cost_estimate=pl.CostEstimate(
            flops=2 * requests * step_count * weights,
            bytes_accessed=2 * weights,
            transcendentals=0,
        ),
        name="project",
    )(
        after,
        new_hidden,
        norm_gain.reshape(width // HD, HD),
        pltpu.with_memory_space_constraint(w_query, pltpu.VMEM),
        pltpu.with_memory_space_constraint(w_keyval, pltpu.VMEM),
        *([kept_blocks] if direct else []),
    )


def place_kernel(source_blocks, heads_local, kept_ref, after_ref, *refs):
    del after_ref
    *by_offset, cache_ref, sem = refs
    me = lax.axis_index("seq")
    request, local = split_index(me, heads_local)
    head = lax.axis_index("head") * heads_local + local
    previous, slot = jnp.int32(-1), jnp.int32(0)
    for k in range(kept_ref.shape[1]):
        source, _ = split_index(kept_ref[request, k, head], source_blocks)
        slot = jnp.where(source == previous, jnp.minimum(slot + 1, MOST - 1), 0)
        previous = source
        rows = pl.ds(pl.multiple_of(slot * BLK, BLK), BLK)
        target = cache_ref.at[0, 0, pl.ds(k * BLK, BLK)]
        for offset, ref in enumerate(by_offset):
            pl.when(jnp.bitwise_xor(me, offset) == source)(
                pltpu.make_async_copy(ref.at[rows], target, sem).start
            )
    pltpu.make_async_copy(cache_ref, cache_ref, sem).wait()


def place(kept_blocks, after, blocks, source_blocks, heads_local):
    kept_count = kept_blocks.shape[1]
    anywhere = pl.BlockSpec(memory_space=pl.ANY)
    return pl.pallas_call(
        functools.partial(place_kernel, source_blocks, heads_local),
        out_shape=jax.ShapeDtypeStruct((1, 1, kept_count * BLK, 2 * HD), jnp.bfloat16),
        in_specs=[pl.BlockSpec(memory_space=pltpu.SMEM)] + [anywhere] * (1 + len(blocks)),
        out_specs=anywhere,
        scratch_shapes=[pltpu.SemaphoreType.DMA],
        compiler_params=pltpu.CompilerParams(vmem_limit_bytes=8 * 1024 * 1024),
        cost_estimate=pl.CostEstimate(flops=10**9, bytes_accessed=0, transcendentals=0),
        name="place",
    )(kept_blocks, after, *blocks)


def attend_kernel(direct, source_blocks, heads_local, which_ref, cos_ref, sin_ref, *refs):
    step_count = cos_ref.shape[0] // 2
    if direct:
        by_offset, parts_refs, attended_ref = refs[:4][::-1], refs[4:8][::-1], refs[8]
        total = sum(ref[...] for ref in parts_refs)
    else:
        parts_ref, blocks_ref, attended_ref, cache_ref, sem, kept = refs
        kept_count = which_ref.shape[1]
        me = lax.axis_index("seq")
        request, local = split_index(me, heads_local)
        head = lax.axis_index("head") * heads_local + local

        def start_copy(k, carry):
            previous, slot = carry
            source, _ = split_index(which_ref[request, k, head], source_blocks)
            slot = jnp.where(source == previous, jnp.minimum(slot + 1, MOST - 1), 0)
            target = kept.at[pl.ds(pl.multiple_of(k * BLK, BLK), BLK)]
            rows = pl.ds(pl.multiple_of(slot * BLK, BLK), BLK)
            pltpu.make_async_copy(blocks_ref.at[source, rows], target, sem).start()
            return source, slot

        lax.fori_loop(0, kept_count, start_copy, (jnp.int32(-1), jnp.int32(0)))
        total = jnp.sum(parts_ref[...], axis=0)
        pltpu.make_async_copy(kept, kept, sem).wait()
        pltpu.make_async_copy(kept, cache_ref.at[0, 0], sem).start()
    query_rows = QPK * step_count
    inverse = lax.rsqrt(total[query_rows + 2 * step_count :] * (1.0 / D) + EPS)
    cosine, sine = cos_ref[...], sin_ref[...]
    query = total[:query_rows].reshape(QPK // 2, 2 * step_count, HD) * inverse[None]
    query = rotate(query, cosine[None], sine[None]).reshape(query_rows, HD).astype(jnp.bfloat16)
    keyval = total[query_rows : query_rows + 2 * step_count] * inverse
    new_key = rotate(keyval, cosine, sine).astype(jnp.bfloat16)
    new_value = jnp.concatenate([keyval[step_count:], keyval[:step_count]], axis=0)
    new_value = new_value.astype(jnp.bfloat16)
    scale = 1.0 / math.sqrt(HD)
    score = lax.dot_general(query, new_key, CONTRACT_LAST, preferred_element_type=jnp.float32)
    row = lax.broadcasted_iota(jnp.int32, score.shape, 0)
    column = lax.broadcasted_iota(jnp.int32, score.shape, 1)
    scores = [jnp.where(column <= split_index(row, step_count)[1], score * scale, -jnp.inf)]
    values = [new_value]

    def add_block(block):
        score = lax.dot_general(
            query, block[:, :HD], CONTRACT_LAST, preferred_element_type=jnp.float32
        )
        scores.append(score * scale)
        values.append(block[:, HD:])

    if direct:
        for offset, ref in enumerate(by_offset):
            add_block(ref[...])
            scores[-1] += which_ref[offset, :1, :]
    else:
        add_block(kept[...])
    row_max = functools.reduce(
        jnp.maximum, [jnp.max(score, axis=1, keepdims=True) for score in scores]
    )
    denominator = jnp.zeros((query_rows, 1), jnp.float32)
    numerator = jnp.zeros((query_rows, HD), jnp.float32)
    for score, value in zip(scores, values):
        weight = jnp.exp(score - row_max)
        denominator += jnp.sum(weight, axis=1, keepdims=True)
        numerator += jnp.dot(
            weight.astype(jnp.bfloat16), value, preferred_element_type=jnp.float32
        )
    attended = (numerator / denominator).astype(jnp.bfloat16)
    if direct:
        attended_ref[...] = attended
    else:
        for i in range(attended_ref.shape[0]):
            attended_ref[i] = attended
        pltpu.make_async_copy(cache_ref, cache_ref, sem).wait()


def attend(which, arrivals, source_blocks, heads_local, step_count, seq_count, direct):
    cosine, sine = rope_tables(source_blocks * BLK * seq_count, step_count)
    shape = (QPK * step_count, HD)
    vmem = pl.BlockSpec(memory_space=pltpu.VMEM)
    if direct:
        shapes = [jax.ShapeDtypeStruct(shape, jnp.bfloat16)]
        out_specs = [vmem]
        scratch = []
    else:
        cache = (1, 1, which.shape[1] * BLK, 2 * HD)
        shapes = [
            jax.ShapeDtypeStruct((seq_count,) + shape, jnp.bfloat16),
            jax.ShapeDtypeStruct(cache, jnp.bfloat16),
        ]
        out_specs = [vmem, pl.BlockSpec(memory_space=pl.ANY)]
        scratch = [pltpu.SemaphoreType.DMA, pltpu.VMEM(cache[2:], jnp.bfloat16)]
    return pl.pallas_call(
        functools.partial(attend_kernel, direct, source_blocks, heads_local),
        out_shape=shapes,
        in_specs=[vmem if direct else pl.BlockSpec(memory_space=pltpu.SMEM)] + [vmem] * (2 + len(arrivals)),
        out_specs=out_specs,
        scratch_shapes=scratch,
        compiler_params=pltpu.CompilerParams(vmem_limit_bytes=16 * 1024 * 1024),
        cost_estimate=pl.CostEstimate(flops=10**10, bytes_accessed=0, transcendentals=0),
        name="attend",
    )(which, jnp.asarray(cosine), jnp.asarray(sine), *arrivals)


def merge_heads(first, second, step_count):
    pieces = []
    for h in range(QPK):
        rows = slice(h * step_count, (h + 1) * step_count)
        pieces.append(jnp.concatenate([first[rows], second[rows]], axis=0))
    return jnp.concatenate(pieces, axis=1).astype(jnp.bfloat16)


def output_same_kernel(w_ref, own_ref, second_ref, out_ref):
    me = lax.axis_index("seq")
    out_ref[...] = output_terms(w_ref, jnp.bitwise_and(me, 1), me >= 2, own_ref, second_ref)


def output_other_kernel(w_ref, above_ref, below_ref, addend_ref, out_ref):
    me = lax.axis_index("seq")
    even = jnp.bitwise_and(me, 1) == 0
    below = below_ref[...].astype(jnp.float32)
    above = above_ref[...].astype(jnp.float32)
    first = jnp.where(even, above, below)
    third = jnp.where(even, below, above)
    terms = output_terms(w_ref, 1 - jnp.bitwise_and(me, 1), me >= 2, first, third)
    out_ref[...] = (terms + addend_ref[...]).astype(out_ref.dtype)


def output_terms(w_ref, local, second, same, other):
    same = same[...].astype(jnp.float32)
    other = other[...].astype(jnp.float32)
    merged = merge_heads(
        jnp.where(second, other, same),
        jnp.where(second, same, other),
        same.shape[0] // QPK,
    )
    depth = w_ref.shape[0] // 2
    weights = w_ref[pl.ds(pl.multiple_of(local * depth, depth), depth), :]
    return jnp.dot(merged, weights, preferred_element_type=jnp.float32)


def output_half(kernel, dtype, w_out, values, *arrivals):
    rows = 2 * values.shape[0] // QPK
    vmem = pl.BlockSpec(memory_space=pltpu.VMEM)
    return pl.pallas_call(
        kernel,
        out_shape=jax.ShapeDtypeStruct((rows, w_out.shape[1]), dtype),
        in_specs=[vmem] * (2 + len(arrivals)),
        out_specs=vmem,
        compiler_params=pltpu.CompilerParams(vmem_limit_bytes=8 * 1024 * 1024),
        cost_estimate=pl.CostEstimate(flops=10**9, bytes_accessed=0, transcendentals=0),
        name="output_half",
    )(w_out, values, *arrivals)


def output_kernel(heads_local, w_ref, gathered_ref, out_ref):
    pair_count, query_rows, _ = gathered_ref.shape
    step_count = query_rows // QPK
    pairs = [gathered_ref[p].astype(jnp.float32) for p in range(pair_count)]
    requests = pair_count // heads_local
    pieces = []
    for l in range(heads_local):
        for h in range(QPK):
            rows = slice(h * step_count, (h + 1) * step_count)
            pieces.append(
                jnp.concatenate(
                    [pairs[r * heads_local + l][rows] for r in range(requests)], axis=0
                )
            )
    merged = jnp.concatenate(pieces, axis=1).astype(jnp.bfloat16)
    out_ref[...] = jnp.dot(merged, w_ref[...], preferred_element_type=jnp.float32)


def output(gathered, w_out, heads_local):
    pair_count, query_rows, _ = gathered.shape
    rows = pair_count // heads_local * (query_rows // QPK)
    vmem = pl.BlockSpec(memory_space=pltpu.VMEM)
    return pl.pallas_call(
        functools.partial(output_kernel, heads_local),
        out_shape=jax.ShapeDtypeStruct((rows, w_out.shape[1]), jnp.float32),
        in_specs=[vmem] * 2,
        out_specs=vmem,
        compiler_params=pltpu.CompilerParams(vmem_limit_bytes=8 * 1024 * 1024),
        name="output_projection",
    )(w_out, gathered)


def shards(source_cache, kept_blocks, new_hidden, norm_gain, w_query, w_keyval, w_out):
    seq_count = lax.axis_size("seq")
    head_count = lax.axis_size("head")
    requests, heads_local, source_tokens, _ = source_cache.shape
    _, step_count, width = new_hidden.shape
    pair_count = requests * heads_local

    kept_blocks = kept_blocks.transpose(0, 2, 1)
    source_blocks = source_tokens // BLK
    direct = is_direct(seq_count) and heads_local == 2 and requests == 2
    weights = (new_hidden, norm_gain, w_query, w_keyval)
    w_out = pltpu.with_memory_space_constraint(w_out, pltpu.VMEM)
    shape = (source_blocks, heads_local, step_count, seq_count, direct)
    if direct:
        partners = range(1, seq_count)
        blocks = list(pick(kept_blocks, source_cache, direct))
        *parts, mask = project(blocks[0], *weights, kept_blocks, source_blocks, direct)
        blocks = [blocks[0]] + [swap(blocks[k], "seq", k) for k in partners]
        parts[1], blocks[3] = lax.optimization_barrier((parts[1], blocks[3]))
        parts = [parts[0]] + [swap(parts[k], "seq", k) for k in partners]
        arrivals = blocks[::-1] + [parts[k] for k in TERM_ORDER]
        (attended,) = attend(mask, arrivals, *shape)
        kept_cache = place(kept_blocks, attended, blocks, source_blocks, heads_local)
        below, second, above = [shift(attended, "seq", step) for step in (1, 2, -1)]
        second, below = lax.optimization_barrier((second, below))
        terms = output_half(output_same_kernel, jnp.float32, w_out, attended, second)
        terms = output_half(output_other_kernel, jnp.bfloat16, w_out, above, below, terms)
    else:
        (blocks,) = pick(kept_blocks, source_cache, direct)
        (parts,) = project(blocks, *weights, kept_blocks, source_blocks, direct)
        arrivals = [all_to_all(parts, "seq"), all_to_all(blocks, "seq")]
        attended, kept_cache = attend(kept_blocks, arrivals, *shape)
        terms = output(all_to_all(attended, "seq"), w_out, heads_local)
    if is_direct(head_count):
        terms = terms.astype(jnp.bfloat16)
        others = [swap(terms, "head", k) for k in range(1, head_count)]
        others[0], others[1], others[2], kept_cache = lax.optimization_barrier((others[0], others[1], others[2], kept_cache))
        own, core, along, across = [t.astype(jnp.float32) for t in [terms] + others]
        summed = (own + core) + (along + across)
    else:
        summed = lax.psum(terms, "head")
    summed = summed.reshape(requests, step_count, width)
    decoded = (new_hidden.astype(jnp.float32) + summed).astype(jnp.bfloat16)
    return (kept_cache, decoded)


def solution(mesh):
    in_specs = (
        P("groups", "head", "seq", None),
        P("groups", None, None),
        P("groups", None, "seq"),
        P("seq"),
        P("seq", "head"),
        P("seq", "head", None),
        P("head", "seq"),
    )
    out_specs = (P("head", ("groups", "seq"), None, None), P("groups", None, "seq"))
    return jax.shard_map(shards, mesh=mesh, in_specs=in_specs, out_specs=out_specs, check_vma=False)
```

```python
import functools
import math

import jax
import jax.numpy as jnp
import numpy as np
from jax import lax
from jax.experimental import pallas as pl
from jax.experimental.pallas import tpu as pltpu
from jax.sharding import PartitionSpec as P

D = 8192
HD = 128
QPK = 8
BLK = 128
MOST = 2
ROPE_BASE = 500000.0
TERM_ORDER = (2, 1, 3, 0)
EPS = 1e-05

CONTRACT_LAST = (((1,), (1,)), ((), ()))


def rope_tables(prompt_length, step_count):
    positions = prompt_length + np.arange(2 * step_count) % step_count
    frequency = ROPE_BASE ** (-np.arange(HD // 2, dtype=np.float64) * 2.0 / HD)
    angles = positions[:, None] * frequency[None, :]
    cosine = np.concatenate([np.cos(angles)] * 2, axis=1)
    sine = np.concatenate([-np.sin(angles), np.sin(angles)], axis=1)
    return cosine.astype(np.float32), sine.astype(np.float32)


def rotate(v, cosine, sine):
    swapped = jnp.concatenate([v[..., HD // 2 :], v[..., : HD // 2]], axis=-1)
    return v * cosine + swapped * sine


def is_direct(count):
    return count == 4


def swap(outgoing, axis, offset):
    count = lax.axis_size(axis)
    return lax.ppermute(outgoing, axis, [(i, i ^ offset) for i in range(count)])


def shift(outgoing, axis, step):
    count = lax.axis_size(axis)
    return lax.ppermute(outgoing, axis, [(i, (i + step) % count) for i in range(count)])


def all_to_all(outgoing, axis):
    return lax.all_to_all(outgoing, axis, split_axis=0, concat_axis=0, tiled=True)


def split_index(index, size):
    if size & (size - 1):
        return lax.div(index, size), lax.rem(index, size)
    shift = jnp.full_like(index, size.bit_length() - 1)
    return lax.shift_right_logical(index, shift), jnp.bitwise_and(index, size - 1)


def picked_rows(kept_ref, cache_shape, pair):
    _, heads_local, source_tokens, _ = cache_shape
    source_blocks = source_tokens // BLK
    kept_count = kept_ref.shape[1]
    first_block = lax.axis_index("seq") * source_blocks
    request, local = split_index(pair, heads_local)
    head = lax.axis_index("head") * heads_local + local

    def count(k, total):
        return total + (kept_ref[request, k, head] < first_block).astype(jnp.int32)

    start = lax.fori_loop(0, kept_count, count, jnp.int32(0), unroll=kept_count <= 8)
    places = []
    for slot in range(MOST):
        rank = jnp.minimum(start + slot, kept_count - 1)
        block = jnp.clip(kept_ref[request, rank, head] - first_block, 0, source_blocks - 1)
        places.append((request, local, pl.ds(pl.multiple_of(block * BLK, BLK), BLK)))
    return places


def pick_near_kernel(kept_hbm_ref, cache_ref, *refs):
    *outs, kept_ref, cache, kept_sem, sem = refs
    heads_local = cache.shape[1]
    me = lax.axis_index("seq")
    kept_copy = pltpu.make_async_copy(kept_hbm_ref, kept_ref, kept_sem)
    kept_copy.start()

    def pair_copy(pair):
        place = split_index(pair, heads_local)
        return pltpu.make_async_copy(cache_ref.at[place], cache.at[place], sem.at[pair])

    offsets = list(reversed(range(len(outs))))
    copies = {offset: pair_copy(jnp.bitwise_xor(me, offset)) for offset in offsets}
    for offset in offsets:
        copies[offset].start()
    kept_copy.wait()
    for offset in offsets:
        places = picked_rows(kept_ref, cache.shape, jnp.bitwise_xor(me, offset))
        copies[offset].wait()
        for slot, (request, local, rows) in enumerate(places):
            outs[offset][slot * BLK : (slot + 1) * BLK, :] = cache[request, local, rows, :]


def pick_all_kernel(kept_hbm_ref, cache_ref, out_ref, kept_ref, sem):
    pltpu.sync_copy(kept_hbm_ref, kept_ref)

    def pair_body(pair, carry):
        for slot, place in enumerate(picked_rows(kept_ref, cache_ref.shape, pair)):
            pltpu.make_async_copy(
                cache_ref.at[place], out_ref.at[pair, pl.ds(slot * BLK, BLK)], sem
            ).start()
        return carry

    lax.fori_loop(0, out_ref.shape[0], pair_body, 0)
    pltpu.make_async_copy(out_ref, out_ref, sem).wait()


def pick(kept_blocks, source_cache, direct):
    requests, heads_local, _, row_width = source_cache.shape
    pair_count = requests * heads_local
    block = (MOST * BLK, row_width)
    kept_scratch = pltpu.SMEM(kept_blocks.shape, jnp.int32)
    if direct:
        shapes = [jax.ShapeDtypeStruct(block, jnp.bfloat16)] * pair_count
        scratch = [
            kept_scratch,
            pltpu.VMEM(source_cache.shape, jnp.bfloat16),
            pltpu.SemaphoreType.DMA,
            pltpu.SemaphoreType.DMA((pair_count,)),
        ]
    else:
        shapes = [jax.ShapeDtypeStruct((pair_count,) + block, jnp.bfloat16)]
        scratch = [kept_scratch, pltpu.SemaphoreType.DMA]
    return pl.pallas_call(
        pick_near_kernel if direct else pick_all_kernel,
        out_shape=shapes,
        in_specs=[pl.BlockSpec(memory_space=pl.ANY)] * 2,
        out_specs=[pl.BlockSpec(memory_space=pltpu.VMEM)] * len(shapes),
        scratch_shapes=scratch,
        compiler_params=pltpu.CompilerParams(vmem_limit_bytes=8 * 1024 * 1024),
        cost_estimate=pl.CostEstimate(flops=10**10, bytes_accessed=0, transcendentals=0),
        name="pick_blocks",
    )(
        pltpu.with_memory_space_constraint(kept_blocks, pltpu.HBM),
        pltpu.with_memory_space_constraint(source_cache, pltpu.HBM),
    )


def interleave(rows):
    count, width = rows.shape
    chunks = width // HD
    stacked = jnp.concatenate(
        [rows[:, c * HD : (c + 1) * HD] for c in range(chunks)], axis=0
    ).astype(jnp.bfloat16)
    source = lax.broadcasted_iota(jnp.int32, (HD, 4 * HD), 0)
    target = lax.broadcasted_iota(jnp.int32, (HD, 4 * HD), 1)
    place = jnp.where(target < 2 * HD, 2 * source, 2 * source + 1 + 2 * HD)
    spread = (place == target).astype(jnp.bfloat16)
    wide = jnp.dot(stacked, spread, preferred_element_type=jnp.float32)
    return [
        jnp.concatenate(
            [
                wide[c * count : (c + 1) * count, : 2 * HD],
                wide[c * count : (c + 1) * count, 2 * HD :],
            ],
            axis=0,
        ).astype(jnp.bfloat16)
        for c in range(chunks)
    ]


def project_kernel(direct, source_blocks, after_ref, hidden_ref, gain_ref, wq_ref, wkv_ref, *refs):
    del after_ref
    outs = refs
    if direct:
        kept_ref, *outs, mask_ref = refs
    requests, step_count, width = hidden_ref.shape
    heads_local = wkv_ref.shape[1]
    row_count = requests * step_count
    me = lax.axis_index("seq")
    hidden = jnp.concatenate(
        [hidden_ref[r].astype(jnp.float32) for r in range(requests)], axis=0
    )
    square = jnp.sum(hidden * hidden, axis=1, keepdims=True)
    gain = gain_ref[...].astype(jnp.float32)
    scaled = jnp.concatenate(
        [hidden[:, c * HD : (c + 1) * HD] * gain[c : c + 1] for c in range(width // HD)], axis=1
    ).astype(jnp.bfloat16)
    query = jnp.dot(scaled, wq_ref[...], preferred_element_type=jnp.float32)
    keyval = jnp.zeros((heads_local * row_count, wkv_ref.shape[2]), jnp.float32)
    for c, spread in enumerate(interleave(scaled.astype(jnp.float32))):
        alternate = wkv_ref[c * HD : (c + 1) * HD].reshape(heads_local * HD, wkv_ref.shape[2])
        keyval += jnp.dot(spread, alternate, preferred_element_type=jnp.float32)

    def pieces_of(r, l):
        steps = slice(r * step_count, (r + 1) * step_count)
        square_rows = jnp.broadcast_to(square[steps], (step_count, HD))
        own = keyval[l * row_count + r * step_count : l * row_count + (r + 1) * step_count]
        heads = [query[steps, (l * QPK + h) * HD : (l * QPK + h + 1) * HD] for h in range(QPK)]
        return heads + [own[:, :HD], own[:, HD:], square_rows, square_rows]

    def write_pair(out_ref, pieces):
        for j, piece in enumerate(pieces):
            out_ref[j * step_count : (j + 1) * step_count, :] = piece

    for r in range(requests):
        for l in range(heads_local):
            pair = r * heads_local + l
            pieces = pieces_of(r, l)
            if not direct:
                write_pair(outs[0].at[pair], pieces)
                continue
            for offset, out_ref in enumerate(outs):
                pl.when(jnp.bitwise_xor(me, offset) == pair)(
                    functools.partial(write_pair, out_ref, pieces)
                )
    if direct:
        request, local = split_index(me, heads_local)
        head = lax.axis_index("head") * heads_local + local
        kept = jnp.where(request == 0, kept_ref[0], kept_ref[1]).astype(jnp.float32)
        lane = lax.broadcasted_iota(jnp.int32, kept.shape, 1)
        kept = jnp.sum(jnp.where(lane == head, kept, 0.0), axis=1, keepdims=True)
        column = lax.broadcasted_iota(jnp.int32, mask_ref.shape[1:], 1).astype(jnp.float32)
        for offset in range(mask_ref.shape[0]):
            first_block = (jnp.bitwise_xor(me, offset) * source_blocks).astype(jnp.float32)
            here = (kept >= first_block) & (kept < first_block + source_blocks)
            filled = jnp.sum(jnp.where(here, float(BLK), 0.0), axis=0, keepdims=True)
            mask_ref[offset] = jnp.where(column < filled, 0.0, -jnp.inf)


def project(after, new_hidden, norm_gain, w_query, w_keyval, kept_blocks, source_blocks, direct):
    requests, step_count, width = new_hidden.shape
    pair_count = requests * w_keyval.shape[1]
    terms = ((QPK + 4) * step_count, HD)
    if direct:
        shapes = [jax.ShapeDtypeStruct(terms, jnp.float32)] * pair_count
        shapes.append(jax.ShapeDtypeStruct((pair_count, 8, MOST * BLK), jnp.float32))
    else:
        shapes = [jax.ShapeDtypeStruct((pair_count,) + terms, jnp.float32)]
    vmem = pl.BlockSpec(memory_space=pltpu.VMEM)
    weights = w_query.size + w_keyval.size
    return pl.pallas_call(
        functools.partial(project_kernel, direct, source_blocks),
        out_shape=shapes,
        in_specs=[pl.BlockSpec(memory_space=pl.ANY)] + [vmem] * (4 + direct),
        out_specs=[vmem] * len(shapes),
        compiler_params=pltpu.CompilerParams(vmem_limit_bytes=8 * 1024 * 1024),
        cost_estimate=pl.CostEstimate(
            flops=2 * requests * step_count * weights,
            bytes_accessed=2 * weights,
            transcendentals=0,
        ),
        name="project",
    )(
        after,
        new_hidden,
        norm_gain.reshape(width // HD, HD),
        pltpu.with_memory_space_constraint(w_query, pltpu.VMEM),
        pltpu.with_memory_space_constraint(w_keyval, pltpu.VMEM),
        *([kept_blocks] if direct else []),
    )


def place_kernel(source_blocks, heads_local, kept_ref, after_ref, *refs):
    del after_ref
    *by_offset, cache_ref, sem = refs
    me = lax.axis_index("seq")
    request, local = split_index(me, heads_local)
    head = lax.axis_index("head") * heads_local + local
    previous, slot = jnp.int32(-1), jnp.int32(0)
    for k in range(kept_ref.shape[1]):
        source, _ = split_index(kept_ref[request, k, head], source_blocks)
        slot = jnp.where(source == previous, jnp.minimum(slot + 1, MOST - 1), 0)
        previous = source
        rows = pl.ds(pl.multiple_of(slot * BLK, BLK), BLK)
        target = cache_ref.at[0, 0, pl.ds(k * BLK, BLK)]
        for offset, ref in enumerate(by_offset):
            pl.when(jnp.bitwise_xor(me, offset) == source)(
                pltpu.make_async_copy(ref.at[rows], target, sem).start
            )
    pltpu.make_async_copy(cache_ref, cache_ref, sem).wait()


def place(kept_blocks, after, blocks, source_blocks, heads_local):
    kept_count = kept_blocks.shape[1]
    anywhere = pl.BlockSpec(memory_space=pl.ANY)
    return pl.pallas_call(
        functools.partial(place_kernel, source_blocks, heads_local),
        out_shape=jax.ShapeDtypeStruct((1, 1, kept_count * BLK, 2 * HD), jnp.bfloat16),
        in_specs=[pl.BlockSpec(memory_space=pltpu.SMEM)] + [anywhere] * (1 + len(blocks)),
        out_specs=anywhere,
        scratch_shapes=[pltpu.SemaphoreType.DMA],
        compiler_params=pltpu.CompilerParams(vmem_limit_bytes=8 * 1024 * 1024),
        cost_estimate=pl.CostEstimate(flops=10**9, bytes_accessed=0, transcendentals=0),
        name="place",
    )(kept_blocks, after, *blocks)


def attend_kernel(direct, source_blocks, heads_local, which_ref, cos_ref, sin_ref, *refs):
    step_count = cos_ref.shape[0] // 2
    if direct:
        by_offset, parts_refs, attended_ref = refs[:4][::-1], refs[4:8][::-1], refs[8]
        total = sum(ref[...] for ref in parts_refs)
    else:
        parts_ref, blocks_ref, attended_ref, cache_ref, sem, kept = refs
        kept_count = which_ref.shape[1]
        me = lax.axis_index("seq")
        request, local = split_index(me, heads_local)
        head = lax.axis_index("head") * heads_local + local

        def start_copy(k, carry):
            previous, slot = carry
            source, _ = split_index(which_ref[request, k, head], source_blocks)
            slot = jnp.where(source == previous, jnp.minimum(slot + 1, MOST - 1), 0)
            target = kept.at[pl.ds(pl.multiple_of(k * BLK, BLK), BLK)]
            rows = pl.ds(pl.multiple_of(slot * BLK, BLK), BLK)
            pltpu.make_async_copy(blocks_ref.at[source, rows], target, sem).start()
            return source, slot

        lax.fori_loop(0, kept_count, start_copy, (jnp.int32(-1), jnp.int32(0)))
        total = jnp.sum(parts_ref[...], axis=0)
        pltpu.make_async_copy(kept, kept, sem).wait()
        pltpu.make_async_copy(kept, cache_ref.at[0, 0], sem).start()
    query_rows = QPK * step_count
    inverse = lax.rsqrt(total[query_rows + 2 * step_count :] * (1.0 / D) + EPS)
    cosine, sine = cos_ref[...], sin_ref[...]
    query = total[:query_rows].reshape(QPK // 2, 2 * step_count, HD) * inverse[None]
    query = rotate(query, cosine[None], sine[None]).reshape(query_rows, HD).astype(jnp.bfloat16)
    keyval = total[query_rows : query_rows + 2 * step_count] * inverse
    new_key = rotate(keyval, cosine, sine).astype(jnp.bfloat16)
    new_value = jnp.concatenate([keyval[step_count:], keyval[:step_count]], axis=0)
    new_value = new_value.astype(jnp.bfloat16)
    scale = 1.0 / math.sqrt(HD)
    score = lax.dot_general(query, new_key, CONTRACT_LAST, preferred_element_type=jnp.float32)
    row = lax.broadcasted_iota(jnp.int32, score.shape, 0)
    column = lax.broadcasted_iota(jnp.int32, score.shape, 1)
    scores = [jnp.where(column <= split_index(row, step_count)[1], score * scale, -jnp.inf)]
    values = [new_value]

    def add_block(block):
        score = lax.dot_general(
            query, block[:, :HD], CONTRACT_LAST, preferred_element_type=jnp.float32
        )
        scores.append(score * scale)
        values.append(block[:, HD:])

    if direct:
        for offset, ref in enumerate(by_offset):
            add_block(ref[...])
            scores[-1] += which_ref[offset, :1, :]
    else:
        add_block(kept[...])
    row_max = functools.reduce(
        jnp.maximum, [jnp.max(score, axis=1, keepdims=True) for score in scores]
    )
    denominator = jnp.zeros((query_rows, 1), jnp.float32)
    numerator = jnp.zeros((query_rows, HD), jnp.float32)
    for score, value in zip(scores, values):
        weight = jnp.exp(score - row_max)
        denominator += jnp.sum(weight, axis=1, keepdims=True)
        numerator += jnp.dot(
            weight.astype(jnp.bfloat16), value, preferred_element_type=jnp.float32
        )
    attended = (numerator / denominator).astype(jnp.bfloat16)
    if direct:
        attended_ref[...] = attended
    else:
        for i in range(attended_ref.shape[0]):
            attended_ref[i] = attended
        pltpu.make_async_copy(cache_ref, cache_ref, sem).wait()


def attend(which, arrivals, source_blocks, heads_local, step_count, seq_count, direct):
    cosine, sine = rope_tables(source_blocks * BLK * seq_count, step_count)
    shape = (QPK * step_count, HD)
    vmem = pl.BlockSpec(memory_space=pltpu.VMEM)
    if direct:
        shapes = [jax.ShapeDtypeStruct(shape, jnp.bfloat16)]
        out_specs = [vmem]
        scratch = []
    else:
        cache = (1, 1, which.shape[1] * BLK, 2 * HD)
        shapes = [
            jax.ShapeDtypeStruct((seq_count,) + shape, jnp.bfloat16),
            jax.ShapeDtypeStruct(cache, jnp.bfloat16),
        ]
        out_specs = [vmem, pl.BlockSpec(memory_space=pl.ANY)]
        scratch = [pltpu.SemaphoreType.DMA, pltpu.VMEM(cache[2:], jnp.bfloat16)]
    return pl.pallas_call(
        functools.partial(attend_kernel, direct, source_blocks, heads_local),
        out_shape=shapes,
        in_specs=[vmem if direct else pl.BlockSpec(memory_space=pltpu.SMEM)] + [vmem] * (2 + len(arrivals)),
        out_specs=out_specs,
        scratch_shapes=scratch,
        compiler_params=pltpu.CompilerParams(vmem_limit_bytes=16 * 1024 * 1024),
        cost_estimate=pl.CostEstimate(flops=10**10, bytes_accessed=0, transcendentals=0),
        name="attend",
    )(which, jnp.asarray(cosine), jnp.asarray(sine), *arrivals)


def merge_heads(first, second, step_count):
    pieces = []
    for h in range(QPK):
        rows = slice(h * step_count, (h + 1) * step_count)
        pieces.append(jnp.concatenate([first[rows], second[rows]], axis=0))
    return jnp.concatenate(pieces, axis=1).astype(jnp.bfloat16)


def output_same_kernel(w_ref, own_ref, second_ref, out_ref):
    me = lax.axis_index("seq")
    out_ref[...] = output_terms(w_ref, jnp.bitwise_and(me, 1), me >= 2, own_ref, second_ref)


def output_other_kernel(w_ref, above_ref, below_ref, addend_ref, out_ref):
    me = lax.axis_index("seq")
    even = jnp.bitwise_and(me, 1) == 0
    below = below_ref[...].astype(jnp.float32)
    above = above_ref[...].astype(jnp.float32)
    first = jnp.where(even, above, below)
    third = jnp.where(even, below, above)
    terms = output_terms(w_ref, 1 - jnp.bitwise_and(me, 1), me >= 2, first, third)
    out_ref[...] = (terms + addend_ref[...]).astype(out_ref.dtype)


def output_terms(w_ref, local, second, same, other):
    same = same[...].astype(jnp.float32)
    other = other[...].astype(jnp.float32)
    merged = merge_heads(
        jnp.where(second, other, same),
        jnp.where(second, same, other),
        same.shape[0] // QPK,
    )
    depth = w_ref.shape[0] // 2
    weights = w_ref[pl.ds(pl.multiple_of(local * depth, depth), depth), :]
    return jnp.dot(merged, weights, preferred_element_type=jnp.float32)


def output_half(kernel, dtype, w_out, values, *arrivals):
    rows = 2 * values.shape[0] // QPK
    vmem = pl.BlockSpec(memory_space=pltpu.VMEM)
    return pl.pallas_call(
        kernel,
        out_shape=jax.ShapeDtypeStruct((rows, w_out.shape[1]), dtype),
        in_specs=[vmem] * (2 + len(arrivals)),
        out_specs=vmem,
        compiler_params=pltpu.CompilerParams(vmem_limit_bytes=8 * 1024 * 1024),
        cost_estimate=pl.CostEstimate(flops=10**9, bytes_accessed=0, transcendentals=0),
        name="output_half",
    )(w_out, values, *arrivals)


def output_kernel(heads_local, w_ref, gathered_ref, out_ref):
    pair_count, query_rows, _ = gathered_ref.shape
    step_count = query_rows // QPK
    pairs = [gathered_ref[p].astype(jnp.float32) for p in range(pair_count)]
    requests = pair_count // heads_local
    pieces = []
    for l in range(heads_local):
        for h in range(QPK):
            rows = slice(h * step_count, (h + 1) * step_count)
            pieces.append(
                jnp.concatenate(
                    [pairs[r * heads_local + l][rows] for r in range(requests)], axis=0
                )
            )
    merged = jnp.concatenate(pieces, axis=1).astype(jnp.bfloat16)
    out_ref[...] = jnp.dot(merged, w_ref[...], preferred_element_type=jnp.float32)


def output(gathered, w_out, heads_local):
    pair_count, query_rows, _ = gathered.shape
    rows = pair_count // heads_local * (query_rows // QPK)
    vmem = pl.BlockSpec(memory_space=pltpu.VMEM)
    return pl.pallas_call(
        functools.partial(output_kernel, heads_local),
        out_shape=jax.ShapeDtypeStruct((rows, w_out.shape[1]), jnp.float32),
        in_specs=[vmem] * 2,
        out_specs=vmem,
        compiler_params=pltpu.CompilerParams(vmem_limit_bytes=8 * 1024 * 1024),
        name="output_projection",
    )(w_out, gathered)


def shards(source_cache, kept_blocks, new_hidden, norm_gain, w_query, w_keyval, w_out):
    seq_count = lax.axis_size("seq")
    head_count = lax.axis_size("head")
    requests, heads_local, source_tokens, _ = source_cache.shape
    _, step_count, width = new_hidden.shape
    pair_count = requests * heads_local

    kept_blocks = kept_blocks.transpose(0, 2, 1)
    source_blocks = source_tokens // BLK
    direct = is_direct(seq_count) and heads_local == 2 and requests == 2
    weights = (new_hidden, norm_gain, w_query, w_keyval)
    w_out = pltpu.with_memory_space_constraint(w_out, pltpu.VMEM)
    shape = (source_blocks, heads_local, step_count, seq_count, direct)
    if direct:
        partners = range(1, seq_count)
        blocks = list(pick(kept_blocks, source_cache, direct))
        *parts, mask = project(blocks[0], *weights, kept_blocks, source_blocks, direct)
        blocks = [blocks[0]] + [swap(blocks[k], "seq", k) for k in partners]
        parts[3], blocks[3] = lax.optimization_barrier((parts[3], blocks[3]))
        parts = [parts[0]] + [swap(parts[k], "seq", k) for k in partners]
        arrivals = blocks[::-1] + [parts[k] for k in TERM_ORDER]
        (attended,) = attend(mask, arrivals, *shape)
        kept_cache = place(kept_blocks, attended, blocks, source_blocks, heads_local)
        below, second, above = [shift(attended, "seq", step) for step in (1, 2, -1)]
        second, below = lax.optimization_barrier((second, below))
        terms = output_half(output_same_kernel, jnp.float32, w_out, attended, second)
        terms = output_half(output_other_kernel, jnp.bfloat16, w_out, above, below, terms)
    else:
        (blocks,) = pick(kept_blocks, source_cache, direct)
        (parts,) = project(blocks, *weights, kept_blocks, source_blocks, direct)
        arrivals = [all_to_all(parts, "seq"), all_to_all(blocks, "seq")]
        attended, kept_cache = attend(kept_blocks, arrivals, *shape)
        terms = output(all_to_all(attended, "seq"), w_out, heads_local)
    if is_direct(head_count):
        terms = terms.astype(jnp.bfloat16)
        others = [swap(terms, "head", k) for k in range(1, head_count)]
        others[0], others[1], others[2], kept_cache = lax.optimization_barrier((others[0], others[1], others[2], kept_cache))
        own, core, along, across = [t.astype(jnp.float32) for t in [terms] + others]
        summed = (own + core) + (along + across)
    else:
        summed = lax.psum(terms, "head")
    summed = summed.reshape(requests, step_count, width)
    decoded = (new_hidden.astype(jnp.float32) + summed).astype(jnp.bfloat16)
    return (kept_cache, decoded)


def solution(mesh):
    in_specs = (
        P("groups", "head", "seq", None),
        P("groups", None, None),
        P("groups", None, "seq"),
        P("seq"),
        P("seq", "head"),
        P("seq", "head", None),
        P("head", "seq"),
    )
    out_specs = (P("head", ("groups", "seq"), None, None), P("groups", None, "seq"))
    return jax.shard_map(shards, mesh=mesh, in_specs=in_specs, out_specs=out_specs, check_vma=False)
```

```python
import functools
import math

import jax
import jax.numpy as jnp
import numpy as np
from jax import lax
from jax.experimental import pallas as pl
from jax.experimental.pallas import tpu as pltpu
from jax.sharding import PartitionSpec as P

D = 8192
HD = 128
QPK = 8
BLK = 128
MOST = 2
ROPE_BASE = 500000.0
TERM_ORDER = (2, 3, 1, 0)
EPS = 1e-05

CONTRACT_LAST = (((1,), (1,)), ((), ()))


def rope_tables(prompt_length, step_count):
    positions = prompt_length + np.arange(2 * step_count) % step_count
    frequency = ROPE_BASE ** (-np.arange(HD // 2, dtype=np.float64) * 2.0 / HD)
    angles = positions[:, None] * frequency[None, :]
    cosine = np.concatenate([np.cos(angles)] * 2, axis=1)
    sine = np.concatenate([-np.sin(angles), np.sin(angles)], axis=1)
    return cosine.astype(np.float32), sine.astype(np.float32)


def rotate(v, cosine, sine):
    swapped = jnp.concatenate([v[..., HD // 2 :], v[..., : HD // 2]], axis=-1)
    return v * cosine + swapped * sine


def is_direct(count):
    return count == 4


def swap(outgoing, axis, offset):
    count = lax.axis_size(axis)
    return lax.ppermute(outgoing, axis, [(i, i ^ offset) for i in range(count)])


def shift(outgoing, axis, step):
    count = lax.axis_size(axis)
    return lax.ppermute(outgoing, axis, [(i, (i + step) % count) for i in range(count)])


def all_to_all(outgoing, axis):
    return lax.all_to_all(outgoing, axis, split_axis=0, concat_axis=0, tiled=True)


def split_index(index, size):
    if size & (size - 1):
        return lax.div(index, size), lax.rem(index, size)
    shift = jnp.full_like(index, size.bit_length() - 1)
    return lax.shift_right_logical(index, shift), jnp.bitwise_and(index, size - 1)


def picked_rows(kept_ref, cache_shape, pair):
    _, heads_local, source_tokens, _ = cache_shape
    source_blocks = source_tokens // BLK
    kept_count = kept_ref.shape[1]
    first_block = lax.axis_index("seq") * source_blocks
    request, local = split_index(pair, heads_local)
    head = lax.axis_index("head") * heads_local + local

    def count(k, total):
        return total + (kept_ref[request, k, head] < first_block).astype(jnp.int32)

    start = lax.fori_loop(0, kept_count, count, jnp.int32(0), unroll=kept_count <= 8)
    places = []
    for slot in range(MOST):
        rank = jnp.minimum(start + slot, kept_count - 1)
        block = jnp.clip(kept_ref[request, rank, head] - first_block, 0, source_blocks - 1)
        places.append((request, local, pl.ds(pl.multiple_of(block * BLK, BLK), BLK)))
    return places


def pick_near_kernel(offsets, kept_hbm_ref, cache_ref, *refs):
    *outs, kept_ref, cache, kept_sem, sem = refs
    heads_local = cache.shape[1]
    me = lax.axis_index("seq")
    kept_copy = pltpu.make_async_copy(kept_hbm_ref, kept_ref, kept_sem)
    kept_copy.start()

    def pair_copy(pair):
        place = split_index(pair, heads_local)
        return pltpu.make_async_copy(cache_ref.at[place], cache.at[place], sem.at[pair])

    copies = {offset: pair_copy(jnp.bitwise_xor(me, offset)) for offset in offsets}
    for offset in offsets:
        copies[offset].start()
    kept_copy.wait()
    for offset in offsets:
        places = picked_rows(kept_ref, cache.shape, jnp.bitwise_xor(me, offset))
        copies[offset].wait()
        for slot, (request, local, rows) in enumerate(places):
            outs[offsets.index(offset)][slot * BLK : (slot + 1) * BLK, :] = cache[request, local, rows, :]


def pick_all_kernel(kept_hbm_ref, cache_ref, out_ref, kept_ref, sem):
    pltpu.sync_copy(kept_hbm_ref, kept_ref)

    def pair_body(pair, carry):
        for slot, place in enumerate(picked_rows(kept_ref, cache_ref.shape, pair)):
            pltpu.make_async_copy(
                cache_ref.at[place], out_ref.at[pair, pl.ds(slot * BLK, BLK)], sem
            ).start()
        return carry

    lax.fori_loop(0, out_ref.shape[0], pair_body, 0)
    pltpu.make_async_copy(out_ref, out_ref, sem).wait()


def pick(kept_blocks, source_cache, offsets):
    requests, heads_local, _, row_width = source_cache.shape
    pair_count = requests * heads_local
    block = (MOST * BLK, row_width)
    kept_scratch = pltpu.SMEM(kept_blocks.shape, jnp.int32)
    if offsets:
        shapes = [jax.ShapeDtypeStruct(block, jnp.bfloat16)] * len(offsets)
        scratch = [
            kept_scratch,
            pltpu.VMEM(source_cache.shape, jnp.bfloat16),
            pltpu.SemaphoreType.DMA,
            pltpu.SemaphoreType.DMA((pair_count,)),
        ]
    else:
        shapes = [jax.ShapeDtypeStruct((pair_count,) + block, jnp.bfloat16)]
        scratch = [kept_scratch, pltpu.SemaphoreType.DMA]
    return pl.pallas_call(
        functools.partial(pick_near_kernel, offsets) if offsets else pick_all_kernel,
        out_shape=shapes,
        in_specs=[pl.BlockSpec(memory_space=pl.ANY)] * 2,
        out_specs=[pl.BlockSpec(memory_space=pltpu.VMEM)] * len(shapes),
        scratch_shapes=scratch,
        compiler_params=pltpu.CompilerParams(vmem_limit_bytes=8 * 1024 * 1024),
        cost_estimate=pl.CostEstimate(
            flops=10**6 if offsets == (0,) else 10**10, bytes_accessed=0, transcendentals=0
        ),
        name="pick_blocks",
    )(
        pltpu.with_memory_space_constraint(kept_blocks, pltpu.HBM),
        pltpu.with_memory_space_constraint(source_cache, pltpu.HBM),
    )


def interleave(rows):
    count, width = rows.shape
    chunks = width // HD
    stacked = jnp.concatenate(
        [rows[:, c * HD : (c + 1) * HD] for c in range(chunks)], axis=0
    ).astype(jnp.bfloat16)
    source = lax.broadcasted_iota(jnp.int32, (HD, 4 * HD), 0)
    target = lax.broadcasted_iota(jnp.int32, (HD, 4 * HD), 1)
    place = jnp.where(target < 2 * HD, 2 * source, 2 * source + 1 + 2 * HD)
    spread = (place == target).astype(jnp.bfloat16)
    wide = jnp.dot(stacked, spread, preferred_element_type=jnp.float32)
    return [
        jnp.concatenate(
            [
                wide[c * count : (c + 1) * count, : 2 * HD],
                wide[c * count : (c + 1) * count, 2 * HD :],
            ],
            axis=0,
        ).astype(jnp.bfloat16)
        for c in range(chunks)
    ]


def project_kernel(direct, source_blocks, after_ref, hidden_ref, gain_ref, wq_ref, wkv_ref, *refs):
    del after_ref
    outs = refs
    if direct:
        kept_ref, *outs, mask_ref = refs
    requests, step_count, width = hidden_ref.shape
    heads_local = wkv_ref.shape[1]
    row_count = requests * step_count
    me = lax.axis_index("seq")
    hidden = jnp.concatenate(
        [hidden_ref[r].astype(jnp.float32) for r in range(requests)], axis=0
    )
    square = jnp.sum(hidden * hidden, axis=1, keepdims=True)
    gain = gain_ref[...].astype(jnp.float32)
    scaled = jnp.concatenate(
        [hidden[:, c * HD : (c + 1) * HD] * gain[c : c + 1] for c in range(width // HD)], axis=1
    ).astype(jnp.bfloat16)
    query = jnp.dot(scaled, wq_ref[...], preferred_element_type=jnp.float32)
    keyval = jnp.zeros((heads_local * row_count, wkv_ref.shape[2]), jnp.float32)
    for c, spread in enumerate(interleave(scaled.astype(jnp.float32))):
        alternate = wkv_ref[c * HD : (c + 1) * HD].reshape(heads_local * HD, wkv_ref.shape[2])
        keyval += jnp.dot(spread, alternate, preferred_element_type=jnp.float32)

    def pieces_of(r, l):
        steps = slice(r * step_count, (r + 1) * step_count)
        square_rows = jnp.broadcast_to(square[steps], (step_count, HD))
        own = keyval[l * row_count + r * step_count : l * row_count + (r + 1) * step_count]
        heads = [query[steps, (l * QPK + h) * HD : (l * QPK + h + 1) * HD] for h in range(QPK)]
        return heads + [own[:, :HD], own[:, HD:], square_rows, square_rows]

    def write_pair(out_ref, pieces):
        for j, piece in enumerate(pieces):
            out_ref[j * step_count : (j + 1) * step_count, :] = piece

    for r in range(requests):
        for l in range(heads_local):
            pair = r * heads_local + l
            pieces = pieces_of(r, l)
            if not direct:
                write_pair(outs[0].at[pair], pieces)
                continue
            for offset, out_ref in enumerate(outs):
                pl.when(jnp.bitwise_xor(me, offset) == pair)(
                    functools.partial(write_pair, out_ref, pieces)
                )
    if direct:
        request, local = split_index(me, heads_local)
        head = lax.axis_index("head") * heads_local + local
        kept = jnp.where(request == 0, kept_ref[0], kept_ref[1]).astype(jnp.float32)
        lane = lax.broadcasted_iota(jnp.int32, kept.shape, 1)
        kept = jnp.sum(jnp.where(lane == head, kept, 0.0), axis=1, keepdims=True)
        column = lax.broadcasted_iota(jnp.int32, mask_ref.shape[1:], 1).astype(jnp.float32)
        for offset in range(mask_ref.shape[0]):
            first_block = (jnp.bitwise_xor(me, offset) * source_blocks).astype(jnp.float32)
            here = (kept >= first_block) & (kept < first_block + source_blocks)
            filled = jnp.sum(jnp.where(here, float(BLK), 0.0), axis=0, keepdims=True)
            mask_ref[offset] = jnp.where(column < filled, 0.0, -jnp.inf)


def project(after, new_hidden, norm_gain, w_query, w_keyval, kept_blocks, source_blocks, direct):
    requests, step_count, width = new_hidden.shape
    pair_count = requests * w_keyval.shape[1]
    terms = ((QPK + 4) * step_count, HD)
    if direct:
        shapes = [jax.ShapeDtypeStruct(terms, jnp.float32)] * pair_count
        shapes.append(jax.ShapeDtypeStruct((pair_count, 8, MOST * BLK), jnp.float32))
    else:
        shapes = [jax.ShapeDtypeStruct((pair_count,) + terms, jnp.float32)]
    vmem = pl.BlockSpec(memory_space=pltpu.VMEM)
    weights = w_query.size + w_keyval.size
    return pl.pallas_call(
        functools.partial(project_kernel, direct, source_blocks),
        out_shape=shapes,
        in_specs=[pl.BlockSpec(memory_space=pl.ANY)] + [vmem] * (4 + direct),
        out_specs=[vmem] * len(shapes),
        compiler_params=pltpu.CompilerParams(vmem_limit_bytes=8 * 1024 * 1024),
        cost_estimate=pl.CostEstimate(
            flops=2 * requests * step_count * weights,
            bytes_accessed=2 * weights,
            transcendentals=0,
        ),
        name="project",
    )(
        after,
        new_hidden,
        norm_gain.reshape(width // HD, HD),
        pltpu.with_memory_space_constraint(w_query, pltpu.VMEM),
        pltpu.with_memory_space_constraint(w_keyval, pltpu.VMEM),
        *([kept_blocks] if direct else []),
    )


def place_kernel(source_blocks, heads_local, kept_ref, after_ref, *refs):
    del after_ref
    *by_offset, cache_ref, sem = refs
    me = lax.axis_index("seq")
    request, local = split_index(me, heads_local)
    head = lax.axis_index("head") * heads_local + local
    previous, slot = jnp.int32(-1), jnp.int32(0)
    for k in range(kept_ref.shape[1]):
        source, _ = split_index(kept_ref[request, k, head], source_blocks)
        slot = jnp.where(source == previous, jnp.minimum(slot + 1, MOST - 1), 0)
        previous = source
        rows = pl.ds(pl.multiple_of(slot * BLK, BLK), BLK)
        target = cache_ref.at[0, 0, pl.ds(k * BLK, BLK)]
        for offset, ref in enumerate(by_offset):
            pl.when(jnp.bitwise_xor(me, offset) == source)(
                pltpu.make_async_copy(ref.at[rows], target, sem).start
            )
    pltpu.make_async_copy(cache_ref, cache_ref, sem).wait()


def place(kept_blocks, after, blocks, source_blocks, heads_local):
    kept_count = kept_blocks.shape[1]
    anywhere = pl.BlockSpec(memory_space=pl.ANY)
    return pl.pallas_call(
        functools.partial(place_kernel, source_blocks, heads_local),
        out_shape=jax.ShapeDtypeStruct((1, 1, kept_count * BLK, 2 * HD), jnp.bfloat16),
        in_specs=[pl.BlockSpec(memory_space=pltpu.SMEM)] + [anywhere] * (1 + len(blocks)),
        out_specs=anywhere,
        scratch_shapes=[pltpu.SemaphoreType.DMA],
        compiler_params=pltpu.CompilerParams(vmem_limit_bytes=8 * 1024 * 1024),
        cost_estimate=pl.CostEstimate(flops=10**9, bytes_accessed=0, transcendentals=0),
        name="place",
    )(kept_blocks, after, *blocks)


def attend_kernel(direct, source_blocks, heads_local, which_ref, cos_ref, sin_ref, *refs):
    step_count = cos_ref.shape[0] // 2
    if direct:
        by_offset, parts_refs, attended_ref = refs[:4][::-1], refs[4:8][::-1], refs[8]
        total = sum(ref[...] for ref in parts_refs)
    else:
        parts_ref, blocks_ref, attended_ref, cache_ref, sem, kept = refs
        kept_count = which_ref.shape[1]
        me = lax.axis_index("seq")
        request, local = split_index(me, heads_local)
        head = lax.axis_index("head") * heads_local + local

        def start_copy(k, carry):
            previous, slot = carry
            source, _ = split_index(which_ref[request, k, head], source_blocks)
            slot = jnp.where(source == previous, jnp.minimum(slot + 1, MOST - 1), 0)
            target = kept.at[pl.ds(pl.multiple_of(k * BLK, BLK), BLK)]
            rows = pl.ds(pl.multiple_of(slot * BLK, BLK), BLK)
            pltpu.make_async_copy(blocks_ref.at[source, rows], target, sem).start()
            return source, slot

        lax.fori_loop(0, kept_count, start_copy, (jnp.int32(-1), jnp.int32(0)))
        total = jnp.sum(parts_ref[...], axis=0)
        pltpu.make_async_copy(kept, kept, sem).wait()
        pltpu.make_async_copy(kept, cache_ref.at[0, 0], sem).start()
    query_rows = QPK * step_count
    inverse = lax.rsqrt(total[query_rows + 2 * step_count :] * (1.0 / D) + EPS)
    cosine, sine = cos_ref[...], sin_ref[...]
    query = total[:query_rows].reshape(QPK // 2, 2 * step_count, HD) * inverse[None]
    query = rotate(query, cosine[None], sine[None]).reshape(query_rows, HD).astype(jnp.bfloat16)
    keyval = total[query_rows : query_rows + 2 * step_count] * inverse
    new_key = rotate(keyval, cosine, sine).astype(jnp.bfloat16)
    new_value = jnp.concatenate([keyval[step_count:], keyval[:step_count]], axis=0)
    new_value = new_value.astype(jnp.bfloat16)
    scale = 1.0 / math.sqrt(HD)
    score = lax.dot_general(query, new_key, CONTRACT_LAST, preferred_element_type=jnp.float32)
    row = lax.broadcasted_iota(jnp.int32, score.shape, 0)
    column = lax.broadcasted_iota(jnp.int32, score.shape, 1)
    scores = [jnp.where(column <= split_index(row, step_count)[1], score * scale, -jnp.inf)]
    values = [new_value]

    def add_block(block):
        score = lax.dot_general(
            query, block[:, :HD], CONTRACT_LAST, preferred_element_type=jnp.float32
        )
        scores.append(score * scale)
        values.append(block[:, HD:])

    if direct:
        for offset, ref in enumerate(by_offset):
            add_block(ref[...])
            scores[-1] += which_ref[offset, :1, :]
    else:
        add_block(kept[...])
    row_max = functools.reduce(
        jnp.maximum, [jnp.max(score, axis=1, keepdims=True) for score in scores]
    )
    denominator = jnp.zeros((query_rows, 1), jnp.float32)
    numerator = jnp.zeros((query_rows, HD), jnp.float32)
    for score, value in zip(scores, values):
        weight = jnp.exp(score - row_max)
        denominator += jnp.sum(weight, axis=1, keepdims=True)
        numerator += jnp.dot(
            weight.astype(jnp.bfloat16), value, preferred_element_type=jnp.float32
        )
    attended = (numerator / denominator).astype(jnp.bfloat16)
    if direct:
        attended_ref[...] = attended
    else:
        for i in range(attended_ref.shape[0]):
            attended_ref[i] = attended
        pltpu.make_async_copy(cache_ref, cache_ref, sem).wait()


def attend(which, arrivals, source_blocks, heads_local, step_count, seq_count, direct):
    cosine, sine = rope_tables(source_blocks * BLK * seq_count, step_count)
    shape = (QPK * step_count, HD)
    vmem = pl.BlockSpec(memory_space=pltpu.VMEM)
    if direct:
        shapes = [jax.ShapeDtypeStruct(shape, jnp.bfloat16)]
        out_specs = [vmem]
        scratch = []
    else:
        cache = (1, 1, which.shape[1] * BLK, 2 * HD)
        shapes = [
            jax.ShapeDtypeStruct((seq_count,) + shape, jnp.bfloat16),
            jax.ShapeDtypeStruct(cache, jnp.bfloat16),
        ]
        out_specs = [vmem, pl.BlockSpec(memory_space=pl.ANY)]
        scratch = [pltpu.SemaphoreType.DMA, pltpu.VMEM(cache[2:], jnp.bfloat16)]
    return pl.pallas_call(
        functools.partial(attend_kernel, direct, source_blocks, heads_local),
        out_shape=shapes,
        in_specs=[vmem if direct else pl.BlockSpec(memory_space=pltpu.SMEM)] + [vmem] * (2 + len(arrivals)),
        out_specs=out_specs,
        scratch_shapes=scratch,
        compiler_params=pltpu.CompilerParams(vmem_limit_bytes=16 * 1024 * 1024),
        cost_estimate=pl.CostEstimate(flops=10**10, bytes_accessed=0, transcendentals=0),
        name="attend",
    )(which, jnp.asarray(cosine), jnp.asarray(sine), *arrivals)


def merge_heads(first, second, step_count):
    pieces = []
    for h in range(QPK):
        rows = slice(h * step_count, (h + 1) * step_count)
        pieces.append(jnp.concatenate([first[rows], second[rows]], axis=0))
    return jnp.concatenate(pieces, axis=1).astype(jnp.bfloat16)


def output_same_kernel(w_ref, own_ref, second_ref, out_ref):
    me = lax.axis_index("seq")
    out_ref[...] = output_terms(w_ref, jnp.bitwise_and(me, 1), me >= 2, own_ref, second_ref)


def output_other_kernel(w_ref, above_ref, below_ref, addend_ref, out_ref):
    me = lax.axis_index("seq")
    even = jnp.bitwise_and(me, 1) == 0
    below = below_ref[...].astype(jnp.float32)
    above = above_ref[...].astype(jnp.float32)
    first = jnp.where(even, above, below)
    third = jnp.where(even, below, above)
    terms = output_terms(w_ref, 1 - jnp.bitwise_and(me, 1), me >= 2, first, third)
    out_ref[...] = (terms + addend_ref[...]).astype(out_ref.dtype)


def output_terms(w_ref, local, second, same, other):
    same = same[...].astype(jnp.float32)
    other = other[...].astype(jnp.float32)
    merged = merge_heads(
        jnp.where(second, other, same),
        jnp.where(second, same, other),
        same.shape[0] // QPK,
    )
    depth = w_ref.shape[0] // 2
    weights = w_ref[pl.ds(pl.multiple_of(local * depth, depth), depth), :]
    return jnp.dot(merged, weights, preferred_element_type=jnp.float32)


def output_half(kernel, dtype, w_out, values, *arrivals):
    rows = 2 * values.shape[0] // QPK
    vmem = pl.BlockSpec(memory_space=pltpu.VMEM)
    return pl.pallas_call(
        kernel,
        out_shape=jax.ShapeDtypeStruct((rows, w_out.shape[1]), dtype),
        in_specs=[vmem] * (2 + len(arrivals)),
        out_specs=vmem,
        compiler_params=pltpu.CompilerParams(vmem_limit_bytes=8 * 1024 * 1024),
        cost_estimate=pl.CostEstimate(flops=10**9, bytes_accessed=0, transcendentals=0),
        name="output_half",
    )(w_out, values, *arrivals)


def output_kernel(heads_local, w_ref, gathered_ref, out_ref):
    pair_count, query_rows, _ = gathered_ref.shape
    step_count = query_rows // QPK
    pairs = [gathered_ref[p].astype(jnp.float32) for p in range(pair_count)]
    requests = pair_count // heads_local
    pieces = []
    for l in range(heads_local):
        for h in range(QPK):
            rows = slice(h * step_count, (h + 1) * step_count)
            pieces.append(
                jnp.concatenate(
                    [pairs[r * heads_local + l][rows] for r in range(requests)], axis=0
                )
            )
    merged = jnp.concatenate(pieces, axis=1).astype(jnp.bfloat16)
    out_ref[...] = jnp.dot(merged, w_ref[...], preferred_element_type=jnp.float32)


def output(gathered, w_out, heads_local):
    pair_count, query_rows, _ = gathered.shape
    rows = pair_count // heads_local * (query_rows // QPK)
    vmem = pl.BlockSpec(memory_space=pltpu.VMEM)
    return pl.pallas_call(
        functools.partial(output_kernel, heads_local),
        out_shape=jax.ShapeDtypeStruct((rows, w_out.shape[1]), jnp.float32),
        in_specs=[vmem] * 2,
        out_specs=vmem,
        compiler_params=pltpu.CompilerParams(vmem_limit_bytes=8 * 1024 * 1024),
        name="output_projection",
    )(w_out, gathered)


def shards(source_cache, kept_blocks, new_hidden, norm_gain, w_query, w_keyval, w_out):
    seq_count = lax.axis_size("seq")
    head_count = lax.axis_size("head")
    requests, heads_local, source_tokens, _ = source_cache.shape
    _, step_count, width = new_hidden.shape
    pair_count = requests * heads_local

    kept_blocks = kept_blocks.transpose(0, 2, 1)
    source_blocks = source_tokens // BLK
    direct = is_direct(seq_count) and heads_local == 2 and requests == 2
    weights = (new_hidden, norm_gain, w_query, w_keyval)
    w_out = pltpu.with_memory_space_constraint(w_out, pltpu.VMEM)
    shape = (source_blocks, heads_local, step_count, seq_count, direct)
    if direct:
        partners = range(1, seq_count)
        third, second, first = pick(kept_blocks, source_cache, (3, 2, 1))
        *parts, mask = project(first, *weights, kept_blocks, source_blocks, direct)
        later, parts[0] = lax.optimization_barrier((kept_blocks, parts[0]))
        (own,) = pick(later, source_cache, (0,))
        blocks = [own, first, second, third]
        blocks = [blocks[0]] + [swap(blocks[k], "seq", k) for k in partners]
        parts[1], blocks[3] = lax.optimization_barrier((parts[1], blocks[3]))
        parts = [parts[0]] + [swap(parts[k], "seq", k) for k in partners]
        arrivals = blocks[::-1] + [parts[k] for k in TERM_ORDER]
        (attended,) = attend(mask, arrivals, *shape)
        kept_cache = place(kept_blocks, attended, blocks, source_blocks, heads_local)
        below, second, above = [shift(attended, "seq", step) for step in (1, 2, -1)]
        second, below = lax.optimization_barrier((second, below))
        terms = output_half(output_same_kernel, jnp.float32, w_out, attended, second)
        terms = output_half(output_other_kernel, jnp.bfloat16, w_out, above, below, terms)
    else:
        (blocks,) = pick(kept_blocks, source_cache, ())
        (parts,) = project(blocks, *weights, kept_blocks, source_blocks, direct)
        arrivals = [all_to_all(parts, "seq"), all_to_all(blocks, "seq")]
        attended, kept_cache = attend(kept_blocks, arrivals, *shape)
        terms = output(all_to_all(attended, "seq"), w_out, heads_local)
    if is_direct(head_count):
        terms = terms.astype(jnp.bfloat16)
        others = [swap(terms, "head", k) for k in range(1, head_count)]
        others[0], others[1], others[2], kept_cache = lax.optimization_barrier((others[0], others[1], others[2], kept_cache))
        own, core, along, across = [t.astype(jnp.float32) for t in [terms] + others]
        summed = (own + core) + (along + across)
    else:
        summed = lax.psum(terms, "head")
    summed = summed.reshape(requests, step_count, width)
    decoded = (new_hidden.astype(jnp.float32) + summed).astype(jnp.bfloat16)
    return (kept_cache, decoded)


def solution(mesh):
    in_specs = (
        P("groups", "head", "seq", None),
        P("groups", None, None),
        P("groups", None, "seq"),
        P("seq"),
        P("seq", "head"),
        P("seq", "head", None),
        P("head", "seq"),
    )
    out_specs = (P("head", ("groups", "seq"), None, None), P("groups", None, "seq"))
    return jax.shard_map(shards, mesh=mesh, in_specs=in_specs, out_specs=out_specs, check_vma=False)
```
